32 devices in a mesh: tx: 8 (over z, x), ty: 4 (over y, core).
Axes of the slice: x: 2, y: 2, z: 4, core: 2. Of those that a mesh axis runs over, the one named last changes fastest.
Arguments:
- sar_image: bfloat16 [2, 2048, 512], P(None, ('tx', 'ty')), may hold values from -6 to 6
- kernel_first: bfloat16 [16, 2, 3, 3], replicated, may hold values from -2 to 2
- kernel_second: bfloat16 [16, 16, 3, 3], replicated, may hold values from -0.75 to 0.75
- kernel_third: bfloat16 [16, 16, 3, 3], replicated, may hold values from -0.75 to 0.75
- kernel_last: bfloat16 [1, 16, 3, 3], replicated, may hold values from -1 to 1
- geo_weight: float32 [2048, 512], P(('tx', 'ty')), may hold values from 0.25 to 1
- cell_index: int32 [2048, 512], P(('tx', 'ty')), may hold values from 0 to 511
- block_tile: int32 [2048, 1], P(('tx', 'ty')), may hold values from 0 to 31; in each aligned block of 64 rows (0 to 63, 64 to 127, ...) at most 4 rows name the same one
- block_row: int32 [2048, 1], P(('tx', 'ty')), may hold values from 0 to 254
- depth: float32 [2048, 1024], P('tx', 'ty'), may hold values from 0.1 to 1
- slope: float32 [2048, 1024], P('tx', 'ty'), may hold values from 0.01 to 1
- flow_dir: int32 [2048, 1024], P('tx', 'ty'), may hold values from 0 to 7
- rain: float32 [2048, 1024], P('tx', 'ty'), may hold values from 0 to 0.1
Outputs:
- water_fraction: bfloat16 [2048, 512], P(('tx', 'ty'))
- level: float32 [2048, 1024], P('tx', 'ty')
The draws below stay inside these ranges and needn't reach their ends.
Inputs may be any that keep to these rules, and one draw needn't show every extreme that they name: `block_tile`: in the rows of one device no tile is named more than 4 times, a bound that some block reaches.
All inputs are finite; a program needn't handle non-finite values.
Results may differ from the reference program's by a relative error of at most 0.003.
The reference program's roundings to bfloat16 on the way count: a program that leaves them out, or rounds other values in their place, can miss the bound.
Values may be sent and summed in bfloat16 or wider, within the bound.
No kernel may reach another device: no remote copies, remote signals or barrier semaphores. Data moves between devices by JAX's collectives and lax.ppermute only.
A program may use at most 128 MiB of HBM per device.

```python
import math
import jax
import jax.numpy as jnp
import numpy as np
from jax import lax

POLAR = 2
CHANNELS = 16
AZ_DEV = 64
RANGE_PX = 512
TILE_ROWS = 256
TILE_COLS = 256
WIN_ROWS = 2
SUBSTEPS = 8
AZ_ROWS = 2048
WIN_CELLS = 512
CAPACITY = 4
MAP_ROWS = 2048
MAP_COLS = 1024
N_TY = 4
DEVICES = 32


def place_ends(entries, own_key, least, largest):
    spot = [jax.random.randint(jax.random.fold_in(own_key, axis), (), 0, length) for axis, length in enumerate(entries.shape)]
    widest = entries.shape.index(max(entries.shape))
    neighbour = spot[:widest] + [(spot[widest] + 1) % entries.shape[widest]] + spot[widest + 1:]
    return entries.at[tuple(spot)].set(least).at[tuple(neighbour)].set(largest)


def block_levels(own_key, dims, split, low, top_value):
    factor_of = 1.0
    for dim, parts in split:
        draws = jax.random.uniform(jax.random.fold_in(jax.random.fold_in(own_key, 6), dim), (parts,), jnp.float32, low / len(split), top_value / len(split))
        factor_of = factor_of * jnp.repeat(jnp.exp(draws), dims[dim] // parts).reshape((-1,) + (1,) * (len(dims) - 1 - dim))
    return factor_of


def assign_block(rng, own, number, rows, amount, top, bound, skew):
    order = jax.random.permutation(rng, amount)
    packed, ordinary = load_shares(amount, rows * top, bound, skew, True), load_shares(amount, rows * top, bound, skew, False)
    places = jnp.arange(amount)

    def named(sizes, turn):
        used = int((sizes > 0).sum())
        fixed = max(1, used // 4)
        shifted = fixed + (places - fixed + turn * (used - fixed)) % max(1, amount - fixed)
        return jnp.zeros((amount,), jnp.int32).at[order[jnp.where(places < fixed, places, shifted)]].set(jnp.asarray(sizes, jnp.int32))

    sizes = jnp.where(number % 4 == 0, named(packed, number // 4), named(ordinary, number - number // 4 - 1))
    mixed = jax.random.permutation(jax.random.fold_in(own, 3), amount)
    donor, sink = mixed[0:amount // 2 * 2:2], mixed[1:amount // 2 * 2:2]
    room = jnp.minimum(sizes[donor] - 1, bound - sizes[sink]) // 2
    room = jnp.where((donor == order[0]) | (sink == order[0]) | (sizes[sink] == 0), 0, jnp.maximum(room, 0))
    shifted = jax.random.randint(jax.random.fold_in(own, 4), (amount // 2,), 0, 1 << 20) % (room + 1)
    sizes = sizes.at[donor].add(-shifted).at[sink].add(shifted)
    items = jnp.searchsorted(jnp.cumsum(sizes), jnp.arange(rows * top), side="right").astype(jnp.int32)
    listing = items.reshape(top, rows).T
    listing = listing[jax.random.permutation(jax.random.fold_in(own, 1), rows)]
    turn = jax.random.randint(jax.random.fold_in(own, 2), (rows, 1), 0, top)
    return jnp.take_along_axis(listing, (jnp.arange(top)[None, :] + turn) % top, axis=1)


def load_shares(count, total, limit, skew, full):
    weights = [(1 << 20) // math.isqrt(rank ** skew) + 1 for rank in range(1, count + 1)]
    largest = limit if full else min(limit, max(-(-total // count), total * weights[0] // sum(weights)))
    least = 1 if total - largest >= count - 1 else 0
    holding, surplus = [largest] + [least] * (count - 1), total - largest - least * (count - 1)
    while surplus > 0:
        movable = [i for i in range(1, count) if holding[i] < largest] or [i for i in range(1, count) if holding[i] < limit]
        mass, budget = sum([weights[i] for i in movable]), surplus
        for i in movable:
            addition = min(limit - holding[i], max(1, budget * weights[i] // mass), surplus)
            holding[i] = holding[i] + addition
            surplus = surplus - addition
    return np.array(holding)


def centred(stream_key, shape, spread, most, shards=(), kind=jnp.bfloat16):
    drawn = spread * jax.random.normal(stream_key, shape, jnp.float32)
    if shards:
        drawn = drawn * block_levels(stream_key, shape, shards, -0.22, 0.18)
    return jnp.clip(drawn, -most, most).astype(kind)


def setup_inputs(seed: int = 0) -> dict:
    seeds = jax.random.split(jax.random.key(seed), 14)
    sar_image = centred(seeds[0], (POLAR, AZ_ROWS, RANGE_PX), 1.0, 6.0, ((1, 32),))
    kernel_first = centred(seeds[1], (CHANNELS, POLAR, 3, 3), (9 * POLAR // 2) ** -0.5, 2.0)
    kernel_second = centred(seeds[2], (CHANNELS, CHANNELS, 3, 3), (9 * CHANNELS // 2) ** -0.5, 0.75)
    kernel_third = centred(seeds[3], (CHANNELS, CHANNELS, 3, 3), (9 * CHANNELS // 2) ** -0.5, 0.75)
    kernel_last = centred(seeds[4], (1, CHANNELS, 3, 3), (9 * CHANNELS // 4) ** -0.5, 1.0)
    geo_weight = jnp.clip(0.25 + 0.75 * jax.random.uniform(seeds[5], (AZ_ROWS, RANGE_PX), jnp.float32) ** block_levels(seeds[5], (AZ_ROWS, RANGE_PX), ((0, 32),), -0.2, 0.2), 0.25, 1.0)
    cell_index = place_ends(jax.random.randint(seeds[6], (AZ_ROWS, RANGE_PX), 0, WIN_CELLS), jax.random.fold_in(seeds[6], 1), 0, WIN_CELLS - 1).astype(jnp.int32)
    block_tile_keys = jax.random.split(jax.random.fold_in(seeds[7], 1), AZ_ROWS // AZ_DEV)
    block_tile_turns = jax.random.permutation(jax.random.fold_in(seeds[7], 3), AZ_ROWS // AZ_DEV)
    block_tile = jax.vmap(lambda own, number: assign_block(jax.random.fold_in(seeds[7], 2), own, number, AZ_DEV, DEVICES, 1, CAPACITY, 2))(block_tile_keys, block_tile_turns).reshape((AZ_ROWS, 1))
    block_row = place_ends(jax.random.randint(seeds[8], (AZ_ROWS, 1), 0, TILE_ROWS - WIN_ROWS + 1), jax.random.fold_in(seeds[8], 1), 0, TILE_ROWS - WIN_ROWS).astype(jnp.int32)
    depth = jnp.clip(0.1 + 0.9 * jax.random.uniform(seeds[9], (MAP_ROWS, MAP_COLS), jnp.float32) ** block_levels(seeds[9], (MAP_ROWS, MAP_COLS), ((0, 8), (1, 4)), -0.2, 0.2), 0.1, 1.0)
    slope = jnp.clip(jnp.exp(math.log(1.0) - 4.6051702 * jax.random.uniform(seeds[10], (MAP_ROWS, MAP_COLS), jnp.float32) ** block_levels(seeds[10], (MAP_ROWS, MAP_COLS), ((0, 8), (1, 4)), -0.2, 0.2)), 0.01, 1.0)
    flow_dir = place_ends(jax.random.randint(seeds[11], (MAP_ROWS, MAP_COLS), 0, 8), jax.random.fold_in(seeds[11], 1), 0, 7).astype(jnp.int32)
    rain = jnp.clip(0.1 * jax.random.uniform(seeds[12], (MAP_ROWS, MAP_COLS), jnp.float32) ** block_levels(seeds[12], (MAP_ROWS, MAP_COLS), ((0, 8), (1, 4)), -0.2, 0.2), 0.0, 0.1)
    return {"sar_image": sar_image, "kernel_first": kernel_first, "kernel_second": kernel_second, "kernel_third": kernel_third, "kernel_last": kernel_last, "geo_weight": geo_weight, "cell_index": cell_index, "block_tile": block_tile, "block_row": block_row, "depth": depth, "slope": slope, "flow_dir": flow_dir, "rain": rain}


wet_depth = 0.5
runoff_coef = 0.25
neighbour_steps = ((-1, -1), (-1, 0), (-1, 1), (0, -1), (0, 1), (1, -1), (1, 0), (1, 1))

def conv_rows(activation, kernel):
    result = lax.conv_general_dilated(activation[None], kernel, (1, 1), ((0, 0), (1, 1)), dimension_numbers=('NCHW', 'OIHW', 'NCHW'), preferred_element_type=jnp.float32)
    return result[0]

def swath_block(padded_image, start, kernels):
    activation = lax.dynamic_slice_in_dim(padded_image, start, AZ_DEV + 8, 1)
    for layer_no in range(3):
        result = conv_rows(activation, kernels[layer_no])
        rowpos = start - 4 + layer_no + 1 + jnp.arange(result.shape[1], dtype=jnp.int32)
        inside = ((rowpos >= 0) & (rowpos < AZ_ROWS)).astype(jnp.float32)
        activation = (jnp.maximum(result, 0.0) * inside[None, :, None]).astype(jnp.bfloat16)
    logit = conv_rows(activation, kernels[3])
    return jax.nn.sigmoid(logit[0]).astype(jnp.bfloat16)

def water_map(sar_image, kernels):
    padded_image = jnp.pad(sar_image, ((0, 0), (4, 4), (0, 0)))
    starts = jnp.arange(AZ_ROWS // AZ_DEV, dtype=jnp.int32) * AZ_DEV

    def one_block(start):
        return swath_block(padded_image, start, kernels)
    blocks = lax.map(one_block, starts)
    return blocks.reshape(AZ_ROWS, RANGE_PX)

def regrid(fraction, geo_weight, cell_index, block_tile, block_row):
    tile_row = block_tile[:, 0] // N_TY
    tile_col = block_tile[:, 0] % N_TY
    map_row = (tile_row * TILE_ROWS + block_row[:, 0])[:, None] + cell_index // TILE_COLS
    map_col = (tile_col * TILE_COLS)[:, None] + cell_index % TILE_COLS
    flat_ids = (map_row * MAP_COLS + map_col).reshape(-1)
    weighted = fraction.astype(jnp.float32) * geo_weight
    observed = jax.ops.segment_sum(weighted.reshape(-1), flat_ids, MAP_ROWS * MAP_COLS)
    covered = jax.ops.segment_sum(geo_weight.reshape(-1), flat_ids, MAP_ROWS * MAP_COLS)
    return (observed.reshape(MAP_ROWS, MAP_COLS), covered.reshape(MAP_ROWS, MAP_COLS))

def inflow(runoff_pad, dir_pad, extent_rows, extent_cols):
    inflow_sum = jnp.zeros((extent_rows, extent_cols), jnp.float32)
    for dir_code, (row_step, col_step) in enumerate(neighbour_steps):
        source_runoff = runoff_pad[1 - row_step:1 - row_step + extent_rows, 1 - col_step:1 - col_step + extent_cols]
        source_dir = dir_pad[1 - row_step:1 - row_step + extent_rows, 1 - col_step:1 - col_step + extent_cols]
        inflow_sum = inflow_sum + jnp.where(source_dir == dir_code, source_runoff, 0.0)
    return inflow_sum

def reference(sar_image, kernel_first, kernel_second, kernel_third, kernel_last, geo_weight, cell_index, block_tile, block_row, depth, slope, flow_dir, rain):
    kernels = (kernel_first, kernel_second, kernel_third, kernel_last)
    fraction = water_map(sar_image, kernels)
    observed, covered = regrid(fraction, geo_weight, cell_index, block_tile, block_row)
    wet = depth / (depth + wet_depth)
    innovation = (observed - covered * wet) / (covered + 1.0)
    level = depth * jnp.exp(innovation)
    conveyance = runoff_coef * jnp.sqrt(slope)
    dir_pad = jnp.pad(flow_dir, 1)
    for substep in range(SUBSTEPS):
        runoff = conveyance * level * jnp.cbrt(level) * jnp.cbrt(level)
        level = level + rain - runoff + inflow(jnp.pad(runoff, 1), dir_pad, MAP_ROWS, MAP_COLS)
    return (fraction, level)
```

```python
import functools

import jax
import jax.numpy as jnp
from jax import lax
from jax.experimental import pallas as pl
from jax.experimental.pallas import tpu as pltpu
from jax.sharding import PartitionSpec as P

WIN_ROWS = 2
SUBSTEPS = 8
CH = 16
OUT_LINES = 14
IN_LINES = OUT_LINES + 2
HALO_LINES = 4
LANES = 128
VMEM_LIMIT = 48 * 1024 * 1024

wet_depth = 0.5
runoff_coef = 0.25
bf16 = jnp.bfloat16
f32 = jnp.float32


def iota(shape, dim):
    return lax.broadcasted_iota(jnp.int32, shape, dim)


def dot(a, b):
    return lax.dot_general(a, b, (((1,), (0,)), ((), ())), preferred_element_type=f32)


def dot_t(a, b):
    return lax.dot_general(a, b, (((1,), (1,)), ((), ())), preferred_element_type=f32)


def pixel_shifts(x):
    width = x.shape[1]
    pix = iota(x.shape, 1)
    before = jnp.where(pix == 0, 0.0, pltpu.roll(x, 1, 1))
    after = jnp.where(pix == width - 1, 0.0, pltpu.roll(x, width - 1, 1))
    return before, after


def band_weights(tiled, rows, cols, per_row, line_of):
    out_line = iota((rows, cols), 0) // per_row
    off = line_of(iota((rows, cols), 1)) - out_line
    out = jnp.zeros((rows, cols), f32)
    for ky in range(3):
        out = jnp.where(off == ky, tiled[ky], out)
    return out.astype(bf16)


def stack_rows(x, times):
    return jnp.broadcast_to(x[None], (times,) + x.shape).reshape(times * x.shape[0], x.shape[1])


def swath_kernel(
    devices, capacity,
    sar_ref, top_ref, bot_ref, wk_ref, gw_ref, cell_ref, tile_ref, row_ref,
    frac_ref, send_ref,
    s_ref, xa_ref, xb_ref, x3_ref, obs_ref, wnd_ref,
):
    lines, px = gw_ref.shape
    blocks = (lines + 2 * HALO_LINES - 2) // OUT_LINES
    frame = lines + 2 * HALO_LINES
    total = frame + 2
    me = lax.axis_index("tx") * lax.axis_size("ty") + lax.axis_index("ty")
    first = me == 0
    last = me == devices - 1

    for ch in range(2):
        s_ref[ch, 0:HALO_LINES, :] = top_ref[ch].astype(f32)
        s_ref[ch, HALO_LINES : HALO_LINES + lines, :] = sar_ref[ch].astype(f32)
        s_ref[ch, HALO_LINES + lines : frame, :] = bot_ref[ch].astype(f32)

    rows = OUT_LINES * CH
    cols = IN_LINES * CH
    spread = (iota((CH, cols), 1) % CH == iota((CH, cols), 0)).astype(bf16)

    cols1 = 3 * 2 * IN_LINES
    spread1 = (iota((CH, cols1), 1) // IN_LINES == iota((CH, cols1), 0)).astype(bf16)
    wide1 = dot(wk_ref[0:48, :], spread1)
    w1 = band_weights(
        [stack_rows(wide1[ky * CH : (ky + 1) * CH], OUT_LINES) for ky in range(3)],
        rows, cols1, CH, lambda k: k % IN_LINES,
    )

    def mid_weights(base):
        wide = dot(wk_ref[base : base + 144, :], spread)
        return [
            band_weights(
                [stack_rows(wide[(ky * 3 + kx) * CH : (ky * 3 + kx + 1) * CH], OUT_LINES) for ky in range(3)],
                rows, cols, CH, lambda k: k // CH,
            )
            for kx in range(3)
        ]

    def put(ref, line, acc):
        feat = jnp.maximum(acc, 0.0)
        at = pl.ds(line * CH, rows)
        if len(ref.shape) == 2:
            ref[at, :] = feat.astype(bf16)
            return
        before, after = pixel_shifts(feat)
        ref[0, at, :] = before.astype(bf16)
        ref[1, at, :] = feat.astype(bf16)
        ref[2, at, :] = after.astype(bf16)

    def clear(ref, lo, hi):
        shape = ref.shape[:-2] + ((hi - lo) * CH, px)
        ref[..., lo * CH : hi * CH, :] = jnp.zeros(shape, bf16)

    def outside(ref):
        @pl.when(first)
        def _():
            clear(ref, 0, HALO_LINES)

        @pl.when(last)
        def _():
            clear(ref, HALO_LINES + lines, frame)

    for b in range(blocks):
        at = b * OUT_LINES
        x = jnp.concatenate([s_ref[0, at : at + IN_LINES, :], s_ref[1, at : at + IN_LINES, :]], 0)
        before, after = pixel_shifts(x)
        put(xa_ref, 1 + at, dot(w1, jnp.concatenate([before, x, after], 0).astype(bf16)))
    clear(xa_ref, frame - 1, total)
    outside(xa_ref)

    for base, src, dst, line in ((48, xa_ref, xb_ref, 2), (192, xb_ref, x3_ref, 3)):
        w = mid_weights(base)
        for b in range(blocks):
            at = pl.ds((line - 1 + b * OUT_LINES) * CH, cols)
            acc = dot(w[0], src[0, at, :]) + dot(w[1], src[1, at, :]) + dot(w[2], src[2, at, :])
            put(dst, line + b * OUT_LINES, acc)
        if len(dst.shape) == 3:
            clear(dst, frame, total)
        outside(dst)

    cols4 = (lines + 2) * CH
    spread4 = (iota((CH, cols4), 1) % CH == iota((CH, cols4), 0)).astype(bf16)
    wide4 = dot(wk_ref[336:352, :], spread4)
    w4 = [
        band_weights(
            [jnp.broadcast_to(wide4[ky * 3 + kx : ky * 3 + kx + 1], (lines, cols4)) for ky in range(3)],
            lines, cols4, 1, lambda k: k // CH,
        )
        for kx in range(3)
    ]
    parts = dot(jnp.concatenate(w4, 0), x3_ref[(HALO_LINES - 1) * CH : (HALO_LINES + lines + 1) * CH, :])
    from_before, _ = pixel_shifts(parts[0:lines])
    _, from_after = pixel_shifts(parts[2 * lines : 3 * lines])
    logit = from_before + parts[lines : 2 * lines] + from_after
    frac = (1.0 / (1.0 + jnp.exp(-logit))).astype(bf16)
    frac_ref[...] = frac
    obs_ref[...] = frac.astype(f32) * gw_ref[...]

    kind = iota((8, px), 0)
    lane_col = iota((LANES, px), 0)
    group = 8

    def window_group(g, carry):
        at = pl.ds(pl.multiple_of(g * group, group), group)
        cell = cell_ref[at, :]
        obs = obs_ref[at, :]
        cov = gw_ref[at, :]
        part = cell // LANES
        col = cell % LANES
        for i in range(group):
            value = jnp.where(kind < 4, obs[i : i + 1], cov[i : i + 1])
            value = jnp.where(kind % 4 == part[i : i + 1], value, 0.0)
            coarse = value.astype(bf16).astype(f32)
            left = jnp.concatenate([coarse, value - coarse], 0).astype(bf16)
            hot = jnp.where(lane_col == col[i : i + 1], 1.0, 0.0).astype(bf16)
            sums = dot_t(left, hot)
            wnd_ref[pl.ds(pl.multiple_of(g * (8 * group) + 8 * i, 8), 8), :] = sums[0:8] + sums[8:16]
        return carry

    lax.fori_loop(0, lines // group, window_group, 0)

    tile = tile_ref[...].astype(f32)
    same = iota((lines, lines), 0) == iota((lines, lines), 1)
    tile_sub = jnp.sum(jnp.where(same, jnp.broadcast_to(tile, (lines, lines)), 0.0), 1, keepdims=True)
    rival = (tile_sub == tile) & (iota((lines, lines), 0) < iota((lines, lines), 1))
    slot = tile * capacity + jnp.sum(jnp.where(rival, 1.0, 0.0), 0, keepdims=True)
    wnd_rows = 8 * lines
    widen = (iota((lines, wnd_rows), 1) // 8 == iota((lines, wnd_rows), 0)).astype(bf16)
    slot_wide = dot(jnp.broadcast_to(slot, (8, lines)).astype(bf16), widen)[0:1]
    place = slot_wide.astype(jnp.int32) * 4 + (iota((1, wnd_rows), 1) // 2) % 4
    slots = devices * capacity * 4
    perm = jnp.where(iota((slots, wnd_rows), 0) == place, 1.0, 0.0).astype(bf16)
    wnd = wnd_ref[...]
    half = iota((wnd_rows, LANES), 0) % 2
    own_line = iota((wnd_rows, lines), 0) // 8 == iota((wnd_rows, lines), 1)
    row_part = jnp.where(own_line, jnp.broadcast_to(row_ref[...].astype(f32), (wnd_rows, lines)), 0.0)
    row_wide = dot(row_part.astype(bf16), jnp.ones((lines, LANES), bf16))
    goods = jnp.concatenate(
        [jnp.where(half == 0, wnd, 0.0), jnp.where(half == 1, wnd, 0.0), jnp.where(half == 0, row_wide, 0.0)], 1
    ).astype(bf16)
    send_ref[...] = dot(perm, goods).astype(bf16)


def transposed(x):
    return jnp.transpose(x, (1, 0))


def level_kernel(got_ref, depth_ref, slope_ref, dir_ref, rain_ref, level_ref, top_ref, bot_ref, left_ref, right_ref):
    tile_rows, tile_cols = depth_ref.shape
    k = got_ref.shape[0]
    line = transposed(got_ref[:, tile_cols:].astype(f32))[0:1]
    lane = iota((1, k), 1)
    target = line.astype(jnp.int32) + lane % 2 + tile_rows * ((lane // 2) % 2)
    placer = jnp.where(iota((2 * tile_rows, k), 0) == target, 1.0, 0.0).astype(bf16)
    summed = dot(placer, got_ref[:, 0:tile_cols])
    observed = summed[0:tile_rows]
    covered = summed[tile_rows:]
    depth = depth_ref[...]
    wet = depth / (depth + wet_depth)
    innovation = (observed - covered * wet) / (covered + 1.0)
    level = depth * jnp.exp(innovation)
    level_ref[...] = level
    conveyance = runoff_coef * jnp.sqrt(slope_ref[...])
    fields = (level, rain_ref[...], conveyance, dir_ref[...].astype(f32))
    h = SUBSTEPS
    top_ref[...] = jnp.concatenate([x[0:h] for x in fields], 0).astype(bf16)
    bot_ref[...] = jnp.concatenate([x[tile_rows - h :] for x in fields], 0).astype(bf16)
    left_ref[...] = jnp.concatenate([transposed(x[:, 0:LANES])[0:h] for x in fields], 0).astype(bf16)
    right_ref[...] = jnp.concatenate(
        [transposed(x[:, tile_cols - LANES :])[LANES - h :] for x in fields], 0
    ).astype(bf16)


def flow_kernel(
    level_ref, slope_ref, dir_ref, rain_ref, above_ref, below_ref, left_ref, right_ref,
    out_ref,
    rain_s, conv_s, m_ref, part_ref, up_ref, down_ref,
):
    tile_rows, tile_cols = level_ref.shape
    h = SUBSTEPS
    wide_rows = tile_rows + 2 * h
    wide_cols = tile_cols + LANES

    gap = jnp.zeros((LANES - 2 * h, 2 * tile_cols), f32)

    def widened(field, own):
        at = slice(field * h, (field + 1) * h)
        rights = jnp.concatenate(
            [right_ref[...], below_ref[:, tile_cols : tile_cols + LANES], above_ref[:, tile_cols : tile_cols + LANES]], 1
        )
        lefts = jnp.concatenate(
            [left_ref[...], below_ref[:, tile_cols + LANES :], above_ref[:, tile_cols + LANES :]], 1
        )
        side = transposed(jnp.concatenate([rights.astype(f32)[at], gap, lefts.astype(f32)[at]], 0))
        above = jnp.concatenate([above_ref[:, 0:tile_cols].astype(f32)[at], side[tile_rows + 2 * LANES - h :]], 1)
        below = jnp.concatenate([below_ref[:, 0:tile_cols].astype(f32)[at], side[tile_rows : tile_rows + h]], 1)
        mid = jnp.concatenate([own, side[0:tile_rows]], 1)
        return jnp.concatenate([above, mid, below], 0)

    zeros = jnp.zeros((h, wide_cols), f32)
    for buf in range(2):
        for ref in (up_ref, down_ref):
            ref[buf, 0:h, :] = zeros
            ref[buf, h + wide_rows :, :] = zeros
    part_ref[0] = widened(0, level_ref[...])
    rain_s[...] = widened(1, rain_ref[...])
    conv = widened(2, runoff_coef * jnp.sqrt(slope_ref[...]))
    conv_s[...] = conv
    code = widened(3, dir_ref[...].astype(f32))
    sides = (-1, 0, 1, -1, 1, -1, 0, 1)
    for direction, side in enumerate(sides):
        share = jnp.where(code == direction, conv, 0.0)
        m_ref[direction] = pltpu.roll(share, side % wide_cols, 1) if side else share

    chunk = 16

    def level_at(buf, r, n, step):
        level = part_ref[buf, r : r + n, :]
        if step:
            level = level + up_ref[buf, h + r + 1 : h + r + 1 + n, :] + down_ref[buf, h + r - 1 : h + r - 1 + n, :]
        return level

    for step in range(SUBSTEPS):
        buf, new = step % 2, (step + 1) % 2
        for r in range(0, wide_rows, chunk):
            level = level_at(buf, r, chunk, step)
            power = level * jnp.exp((2.0 / 3.0) * jnp.log(jnp.maximum(jnp.abs(level), 1e-30)))
            from_right = pltpu.roll(power, wide_cols - 1, 1)
            from_left = pltpu.roll(power, 1, 1)
            m = [m_ref[d, r : r + chunk, :] for d in range(8)]
            up_ref[new, h + r : h + r + chunk, :] = m[0] * from_right + m[1] * power + m[2] * from_left
            down_ref[new, h + r : h + r + chunk, :] = m[5] * from_right + m[6] * power + m[7] * from_left
            part_ref[new, r : r + chunk, :] = (
                level + rain_s[r : r + chunk, :] - conv_s[r : r + chunk, :] * power
                + (m[3] * from_right + m[4] * from_left)
            )
    buf = SUBSTEPS % 2
    out_ref[...] = level_at(buf, h, tile_rows, SUBSTEPS)[:, 0:tile_cols]


def vmem_specs(n):
    return [pl.BlockSpec(memory_space=pltpu.VMEM)] * n


def kernel_rows(kernel_first, kernel_second, kernel_third, kernel_last):
    first = jnp.transpose(kernel_first, (2, 0, 3, 1)).reshape(3 * CH, 6)
    first = jnp.pad(first, ((0, 0), (0, CH - 6)))
    mids = [jnp.transpose(k, (2, 3, 0, 1)).reshape(9 * CH, CH) for k in (kernel_second, kernel_third)]
    last = jnp.transpose(kernel_last[0], (1, 2, 0)).reshape(9, CH)
    last = jnp.pad(last, ((0, CH - 9), (0, 0)))
    return jnp.concatenate([first, *mids, last], 0)


def per_device(
    sar_image, kernel_first, kernel_second, kernel_third, kernel_last,
    geo_weight, cell_index, block_tile, block_row, depth, slope, flow_dir, rain,
):
    both = ("tx", "ty")
    devices = lax.axis_size(both)
    az_lines, range_px = geo_weight.shape
    tile_rows, tile_cols = depth.shape
    capacity = max(2, 2 * az_lines // devices)

    def steps(axis):
        size = lax.axis_size(axis)
        up = [(i, i + 1) for i in range(size - 1)]
        return up, [(j, i) for i, j in up]

    up, down = steps(both)
    top = lax.ppermute(sar_image[:, az_lines - HALO_LINES :], both, up)
    bot = lax.ppermute(sar_image[:, :HALO_LINES], both, down)
    weights = kernel_rows(kernel_first, kernel_second, kernel_third, kernel_last)

    params = pltpu.CompilerParams(vmem_limit_bytes=VMEM_LIMIT)
    slots = devices * capacity * 4
    frame = az_lines + 2 * HALO_LINES
    feats = (frame + 2) * CH
    send_lanes = tile_cols + LANES
    fraction, send = pl.pallas_call(
        functools.partial(swath_kernel, devices, capacity),
        out_shape=(
            jax.ShapeDtypeStruct((az_lines, range_px), bf16),
            jax.ShapeDtypeStruct((slots, send_lanes), bf16),
        ),
        in_specs=vmem_specs(8),
        out_specs=tuple(vmem_specs(2)),
        scratch_shapes=[
            pltpu.VMEM((2, frame + 8, range_px), f32),
            pltpu.VMEM((3, feats, range_px), bf16),
            pltpu.VMEM((3, feats, range_px), bf16),
            pltpu.VMEM((feats, range_px), bf16),
            pltpu.VMEM((az_lines, range_px), f32),
            pltpu.VMEM((8 * az_lines, LANES), f32),
        ],
        compiler_params=params,
        name="swath",
    )(
        sar_image, top, bot, weights, geo_weight, cell_index,
        block_tile.reshape(1, az_lines), block_row.reshape(1, az_lines),
    )

    got = lax.all_to_all(
        send.reshape(devices, capacity * 4, send_lanes), both, split_axis=0, concat_axis=0, tiled=True
    ).reshape(slots, send_lanes)

    edge = jax.ShapeDtypeStruct((4 * SUBSTEPS, tile_cols), bf16)
    level, top_rows, bot_rows, left_cols, right_cols = pl.pallas_call(
        level_kernel,
        out_shape=(jax.ShapeDtypeStruct((tile_rows, tile_cols), f32), edge, edge, edge, edge),
        in_specs=vmem_specs(5),
        out_specs=tuple(vmem_specs(5)),
        compiler_params=params,
        name="level",
    )(got, depth, slope, flow_dir, rain)

    up, down = steps("ty")
    left = lax.ppermute(right_cols, "ty", up)
    right = lax.ppermute(left_cols, "ty", down)
    up, down = steps("tx")
    cut = tile_cols - LANES
    above = lax.ppermute(jnp.concatenate([bot_rows, right[:, cut:], left[:, cut:]], 1), "tx", up)
    below = lax.ppermute(jnp.concatenate([top_rows, right[:, :LANES], left[:, :LANES]], 1), "tx", down)

    wide_rows = tile_rows + 2 * SUBSTEPS
    wide_cols = tile_cols + LANES
    level = pl.pallas_call(
        flow_kernel,
        out_shape=jax.ShapeDtypeStruct((tile_rows, tile_cols), f32),
        in_specs=vmem_specs(8),
        out_specs=vmem_specs(1)[0],
        scratch_shapes=[
            pltpu.VMEM((wide_rows, wide_cols), f32),
            pltpu.VMEM((wide_rows, wide_cols), f32),
            pltpu.VMEM((8, wide_rows, wide_cols), f32),
            pltpu.VMEM((2, wide_rows, wide_cols), f32),
            pltpu.VMEM((2, wide_rows + 2 * SUBSTEPS, wide_cols), f32),
            pltpu.VMEM((2, wide_rows + 2 * SUBSTEPS, wide_cols), f32),
        ],
        compiler_params=params,
        name="flow",
    )(level, slope, flow_dir, rain, above, below, left, right)
    return (fraction, level)


def solution(mesh):
    placed = (
        P(None, ("tx", "ty"), None),
        P(),
        P(),
        P(),
        P(),
        P(("tx", "ty"), None),
        P(("tx", "ty"), None),
        P(("tx", "ty"), None),
        P(("tx", "ty"), None),
        P("tx", "ty"),
        P("tx", "ty"),
        P("tx", "ty"),
        P("tx", "ty"),
    )
    return jax.shard_map(
        per_device,
        mesh=mesh,
        in_specs=placed,
        out_specs=(P(("tx", "ty"), None), P("tx", "ty")),
        check_vma=False,
    )
```

```python
import functools

import jax
import jax.numpy as jnp
from jax import lax
from jax.experimental import pallas as pl
from jax.experimental.pallas import tpu as pltpu
from jax.sharding import PartitionSpec as P

WIN_ROWS = 2
SUBSTEPS = 8
CH = 16
OUT_LINES = 14
IN_LINES = OUT_LINES + 2
HALO_LINES = 4
LANES = 128
VMEM_LIMIT = 48 * 1024 * 1024

wet_depth = 0.5
runoff_coef = 0.25
bf16 = jnp.bfloat16
f32 = jnp.float32


def iota(shape, dim):
    return lax.broadcasted_iota(jnp.int32, shape, dim)


def dot(a, b):
    return lax.dot_general(a, b, (((1,), (0,)), ((), ())), preferred_element_type=f32)


def dot_t(a, b):
    return lax.dot_general(a, b, (((1,), (1,)), ((), ())), preferred_element_type=f32)


def pixel_shifts(x):
    width = x.shape[1]
    pix = iota(x.shape, 1)
    before = jnp.where(pix == 0, 0.0, pltpu.roll(x, 1, 1))
    after = jnp.where(pix == width - 1, 0.0, pltpu.roll(x, width - 1, 1))
    return before, after


def band_weights(tiled, rows, cols, per_row, line_of):
    out_line = iota((rows, cols), 0) // per_row
    off = line_of(iota((rows, cols), 1)) - out_line
    out = jnp.zeros((rows, cols), f32)
    for ky in range(3):
        out = jnp.where(off == ky, tiled[ky], out)
    return out.astype(bf16)


def stack_rows(x, times):
    return jnp.broadcast_to(x[None], (times,) + x.shape).reshape(times * x.shape[0], x.shape[1])


def swath_kernel(
    devices, capacity,
    sar_ref, top_ref, bot_ref, wk_ref, gw_ref, cell_ref, tile_ref, row_ref,
    frac_ref, send_ref,
    s_ref, xa_ref, xb_ref, x3_ref, obs_ref, wnd_ref,
):
    lines, px = gw_ref.shape
    blocks = (lines + 2 * HALO_LINES - 2) // OUT_LINES
    frame = lines + 2 * HALO_LINES
    total = frame + 2
    me = lax.axis_index("tx") * lax.axis_size("ty") + lax.axis_index("ty")
    n_ty = lax.axis_size("ty")
    first = me == 0
    last = me == devices - 1

    for ch in range(2):
        s_ref[ch, 0:HALO_LINES, :] = top_ref[ch].astype(f32)
        s_ref[ch, HALO_LINES : HALO_LINES + lines, :] = sar_ref[ch].astype(f32)
        s_ref[ch, HALO_LINES + lines : frame, :] = bot_ref[ch].astype(f32)

    rows = OUT_LINES * CH
    cols = IN_LINES * CH
    spread = (iota((CH, cols), 1) % CH == iota((CH, cols), 0)).astype(bf16)

    cols1 = 3 * 2 * IN_LINES
    spread1 = (iota((CH, cols1), 1) // IN_LINES == iota((CH, cols1), 0)).astype(bf16)
    wide1 = dot(wk_ref[0:48, :], spread1)
    w1 = band_weights(
        [stack_rows(wide1[ky * CH : (ky + 1) * CH], OUT_LINES) for ky in range(3)],
        rows, cols1, CH, lambda k: k % IN_LINES,
    )

    def mid_weights(base):
        wide = dot(wk_ref[base : base + 144, :], spread)
        return [
            band_weights(
                [stack_rows(wide[(ky * 3 + kx) * CH : (ky * 3 + kx + 1) * CH], OUT_LINES) for ky in range(3)],
                rows, cols, CH, lambda k: k // CH,
            )
            for kx in range(3)
        ]

    def put(ref, line, acc):
        feat = jnp.maximum(acc, 0.0)
        at = pl.ds(line * CH, rows)
        if len(ref.shape) == 2:
            ref[at, :] = feat.astype(bf16)
            return
        before, after = pixel_shifts(feat)
        ref[0, at, :] = before.astype(bf16)
        ref[1, at, :] = feat.astype(bf16)
        ref[2, at, :] = after.astype(bf16)

    def clear(ref, lo, hi):
        shape = ref.shape[:-2] + ((hi - lo) * CH, px)
        ref[..., lo * CH : hi * CH, :] = jnp.zeros(shape, bf16)

    def outside(ref):
        @pl.when(first)
        def _():
            clear(ref, 0, HALO_LINES)

        @pl.when(last)
        def _():
            clear(ref, HALO_LINES + lines, frame)

    for b in range(blocks):
        at = b * OUT_LINES
        x = jnp.concatenate([s_ref[0, at : at + IN_LINES, :], s_ref[1, at : at + IN_LINES, :]], 0)
        before, after = pixel_shifts(x)
        put(xa_ref, 1 + at, dot(w1, jnp.concatenate([before, x, after], 0).astype(bf16)))
    clear(xa_ref, frame - 1, total)
    outside(xa_ref)

    for base, src, dst, line in ((48, xa_ref, xb_ref, 2), (192, xb_ref, x3_ref, 3)):
        w = mid_weights(base)
        for b in range(blocks):
            at = pl.ds((line - 1 + b * OUT_LINES) * CH, cols)
            acc = dot(w[0], src[0, at, :]) + dot(w[1], src[1, at, :]) + dot(w[2], src[2, at, :])
            put(dst, line + b * OUT_LINES, acc)
        if len(dst.shape) == 3:
            clear(dst, frame, total)
        outside(dst)

    cols4 = (lines + 2) * CH
    spread4 = (iota((CH, cols4), 1) % CH == iota((CH, cols4), 0)).astype(bf16)
    wide4 = dot(wk_ref[336:352, :], spread4)
    w4 = [
        band_weights(
            [jnp.broadcast_to(wide4[ky * 3 + kx : ky * 3 + kx + 1], (lines, cols4)) for ky in range(3)],
            lines, cols4, 1, lambda k: k // CH,
        )
        for kx in range(3)
    ]
    parts = dot(jnp.concatenate(w4, 0), x3_ref[(HALO_LINES - 1) * CH : (HALO_LINES + lines + 1) * CH, :])
    from_before, _ = pixel_shifts(parts[0:lines])
    _, from_after = pixel_shifts(parts[2 * lines : 3 * lines])
    logit = from_before + parts[lines : 2 * lines] + from_after
    frac = (1.0 / (1.0 + jnp.exp(-logit))).astype(bf16)
    frac_ref[...] = frac
    obs_ref[...] = frac.astype(f32) * gw_ref[...]

    kind = iota((8, px), 0)
    lane_col = iota((LANES, px), 0)
    group = 8

    def window_group(g, carry):
        at = pl.ds(pl.multiple_of(g * group, group), group)
        cell = cell_ref[at, :]
        obs = obs_ref[at, :]
        cov = gw_ref[at, :]
        part = cell // LANES
        col = cell % LANES
        for i in range(group):
            value = jnp.where(kind < 4, obs[i : i + 1], cov[i : i + 1])
            value = jnp.where(kind % 4 == part[i : i + 1], value, 0.0)
            coarse = value.astype(bf16).astype(f32)
            left = jnp.concatenate([coarse, value - coarse], 0).astype(bf16)
            hot = jnp.where(lane_col == col[i : i + 1], 1.0, 0.0).astype(bf16)
            sums = dot_t(left, hot)
            wnd_ref[pl.ds(pl.multiple_of(g * (8 * group) + 8 * i, 8), 8), :] = sums[0:8] + sums[8:16]
        return carry

    lax.fori_loop(0, lines // group, window_group, 0)

    tile = tile_ref[...].astype(f32)
    same = iota((lines, lines), 0) == iota((lines, lines), 1)
    tile_sub = jnp.sum(jnp.where(same, jnp.broadcast_to(tile, (lines, lines)), 0.0), 1, keepdims=True)
    rival = (tile_sub == tile) & (iota((lines, lines), 0) < iota((lines, lines), 1))
    by_column = (tile_ref[...] % n_ty) * (devices // n_ty) + tile_ref[...] // n_ty
    slot = by_column.astype(f32) * capacity + jnp.sum(jnp.where(rival, 1.0, 0.0), 0, keepdims=True)
    wnd_rows = 8 * lines
    widen = (iota((lines, wnd_rows), 1) // 8 == iota((lines, wnd_rows), 0)).astype(bf16)
    slot_wide = dot(jnp.broadcast_to(slot, (8, lines)).astype(bf16), widen)[0:1]
    place = slot_wide.astype(jnp.int32) * 4 + (iota((1, wnd_rows), 1) // 2) % 4
    slots = devices * capacity * 4
    perm = jnp.where(iota((slots, wnd_rows), 0) == place, 1.0, 0.0).astype(bf16)
    wnd = wnd_ref[...]
    half = iota((wnd_rows, LANES), 0) % 2
    own_line = iota((wnd_rows, lines), 0) // 8 == iota((wnd_rows, lines), 1)
    row_part = jnp.where(own_line, jnp.broadcast_to(row_ref[...].astype(f32), (wnd_rows, lines)), 0.0)
    row_wide = dot(row_part.astype(bf16), jnp.ones((lines, LANES), bf16))
    goods = jnp.concatenate(
        [jnp.where(half == 0, wnd, 0.0), jnp.where(half == 1, wnd, 0.0), jnp.where(half == 0, row_wide, 0.0)], 1
    ).astype(bf16)
    send_ref[...] = dot(perm, goods).astype(bf16)


def transposed(x):
    return jnp.transpose(x, (1, 0))


def level_kernel(got_ref, depth_ref, slope_ref, dir_ref, rain_ref, level_ref, top_ref, bot_ref, left_ref, right_ref):
    tile_rows, tile_cols = depth_ref.shape
    k = got_ref.shape[0]
    line = transposed(got_ref[:, tile_cols:].astype(f32))[0:1]
    lane = iota((1, k), 1)
    target = line.astype(jnp.int32) + lane % 2 + tile_rows * ((lane // 2) % 2)
    placer = jnp.where(iota((2 * tile_rows, k), 0) == target, 1.0, 0.0).astype(bf16)
    summed = dot(placer, got_ref[:, 0:tile_cols])
    observed = summed[0:tile_rows]
    covered = summed[tile_rows:]
    depth = depth_ref[...]
    wet = depth / (depth + wet_depth)
    innovation = (observed - covered * wet) / (covered + 1.0)
    level = depth * jnp.exp(innovation)
    level_ref[...] = level
    conveyance = runoff_coef * jnp.sqrt(slope_ref[...])
    fields = (level, rain_ref[...], conveyance, dir_ref[...].astype(f32))
    h = SUBSTEPS
    top_ref[...] = jnp.concatenate([x[0:h] for x in fields], 0).astype(bf16)
    bot_ref[...] = jnp.concatenate([x[tile_rows - h :] for x in fields], 0).astype(bf16)
    left_ref[...] = jnp.concatenate([transposed(x[:, 0:LANES])[0:h] for x in fields], 0).astype(bf16)
    right_ref[...] = jnp.concatenate(
        [transposed(x[:, tile_cols - LANES :])[LANES - h :] for x in fields], 0
    ).astype(bf16)


def flow_kernel(
    level_ref, slope_ref, dir_ref, rain_ref, above_ref, below_ref, left_ref, right_ref,
    out_ref,
    rain_s, conv_s, m_ref, part_ref, up_ref, down_ref,
):
    tile_rows, tile_cols = level_ref.shape
    h = SUBSTEPS
    wide_rows = tile_rows + 2 * h
    wide_cols = tile_cols + LANES

    gap = jnp.zeros((LANES - 2 * h, 2 * tile_cols), f32)

    def widened(field, own):
        at = slice(field * h, (field + 1) * h)
        rights = jnp.concatenate(
            [right_ref[...], below_ref[:, tile_cols : tile_cols + LANES], above_ref[:, tile_cols : tile_cols + LANES]], 1
        )
        lefts = jnp.concatenate(
            [left_ref[...], below_ref[:, tile_cols + LANES :], above_ref[:, tile_cols + LANES :]], 1
        )
        side = transposed(jnp.concatenate([rights.astype(f32)[at], gap, lefts.astype(f32)[at]], 0))
        above = jnp.concatenate([above_ref[:, 0:tile_cols].astype(f32)[at], side[tile_rows + 2 * LANES - h :]], 1)
        below = jnp.concatenate([below_ref[:, 0:tile_cols].astype(f32)[at], side[tile_rows : tile_rows + h]], 1)
        mid = jnp.concatenate([own, side[0:tile_rows]], 1)
        return jnp.concatenate([above, mid, below], 0)

    zeros = jnp.zeros((h, wide_cols), f32)
    for buf in range(2):
        for ref in (up_ref, down_ref):
            ref[buf, 0:h, :] = zeros
            ref[buf, h + wide_rows :, :] = zeros
    part_ref[0] = widened(0, level_ref[...])
    rain_s[...] = widened(1, rain_ref[...])
    conv = widened(2, runoff_coef * jnp.sqrt(slope_ref[...]))
    conv_s[...] = conv
    code = widened(3, dir_ref[...].astype(f32))
    sides = (-1, 0, 1, -1, 1, -1, 0, 1)
    for direction, side in enumerate(sides):
        share = jnp.where(code == direction, conv, 0.0)
        m_ref[direction] = pltpu.roll(share, side % wide_cols, 1) if side else share

    chunk = 16

    def level_at(buf, r, n, step):
        level = part_ref[buf, r : r + n, :]
        if step:
            level = level + up_ref[buf, h + r + 1 : h + r + 1 + n, :] + down_ref[buf, h + r - 1 : h + r - 1 + n, :]
        return level

    for step in range(SUBSTEPS):
        buf, new = step % 2, (step + 1) % 2
        for r in range(0, wide_rows, chunk):
            level = level_at(buf, r, chunk, step)
            power = level * jnp.exp((2.0 / 3.0) * jnp.log(jnp.maximum(jnp.abs(level), 1e-30)))
            from_right = pltpu.roll(power, wide_cols - 1, 1)
            from_left = pltpu.roll(power, 1, 1)
            m = [m_ref[d, r : r + chunk, :] for d in range(8)]
            up_ref[new, h + r : h + r + chunk, :] = m[0] * from_right + m[1] * power + m[2] * from_left
            down_ref[new, h + r : h + r + chunk, :] = m[5] * from_right + m[6] * power + m[7] * from_left
            part_ref[new, r : r + chunk, :] = (
                level + rain_s[r : r + chunk, :] - conv_s[r : r + chunk, :] * power
                + (m[3] * from_right + m[4] * from_left)
            )
    buf = SUBSTEPS % 2
    out_ref[...] = level_at(buf, h, tile_rows, SUBSTEPS)[:, 0:tile_cols]


def vmem_specs(n):
    return [pl.BlockSpec(memory_space=pltpu.VMEM)] * n


def kernel_rows(kernel_first, kernel_second, kernel_third, kernel_last):
    first = jnp.transpose(kernel_first, (2, 0, 3, 1)).reshape(3 * CH, 6)
    first = jnp.pad(first, ((0, 0), (0, CH - 6)))
    mids = [jnp.transpose(k, (2, 3, 0, 1)).reshape(9 * CH, CH) for k in (kernel_second, kernel_third)]
    last = jnp.transpose(kernel_last[0], (1, 2, 0)).reshape(9, CH)
    last = jnp.pad(last, ((0, CH - 9), (0, 0)))
    return jnp.concatenate([first, *mids, last], 0)


def per_device(
    sar_image, kernel_first, kernel_second, kernel_third, kernel_last,
    geo_weight, cell_index, block_tile, block_row, depth, slope, flow_dir, rain,
):
    both = ("tx", "ty")
    devices = lax.axis_size(both)
    az_lines, range_px = geo_weight.shape
    tile_rows, tile_cols = depth.shape
    capacity = max(2, 2 * az_lines // devices)

    def steps(axis):
        size = lax.axis_size(axis)
        up = [(i, i + 1) for i in range(size - 1)]
        return up, [(j, i) for i, j in up]

    up, down = steps(both)
    top = lax.ppermute(sar_image[:, az_lines - HALO_LINES :], both, up)
    bot = lax.ppermute(sar_image[:, :HALO_LINES], both, down)
    weights = kernel_rows(kernel_first, kernel_second, kernel_third, kernel_last)

    params = pltpu.CompilerParams(vmem_limit_bytes=VMEM_LIMIT)
    slots = devices * capacity * 4
    frame = az_lines + 2 * HALO_LINES
    feats = (frame + 2) * CH
    send_lanes = tile_cols + LANES
    fraction, send = pl.pallas_call(
        functools.partial(swath_kernel, devices, capacity),
        out_shape=(
            jax.ShapeDtypeStruct((az_lines, range_px), bf16),
            jax.ShapeDtypeStruct((slots, send_lanes), bf16),
        ),
        in_specs=vmem_specs(8),
        out_specs=tuple(vmem_specs(2)),
        scratch_shapes=[
            pltpu.VMEM((2, frame + 8, range_px), f32),
            pltpu.VMEM((3, feats, range_px), bf16),
            pltpu.VMEM((3, feats, range_px), bf16),
            pltpu.VMEM((feats, range_px), bf16),
            pltpu.VMEM((az_lines, range_px), f32),
            pltpu.VMEM((8 * az_lines, LANES), f32),
        ],
        compiler_params=params,
        name="swath",
    )(
        sar_image, top, bot, weights, geo_weight, cell_index,
        block_tile.reshape(1, az_lines), block_row.reshape(1, az_lines),
    )

    n_tx, n_ty = lax.axis_size("tx"), lax.axis_size("ty")
    got = lax.all_to_all(
        send.reshape(n_ty, n_tx, capacity * 4, send_lanes), "ty", split_axis=0, concat_axis=0, tiled=True
    )
    got = lax.all_to_all(got, "tx", split_axis=1, concat_axis=1, tiled=True).reshape(slots, send_lanes)

    edge = jax.ShapeDtypeStruct((4 * SUBSTEPS, tile_cols), bf16)
    level, top_rows, bot_rows, left_cols, right_cols = pl.pallas_call(
        level_kernel,
        out_shape=(jax.ShapeDtypeStruct((tile_rows, tile_cols), f32), edge, edge, edge, edge),
        in_specs=vmem_specs(5),
        out_specs=tuple(vmem_specs(5)),
        compiler_params=params,
        name="level",
    )(got, depth, slope, flow_dir, rain)

    up, down = steps("ty")
    left = lax.ppermute(right_cols, "ty", up)
    right = lax.ppermute(left_cols, "ty", down)
    up, down = steps("tx")
    cut = tile_cols - LANES
    above = lax.ppermute(jnp.concatenate([bot_rows, right[:, cut:], left[:, cut:]], 1), "tx", up)
    below = lax.ppermute(jnp.concatenate([top_rows, right[:, :LANES], left[:, :LANES]], 1), "tx", down)

    wide_rows = tile_rows + 2 * SUBSTEPS
    wide_cols = tile_cols + LANES
    level = pl.pallas_call(
        flow_kernel,
        out_shape=jax.ShapeDtypeStruct((tile_rows, tile_cols), f32),
        in_specs=vmem_specs(8),
        out_specs=vmem_specs(1)[0],
        scratch_shapes=[
            pltpu.VMEM((wide_rows, wide_cols), f32),
            pltpu.VMEM((wide_rows, wide_cols), f32),
            pltpu.VMEM((8, wide_rows, wide_cols), f32),
            pltpu.VMEM((2, wide_rows, wide_cols), f32),
            pltpu.VMEM((2, wide_rows + 2 * SUBSTEPS, wide_cols), f32),
            pltpu.VMEM((2, wide_rows + 2 * SUBSTEPS, wide_cols), f32),
        ],
        compiler_params=params,
        name="flow",
    )(level, slope, flow_dir, rain, above, below, left, right)
    return (fraction, level)


def solution(mesh):
    placed = (
        P(None, ("tx", "ty"), None),
        P(),
        P(),
        P(),
        P(),
        P(("tx", "ty"), None),
        P(("tx", "ty"), None),
        P(("tx", "ty"), None),
        P(("tx", "ty"), None),
        P("tx", "ty"),
        P("tx", "ty"),
        P("tx", "ty"),
        P("tx", "ty"),
    )
    return jax.shard_map(
        per_device,
        mesh=mesh,
        in_specs=placed,
        out_specs=(P(("tx", "ty"), None), P("tx", "ty")),
        check_vma=False,
    )
```

```python
import functools

import jax
import jax.numpy as jnp
from jax import lax
from jax.experimental import pallas as pl
from jax.experimental.pallas import tpu as pltpu
from jax.sharding import PartitionSpec as P

WIN_ROWS = 2
SUBSTEPS = 8
CH = 16
OUT_LINES = 14
IN_LINES = OUT_LINES + 2
HALO_LINES = 4
LANES = 128
VMEM_LIMIT = 48 * 1024 * 1024

wet_depth = 0.5
runoff_coef = 0.25
bf16 = jnp.bfloat16
f32 = jnp.float32


def iota(shape, dim):
    return lax.broadcasted_iota(jnp.int32, shape, dim)


def dot(a, b):
    return lax.dot_general(a, b, (((1,), (0,)), ((), ())), preferred_element_type=f32)


def dot_0(a, b):
    return lax.dot_general(a, b, (((0,), (0,)), ((), ())), preferred_element_type=f32)


def dot_t(a, b):
    return lax.dot_general(a, b, (((1,), (1,)), ((), ())), preferred_element_type=f32)


def pixel_shifts(x):
    width = x.shape[1]
    pix = iota(x.shape, 1)
    before = jnp.where(pix == 0, 0.0, pltpu.roll(x, 1, 1))
    after = jnp.where(pix == width - 1, 0.0, pltpu.roll(x, width - 1, 1))
    return before, after


def band_weights(tiled, rows, cols, per_row, line_of):
    out_line = iota((rows, cols), 0) // per_row
    off = line_of(iota((rows, cols), 1)) - out_line
    out = jnp.zeros((rows, cols), f32)
    for ky in range(3):
        out = jnp.where(off == ky, tiled[ky], out)
    return out.astype(bf16)


def stack_rows(x, times):
    return jnp.broadcast_to(x[None], (times,) + x.shape).reshape(times * x.shape[0], x.shape[1])


def edge_kernel(sar_ref, depth_ref, slope_ref, rain_ref, dir_ref, up_ref, down_ref):
    lines, px = sar_ref.shape[1:]
    cols = depth_ref.shape[1]
    h = SUBSTEPS
    fields = (
        depth_ref[...],
        runoff_coef * jnp.sqrt(slope_ref[...]),
        rain_ref[...],
        dir_ref[...].astype(f32),
    )
    zeros = jnp.zeros((8, px), f32)
    for ref, lo, strip in (
        (up_ref, lines - HALO_LINES, lambda x: jnp.transpose(x[:, cols - LANES :], (1, 0))[LANES - h :]),
        (down_ref, 0, lambda x: jnp.transpose(x[:, 0:LANES], (1, 0))[0:h]),
    ):
        image = [sar_ref[ch].astype(f32)[lo : lo + HALO_LINES] for ch in range(2)]
        strips = [strip(x) for x in fields]
        ref[...] = jnp.concatenate(
            [jnp.concatenate(strips[0:2], 1), jnp.concatenate(strips[2:4], 1), *image, zeros], 0
        ).astype(bf16)


def strips_of(ref, keep):
    both = jnp.where(keep, ref[0:16, :].astype(f32), 0.0)
    cols = both.shape[1] // 2
    return [both[0:8, 0:cols], both[0:8, cols:], both[8:16, 0:cols], both[8:16, cols:]]


def swath_kernel(
    devices, capacity,
    sar_ref, above_ref, below_ref, k1_ref, k2_ref, k3_ref, k4_ref, gw_any, cell_any, tile_any, row_any,
    frac_ref, send_ref,
    s_ref, xa_ref, xb_ref, x3_ref, obs_ref, wnd_ref, t1_ref, t4_ref, gw_ref, cell_ref, tile_ref, row_ref, sems,
):
    late = [
        pltpu.make_async_copy(src, dst, sems.at[i])
        for i, (src, dst) in enumerate(
            ((gw_any, gw_ref), (cell_any, cell_ref), (tile_any, tile_ref), (row_any, row_ref))
        )
    ]
    for copy in late:
        copy.start()
    lines, px = gw_ref.shape
    blocks = (lines + 2 * HALO_LINES - 2) // OUT_LINES
    frame = lines + 2 * HALO_LINES
    total = frame + 2
    n_ty = lax.axis_size("ty")
    me = lax.axis_index("tx") * n_ty + lax.axis_index("ty")
    first = me == 0
    last = me == devices - 1
    above = above_ref[16:32, :].astype(f32)
    below = below_ref[16:32, :].astype(f32)

    for ch in range(2):
        s_ref[ch, 0:HALO_LINES, :] = above[ch * HALO_LINES : (ch + 1) * HALO_LINES]
        s_ref[ch, HALO_LINES : HALO_LINES + lines, :] = sar_ref[ch].astype(f32)
        s_ref[ch, HALO_LINES + lines : frame, :] = below[ch * HALO_LINES : (ch + 1) * HALO_LINES]

    rows = OUT_LINES * CH
    cols = IN_LINES * CH
    spread = (iota((CH, cols), 1) % CH == iota((CH, cols), 0)).astype(bf16)

    cols1 = 3 * 2 * IN_LINES
    spread1 = (iota((8, cols1), 1) // IN_LINES == iota((8, cols1), 0)).astype(bf16)
    t1_ref[...] = jnp.zeros(t1_ref.shape, f32)
    t4_ref[...] = jnp.zeros(t4_ref.shape, f32)
    for ky in range(3):
        for kx in range(3):
            t1_ref[ky * 8 + 2 * kx : ky * 8 + 2 * kx + 2, :] = k1_ref[ky, kx].astype(f32)
        t4_ref[ky * 3 : ky * 3 + 3, :] = k4_ref[ky].astype(f32)
    w1 = band_weights(
        [stack_rows(dot_0(t1_ref[ky * 8 : ky * 8 + 8, :].astype(bf16), spread1), OUT_LINES) for ky in range(3)],
        rows, cols1, CH, lambda k: k % IN_LINES,
    )

    def mid_weights(ref):
        wide = dot(ref[...], spread)
        return [
            band_weights(
                [stack_rows(wide[(ky * 3 + kx) * CH : (ky * 3 + kx + 1) * CH], OUT_LINES) for ky in range(3)],
                rows, cols, CH, lambda k: k // CH,
            )
            for kx in range(3)
        ]

    def put(ref, line, acc):
        feat = jnp.maximum(acc, 0.0)
        at = pl.ds(line * CH, rows)
        if len(ref.shape) == 2:
            ref[at, :] = feat.astype(bf16)
            return
        before, after = pixel_shifts(feat)
        ref[0, at, :] = before.astype(bf16)
        ref[1, at, :] = feat.astype(bf16)
        ref[2, at, :] = after.astype(bf16)

    def clear(ref, lo, hi):
        shape = ref.shape[:-2] + ((hi - lo) * CH, px)
        ref[..., lo * CH : hi * CH, :] = jnp.zeros(shape, bf16)

    def outside(ref):
        @pl.when(first)
        def _():
            clear(ref, 0, HALO_LINES)

        @pl.when(last)
        def _():
            clear(ref, HALO_LINES + lines, frame)

    for b in range(blocks):
        at = b * OUT_LINES
        x = jnp.concatenate([s_ref[0, at : at + IN_LINES, :], s_ref[1, at : at + IN_LINES, :]], 0)
        before, after = pixel_shifts(x)
        put(xa_ref, 1 + at, dot(w1, jnp.concatenate([before, x, after], 0).astype(bf16)))
    clear(xa_ref, frame - 1, total)
    outside(xa_ref)

    for k_ref, src, dst, line in ((k2_ref, xa_ref, xb_ref, 2), (k3_ref, xb_ref, x3_ref, 3)):
        w = mid_weights(k_ref)
        for b in range(blocks):
            at = pl.ds((line - 1 + b * OUT_LINES) * CH, cols)
            acc = dot(w[0], src[0, at, :]) + dot(w[1], src[1, at, :]) + dot(w[2], src[2, at, :])
            put(dst, line + b * OUT_LINES, acc)
        if len(dst.shape) == 3:
            clear(dst, frame, total)
        outside(dst)

    cols4 = (lines + 2) * CH
    spread4 = (iota((CH, cols4), 1) % CH == iota((CH, cols4), 0)).astype(bf16)
    wide4 = dot(t4_ref[...].astype(bf16), spread4)
    w4 = [
        band_weights(
            [jnp.broadcast_to(wide4[ky * 3 + kx : ky * 3 + kx + 1], (lines, cols4)) for ky in range(3)],
            lines, cols4, 1, lambda k: k // CH,
        )
        for kx in range(3)
    ]
    parts = dot(jnp.concatenate(w4, 0), x3_ref[(HALO_LINES - 1) * CH : (HALO_LINES + lines + 1) * CH, :])
    from_before, _ = pixel_shifts(parts[0:lines])
    _, from_after = pixel_shifts(parts[2 * lines : 3 * lines])
    logit = from_before + parts[lines : 2 * lines] + from_after
    frac = (1.0 / (1.0 + jnp.exp(-logit))).astype(bf16)
    frac_ref[...] = frac
    for copy in late:
        copy.wait()
    obs_ref[...] = frac.astype(f32) * gw_ref[...]

    kind = iota((8, px), 0)
    lane_col = iota((LANES, px), 0)
    group = 8

    def window_group(g, carry):
        at = pl.ds(pl.multiple_of(g * group, group), group)
        cell = cell_ref[at, :]
        obs = obs_ref[at, :]
        cov = gw_ref[at, :]
        part = cell // LANES
        col = cell % LANES
        for i in range(group):
            value = jnp.where(kind < 4, obs[i : i + 1], cov[i : i + 1])
            value = jnp.where(kind % 4 == part[i : i + 1], value, 0.0)
            coarse = value.astype(bf16).astype(f32)
            left = jnp.concatenate([coarse, value - coarse], 0).astype(bf16)
            hot = jnp.where(lane_col == col[i : i + 1], 1.0, 0.0).astype(bf16)
            sums = dot_t(left, hot)
            wnd_ref[pl.ds(pl.multiple_of(g * (8 * group) + 8 * i, 8), 8), :] = sums[0:8] + sums[8:16]
        return carry

    lax.fori_loop(0, lines // group, window_group, 0)

    tile = tile_ref[...].astype(f32)
    same = iota((lines, lines), 0) == iota((lines, lines), 1)
    tile_sub = jnp.sum(jnp.where(same, jnp.broadcast_to(tile, (lines, lines)), 0.0), 1, keepdims=True)
    rival = (tile_sub == tile) & (iota((lines, lines), 0) < iota((lines, lines), 1))
    slot = tile * capacity + jnp.sum(jnp.where(rival, 1.0, 0.0), 0, keepdims=True)
    wnd_rows = 8 * lines
    widen = (iota((lines, wnd_rows), 1) // 8 == iota((lines, wnd_rows), 0)).astype(bf16)
    slot_wide = dot(jnp.broadcast_to(slot, (8, lines)).astype(bf16), widen)[0:1]
    place = slot_wide.astype(jnp.int32) * 4 + (iota((1, wnd_rows), 1) // 2) % 4
    slots = devices * capacity * 4
    perm = jnp.where(iota((slots, wnd_rows), 0) == place, 1.0, 0.0).astype(bf16)
    wnd = wnd_ref[...]
    half = iota((wnd_rows, LANES), 0) % 2
    own_line = iota((wnd_rows, lines), 0) // 8 == iota((wnd_rows, lines), 1)
    row_part = jnp.where(own_line, jnp.broadcast_to(row_ref[...].astype(f32), (wnd_rows, lines)), 0.0)
    row_wide = dot(row_part.astype(bf16), jnp.ones((lines, LANES), bf16))
    goods = jnp.concatenate(
        [jnp.where(half == 0, wnd, 0.0), jnp.where(half == 1, wnd, 0.0), jnp.where(half == 0, row_wide, 0.0)], 1
    ).astype(bf16)
    sorted_rows = dot(perm, goods)
    per_tile = 4 * capacity
    none = jnp.zeros((per_tile, LANES), f32)
    cut = sorted_rows.shape[1] - LANES

    def of_right(x):
        return jnp.concatenate([x[per_tile:], none], 0)

    def of_left(x):
        return jnp.concatenate([none, x[: slots - per_tile]], 0)

    spot = iota((slots, LANES), 1)
    column = (iota((slots, LANES), 0) // per_tile) % n_ty
    row_own = sorted_rows[:, cut:]
    side = jnp.where((spot < SUBSTEPS) & (column < n_ty - 1), of_right(sorted_rows[:, 0:LANES]), 0.0)
    side = jnp.where((spot >= LANES - SUBSTEPS) & (column > 0), of_left(sorted_rows[:, cut - LANES : cut]), side)
    for turn, value in enumerate((row_own, of_right(row_own), of_left(row_own))):
        side = jnp.where(spot == SUBSTEPS + turn, value, side)
    send_ref[...] = jnp.concatenate([sorted_rows[:, 0:cut], side], 1).astype(bf16)


def transposed(x):
    return jnp.transpose(x, (1, 0))


def level_kernel(
    got_ref, from_left_ref, from_right_ref, depth_ref, slope_ref, rain_ref, dir_ref,
    level_ref, side_ref, top_ref, bot_ref,
):
    tile_rows, tile_cols = depth_ref.shape
    k = got_ref.shape[0]
    h = SUBSTEPS
    extra = got_ref[:, tile_cols:].astype(f32)
    lines = transposed(extra)
    lane = iota((1, k), 1)
    offset = lane % 2 + tile_rows * ((lane // 2) % 2)

    def placer(turn):
        target = lines[h + turn : h + turn + 1].astype(jnp.int32) + offset
        return jnp.where(iota((2 * tile_rows, k), 0) == target, 1.0, 0.0).astype(bf16)

    spot = iota((k, LANES), 1)
    rights = jnp.where(spot < h, extra, 0.0).astype(bf16)
    lefts = jnp.where(spot >= LANES - h, extra, 0.0).astype(bf16)
    summed = dot(placer(0), got_ref[:, 0:tile_cols])
    summed_side = dot(placer(1), rights) + dot(placer(2), lefts)

    ty = lax.axis_index("ty")
    left = strips_of(from_left_ref, ty > 0)
    right = strips_of(from_right_ref, ty < lax.axis_size("ty") - 1)
    gap = jnp.zeros((LANES - 2 * h, tile_rows), f32)
    depth_side, conv_side, rain_side, code_side = [
        transposed(jnp.concatenate([r, gap, l], 0)) for r, l in zip(right, left)
    ]

    def analysed(sums, depth):
        observed = sums[0:tile_rows]
        covered = sums[tile_rows:]
        wet = depth / (depth + wet_depth)
        innovation = (observed - covered * wet) / (covered + 1.0)
        return depth * jnp.exp(innovation)

    level = analysed(summed, depth_ref[...])
    level_ref[...] = level
    sides = (analysed(summed_side, depth_side), rain_side, conv_side, code_side)
    owns = (level, rain_ref, slope_ref, dir_ref)

    def end_rows(at):
        own = [x[at, :] for x in owns]
        own[2] = runoff_coef * jnp.sqrt(own[2])
        own[3] = own[3].astype(f32)
        return jnp.concatenate([jnp.concatenate([o, x[at]], 1) for o, x in zip(own, sides)], 0).astype(bf16)

    for i, x in enumerate(sides):
        side_ref[i] = x
    top_ref[...] = end_rows(slice(0, h))
    bot_ref[...] = end_rows(slice(tile_rows - h, tile_rows))


def flow_kernel(
    level_ref, side_ref, slope_ref, dir_ref, rain_ref, above_ref, below_ref,
    out_ref,
    rain_s, conv_s, m_ref, part_ref, up_ref, down_ref,
):
    tile_rows, tile_cols = level_ref.shape
    h = SUBSTEPS
    wide_rows = tile_rows + 2 * h
    wide_cols = tile_cols + LANES

    def widened(field, own):
        at = slice(field * h, (field + 1) * h)
        mid = jnp.concatenate([own, side_ref[field]], 1)
        return jnp.concatenate([above_ref[...].astype(f32)[at], mid, below_ref[...].astype(f32)[at]], 0)

    zeros = jnp.zeros((h, wide_cols), f32)
    for buf in range(2):
        for ref in (up_ref, down_ref):
            ref[buf, 0:h, :] = zeros
            ref[buf, h + wide_rows :, :] = zeros
    part_ref[0] = widened(0, level_ref[...])
    rain_s[...] = widened(1, rain_ref[...])
    conv = widened(2, runoff_coef * jnp.sqrt(slope_ref[...]))
    conv_s[...] = conv
    code = widened(3, dir_ref[...].astype(f32))
    sides = (-1, 0, 1, -1, 1, -1, 0, 1)
    for direction, side in enumerate(sides):
        share = jnp.where(code == direction, conv, 0.0)
        m_ref[direction] = pltpu.roll(share, side % wide_cols, 1) if side else share

    chunk = 16

    def level_at(buf, r, n, step):
        level = part_ref[buf, r : r + n, :]
        if step:
            level = level + up_ref[buf, h + r + 1 : h + r + 1 + n, :] + down_ref[buf, h + r - 1 : h + r - 1 + n, :]
        return level

    for step in range(SUBSTEPS):
        buf, new = step % 2, (step + 1) % 2
        for r in range(0, wide_rows, chunk):
            level = level_at(buf, r, chunk, step)
            power = level * jnp.exp((2.0 / 3.0) * jnp.log(jnp.maximum(jnp.abs(level), 1e-30)))
            from_right = pltpu.roll(power, wide_cols - 1, 1)
            from_left = pltpu.roll(power, 1, 1)
            m = [m_ref[d, r : r + chunk, :] for d in range(8)]
            up_ref[new, h + r : h + r + chunk, :] = m[0] * from_right + m[1] * power + m[2] * from_left
            down_ref[new, h + r : h + r + chunk, :] = m[5] * from_right + m[6] * power + m[7] * from_left
            part_ref[new, r : r + chunk, :] = (
                level + rain_s[r : r + chunk, :] - conv_s[r : r + chunk, :] * power
                + (m[3] * from_right + m[4] * from_left)
            )
    buf = SUBSTEPS % 2
    out_ref[...] = level_at(buf, h, tile_rows, SUBSTEPS)[:, 0:tile_cols]


def vmem_specs(n):
    return [pl.BlockSpec(memory_space=pltpu.VMEM)] * n


def per_device(
    sar_image, kernel_first, kernel_second, kernel_third, kernel_last,
    geo_weight, cell_index, block_tile, block_row, depth, slope, flow_dir, rain,
):
    both = ("tx", "ty")
    devices = lax.axis_size(both)
    az_lines, range_px = geo_weight.shape
    tile_rows, tile_cols = depth.shape
    capacity = max(2, 2 * az_lines // devices)

    def steps(axis):
        size = lax.axis_size(axis)
        up = [(i, i + 1) for i in range(size - 1)]
        return up, [(j, i) for i, j in up]

    params = pltpu.CompilerParams(vmem_limit_bytes=VMEM_LIMIT)
    up, down = steps(both)
    message = jax.ShapeDtypeStruct((32, range_px), bf16)
    to_next, to_previous = pl.pallas_call(
        edge_kernel,
        out_shape=(message, message),
        in_specs=vmem_specs(5),
        out_specs=tuple(vmem_specs(2)),
        compiler_params=params,
        name="edges",
    )(sar_image, depth, slope, rain, flow_dir)
    from_previous = lax.ppermute(to_next, both, up)
    from_next = lax.ppermute(to_previous, both, down)

    slots = devices * capacity * 4
    frame = az_lines + 2 * HALO_LINES
    feats = (frame + 2) * CH
    send_lanes = tile_cols + LANES
    late = (
        geo_weight, cell_index, block_tile.reshape(1, az_lines), block_row.reshape(1, az_lines),
    )
    fraction, send = pl.pallas_call(
        functools.partial(swath_kernel, devices, capacity),
        out_shape=(
            jax.ShapeDtypeStruct((az_lines, range_px), bf16),
            jax.ShapeDtypeStruct((slots, send_lanes), bf16),
        ),
        in_specs=vmem_specs(7) + [pl.BlockSpec(memory_space=pl.ANY)] * 4,
        out_specs=tuple(vmem_specs(2)),
        scratch_shapes=[
            pltpu.VMEM((2, frame + 8, range_px), f32),
            pltpu.VMEM((3, feats, range_px), bf16),
            pltpu.VMEM((3, feats, range_px), bf16),
            pltpu.VMEM((feats, range_px), bf16),
            pltpu.VMEM((az_lines, range_px), f32),
            pltpu.VMEM((8 * az_lines, LANES), f32),
            pltpu.VMEM((24, CH), f32),
            pltpu.VMEM((16, CH), f32),
            *[pltpu.VMEM(x.shape, x.dtype) for x in late],
            pltpu.SemaphoreType.DMA((4,)),
        ],
        compiler_params=params,
        name="swath",
    )(
        sar_image, from_previous, from_next,
        jnp.transpose(kernel_first, (2, 3, 1, 0)),
        jnp.transpose(kernel_second, (2, 3, 0, 1)).reshape(9 * CH, CH),
        jnp.transpose(kernel_third, (2, 3, 0, 1)).reshape(9 * CH, CH),
        jnp.transpose(kernel_last[0], (1, 2, 0)),
        *late,
    )

    got = lax.all_to_all(
        send.reshape(devices, capacity * 4, send_lanes), both, split_axis=0, concat_axis=0, tiled=True
    ).reshape(slots, send_lanes)

    edge = jax.ShapeDtypeStruct((4 * SUBSTEPS, send_lanes), bf16)
    level, side, top_rows, bot_rows = pl.pallas_call(
        level_kernel,
        out_shape=(
            jax.ShapeDtypeStruct((tile_rows, tile_cols), f32),
            jax.ShapeDtypeStruct((4, tile_rows, LANES), f32),
            edge,
            edge,
        ),
        in_specs=vmem_specs(7),
        out_specs=tuple(vmem_specs(4)),
        compiler_params=params,
        name="level",
    )(got, from_previous, from_next, depth, slope, rain, flow_dir)

    up, down = steps("tx")
    above = lax.ppermute(bot_rows, "tx", up)
    below = lax.ppermute(top_rows, "tx", down)

    wide_rows = tile_rows + 2 * SUBSTEPS
    wide_cols = tile_cols + LANES
    level = pl.pallas_call(
        flow_kernel,
        out_shape=jax.ShapeDtypeStruct((tile_rows, tile_cols), f32),
        in_specs=vmem_specs(7),
        out_specs=vmem_specs(1)[0],
        scratch_shapes=[
            pltpu.VMEM((wide_rows, wide_cols), f32),
            pltpu.VMEM((wide_rows, wide_cols), f32),
            pltpu.VMEM((8, wide_rows, wide_cols), f32),
            pltpu.VMEM((2, wide_rows, wide_cols), f32),
            pltpu.VMEM((2, wide_rows + 2 * SUBSTEPS, wide_cols), f32),
            pltpu.VMEM((2, wide_rows + 2 * SUBSTEPS, wide_cols), f32),
        ],
        compiler_params=params,
        name="flow",
    )(level, side, slope, flow_dir, rain, above, below)
    return (fraction, level)


def solution(mesh):
    placed = (
        P(None, ("tx", "ty"), None),
        P(),
        P(),
        P(),
        P(),
        P(("tx", "ty"), None),
        P(("tx", "ty"), None),
        P(("tx", "ty"), None),
        P(("tx", "ty"), None),
        P("tx", "ty"),
        P("tx", "ty"),
        P("tx", "ty"),
        P("tx", "ty"),
    )
    return jax.shard_map(
        per_device,
        mesh=mesh,
        in_specs=placed,
        out_specs=(P(("tx", "ty"), None), P("tx", "ty")),
        check_vma=False,
    )
```

```python
import functools

import jax
import jax.numpy as jnp
from jax import lax
from jax.experimental import pallas as pl
from jax.experimental.pallas import tpu as pltpu
from jax.sharding import PartitionSpec as P

WIN_ROWS = 2
SUBSTEPS = 8
CH = 16
OUT_LINES = 14
IN_LINES = OUT_LINES + 2
HALO_LINES = 4
LANES = 128
VMEM_LIMIT = 48 * 1024 * 1024

wet_depth = 0.5
runoff_coef = 0.25
bf16 = jnp.bfloat16
f32 = jnp.float32


def iota(shape, dim):
    return lax.broadcasted_iota(jnp.int32, shape, dim)


def dot(a, b):
    return lax.dot_general(a, b, (((1,), (0,)), ((), ())), preferred_element_type=f32)


def dot_0(a, b):
    return lax.dot_general(a, b, (((0,), (0,)), ((), ())), preferred_element_type=f32)


def dot_t(a, b):
    return lax.dot_general(a, b, (((1,), (1,)), ((), ())), preferred_element_type=f32)


def pixel_shifts(x):
    width = x.shape[1]
    pix = iota(x.shape, 1)
    before = jnp.where(pix == 0, 0.0, pltpu.roll(x, 1, 1))
    after = jnp.where(pix == width - 1, 0.0, pltpu.roll(x, width - 1, 1))
    return before, after


def band_weights(tiled, rows, cols, per_row, line_of):
    out_line = iota((rows, cols), 0) // per_row
    off = line_of(iota((rows, cols), 1)) - out_line
    out = jnp.zeros((rows, cols), f32)
    for ky in range(3):
        out = jnp.where(off == ky, tiled[ky], out)
    return out.astype(bf16)


def edge_kernel(
    sar_hbm, depth_hbm, slope_hbm, rain_hbm, dir_hbm, up_ref, down_ref,
    last_ref, first_ref, depth_ref, slope_ref, rain_ref, dir_ref, sems,
):
    lines, px = sar_hbm.shape[1:]
    cols = depth_hbm.shape[1]
    h = SUBSTEPS
    copies = [
        pltpu.make_async_copy(src, dst, sems.at[i])
        for i, (src, dst) in enumerate(
            (
                (depth_hbm, depth_ref), (slope_hbm, slope_ref), (rain_hbm, rain_ref), (dir_hbm, dir_ref),
                (sar_hbm.at[:, lines - 16 : lines, :], last_ref), (sar_hbm.at[:, 0:16, :], first_ref),
            )
        )
    ]
    for copy in copies:
        copy.start()
    for copy in copies:
        copy.wait()
    fields = (
        depth_ref[...],
        runoff_coef * jnp.sqrt(slope_ref[...]),
        rain_ref[...],
        dir_ref[...].astype(f32),
    )
    zeros = jnp.zeros((8, px), f32)
    for ref, image_ref, lo, strip in (
        (up_ref, last_ref, 16 - HALO_LINES, lambda x: jnp.transpose(x[:, cols - LANES :], (1, 0))[LANES - h :]),
        (down_ref, first_ref, 0, lambda x: jnp.transpose(x[:, 0:LANES], (1, 0))[0:h]),
    ):
        image = [image_ref[ch].astype(f32)[lo : lo + HALO_LINES] for ch in range(2)]
        strips = [strip(x) for x in fields]
        ref[...] = jnp.concatenate(
            [jnp.concatenate(strips[0:2], 1), jnp.concatenate(strips[2:4], 1), *image, zeros], 0
        ).astype(bf16)


def strips_of(ref, keep):
    both = jnp.where(keep, ref[0:16, :].astype(f32), 0.0)
    cols = both.shape[1] // 2
    return [both[0:8, 0:cols], both[0:8, cols:], both[8:16, 0:cols], both[8:16, cols:]]


def swath_kernel(
    devices, capacity,
    above_ref, below_ref,
    sar_hbm, k1_hbm, k2_hbm, k3_hbm, k4_hbm, gw_hbm, cell_hbm, tile_hbm, row_hbm,
    frac_ref, send_ref,
    sar_ref, k1_ref, k2_ref, k3_ref, k4_ref, gw_ref, cell_ref, tile_ref, row_ref, sems,
    s_ref, xa_ref, xb_ref, x3_ref, w2_ref, w3_ref, w1_ref, t1_ref, t4_ref, logit_ref, obs_ref, wnd_ref,
):
    pairs = (
        (k1_hbm, k1_ref), (k2_hbm, k2_ref), (k3_hbm, k3_ref), (k4_hbm, k4_ref), (sar_hbm, sar_ref),
        (gw_hbm, gw_ref), (cell_hbm, cell_ref), (tile_hbm, tile_ref), (row_hbm, row_ref),
    )
    copies = [pltpu.make_async_copy(src, dst, sems.at[i]) for i, (src, dst) in enumerate(pairs)]
    for copy in copies:
        copy.start()
    lines, px = gw_ref.shape
    blocks = (lines + 2 * HALO_LINES - 2) // OUT_LINES
    frame = lines + 2 * HALO_LINES
    total = xa_ref.shape[0] // CH
    n_ty = lax.axis_size("ty")
    me = lax.axis_index("tx") * n_ty + lax.axis_index("ty")
    first = me == 0
    last = me == devices - 1
    rows = OUT_LINES * CH
    cols = IN_LINES * CH

    out_of = iota((CH, OUT_LINES * cols), 1) // cols
    in_of = iota((CH, OUT_LINES * cols), 1) % cols - iota((CH, OUT_LINES * cols), 0)
    spread = [(in_of == CH * (out_of + ky)).astype(bf16) for ky in range(3)]
    n1 = OUT_LINES * LANES
    group1 = iota((8, n1), 1) % LANES // IN_LINES == iota((8, n1), 0)
    line1 = iota((8, n1), 1) % IN_LINES - iota((8, n1), 1) // LANES
    spread1 = [(group1 & (line1 == ky)).astype(bf16) for ky in range(3)]
    tile4 = (iota((CH, cols), 1) % CH == iota((CH, cols), 0)).astype(bf16)
    t1_ref[...] = jnp.zeros(t1_ref.shape, f32)
    t4_ref[...] = jnp.zeros(t4_ref.shape, f32)

    for copy in copies[0:4]:
        copy.wait()
    for ky in range(3):
        for kx in range(3):
            t1_ref[ky * 8 + 2 * kx : ky * 8 + 2 * kx + 2, :] = k1_ref[ky, kx].astype(f32)
        t4_ref[ky * 3 : ky * 3 + 3, :] = k4_ref[ky].astype(f32)
    wide1 = sum(dot_0(t1_ref[ky * 8 : ky * 8 + 8, :].astype(bf16), spread1[ky]) for ky in range(3))
    for i in range(OUT_LINES):
        w1_ref[i * CH : (i + 1) * CH, :] = wide1[:, i * LANES : (i + 1) * LANES].astype(bf16)
    for k_ref, w_ref in ((k2_ref, w2_ref), (k3_ref, w3_ref)):
        wide = sum(dot(k_ref[ky * 3 * CH : (ky + 1) * 3 * CH, :], spread[ky]) for ky in range(3))
        for kx in range(3):
            for i in range(OUT_LINES):
                w_ref[kx * rows + i * CH : kx * rows + (i + 1) * CH, :] = wide[
                    kx * CH : (kx + 1) * CH, i * cols : (i + 1) * cols
                ].astype(bf16)
    wide4 = dot(t4_ref[...].astype(bf16), tile4)
    w4 = jnp.concatenate(
        [
            band_weights(
                [jnp.broadcast_to(wide4[ky * 3 + kx : ky * 3 + kx + 1], (CH, cols)) for ky in range(3)],
                CH, cols, 1, lambda k: k // CH,
            )
            for kx in range(3)
        ],
        0,
    )

    def clear(ref, lo, hi):
        ref[lo * CH : hi * CH, :] = jnp.zeros(((hi - lo) * CH, px), bf16)

    def outside(ref):
        @pl.when(first)
        def _():
            clear(ref, 0, HALO_LINES)

        @pl.when(last)
        def _():
            clear(ref, HALO_LINES + lines, frame)

    def merged(sums, n):
        before, _ = pixel_shifts(sums[0:n])
        _, after = pixel_shifts(sums[2 * n : 3 * n])
        return before + sums[n : 2 * n] + after

    for ref, line in ((xa_ref, 1), (xb_ref, 2), (x3_ref, 3)):
        clear(ref, line + blocks * OUT_LINES, total)
    above = above_ref[16:32, :].astype(f32)
    below = below_ref[16:32, :].astype(f32)
    copies[4].wait()
    for ch in range(2):
        s_ref[ch, 0:HALO_LINES, :] = above[ch * HALO_LINES : (ch + 1) * HALO_LINES]
        s_ref[ch, HALO_LINES : HALO_LINES + lines, :] = sar_ref[ch].astype(f32)
        s_ref[ch, HALO_LINES + lines : frame, :] = below[ch * HALO_LINES : (ch + 1) * HALO_LINES]
    pad = jnp.zeros((LANES - 6 * IN_LINES, px), f32)
    for b in range(blocks):
        at = b * OUT_LINES
        x = jnp.concatenate([s_ref[0, at : at + IN_LINES, :], s_ref[1, at : at + IN_LINES, :]], 0)
        before, after = pixel_shifts(x)
        acc = dot(w1_ref[...], jnp.concatenate([before, x, after, pad], 0).astype(bf16))
        xa_ref[(1 + at) * CH : (1 + at) * CH + rows, :] = jnp.maximum(acc, 0.0).astype(bf16)
    outside(xa_ref)

    for w_ref, src, dst, line in ((w2_ref, xa_ref, xb_ref, 2), (w3_ref, xb_ref, x3_ref, 3)):
        for b in range(blocks):
            at = line + b * OUT_LINES
            sums = dot(w_ref[...], src[(at - 1) * CH : (at - 1) * CH + cols, :])
            dst[at * CH : at * CH + rows, :] = jnp.maximum(merged(sums, rows), 0.0).astype(bf16)
        outside(dst)

    for b in range(blocks):
        at = HALO_LINES - 1 + b * OUT_LINES
        sums = dot(w4, x3_ref[at * CH : at * CH + cols, :])
        logit_ref[b * OUT_LINES : b * OUT_LINES + CH, :] = merged(sums, CH)
    frac = (1.0 / (1.0 + jnp.exp(-logit_ref[0:lines, :]))).astype(bf16)
    frac_ref[...] = frac
    for copy in copies[5:]:
        copy.wait()
    obs_ref[...] = frac.astype(f32) * gw_ref[...]

    quarter = wnd_ref.shape[1]
    parts = wnd_ref.shape[0] // lines // 2
    kind = iota((CH, px), 0)
    is_obs = kind < parts
    kind_part = (kind % parts).astype(f32).astype(bf16)
    sub = kind.astype(f32).astype(bf16)
    one = jnp.ones((CH, px), bf16)
    nil = jnp.zeros((CH, px), bf16)
    spots = [sub + g * CH for g in range(quarter // CH)]
    group = 8

    def window_group(g, carry):
        at = pl.ds(pl.multiple_of(g * group, group), group)
        cell = cell_ref[at, :]
        obs = obs_ref[at, :]
        cov = gw_ref[at, :]
        part = (cell // quarter).astype(f32)
        col = (cell % quarter).astype(f32)

        def spread_row(x, i):
            return jnp.broadcast_to(x[i : i + 1], (CH, px)).astype(bf16)

        for i in range(group):
            value = jnp.where(is_obs, obs[i : i + 1], cov[i : i + 1]).astype(bf16)
            left = jnp.where(kind_part == spread_row(part, i), value, nil)
            where_col = spread_row(col, i)
            hot = jnp.concatenate([jnp.where(spot == where_col, one, nil) for spot in spots], 0)
            wnd_ref[pl.ds(pl.multiple_of(g * (CH * group) + CH * i, CH), CH), :] = dot_t(left, hot)
        return carry

    lax.fori_loop(0, lines // group, window_group, 0)

    tile = tile_ref[...].astype(f32)
    same = iota((lines, lines), 0) == iota((lines, lines), 1)
    tile_sub = jnp.sum(jnp.where(same, jnp.broadcast_to(tile, (lines, lines)), 0.0), 1, keepdims=True)
    rival = (tile_sub == tile) & (iota((lines, lines), 0) < iota((lines, lines), 1))
    slot = tile * capacity + jnp.sum(jnp.where(rival, 1.0, 0.0), 0, keepdims=True)
    wnd_rows = wnd_ref.shape[0]
    per_line = wnd_rows // lines
    widen = (iota((lines, wnd_rows), 1) // per_line == iota((lines, wnd_rows), 0)).astype(bf16)
    slot_wide = dot(jnp.broadcast_to(slot, (8, lines)).astype(bf16), widen)[0:1]
    place = slot_wide.astype(jnp.int32) * 4 + (iota((1, wnd_rows), 1) // 4) % 4
    per_tile = 4 * capacity
    slots = devices * per_tile
    perm = jnp.where(iota((slots, wnd_rows), 0) == place, 1.0, 0.0).astype(bf16)
    tile_cols = 4 * quarter
    repeat = (iota((quarter, tile_cols), 1) % quarter == iota((quarter, tile_cols), 0)).astype(bf16)
    tiled = dot(wnd_ref[...].astype(bf16), repeat)
    mine = iota((wnd_rows, tile_cols), 0) % 4 == iota((wnd_rows, tile_cols), 1) // quarter
    by_slot = dot(perm, jnp.where(mine, tiled, 0.0).astype(bf16))
    row_of = dot(
        jnp.where(same, jnp.broadcast_to(row_ref[...].astype(f32), (lines, lines)), 0.0).astype(bf16),
        jnp.ones((lines, LANES), bf16),
    )
    perm_line = jnp.where(iota((slots, lines), 0) // 4 == slot.astype(jnp.int32), 1.0, 0.0).astype(bf16)
    row_own = dot(perm_line, row_of.astype(bf16))

    none = jnp.zeros((per_tile, LANES), f32)

    def of_right(x):
        return jnp.concatenate([x[per_tile:], none], 0)

    def of_left(x):
        return jnp.concatenate([none, x[: slots - per_tile]], 0)

    h = SUBSTEPS
    lane = iota((slots, LANES), 1)
    entry = iota((slots, LANES), 0) % per_tile
    column = iota((slots, LANES), 0) // per_tile % n_ty
    source = iota((LANES, LANES), 0)
    target = iota((LANES, LANES), 1)
    take_first = ((source < h) & (target % h == source)).astype(bf16)
    take_last = ((source >= LANES - h) & (target % h == source - (LANES - h))).astype(bf16)
    right_strip = dot(of_right(by_slot[:, 0:LANES]).astype(bf16), take_first)
    left_strip = dot(of_left(by_slot[:, tile_cols - LANES :]).astype(bf16), take_last)
    right_strip = jnp.where((lane // h == entry) & (column < n_ty - 1), right_strip, 0.0)
    left_strip = jnp.where((lane // h == entry) & (column > 0), left_strip, 0.0)
    info = jnp.zeros((slots, LANES), f32)
    for turn, value in enumerate((row_own, of_right(row_own), of_left(row_own))):
        info = jnp.where(lane == turn * per_tile + entry, value, info)
    extra_row = iota((8 * devices, slots), 0)
    extra_tile = iota((8 * devices, slots), 1) // per_tile
    extra = sum(
        dot((extra_row == 8 * extra_tile + r).astype(bf16), x.astype(bf16))
        for r, x in enumerate((right_strip, left_strip, info))
    )
    halves = [by_slot[:, at : at + LANES].reshape(devices, per_tile, LANES) for at in range(0, tile_cols, LANES)]
    packed = jnp.concatenate([*halves, extra.reshape(devices, 8, LANES)], 1)
    send_ref[...] = packed.reshape(send_ref.shape).astype(bf16)


def transposed(x):
    return jnp.transpose(x, (1, 0))


def level_kernel(
    devices,
    got_ref, from_left_ref, from_right_ref, depth_ref, slope_ref, rain_ref, dir_ref,
    level_ref, side_ref, top_ref, bot_ref,
):
    tile_rows, tile_cols = depth_ref.shape
    h = SUBSTEPS
    halves = tile_cols // LANES
    n = (got_ref.shape[0] // devices - 8) // halves
    k = devices * n
    packed = got_ref[...].astype(f32).reshape(devices, halves * n + 8, LANES)
    main = jnp.concatenate([packed[:, i * n : (i + 1) * n].reshape(k, LANES) for i in range(halves)], 1)
    extra = packed[:, halves * n :]

    entry = iota((k, LANES), 0) % n
    spread = iota((k, LANES), 1) // h == entry

    def strip(r, first):
        rows = jnp.broadcast_to(extra[:, r : r + 1], (devices, n, LANES)).reshape(k, LANES)
        take = iota((LANES, LANES), 0) % h + first == iota((LANES, LANES), 1)
        return dot(jnp.where(spread, rows, 0.0).astype(bf16), take.astype(bf16)).astype(bf16)

    lane = iota((1, k), 1)
    offset = lane % 2 + tile_rows * ((lane // 2) % 2)
    own_source = iota((8 * devices, k), 0) == 8 * (iota((8 * devices, k), 1) // n) + 2
    info = extra.reshape(8 * devices, LANES).astype(bf16)

    def placer(turn):
        pick = (iota((LANES, k), 0) == turn * n + iota((LANES, k), 1) % n).astype(bf16)
        line = jnp.sum(jnp.where(own_source, dot(info, pick), 0.0), 0, keepdims=True)
        target = line.astype(jnp.int32) + offset
        return jnp.where(iota((2 * tile_rows, k), 0) == target, 1.0, 0.0).astype(bf16)

    summed = dot(placer(0), main.astype(bf16))
    summed_side = dot(placer(1), strip(0, 0)) + dot(placer(2), strip(1, LANES - h))

    ty = lax.axis_index("ty")
    left = strips_of(from_left_ref, ty > 0)
    right = strips_of(from_right_ref, ty < lax.axis_size("ty") - 1)
    gap = jnp.zeros((LANES - 2 * h, tile_rows), f32)
    depth_side, conv_side, rain_side, code_side = [
        transposed(jnp.concatenate([r, gap, l], 0)) for r, l in zip(right, left)
    ]

    def analysed(sums, depth):
        observed = sums[0:tile_rows]
        covered = sums[tile_rows:]
        wet = depth / (depth + wet_depth)
        innovation = (observed - covered * wet) / (covered + 1.0)
        return depth * jnp.exp(innovation)

    level = analysed(summed, depth_ref[...])
    level_ref[...] = level
    sides = (analysed(summed_side, depth_side), rain_side, conv_side, code_side)
    owns = (level, rain_ref, slope_ref, dir_ref)

    def end_rows(at):
        own = [x[at, :] for x in owns]
        own[2] = runoff_coef * jnp.sqrt(own[2])
        own[3] = own[3].astype(f32)
        return jnp.concatenate([jnp.concatenate([o, x[at]], 1) for o, x in zip(own, sides)], 0).astype(bf16)

    for i, x in enumerate(sides):
        side_ref[i] = x
    top_ref[...] = end_rows(slice(0, h))
    bot_ref[...] = end_rows(slice(tile_rows - h, tile_rows))


def flow_kernel(
    level_ref, side_ref, slope_ref, dir_ref, rain_ref, above_ref, below_ref,
    out_ref,
    rain_s, conv_s, m_ref, part_ref, up_ref, down_ref,
):
    tile_rows, tile_cols = level_ref.shape
    h = SUBSTEPS
    wide_rows = tile_rows + 2 * h
    wide_cols = tile_cols + LANES

    def widened(field, own):
        at = slice(field * h, (field + 1) * h)
        mid = jnp.concatenate([own, side_ref[field]], 1)
        return jnp.concatenate([above_ref[...].astype(f32)[at], mid, below_ref[...].astype(f32)[at]], 0)

    zeros = jnp.zeros((h, wide_cols), f32)
    for buf in range(2):
        for ref in (up_ref, down_ref):
            ref[buf, 0:h, :] = zeros
            ref[buf, h + wide_rows :, :] = zeros
    part_ref[0] = widened(0, level_ref[...])
    rain_s[...] = widened(1, rain_ref[...])
    conv = widened(2, runoff_coef * jnp.sqrt(slope_ref[...]))
    conv_s[...] = conv
    code = widened(3, dir_ref[...].astype(f32))
    sides = (-1, 0, 1, -1, 1, -1, 0, 1)
    for direction, side in enumerate(sides):
        share = jnp.where(code == direction, conv, 0.0)
        m_ref[direction] = pltpu.roll(share, side % wide_cols, 1) if side else share

    chunk = 16

    def level_at(buf, r, n, step):
        level = part_ref[buf, r : r + n, :]
        if step:
            level = level + up_ref[buf, h + r + 1 : h + r + 1 + n, :] + down_ref[buf, h + r - 1 : h + r - 1 + n, :]
        return level

    for step in range(SUBSTEPS):
        buf, new = step % 2, (step + 1) % 2
        for r in range(0, wide_rows, chunk):
            level = level_at(buf, r, chunk, step)
            power = level * jnp.exp((2.0 / 3.0) * jnp.log(jnp.maximum(jnp.abs(level), 1e-30)))
            from_right = pltpu.roll(power, wide_cols - 1, 1)
            from_left = pltpu.roll(power, 1, 1)
            m = [m_ref[d, r : r + chunk, :] for d in range(8)]
            up_ref[new, h + r : h + r + chunk, :] = m[0] * from_right + m[1] * power + m[2] * from_left
            down_ref[new, h + r : h + r + chunk, :] = m[5] * from_right + m[6] * power + m[7] * from_left
            part_ref[new, r : r + chunk, :] = (
                level + rain_s[r : r + chunk, :] - conv_s[r : r + chunk, :] * power
                + (m[3] * from_right + m[4] * from_left)
            )
    buf = SUBSTEPS % 2
    out_ref[...] = level_at(buf, h, tile_rows, SUBSTEPS)[:, 0:tile_cols]


def hbm_specs(n):
    return [pl.BlockSpec(memory_space=pltpu.HBM)] * n


def vmem_specs(n):
    return [pl.BlockSpec(memory_space=pltpu.VMEM)] * n


def per_device(
    sar_image, kernel_first, kernel_second, kernel_third, kernel_last,
    geo_weight, cell_index, block_tile, block_row, depth, slope, flow_dir, rain,
):
    both = ("tx", "ty")
    devices = lax.axis_size(both)
    az_lines, range_px = geo_weight.shape
    tile_rows, tile_cols = depth.shape
    capacity = max(2, 2 * az_lines // devices)

    def steps(axis):
        size = lax.axis_size(axis)
        up = [(i, i + 1) for i in range(size - 1)]
        return up, [(j, i) for i, j in up]

    params = pltpu.CompilerParams(vmem_limit_bytes=VMEM_LIMIT)
    up, down = steps(both)
    message = jax.ShapeDtypeStruct((32, range_px), bf16)
    to_next, to_previous = pl.pallas_call(
        edge_kernel,
        out_shape=(message, message),
        in_specs=hbm_specs(5),
        out_specs=tuple(vmem_specs(2)),
        scratch_shapes=[
            pltpu.VMEM((2, 16, range_px), bf16),
            pltpu.VMEM((2, 16, range_px), bf16),
            *[pltpu.VMEM(x.shape, x.dtype) for x in (depth, slope, rain, flow_dir)],
            pltpu.SemaphoreType.DMA((6,)),
        ],
        compiler_params=params,
        name="edges",
    )(sar_image, depth, slope, rain, flow_dir)
    from_previous = lax.ppermute(to_next, both, up)
    from_next = lax.ppermute(to_previous, both, down)

    feats = (az_lines + 2 * HALO_LINES + 4) * CH
    rows, cols = OUT_LINES * CH, IN_LINES * CH
    send_rows = tile_cols // LANES * 4 * capacity + 8
    inputs = (
        sar_image,
        jnp.transpose(kernel_first, (2, 3, 1, 0)),
        jnp.transpose(kernel_second, (2, 3, 0, 1)).reshape(9 * CH, CH),
        jnp.transpose(kernel_third, (2, 3, 0, 1)).reshape(9 * CH, CH),
        jnp.transpose(kernel_last[0], (1, 2, 0)),
        geo_weight, cell_index, block_tile.reshape(1, az_lines), block_row.reshape(1, az_lines),
    )
    fraction, send = pl.pallas_call(
        functools.partial(swath_kernel, devices, capacity),
        out_shape=(
            jax.ShapeDtypeStruct((az_lines, range_px), bf16),
            jax.ShapeDtypeStruct((devices * send_rows, LANES), bf16),
        ),
        in_specs=vmem_specs(2) + hbm_specs(9),
        out_specs=tuple(vmem_specs(2)),
        scratch_shapes=[
            *[pltpu.VMEM(x.shape, x.dtype) for x in inputs],
            pltpu.SemaphoreType.DMA((9,)),
            pltpu.VMEM((2, az_lines + 2 * HALO_LINES + 8, range_px), f32),
            pltpu.VMEM((feats, range_px), bf16),
            pltpu.VMEM((feats, range_px), bf16),
            pltpu.VMEM((feats, range_px), bf16),
            pltpu.VMEM((3 * rows, cols), bf16),
            pltpu.VMEM((3 * rows, cols), bf16),
            pltpu.VMEM((rows, LANES), bf16),
            pltpu.VMEM((24, CH), f32),
            pltpu.VMEM((16, CH), f32),
            pltpu.VMEM((az_lines + 2 * CH, range_px), f32),
            pltpu.VMEM((az_lines, range_px), f32),
            pltpu.VMEM((CH * az_lines, tile_cols // 4), f32),
        ],
        compiler_params=params,
        name="swath",
    )(from_previous, from_next, *inputs)

    got = lax.all_to_all(
        send.reshape(devices, send_rows, LANES), both, split_axis=0, concat_axis=0, tiled=True
    ).reshape(devices * send_rows, LANES)

    wide_rows = tile_rows + 2 * SUBSTEPS
    wide_cols = tile_cols + LANES
    edge = jax.ShapeDtypeStruct((4 * SUBSTEPS, wide_cols), bf16)
    level, side, top_rows, bot_rows = pl.pallas_call(
        functools.partial(level_kernel, devices),
        out_shape=(
            jax.ShapeDtypeStruct((tile_rows, tile_cols), f32),
            jax.ShapeDtypeStruct((4, tile_rows, LANES), f32),
            edge,
            edge,
        ),
        in_specs=vmem_specs(7),
        out_specs=tuple(vmem_specs(4)),
        compiler_params=params,
        name="level",
    )(got, from_previous, from_next, depth, slope, rain, flow_dir)

    up, down = steps("tx")
    above = lax.ppermute(bot_rows, "tx", up)
    below = lax.ppermute(top_rows, "tx", down)

    level = pl.pallas_call(
        flow_kernel,
        out_shape=jax.ShapeDtypeStruct((tile_rows, tile_cols), f32),
        in_specs=vmem_specs(7),
        out_specs=vmem_specs(1)[0],
        scratch_shapes=[
            pltpu.VMEM((wide_rows, wide_cols), f32),
            pltpu.VMEM((wide_rows, wide_cols), f32),
            pltpu.VMEM((8, wide_rows, wide_cols), f32),
            pltpu.VMEM((2, wide_rows, wide_cols), f32),
            pltpu.VMEM((2, wide_rows + 2 * SUBSTEPS, wide_cols), f32),
            pltpu.VMEM((2, wide_rows + 2 * SUBSTEPS, wide_cols), f32),
        ],
        compiler_params=params,
        name="flow",
    )(level, side, slope, flow_dir, rain, above, below)
    return (fraction, level)


def solution(mesh):
    placed = (
        P(None, ("tx", "ty"), None),
        P(),
        P(),
        P(),
        P(),
        P(("tx", "ty"), None),
        P(("tx", "ty"), None),
        P(("tx", "ty"), None),
        P(("tx", "ty"), None),
        P("tx", "ty"),
        P("tx", "ty"),
        P("tx", "ty"),
        P("tx", "ty"),
    )
    return jax.shard_map(
        per_device,
        mesh=mesh,
        in_specs=placed,
        out_specs=(P(("tx", "ty"), None), P("tx", "ty")),
        check_vma=False,
    )
```

```python
import functools

import jax
import jax.numpy as jnp
from jax import lax
from jax.experimental import pallas as pl
from jax.experimental.pallas import tpu as pltpu
from jax.sharding import PartitionSpec as P

WIN_ROWS = 2
SUBSTEPS = 8
CH = 16
OUT_LINES = 14
IN_LINES = OUT_LINES + 2
HALO_LINES = 4
LANES = 128
VMEM_LIMIT = 48 * 1024 * 1024
VMEM_MOST = 61920 * 1024

wet_depth = 0.5
runoff_coef = 0.25
bf16 = jnp.bfloat16
f32 = jnp.float32


def iota(shape, dim):
    return lax.broadcasted_iota(jnp.int32, shape, dim)


def quo(x, n):
    assert n & (n - 1) == 0
    return lax.shift_right_logical(x, jnp.int32(n.bit_length() - 1)) if n > 1 else x


def rem(x, n):
    assert n & (n - 1) == 0
    return x & (n - 1)


def dot(a, b):
    return lax.dot_general(a, b, (((1,), (0,)), ((), ())), preferred_element_type=f32)


def dot_0(a, b):
    return lax.dot_general(a, b, (((0,), (0,)), ((), ())), preferred_element_type=f32)


def dot_t(a, b):
    return lax.dot_general(a, b, (((1,), (1,)), ((), ())), preferred_element_type=f32)


def pixel_shifts(x):
    width = x.shape[1]
    pix = iota(x.shape, 1)
    before = jnp.where(pix == 0, 0.0, pltpu.roll(x, 1, 1))
    after = jnp.where(pix == width - 1, 0.0, pltpu.roll(x, width - 1, 1))
    return before, after


def band_weights(tiled, rows, cols, per_row, line_of):
    out_line = quo(iota((rows, cols), 0), per_row)
    off = line_of(iota((rows, cols), 1)) - out_line
    out = jnp.zeros((rows, cols), f32)
    for ky in range(3):
        out = jnp.where(off == ky, tiled[ky], out)
    return out.astype(bf16)


def edge_kernel(
    sar_hbm, depth_hbm, slope_hbm, rain_hbm, dir_hbm, up_ref, down_ref,
    last_ref, first_ref, depth_ref, slope_ref, rain_ref, dir_ref, sems,
):
    lines, px = sar_hbm.shape[1:]
    cols = depth_hbm.shape[1]
    h = SUBSTEPS
    copies = [
        pltpu.make_async_copy(src, dst, sems.at[i])
        for i, (src, dst) in enumerate(
            (
                (depth_hbm, depth_ref), (slope_hbm, slope_ref), (rain_hbm, rain_ref), (dir_hbm, dir_ref),
                (sar_hbm.at[:, lines - 16 : lines, :], last_ref), (sar_hbm.at[:, 0:16, :], first_ref),
            )
        )
    ]
    for copy in copies:
        copy.start()
    for copy in copies:
        copy.wait()
    fields = (
        depth_ref[...],
        runoff_coef * jnp.sqrt(slope_ref[...]),
        rain_ref[...],
        dir_ref[...].astype(f32),
    )
    zeros = jnp.zeros((8, px), f32)
    for ref, image_ref, lo, strip in (
        (up_ref, last_ref, 16 - HALO_LINES, lambda x: jnp.transpose(x[:, cols - LANES :], (1, 0))[LANES - h :]),
        (down_ref, first_ref, 0, lambda x: jnp.transpose(x[:, 0:LANES], (1, 0))[0:h]),
    ):
        image = [image_ref[ch].astype(f32)[lo : lo + HALO_LINES] for ch in range(2)]
        strips = [strip(x) for x in fields]
        ref[...] = jnp.concatenate(
            [jnp.concatenate(strips[0:2], 1), jnp.concatenate(strips[2:4], 1), *image, zeros], 0
        ).astype(bf16)


def strips_of(ref, keep):
    both = jnp.where(keep, ref[0:16, :].astype(f32), 0.0)
    cols = both.shape[1] // 2
    return [both[0:8, 0:cols], both[0:8, cols:], both[8:16, 0:cols], both[8:16, cols:]]


def swath_kernel(
    devices, capacity,
    above_ref, below_ref,
    sar_hbm, k1_hbm, k2_hbm, k3_hbm, k4_hbm, gw_hbm, cell_hbm, tile_hbm, row_hbm,
    frac_ref, send_ref,
    sar_ref, k1_ref, k2_ref, k3_ref, k4_ref, gw_ref, cell_ref, tile_ref, row_ref, sems,
    s_ref, xa_ref, xb_ref, x3_ref, w2_ref, w3_ref, w1_ref, t1_ref, t4_ref, logit_ref, obs_ref, wnd_ref,
):
    pairs = (
        (k1_hbm, k1_ref), (k2_hbm, k2_ref), (k3_hbm, k3_ref), (k4_hbm, k4_ref), (sar_hbm, sar_ref),
        (gw_hbm, gw_ref), (cell_hbm, cell_ref), (tile_hbm, tile_ref), (row_hbm, row_ref),
    )
    copies = [pltpu.make_async_copy(src, dst, sems.at[i]) for i, (src, dst) in enumerate(pairs)]
    for copy in copies:
        copy.start()
    lines, px = gw_ref.shape
    blocks = (lines + 2 * HALO_LINES - 2) // OUT_LINES
    frame = lines + 2 * HALO_LINES
    total = xa_ref.shape[0] // CH
    n_ty = lax.axis_size("ty")
    me = lax.axis_index("tx") * n_ty + lax.axis_index("ty")
    first = me == 0
    last = me == devices - 1
    rows = OUT_LINES * CH
    cols = IN_LINES * CH

    out_of = quo(iota((CH, OUT_LINES * cols), 1), cols)
    in_of = rem(iota((CH, OUT_LINES * cols), 1), cols) - iota((CH, OUT_LINES * cols), 0)
    spread = [(in_of == CH * (out_of + ky)).astype(bf16) for ky in range(3)]
    n1 = OUT_LINES * LANES
    group1 = quo(rem(iota((8, n1), 1), LANES), IN_LINES) == iota((8, n1), 0)
    line1 = rem(iota((8, n1), 1), IN_LINES) - quo(iota((8, n1), 1), LANES)
    spread1 = [(group1 & (line1 == ky)).astype(bf16) for ky in range(3)]
    tile4 = (rem(iota((CH, cols), 1), CH) == iota((CH, cols), 0)).astype(bf16)
    t1_ref[...] = jnp.zeros(t1_ref.shape, f32)
    t4_ref[...] = jnp.zeros(t4_ref.shape, f32)

    for copy in copies[0:4]:
        copy.wait()
    for ky in range(3):
        for kx in range(3):
            t1_ref[ky * 8 + 2 * kx : ky * 8 + 2 * kx + 2, :] = k1_ref[ky, kx].astype(f32)
        t4_ref[ky * 3 : ky * 3 + 3, :] = k4_ref[ky].astype(f32)
    wide1 = sum(dot_0(t1_ref[ky * 8 : ky * 8 + 8, :].astype(bf16), spread1[ky]) for ky in range(3))
    for i in range(OUT_LINES):
        w1_ref[i * CH : (i + 1) * CH, :] = wide1[:, i * LANES : (i + 1) * LANES].astype(bf16)
    for k_ref, w_ref in ((k2_ref, w2_ref), (k3_ref, w3_ref)):
        wide = sum(dot(k_ref[ky * 3 * CH : (ky + 1) * 3 * CH, :], spread[ky]) for ky in range(3))
        for kx in range(3):
            for i in range(OUT_LINES):
                w_ref[kx * rows + i * CH : kx * rows + (i + 1) * CH, :] = wide[
                    kx * CH : (kx + 1) * CH, i * cols : (i + 1) * cols
                ].astype(bf16)
    wide4 = dot(t4_ref[...].astype(bf16), tile4)
    w4 = jnp.concatenate(
        [
            band_weights(
                [jnp.broadcast_to(wide4[ky * 3 + kx : ky * 3 + kx + 1], (CH, cols)) for ky in range(3)],
                CH, cols, 1, lambda k: quo(k, CH),
            )
            for kx in range(3)
        ],
        0,
    )

    def clear(ref, lo, hi):
        ref[lo * CH : hi * CH, :] = jnp.zeros(((hi - lo) * CH, px), bf16)

    def outside(ref):
        @pl.when(first)
        def _():
            clear(ref, 0, HALO_LINES)

        @pl.when(last)
        def _():
            clear(ref, HALO_LINES + lines, frame)

    def merged(sums, n):
        before, _ = pixel_shifts(sums[0:n])
        _, after = pixel_shifts(sums[2 * n : 3 * n])
        return before + sums[n : 2 * n] + after

    for ref, line in ((xa_ref, 1), (xb_ref, 2), (x3_ref, 3)):
        clear(ref, line + blocks * OUT_LINES, total)
    above = above_ref[16:32, :].astype(f32)
    below = below_ref[16:32, :].astype(f32)
    copies[4].wait()
    for ch in range(2):
        s_ref[ch, 0:HALO_LINES, :] = above[ch * HALO_LINES : (ch + 1) * HALO_LINES]
        s_ref[ch, HALO_LINES : HALO_LINES + lines, :] = sar_ref[ch].astype(f32)
        s_ref[ch, HALO_LINES + lines : frame, :] = below[ch * HALO_LINES : (ch + 1) * HALO_LINES]
    pad = jnp.zeros((LANES - 6 * IN_LINES, px), f32)
    for b in range(blocks):
        at = b * OUT_LINES
        x = jnp.concatenate([s_ref[0, at : at + IN_LINES, :], s_ref[1, at : at + IN_LINES, :]], 0)
        before, after = pixel_shifts(x)
        acc = dot(w1_ref[...], jnp.concatenate([before, x, after, pad], 0).astype(bf16))
        xa_ref[(1 + at) * CH : (1 + at) * CH + rows, :] = jnp.maximum(acc, 0.0).astype(bf16)
    outside(xa_ref)

    for w_ref, src, dst, line in ((w2_ref, xa_ref, xb_ref, 2), (w3_ref, xb_ref, x3_ref, 3)):
        for b in range(blocks):
            at = line + b * OUT_LINES
            sums = dot(w_ref[...], src[(at - 1) * CH : (at - 1) * CH + cols, :])
            dst[at * CH : at * CH + rows, :] = jnp.maximum(merged(sums, rows), 0.0).astype(bf16)
        outside(dst)

    for b in range(blocks):
        at = HALO_LINES - 1 + b * OUT_LINES
        sums = dot(w4, x3_ref[at * CH : at * CH + cols, :])
        logit_ref[b * OUT_LINES : b * OUT_LINES + CH, :] = merged(sums, CH)
    frac = (1.0 / (1.0 + jnp.exp(-logit_ref[0:lines, :]))).astype(bf16)
    frac_ref[...] = frac
    for copy in copies[5:]:
        copy.wait()
    obs_ref[...] = frac.astype(f32) * gw_ref[...]

    quarter = wnd_ref.shape[1]
    parts = wnd_ref.shape[0] // lines // 2
    kind = iota((CH, px), 0)
    is_obs = kind < parts
    kind_part = rem(kind, parts).astype(f32).astype(bf16)
    sub = kind.astype(f32).astype(bf16)
    one = jnp.ones((CH, px), bf16)
    nil = jnp.zeros((CH, px), bf16)
    spots = [sub + g * CH for g in range(quarter // CH)]
    group = 8

    def window_group(g, carry):
        at = pl.ds(pl.multiple_of(g * group, group), group)
        cell = cell_ref[at, :]
        obs = obs_ref[at, :]
        cov = gw_ref[at, :]
        part = quo(cell, quarter).astype(f32)
        col = rem(cell, quarter).astype(f32)

        def spread_row(x, i):
            return jnp.broadcast_to(x[i : i + 1], (CH, px)).astype(bf16)

        for i in range(group):
            value = jnp.where(is_obs, obs[i : i + 1], cov[i : i + 1]).astype(bf16)
            left = jnp.where(kind_part == spread_row(part, i), value, nil)
            where_col = spread_row(col, i)
            hot = jnp.concatenate([jnp.where(spot == where_col, one, nil) for spot in spots], 0)
            wnd_ref[pl.ds(pl.multiple_of(g * (CH * group) + CH * i, CH), CH), :] = dot_t(left, hot)
        return carry

    lax.fori_loop(0, lines // group, window_group, 0)

    tile = tile_ref[...].astype(f32)
    same = iota((lines, lines), 0) == iota((lines, lines), 1)
    tile_sub = jnp.sum(jnp.where(same, jnp.broadcast_to(tile, (lines, lines)), 0.0), 1, keepdims=True)
    rival = (tile_sub == tile) & (iota((lines, lines), 0) < iota((lines, lines), 1))
    slot = tile * capacity + jnp.sum(jnp.where(rival, 1.0, 0.0), 0, keepdims=True)
    wnd_rows = wnd_ref.shape[0]
    per_line = wnd_rows // lines
    widen = (quo(iota((lines, wnd_rows), 1), per_line) == iota((lines, wnd_rows), 0)).astype(bf16)
    slot_wide = dot(jnp.broadcast_to(slot, (8, lines)).astype(bf16), widen)[0:1]
    place = slot_wide.astype(jnp.int32) * 4 + rem(quo(iota((1, wnd_rows), 1), 4), 4)
    per_tile = 4 * capacity
    slots = devices * per_tile
    perm = jnp.where(iota((slots, wnd_rows), 0) == place, 1.0, 0.0).astype(bf16)
    tile_cols = 4 * quarter
    repeat = (rem(iota((quarter, tile_cols), 1), quarter) == iota((quarter, tile_cols), 0)).astype(bf16)
    tiled = dot(wnd_ref[...].astype(bf16), repeat)
    mine = rem(iota((wnd_rows, tile_cols), 0), 4) == quo(iota((wnd_rows, tile_cols), 1), quarter)
    by_slot = dot(perm, jnp.where(mine, tiled, 0.0).astype(bf16))
    row_of = dot(
        jnp.where(same, jnp.broadcast_to(row_ref[...].astype(f32), (lines, lines)), 0.0).astype(bf16),
        jnp.ones((lines, LANES), bf16),
    )
    perm_line = jnp.where(quo(iota((slots, lines), 0), 4) == slot.astype(jnp.int32), 1.0, 0.0).astype(bf16)
    row_own = dot(perm_line, row_of.astype(bf16))

    none = jnp.zeros((per_tile, LANES), f32)

    def of_right(x):
        return jnp.concatenate([x[per_tile:], none], 0)

    def of_left(x):
        return jnp.concatenate([none, x[: slots - per_tile]], 0)

    h = SUBSTEPS
    lane = iota((slots, LANES), 1)
    entry = rem(iota((slots, LANES), 0), per_tile)
    column = rem(quo(iota((slots, LANES), 0), per_tile), n_ty)
    source = iota((LANES, LANES), 0)
    target = iota((LANES, LANES), 1)
    take_first = ((source < h) & (rem(target, h) == source)).astype(bf16)
    take_last = ((source >= LANES - h) & (rem(target, h) == source - (LANES - h))).astype(bf16)
    right_strip = dot(of_right(by_slot[:, 0:LANES]).astype(bf16), take_first)
    left_strip = dot(of_left(by_slot[:, tile_cols - LANES :]).astype(bf16), take_last)
    right_strip = jnp.where((quo(lane, h) == entry) & (column < n_ty - 1), right_strip, 0.0)
    left_strip = jnp.where((quo(lane, h) == entry) & (column > 0), left_strip, 0.0)
    info = jnp.zeros((slots, LANES), f32)
    for turn, value in enumerate((row_own, of_right(row_own), of_left(row_own))):
        info = jnp.where(lane == turn * per_tile + entry, value, info)
    extra_row = iota((8 * devices, slots), 0)
    extra_tile = quo(iota((8 * devices, slots), 1), per_tile)
    extra = sum(
        dot((extra_row == 8 * extra_tile + r).astype(bf16), x.astype(bf16))
        for r, x in enumerate((right_strip, left_strip, info))
    )
    halves = [by_slot[:, at : at + LANES].reshape(devices, per_tile, LANES) for at in range(0, tile_cols, LANES)]
    packed = jnp.concatenate([*halves, extra.reshape(devices, 8, LANES)], 1)
    send_ref[...] = packed.reshape(send_ref.shape).astype(bf16)


def transposed(x):
    return jnp.transpose(x, (1, 0))


def level_kernel(
    devices,
    got_ref, from_left_ref, from_right_ref, depth_ref, slope_ref, rain_ref, dir_ref,
    level_ref, side_ref, top_ref, bot_ref,
):
    tile_rows, tile_cols = depth_ref.shape
    h = SUBSTEPS
    halves = tile_cols // LANES
    n = (got_ref.shape[0] // devices - 8) // halves
    k = devices * n
    packed = got_ref[...].astype(f32).reshape(devices, halves * n + 8, LANES)
    main = jnp.concatenate([packed[:, i * n : (i + 1) * n].reshape(k, LANES) for i in range(halves)], 1)
    extra = packed[:, halves * n :]

    entry = rem(iota((k, LANES), 0), n)
    spread = quo(iota((k, LANES), 1), h) == entry

    def strip(r, first):
        rows = jnp.broadcast_to(extra[:, r : r + 1], (devices, n, LANES)).reshape(k, LANES)
        take = rem(iota((LANES, LANES), 0), h) + first == iota((LANES, LANES), 1)
        return dot(jnp.where(spread, rows, 0.0).astype(bf16), take.astype(bf16)).astype(bf16)

    lane = iota((1, k), 1)
    offset = rem(lane, 2) + tile_rows * rem(quo(lane, 2), 2)
    own_source = iota((8 * devices, k), 0) == 8 * quo(iota((8 * devices, k), 1), n) + 2
    info = extra.reshape(8 * devices, LANES).astype(bf16)

    def placer(turn):
        pick = (iota((LANES, k), 0) == turn * n + rem(iota((LANES, k), 1), n)).astype(bf16)
        line = jnp.sum(jnp.where(own_source, dot(info, pick), 0.0), 0, keepdims=True)
        target = line.astype(jnp.int32) + offset
        return jnp.where(iota((2 * tile_rows, k), 0) == target, 1.0, 0.0).astype(bf16)

    summed = dot(placer(0), main.astype(bf16))
    summed_side = dot(placer(1), strip(0, 0)) + dot(placer(2), strip(1, LANES - h))

    ty = lax.axis_index("ty")
    left = strips_of(from_left_ref, ty > 0)
    right = strips_of(from_right_ref, ty < lax.axis_size("ty") - 1)
    gap = jnp.zeros((LANES - 2 * h, tile_rows), f32)
    depth_side, conv_side, rain_side, code_side = [
        transposed(jnp.concatenate([r, gap, l], 0)) for r, l in zip(right, left)
    ]

    def analysed(sums, depth):
        observed = sums[0:tile_rows]
        covered = sums[tile_rows:]
        wet = depth / (depth + wet_depth)
        innovation = (observed - covered * wet) / (covered + 1.0)
        return depth * jnp.exp(innovation)

    level = analysed(summed, depth_ref[...])
    level_ref[...] = level
    sides = (analysed(summed_side, depth_side), rain_side, conv_side, code_side)
    owns = (level, rain_ref, slope_ref, dir_ref)

    def end_rows(at):
        own = [x[at, :] for x in owns]
        own[2] = runoff_coef * jnp.sqrt(own[2])
        own[3] = own[3].astype(f32)
        return jnp.concatenate([jnp.concatenate([o, x[at]], 1) for o, x in zip(own, sides)], 0).astype(bf16)

    for i, x in enumerate(sides):
        side_ref[i] = x
    top_ref[...] = end_rows(slice(0, h))
    bot_ref[...] = end_rows(slice(tile_rows - h, tile_rows))


def flow_kernel(
    level_ref, side_ref, slope_ref, dir_ref, rain_ref, above_ref, below_ref,
    out_ref,
    rain_s, conv_s, m_ref, part_ref, up_ref, down_ref,
):
    tile_rows, tile_cols = level_ref.shape
    h = SUBSTEPS
    wide_rows = tile_rows + 2 * h
    wide_cols = tile_cols + LANES

    def widened(field, own):
        at = slice(field * h, (field + 1) * h)
        mid = jnp.concatenate([own, side_ref[field]], 1)
        return jnp.concatenate([above_ref[...].astype(f32)[at], mid, below_ref[...].astype(f32)[at]], 0)

    zeros = jnp.zeros((h, wide_cols), f32)
    for buf in range(2):
        for ref in (up_ref, down_ref):
            ref[buf, 0:h, :] = zeros
            ref[buf, h + wide_rows :, :] = zeros
    part_ref[0] = widened(0, level_ref[...])
    rain_s[...] = widened(1, rain_ref[...])
    conv = widened(2, runoff_coef * jnp.sqrt(slope_ref[...]))
    conv_s[...] = conv
    code = widened(3, dir_ref[...].astype(f32))
    sides = (-1, 0, 1, -1, 1, -1, 0, 1)
    for direction, side in enumerate(sides):
        share = jnp.where(code == direction, conv, 0.0)
        m_ref[direction] = pltpu.roll(share, side % wide_cols, 1) if side else share

    chunk = 16

    def level_at(buf, r, n, step):
        level = part_ref[buf, r : r + n, :]
        if step:
            level = level + up_ref[buf, h + r + 1 : h + r + 1 + n, :] + down_ref[buf, h + r - 1 : h + r - 1 + n, :]
        return level

    for step in range(SUBSTEPS):
        buf, new = step % 2, (step + 1) % 2
        for r in range(0, wide_rows, chunk):
            level = level_at(buf, r, chunk, step)
            power = level * jnp.exp((2.0 / 3.0) * jnp.log(jnp.maximum(jnp.abs(level), 1e-30)))
            from_right = pltpu.roll(power, wide_cols - 1, 1)
            from_left = pltpu.roll(power, 1, 1)
            m = [m_ref[d, r : r + chunk, :] for d in range(8)]
            up_ref[new, h + r : h + r + chunk, :] = m[0] * from_right + m[1] * power + m[2] * from_left
            down_ref[new, h + r : h + r + chunk, :] = m[5] * from_right + m[6] * power + m[7] * from_left
            part_ref[new, r : r + chunk, :] = (
                level + rain_s[r : r + chunk, :] - conv_s[r : r + chunk, :] * power
                + (m[3] * from_right + m[4] * from_left)
            )
    buf = SUBSTEPS % 2
    out_ref[...] = level_at(buf, h, tile_rows, SUBSTEPS)[:, 0:tile_cols]


def hbm_specs(n):
    return [pl.BlockSpec(memory_space=pltpu.HBM)] * n


def vmem_specs(n):
    return [pl.BlockSpec(memory_space=pltpu.VMEM)] * n


def per_device(
    sar_image, kernel_first, kernel_second, kernel_third, kernel_last,
    geo_weight, cell_index, block_tile, block_row, depth, slope, flow_dir, rain,
):
    both = ("tx", "ty")
    devices = lax.axis_size(both)
    az_lines, range_px = geo_weight.shape
    tile_rows, tile_cols = depth.shape
    capacity = max(2, 2 * az_lines // devices)

    def steps(axis):
        size = lax.axis_size(axis)
        up = [(i, i + 1) for i in range(size - 1)]
        return up, [(j, i) for i, j in up]

    params = pltpu.CompilerParams(vmem_limit_bytes=VMEM_LIMIT)
    up, down = steps(both)
    message = jax.ShapeDtypeStruct((32, range_px), bf16)
    to_next, to_previous = pl.pallas_call(
        edge_kernel,
        out_shape=(message, message),
        in_specs=hbm_specs(5),
        out_specs=tuple(vmem_specs(2)),
        scratch_shapes=[
            pltpu.VMEM((2, 16, range_px), bf16),
            pltpu.VMEM((2, 16, range_px), bf16),
            *[pltpu.VMEM(x.shape, x.dtype) for x in (depth, slope, rain, flow_dir)],
            pltpu.SemaphoreType.DMA((6,)),
        ],
        compiler_params=pltpu.CompilerParams(vmem_limit_bytes=VMEM_MOST),
        name="edges",
    )(sar_image, depth, slope, rain, flow_dir)
    from_previous = lax.ppermute(to_next, both, up)
    from_next = lax.ppermute(to_previous, both, down)

    feats = (az_lines + 2 * HALO_LINES + 4) * CH
    rows, cols = OUT_LINES * CH, IN_LINES * CH
    send_rows = tile_cols // LANES * 4 * capacity + 8
    inputs = (
        sar_image,
        jnp.transpose(kernel_first, (2, 3, 1, 0)),
        jnp.transpose(kernel_second, (2, 3, 0, 1)).reshape(9 * CH, CH),
        jnp.transpose(kernel_third, (2, 3, 0, 1)).reshape(9 * CH, CH),
        jnp.transpose(kernel_last[0], (1, 2, 0)),
        geo_weight, cell_index, block_tile.reshape(1, az_lines), block_row.reshape(1, az_lines),
    )
    fraction, send = pl.pallas_call(
        functools.partial(swath_kernel, devices, capacity),
        out_shape=(
            jax.ShapeDtypeStruct((az_lines, range_px), bf16),
            jax.ShapeDtypeStruct((devices * send_rows, LANES), bf16),
        ),
        in_specs=vmem_specs(2) + hbm_specs(9),
        out_specs=tuple(vmem_specs(2)),
        scratch_shapes=[
            *[pltpu.VMEM(x.shape, x.dtype) for x in inputs],
            pltpu.SemaphoreType.DMA((9,)),
            pltpu.VMEM((2, az_lines + 2 * HALO_LINES + 8, range_px), f32),
            pltpu.VMEM((feats, range_px), bf16),
            pltpu.VMEM((feats, range_px), bf16),
            pltpu.VMEM((feats, range_px), bf16),
            pltpu.VMEM((3 * rows, cols), bf16),
            pltpu.VMEM((3 * rows, cols), bf16),
            pltpu.VMEM((rows, LANES), bf16),
            pltpu.VMEM((24, CH), f32),
            pltpu.VMEM((16, CH), f32),
            pltpu.VMEM((az_lines + 2 * CH, range_px), f32),
            pltpu.VMEM((az_lines, range_px), f32),
            pltpu.VMEM((CH * az_lines, tile_cols // 4), f32),
        ],
        compiler_params=params,
        name="swath",
    )(from_previous, from_next, *inputs)

    got = lax.all_to_all(
        send.reshape(devices, send_rows, LANES), both, split_axis=0, concat_axis=0, tiled=True
    ).reshape(devices * send_rows, LANES)

    wide_rows = tile_rows + 2 * SUBSTEPS
    wide_cols = tile_cols + LANES
    edge = jax.ShapeDtypeStruct((4 * SUBSTEPS, wide_cols), bf16)
    level, side, top_rows, bot_rows = pl.pallas_call(
        functools.partial(level_kernel, devices),
        out_shape=(
            jax.ShapeDtypeStruct((tile_rows, tile_cols), f32),
            jax.ShapeDtypeStruct((4, tile_rows, LANES), f32),
            edge,
            edge,
        ),
        in_specs=vmem_specs(7),
        out_specs=tuple(vmem_specs(4)),
        compiler_params=params,
        name="level",
    )(got, from_previous, from_next, depth, slope, rain, flow_dir)

    up, down = steps("tx")
    above = lax.ppermute(bot_rows, "tx", up)
    below = lax.ppermute(top_rows, "tx", down)

    level = pl.pallas_call(
        flow_kernel,
        out_shape=jax.ShapeDtypeStruct((tile_rows, tile_cols), f32),
        in_specs=vmem_specs(7),
        out_specs=vmem_specs(1)[0],
        scratch_shapes=[
            pltpu.VMEM((wide_rows, wide_cols), f32),
            pltpu.VMEM((wide_rows, wide_cols), f32),
            pltpu.VMEM((8, wide_rows, wide_cols), f32),
            pltpu.VMEM((2, wide_rows, wide_cols), f32),
            pltpu.VMEM((2, wide_rows + 2 * SUBSTEPS, wide_cols), f32),
            pltpu.VMEM((2, wide_rows + 2 * SUBSTEPS, wide_cols), f32),
        ],
        compiler_params=params,
        name="flow",
    )(level, side, slope, flow_dir, rain, above, below)
    return (fraction, level)


def solution(mesh):
    placed = (
        P(None, ("tx", "ty"), None),
        P(),
        P(),
        P(),
        P(),
        P(("tx", "ty"), None),
        P(("tx", "ty"), None),
        P(("tx", "ty"), None),
        P(("tx", "ty"), None),
        P("tx", "ty"),
        P("tx", "ty"),
        P("tx", "ty"),
        P("tx", "ty"),
    )
    return jax.shard_map(
        per_device,
        mesh=mesh,
        in_specs=placed,
        out_specs=(P(("tx", "ty"), None), P("tx", "ty")),
        check_vma=False,
    )
```

```python
import functools

import jax
import jax.numpy as jnp
from jax import lax
from jax.experimental import pallas as pl
from jax.experimental.pallas import tpu as pltpu
from jax.sharding import PartitionSpec as P

WIN_ROWS = 2
SUBSTEPS = 8
CH = 16
OUT_LINES = 14
IN_LINES = OUT_LINES + 2
HALO_LINES = 4
LANES = 128
VMEM_LIMIT = 48 * 1024 * 1024
VMEM_MOST = 61920 * 1024

wet_depth = 0.5
runoff_coef = 0.25
bf16 = jnp.bfloat16
f32 = jnp.float32


def iota(shape, dim):
    return lax.broadcasted_iota(jnp.int32, shape, dim)


def quo(x, n):
    assert n & (n - 1) == 0
    return lax.shift_right_logical(x, jnp.int32(n.bit_length() - 1)) if n > 1 else x


def rem(x, n):
    assert n & (n - 1) == 0
    return x & (n - 1)


def dot(a, b):
    return lax.dot_general(a, b, (((1,), (0,)), ((), ())), preferred_element_type=f32)


def dot_0(a, b):
    return lax.dot_general(a, b, (((0,), (0,)), ((), ())), preferred_element_type=f32)


def dot_t(a, b):
    return lax.dot_general(a, b, (((1,), (1,)), ((), ())), preferred_element_type=f32)


def pixel_shifts(x):
    width = x.shape[1]
    pix = iota(x.shape, 1)
    before = jnp.where(pix == 0, 0.0, pltpu.roll(x, 1, 1))
    after = jnp.where(pix == width - 1, 0.0, pltpu.roll(x, width - 1, 1))
    return before, after


def band_weights(tiled, rows, cols, per_row, line_of):
    out_line = quo(iota((rows, cols), 0), per_row)
    off = line_of(iota((rows, cols), 1)) - out_line
    out = jnp.zeros((rows, cols), f32)
    for ky in range(3):
        out = jnp.where(off == ky, tiled[ky], out)
    return out.astype(bf16)


def edge_kernel(
    sar_hbm, depth_hbm, slope_hbm, rain_hbm, dir_hbm, up_ref, down_ref,
    last_ref, first_ref, depth_ref, slope_ref, rain_ref, dir_ref, sems,
):
    lines, px = sar_hbm.shape[1:]
    cols = depth_hbm.shape[1]
    h = SUBSTEPS
    copies = [
        pltpu.make_async_copy(src, dst, sems.at[i])
        for i, (src, dst) in enumerate(
            (
                (depth_hbm, depth_ref), (slope_hbm, slope_ref), (rain_hbm, rain_ref), (dir_hbm, dir_ref),
                (sar_hbm.at[:, lines - 16 : lines, :], last_ref), (sar_hbm.at[:, 0:16, :], first_ref),
            )
        )
    ]
    for copy in copies:
        copy.start()
    for copy in copies:
        copy.wait()
    fields = (
        depth_ref[...],
        runoff_coef * jnp.sqrt(slope_ref[...]),
        rain_ref[...],
        dir_ref[...].astype(f32),
    )
    zeros = jnp.zeros((8, px), f32)
    for ref, image_ref, lo, strip in (
        (up_ref, last_ref, 16 - HALO_LINES, lambda x: jnp.transpose(x[:, cols - LANES :], (1, 0))[LANES - h :]),
        (down_ref, first_ref, 0, lambda x: jnp.transpose(x[:, 0:LANES], (1, 0))[0:h]),
    ):
        image = [image_ref[ch].astype(f32)[lo : lo + HALO_LINES] for ch in range(2)]
        strips = [strip(x) for x in fields]
        ref[...] = jnp.concatenate(
            [jnp.concatenate(strips[0:2], 1), jnp.concatenate(strips[2:4], 1), *image, zeros], 0
        ).astype(bf16)


def strips_of(ref, keep):
    both = jnp.where(keep, ref[0:16, :].astype(f32), 0.0)
    cols = both.shape[1] // 2
    return [both[0:8, 0:cols], both[0:8, cols:], both[8:16, 0:cols], both[8:16, cols:]]


def prep_kernel(
    devices, capacity,
    k1_hbm, k2_hbm, k3_hbm, k4_hbm, tile_hbm, row_hbm,
    w1_ref, w2_ref, w3_ref, w4_ref, perm_ref, extra_ref,
    k1_ref, k2_ref, k3_ref, k4_ref, tile_ref, row_ref, sems, t1_ref, t4_ref,
):
    pairs = (
        (k1_hbm, k1_ref), (k2_hbm, k2_ref), (k3_hbm, k3_ref), (k4_hbm, k4_ref),
        (tile_hbm, tile_ref), (row_hbm, row_ref),
    )
    copies = [pltpu.make_async_copy(src, dst, sems.at[i]) for i, (src, dst) in enumerate(pairs)]
    for copy in copies:
        copy.start()
    rows = OUT_LINES * CH
    cols = IN_LINES * CH

    out_of = quo(iota((CH, OUT_LINES * cols), 1), cols)
    in_of = rem(iota((CH, OUT_LINES * cols), 1), cols) - iota((CH, OUT_LINES * cols), 0)
    spread = [(in_of == CH * (out_of + ky)).astype(bf16) for ky in range(3)]
    n1 = OUT_LINES * LANES
    group1 = quo(rem(iota((8, n1), 1), LANES), IN_LINES) == iota((8, n1), 0)
    line1 = rem(iota((8, n1), 1), IN_LINES) - quo(iota((8, n1), 1), LANES)
    spread1 = [(group1 & (line1 == ky)).astype(bf16) for ky in range(3)]
    tile4 = (rem(iota((CH, cols), 1), CH) == iota((CH, cols), 0)).astype(bf16)
    t1_ref[...] = jnp.zeros(t1_ref.shape, f32)
    t4_ref[...] = jnp.zeros(t4_ref.shape, f32)
    for copy in copies:
        copy.wait()
    for ky in range(3):
        for kx in range(3):
            t1_ref[ky * 8 + 2 * kx : ky * 8 + 2 * kx + 2, :] = k1_ref[ky, kx].astype(f32)
        t4_ref[ky * 3 : ky * 3 + 3, :] = k4_ref[ky].astype(f32)
    wide1 = sum(dot_0(t1_ref[ky * 8 : ky * 8 + 8, :].astype(bf16), spread1[ky]) for ky in range(3))
    for i in range(OUT_LINES):
        w1_ref[i * CH : (i + 1) * CH, :] = wide1[:, i * LANES : (i + 1) * LANES].astype(bf16)
    for k_ref, w_ref in ((k2_ref, w2_ref), (k3_ref, w3_ref)):
        wide = sum(dot(k_ref[ky * 3 * CH : (ky + 1) * 3 * CH, :], spread[ky]) for ky in range(3))
        for kx in range(3):
            for i in range(OUT_LINES):
                w_ref[kx * rows + i * CH : kx * rows + (i + 1) * CH, :] = wide[
                    kx * CH : (kx + 1) * CH, i * cols : (i + 1) * cols
                ].astype(bf16)
    wide4 = dot(t4_ref[...].astype(bf16), tile4)
    w4_ref[...] = jnp.concatenate(
        [
            band_weights(
                [jnp.broadcast_to(wide4[ky * 3 + kx : ky * 3 + kx + 1], (CH, cols)) for ky in range(3)],
                CH, cols, 1, lambda k: quo(k, CH),
            )
            for kx in range(3)
        ],
        0,
    )

    lines = tile_ref.shape[1]
    tile = tile_ref[...].astype(f32)
    same = iota((lines, lines), 0) == iota((lines, lines), 1)
    tile_sub = jnp.sum(jnp.where(same, jnp.broadcast_to(tile, (lines, lines)), 0.0), 1, keepdims=True)
    rival = (tile_sub == tile) & (iota((lines, lines), 0) < iota((lines, lines), 1))
    slot = tile * capacity + jnp.sum(jnp.where(rival, 1.0, 0.0), 0, keepdims=True)
    slots, wnd_rows = perm_ref.shape
    per_line = wnd_rows // lines
    widen = (quo(iota((lines, wnd_rows), 1), per_line) == iota((lines, wnd_rows), 0)).astype(bf16)
    slot_wide = dot(jnp.broadcast_to(slot, (8, lines)).astype(bf16), widen)[0:1]
    place = slot_wide.astype(jnp.int32) * 4 + rem(quo(iota((1, wnd_rows), 1), 4), 4)
    perm_ref[...] = jnp.where(iota((slots, wnd_rows), 0) == place, 1.0, 0.0).astype(bf16)

    row_of = dot(
        jnp.where(same, jnp.broadcast_to(row_ref[...].astype(f32), (lines, lines)), 0.0).astype(bf16),
        jnp.ones((lines, LANES), bf16),
    )
    perm_line = jnp.where(quo(iota((slots, lines), 0), 4) == slot.astype(jnp.int32), 1.0, 0.0).astype(bf16)
    row_own = dot(perm_line, row_of.astype(bf16))
    per_tile = 4 * capacity
    lane = iota((slots, LANES), 1)
    entry = rem(iota((slots, LANES), 0), per_tile)
    info = jnp.zeros((slots, LANES), f32)
    for turn, value in enumerate((row_own, of_right(row_own, per_tile), of_left(row_own, per_tile))):
        info = jnp.where(lane == turn * per_tile + entry, value, info)
    info = jnp.sum(info.reshape(devices, per_tile, LANES), 1, keepdims=True)
    at = iota((devices, 8, LANES), 1)
    extra_ref[...] = jnp.where(at == 2, info, 0.0).reshape(8 * devices, LANES)


def of_right(x, per_tile):
    return jnp.concatenate([x[per_tile:], jnp.zeros((per_tile, x.shape[1]), x.dtype)], 0)


def of_left(x, per_tile):
    return jnp.concatenate([jnp.zeros((per_tile, x.shape[1]), x.dtype), x[: x.shape[0] - per_tile]], 0)


def swath_kernel(
    devices, capacity,
    above_ref, below_ref, w1_ref, w2_ref, w3_ref, w4_ref, perm_ref, extra_ref,
    sar_hbm, gw_hbm, cell_hbm,
    frac_ref, send_ref,
    sar_ref, gw_ref, cell_ref, sems,
    s_ref, xa_ref, xb_ref, x3_ref, logit_ref, obs_ref, wnd_ref,
):
    pairs = ((sar_hbm, sar_ref), (gw_hbm, gw_ref), (cell_hbm, cell_ref))
    copies = [pltpu.make_async_copy(src, dst, sems.at[i]) for i, (src, dst) in enumerate(pairs)]
    for copy in copies:
        copy.start()
    lines, px = gw_ref.shape
    blocks = (lines + 2 * HALO_LINES - 2) // OUT_LINES
    frame = lines + 2 * HALO_LINES
    total = xa_ref.shape[0] // CH
    n_ty = lax.axis_size("ty")
    me = lax.axis_index("tx") * n_ty + lax.axis_index("ty")
    first = me == 0
    last = me == devices - 1
    rows = OUT_LINES * CH
    cols = IN_LINES * CH

    def clear(ref, lo, hi):
        ref[lo * CH : hi * CH, :] = jnp.zeros(((hi - lo) * CH, px), bf16)

    def outside(ref):
        @pl.when(first)
        def _():
            clear(ref, 0, HALO_LINES)

        @pl.when(last)
        def _():
            clear(ref, HALO_LINES + lines, frame)

    def merged(sums, n):
        before, _ = pixel_shifts(sums[0:n])
        _, after = pixel_shifts(sums[2 * n : 3 * n])
        return before + sums[n : 2 * n] + after

    def by_block(body):
        def step(b, carry):
            body(b)
            return carry

        lax.fori_loop(0, blocks, step, 0)

    def lines_at(b, line, count):
        return pl.ds(pl.multiple_of(b * rows + line * CH, CH), count)

    for ref, line in ((xa_ref, 1), (xb_ref, 2), (x3_ref, 3)):
        clear(ref, line + blocks * OUT_LINES, total)
    above = above_ref[16:32, :].astype(f32)
    below = below_ref[16:32, :].astype(f32)
    copies[0].wait()
    for ch in range(2):
        s_ref[ch, 0:HALO_LINES, :] = above[ch * HALO_LINES : (ch + 1) * HALO_LINES]
        s_ref[ch, HALO_LINES : HALO_LINES + lines, :] = sar_ref[ch].astype(f32)
        s_ref[ch, HALO_LINES + lines : frame, :] = below[ch * HALO_LINES : (ch + 1) * HALO_LINES]
    pad = jnp.zeros((LANES - 6 * IN_LINES, px), f32)
    for b in range(blocks):
        at = b * OUT_LINES
        x = jnp.concatenate([s_ref[0, at : at + IN_LINES, :], s_ref[1, at : at + IN_LINES, :]], 0)
        before, after = pixel_shifts(x)
        acc = dot(w1_ref[...], jnp.concatenate([before, x, after, pad], 0).astype(bf16))
        xa_ref[(1 + at) * CH : (1 + at) * CH + rows, :] = jnp.maximum(acc, 0.0).astype(bf16)
    outside(xa_ref)

    for w_ref, src, dst, line in ((w2_ref, xa_ref, xb_ref, 2), (w3_ref, xb_ref, x3_ref, 3)):

        def conv(b):
            sums = dot(w_ref[...], src[lines_at(b, line - 1, cols), :])
            dst[lines_at(b, line, rows), :] = jnp.maximum(merged(sums, rows), 0.0).astype(bf16)

        by_block(conv)
        outside(dst)

    for b in range(blocks):
        at = HALO_LINES - 1 + b * OUT_LINES
        sums = dot(w4_ref[...], x3_ref[at * CH : at * CH + cols, :])
        logit_ref[b * OUT_LINES : b * OUT_LINES + CH, :] = merged(sums, CH)
    frac = (1.0 / (1.0 + jnp.exp(-logit_ref[0:lines, :]))).astype(bf16)
    frac_ref[...] = frac
    for copy in copies[1:]:
        copy.wait()
    obs_ref[...] = frac.astype(f32) * gw_ref[...]

    quarter = wnd_ref.shape[1]
    parts = wnd_ref.shape[0] // lines // 2
    kind = iota((CH, px), 0)
    is_obs = kind < parts
    kind_part = rem(kind, parts).astype(f32).astype(bf16)
    sub = kind.astype(f32).astype(bf16)
    one = jnp.ones((CH, px), bf16)
    nil = jnp.zeros((CH, px), bf16)
    spots = [sub + g * CH for g in range(quarter // CH)]
    group = 8

    def window_group(g, carry):
        at = pl.ds(pl.multiple_of(g * group, group), group)
        cell = cell_ref[at, :]
        obs = obs_ref[at, :]
        cov = gw_ref[at, :]
        part = quo(cell, quarter).astype(f32)
        col = rem(cell, quarter).astype(f32)

        def spread_row(x, i):
            return jnp.broadcast_to(x[i : i + 1], (CH, px)).astype(bf16)

        for i in range(group):
            value = jnp.where(is_obs, obs[i : i + 1], cov[i : i + 1]).astype(bf16)
            left = jnp.where(kind_part == spread_row(part, i), value, nil)
            where_col = spread_row(col, i)
            hot = jnp.concatenate([jnp.where(spot == where_col, one, nil) for spot in spots], 0)
            wnd_ref[pl.ds(pl.multiple_of(g * (CH * group) + CH * i, CH), CH), :] = dot_t(left, hot)
        return carry

    lax.fori_loop(0, lines // group, window_group, 0)

    per_tile = 4 * capacity
    slots, wnd_rows = perm_ref.shape
    tile_cols = 4 * quarter
    repeat = (rem(iota((quarter, tile_cols), 1), quarter) == iota((quarter, tile_cols), 0)).astype(bf16)
    tiled = dot(wnd_ref[...].astype(bf16), repeat)
    mine = rem(iota((wnd_rows, tile_cols), 0), 4) == quo(iota((wnd_rows, tile_cols), 1), quarter)
    by_slot = dot(perm_ref[...], jnp.where(mine, tiled, 0.0).astype(bf16))
    h = SUBSTEPS
    entry = rem(iota((slots, LANES), 0), per_tile)
    here = quo(iota((slots, LANES), 1), h) == entry
    column = rem(quo(iota((slots, LANES), 0), per_tile), n_ty)
    source = iota((LANES, LANES), 0)
    spot = rem(iota((LANES, LANES), 1), h)

    def strip(x, first_lane, keep):
        take = ((spot + first_lane == source) & (source - first_lane < h)).astype(bf16)
        x = jnp.where(here & keep, dot(x.astype(bf16), take), 0.0)
        return jnp.sum(x.reshape(devices, per_tile, LANES), 1, keepdims=True)

    right_strip = strip(of_right(by_slot[:, 0:LANES], per_tile), 0, column < n_ty - 1)
    left_strip = strip(of_left(by_slot[:, tile_cols - LANES :], per_tile), LANES - h, column > 0)
    at = iota((devices, 8, LANES), 1)
    extra = extra_ref[...].reshape(devices, 8, LANES)
    extra = jnp.where(at == 0, right_strip, jnp.where(at == 1, left_strip, extra))
    halves = [by_slot[:, at : at + LANES].reshape(devices, per_tile, LANES) for at in range(0, tile_cols, LANES)]
    packed = jnp.concatenate([*halves, extra], 1)
    send_ref[...] = packed.reshape(send_ref.shape).astype(bf16)


def transposed(x):
    return jnp.transpose(x, (1, 0))


def level_kernel(
    devices,
    got_ref, from_left_ref, from_right_ref, depth_ref, slope_ref, rain_ref, dir_ref,
    level_ref, side_ref, top_ref, bot_ref,
):
    tile_rows, tile_cols = depth_ref.shape
    h = SUBSTEPS
    halves = tile_cols // LANES
    n = (got_ref.shape[0] // devices - 8) // halves
    k = devices * n
    packed = got_ref[...].astype(f32).reshape(devices, halves * n + 8, LANES)
    main = jnp.concatenate([packed[:, i * n : (i + 1) * n].reshape(k, LANES) for i in range(halves)], 1)
    extra = packed[:, halves * n :]

    entry = rem(iota((k, LANES), 0), n)
    spread = quo(iota((k, LANES), 1), h) == entry

    def strip(r, first):
        rows = jnp.broadcast_to(extra[:, r : r + 1], (devices, n, LANES)).reshape(k, LANES)
        take = rem(iota((LANES, LANES), 0), h) + first == iota((LANES, LANES), 1)
        return dot(jnp.where(spread, rows, 0.0).astype(bf16), take.astype(bf16)).astype(bf16)

    lane = iota((1, k), 1)
    offset = rem(lane, 2) + tile_rows * rem(quo(lane, 2), 2)
    info = jnp.broadcast_to(extra[:, 2:3], (devices, n, LANES)).reshape(k, LANES)
    info = jnp.where(rem(iota((k, LANES), 1), n) == entry, info, 0.0).astype(bf16)
    turns = (quo(iota((LANES, LANES), 0), n) == iota((LANES, LANES), 1)).astype(bf16)
    lines = transposed(dot(info, turns))

    def placer(turn):
        target = lines[turn : turn + 1].astype(jnp.int32) + offset
        return jnp.where(iota((2 * tile_rows, k), 0) == target, 1.0, 0.0).astype(bf16)

    summed = dot(placer(0), main.astype(bf16))
    summed_side = dot(placer(1), strip(0, 0)) + dot(placer(2), strip(1, LANES - h))

    ty = lax.axis_index("ty")
    left = strips_of(from_left_ref, ty > 0)
    right = strips_of(from_right_ref, ty < lax.axis_size("ty") - 1)
    gap = jnp.zeros((LANES - 2 * h, tile_rows), f32)
    depth_side, conv_side, rain_side, code_side = [
        transposed(jnp.concatenate([r, gap, l], 0)) for r, l in zip(right, left)
    ]

    def analysed(sums, depth):
        observed = sums[0:tile_rows]
        covered = sums[tile_rows:]
        wet = depth / (depth + wet_depth)
        innovation = (observed - covered * wet) / (covered + 1.0)
        return depth * jnp.exp(innovation)

    level = analysed(summed, depth_ref[...])
    level_ref[...] = level
    sides = (analysed(summed_side, depth_side), rain_side, conv_side, code_side)
    owns = (level, rain_ref, slope_ref, dir_ref)

    def end_rows(at):
        own = [x[at, :] for x in owns]
        own[2] = runoff_coef * jnp.sqrt(own[2])
        own[3] = own[3].astype(f32)
        return jnp.concatenate([jnp.concatenate([o, x[at]], 1) for o, x in zip(own, sides)], 0).astype(bf16)

    for i, x in enumerate(sides):
        side_ref[i] = x
    top_ref[...] = end_rows(slice(0, h))
    bot_ref[...] = end_rows(slice(tile_rows - h, tile_rows))


def flow_kernel(
    level_ref, side_ref, slope_ref, dir_ref, rain_ref, above_ref, below_ref,
    out_ref,
    rain_s, conv_s, m_ref, part_ref, up_ref, down_ref,
):
    tile_rows, tile_cols = level_ref.shape
    h = SUBSTEPS
    wide_rows = tile_rows + 2 * h
    wide_cols = tile_cols + LANES

    def widened(field, own):
        at = slice(field * h, (field + 1) * h)
        mid = jnp.concatenate([own, side_ref[field]], 1)
        return jnp.concatenate([above_ref[...].astype(f32)[at], mid, below_ref[...].astype(f32)[at]], 0)

    zeros = jnp.zeros((h, wide_cols), f32)
    for ref in (up_ref, down_ref):
        ref[0] = jnp.zeros(ref.shape[1:], f32)
        ref[1, 0:h, :] = zeros
        ref[1, h + wide_rows :, :] = zeros
    part_ref[0] = widened(0, level_ref[...])
    rain_s[...] = widened(1, rain_ref[...])
    conv = widened(2, runoff_coef * jnp.sqrt(slope_ref[...]))
    conv_s[...] = conv
    code = widened(3, dir_ref[...].astype(f32))
    sides = (-1, 0, 1, -1, 1, -1, 0, 1)
    for direction, side in enumerate(sides):
        share = jnp.where(code == direction, conv, 0.0)
        m_ref[direction] = pltpu.roll(share, side % wide_cols, 1) if side else share

    chunk = 16

    def level_at(buf, r, n):
        level = part_ref[buf, r : r + n, :]
        return level + up_ref[buf, h + r + 1 : h + r + 1 + n, :] + down_ref[buf, h + r - 1 : h + r - 1 + n, :]

    def substep(buf, new):
        for r in range(0, wide_rows, chunk):
            level = level_at(buf, r, chunk)
            power = level * jnp.exp((2.0 / 3.0) * jnp.log(jnp.maximum(jnp.abs(level), 1e-30)))
            from_right = pltpu.roll(power, wide_cols - 1, 1)
            from_left = pltpu.roll(power, 1, 1)
            m = [m_ref[d, r : r + chunk, :] for d in range(8)]
            up_ref[new, h + r : h + r + chunk, :] = m[0] * from_right + m[1] * power + m[2] * from_left
            down_ref[new, h + r : h + r + chunk, :] = m[5] * from_right + m[6] * power + m[7] * from_left
            part_ref[new, r : r + chunk, :] = (
                level + rain_s[r : r + chunk, :] - conv_s[r : r + chunk, :] * power
                + (m[3] * from_right + m[4] * from_left)
            )

    def substep_pair(i, carry):
        substep(0, 1)
        substep(1, 0)
        return carry

    lax.fori_loop(0, SUBSTEPS // 2, substep_pair, 0)
    out_ref[...] = level_at(0, h, tile_rows)[:, 0:tile_cols]


def hbm_specs(n):
    return [pl.BlockSpec(memory_space=pltpu.HBM)] * n


def vmem_specs(n):
    return [pl.BlockSpec(memory_space=pltpu.VMEM)] * n


def per_device(
    sar_image, kernel_first, kernel_second, kernel_third, kernel_last,
    geo_weight, cell_index, block_tile, block_row, depth, slope, flow_dir, rain,
):
    both = ("tx", "ty")
    devices = lax.axis_size(both)
    az_lines, range_px = geo_weight.shape
    tile_rows, tile_cols = depth.shape
    capacity = max(2, 2 * az_lines // devices)

    def steps(axis):
        size = lax.axis_size(axis)
        up = [(i, i + 1) for i in range(size - 1)]
        return up, [(j, i) for i, j in up]

    params = pltpu.CompilerParams(vmem_limit_bytes=VMEM_LIMIT)
    up, down = steps(both)
    message = jax.ShapeDtypeStruct((32, range_px), bf16)
    to_next, to_previous = pl.pallas_call(
        edge_kernel,
        out_shape=(message, message),
        in_specs=hbm_specs(5),
        out_specs=tuple(vmem_specs(2)),
        scratch_shapes=[
            pltpu.VMEM((2, 16, range_px), bf16),
            pltpu.VMEM((2, 16, range_px), bf16),
            *[pltpu.VMEM(x.shape, x.dtype) for x in (depth, slope, rain, flow_dir)],
            pltpu.SemaphoreType.DMA((6,)),
        ],
        compiler_params=pltpu.CompilerParams(vmem_limit_bytes=VMEM_MOST),
        name="edges",
    )(sar_image, depth, slope, rain, flow_dir)
    from_previous = lax.ppermute(to_next, both, up)
    from_next = lax.ppermute(to_previous, both, down)

    feats = (az_lines + 2 * HALO_LINES + 4) * CH
    rows, cols = OUT_LINES * CH, IN_LINES * CH
    send_rows = tile_cols // LANES * 4 * capacity + 8
    slots = devices * capacity * 4
    wnd_rows = CH * az_lines
    fixed = (
        jnp.transpose(kernel_first, (2, 3, 1, 0)),
        jnp.transpose(kernel_second, (2, 3, 0, 1)).reshape(9 * CH, CH),
        jnp.transpose(kernel_third, (2, 3, 0, 1)).reshape(9 * CH, CH),
        jnp.transpose(kernel_last[0], (1, 2, 0)),
        block_tile.reshape(1, az_lines), block_row.reshape(1, az_lines),
    )
    prepared = pl.pallas_call(
        functools.partial(prep_kernel, devices, capacity),
        out_shape=(
            jax.ShapeDtypeStruct((rows, LANES), bf16),
            jax.ShapeDtypeStruct((3 * rows, cols), bf16),
            jax.ShapeDtypeStruct((3 * rows, cols), bf16),
            jax.ShapeDtypeStruct((3 * CH, cols), bf16),
            jax.ShapeDtypeStruct((slots, wnd_rows), bf16),
            jax.ShapeDtypeStruct((8 * devices, LANES), f32),
        ),
        in_specs=hbm_specs(6),
        out_specs=tuple(vmem_specs(6)),
        scratch_shapes=[
            *[pltpu.VMEM(x.shape, x.dtype) for x in fixed],
            pltpu.SemaphoreType.DMA((6,)),
            pltpu.VMEM((24, CH), f32),
            pltpu.VMEM((16, CH), f32),
        ],
        compiler_params=params,
        cost_estimate=pl.CostEstimate(flops=2_000_000_000, bytes_accessed=4_000_000, transcendentals=0),
        name="prep",
    )(*fixed)
    inputs = (sar_image, geo_weight, cell_index)
    fraction, send = pl.pallas_call(
        functools.partial(swath_kernel, devices, capacity),
        out_shape=(
            jax.ShapeDtypeStruct((az_lines, range_px), bf16),
            jax.ShapeDtypeStruct((devices * send_rows, LANES), bf16),
        ),
        in_specs=vmem_specs(8) + hbm_specs(3),
        out_specs=tuple(vmem_specs(2)),
        scratch_shapes=[
            *[pltpu.VMEM(x.shape, x.dtype) for x in inputs],
            pltpu.SemaphoreType.DMA((3,)),
            pltpu.VMEM((2, az_lines + 2 * HALO_LINES + 8, range_px), f32),
            pltpu.VMEM((feats, range_px), bf16),
            pltpu.VMEM((feats, range_px), bf16),
            pltpu.VMEM((feats, range_px), bf16),
            pltpu.VMEM((az_lines + 2 * CH, range_px), f32),
            pltpu.VMEM((az_lines, range_px), f32),
            pltpu.VMEM((wnd_rows, tile_cols // 4), f32),
        ],
        compiler_params=params,
        name="swath",
    )(from_previous, from_next, *prepared, *inputs)

    got = lax.all_to_all(
        send.reshape(devices, send_rows, LANES), both, split_axis=0, concat_axis=0, tiled=True
    ).reshape(devices * send_rows, LANES)

    wide_rows = tile_rows + 2 * SUBSTEPS
    wide_cols = tile_cols + LANES
    edge = jax.ShapeDtypeStruct((4 * SUBSTEPS, wide_cols), bf16)
    level, side, top_rows, bot_rows = pl.pallas_call(
        functools.partial(level_kernel, devices),
        out_shape=(
            jax.ShapeDtypeStruct((tile_rows, tile_cols), f32),
            jax.ShapeDtypeStruct((4, tile_rows, LANES), f32),
            edge,
            edge,
        ),
        in_specs=vmem_specs(7),
        out_specs=tuple(vmem_specs(4)),
        compiler_params=params,
        name="level",
    )(got, from_previous, from_next, depth, slope, rain, flow_dir)

    up, down = steps("tx")
    above = lax.ppermute(bot_rows, "tx", up)
    below = lax.ppermute(top_rows, "tx", down)

    level = pl.pallas_call(
        flow_kernel,
        out_shape=jax.ShapeDtypeStruct((tile_rows, tile_cols), f32),
        in_specs=vmem_specs(7),
        out_specs=vmem_specs(1)[0],
        scratch_shapes=[
            pltpu.VMEM((wide_rows, wide_cols), f32),
            pltpu.VMEM((wide_rows, wide_cols), f32),
            pltpu.VMEM((8, wide_rows, wide_cols), f32),
            pltpu.VMEM((2, wide_rows, wide_cols), f32),
            pltpu.VMEM((2, wide_rows + 2 * SUBSTEPS, wide_cols), f32),
            pltpu.VMEM((2, wide_rows + 2 * SUBSTEPS, wide_cols), f32),
        ],
        compiler_params=params,
        name="flow",
    )(level, side, slope, flow_dir, rain, above, below)
    return (fraction, level)


def solution(mesh):
    placed = (
        P(None, ("tx", "ty"), None),
        P(),
        P(),
        P(),
        P(),
        P(("tx", "ty"), None),
        P(("tx", "ty"), None),
        P(("tx", "ty"), None),
        P(("tx", "ty"), None),
        P("tx", "ty"),
        P("tx", "ty"),
        P("tx", "ty"),
        P("tx", "ty"),
    )
    return jax.shard_map(
        per_device,
        mesh=mesh,
        in_specs=placed,
        out_specs=(P(("tx", "ty"), None), P("tx", "ty")),
        check_vma=False,
    )
```

```python
import functools

import jax
import jax.numpy as jnp
from jax import lax
from jax.experimental import pallas as pl
from jax.experimental.pallas import tpu as pltpu
from jax.sharding import PartitionSpec as P

WIN_ROWS = 2
SUBSTEPS = 8
CH = 16
OUT_LINES = 14
IN_LINES = OUT_LINES + 2
HALO_LINES = 4
END_LINES = 8
LANES = 128
VMEM_LIMIT = 48 * 1024 * 1024
VMEM_MOST = 61880 * 1024

wet_depth = 0.5
runoff_coef = 0.25
bf16 = jnp.bfloat16
f32 = jnp.float32


def iota(shape, dim):
    return lax.broadcasted_iota(jnp.int32, shape, dim)


def quo(x, n):
    assert n & (n - 1) == 0
    return lax.shift_right_logical(x, jnp.int32(n.bit_length() - 1)) if n > 1 else x


def rem(x, n):
    assert n & (n - 1) == 0
    return x & (n - 1)


def dot(a, b):
    return lax.dot_general(a, b, (((1,), (0,)), ((), ())), preferred_element_type=f32)


def dot_0(a, b):
    return lax.dot_general(a, b, (((0,), (0,)), ((), ())), preferred_element_type=f32)


def dot_t(a, b):
    return lax.dot_general(a, b, (((1,), (1,)), ((), ())), preferred_element_type=f32)


def pixel_shifts(x):
    width = x.shape[1]
    pix = iota(x.shape, 1).astype(f32).astype(x.dtype)
    end = (width - 1 - iota(x.shape, 1)).astype(f32).astype(x.dtype)
    zero = jnp.zeros(x.shape, x.dtype)
    before = jnp.where(pix == 0, zero, pltpu.roll(x, 1, 1))
    after = jnp.where(end == 0, zero, pltpu.roll(x, width - 1, 1))
    return before, after


def merged(sums, n):
    before, _ = pixel_shifts(sums[0:n])
    _, after = pixel_shifts(sums[2 * n : 3 * n])
    return before + sums[n : 2 * n] + after


def image_columns(x):
    before, after = pixel_shifts(x)
    pad = jnp.zeros((LANES - 3 * x.shape[0], x.shape[1]), f32)
    return jnp.concatenate([before, x, after, pad], 0).astype(bf16)


def sigmoid(x):
    return (1.0 / (1.0 + jnp.exp(-x))).astype(bf16)


def line_windows(cell, obs, cov, quarter):
    px = cell.shape[1]
    kind = iota((CH, px), 0)
    is_obs = kind < CH // 2
    kind_part = rem(kind, CH // 2).astype(f32).astype(bf16)
    sub = kind.astype(f32).astype(bf16)
    one = jnp.ones((CH, px), bf16)
    nil = jnp.zeros((CH, px), bf16)
    part = quo(cell, quarter).astype(f32)
    col = rem(cell, quarter).astype(f32)

    def spread_row(x, i):
        return jnp.broadcast_to(x[i : i + 1], (CH, px)).astype(bf16)

    out = []
    for i in range(cell.shape[0]):
        value = jnp.where(is_obs, obs[i : i + 1], cov[i : i + 1]).astype(bf16)
        left = jnp.where(kind_part == spread_row(part, i), value, nil)
        where_col = spread_row(col, i)
        hot = jnp.concatenate([jnp.where(sub + g * CH == where_col, one, nil) for g in range(quarter // CH)], 0)
        out.append(dot_t(left, hot))
    return out


def window_goods(sums):
    rows, quarter = sums.shape
    cols = 4 * quarter
    repeat = (rem(iota((quarter, cols), 1), quarter) == iota((quarter, cols), 0)).astype(bf16)
    tiled = dot(sums.astype(bf16), repeat)
    mine = rem(iota((rows, cols), 0), 4) == quo(iota((rows, cols), 1), quarter)
    return jnp.where(mine, tiled, 0.0).astype(bf16)


def band_weights(tiled, rows, cols, per_row, line_of):
    out_line = quo(iota((rows, cols), 0), per_row)
    off = line_of(iota((rows, cols), 1)) - out_line
    out = jnp.zeros((rows, cols), f32)
    for ky in range(3):
        out = jnp.where(off == ky, tiled[ky], out)
    return out.astype(bf16)


def edge_kernel(
    sar_hbm, depth_hbm, slope_hbm, rain_hbm, dir_hbm, up_ref, down_ref,
    last_ref, first_ref, depth_ref, slope_ref, rain_ref, dir_ref, sems,
):
    lines, px = sar_hbm.shape[1:]
    cols = depth_hbm.shape[1]
    h = SUBSTEPS
    copies = [
        pltpu.make_async_copy(src, dst, sems.at[i])
        for i, (src, dst) in enumerate(
            (
                (depth_hbm, depth_ref), (slope_hbm, slope_ref), (rain_hbm, rain_ref), (dir_hbm, dir_ref),
                (sar_hbm.at[:, lines - 16 : lines, :], last_ref), (sar_hbm.at[:, 0:16, :], first_ref),
            )
        )
    ]
    for copy in copies:
        copy.start()
    for copy in copies:
        copy.wait()
    fields = (
        depth_ref[...],
        runoff_coef * jnp.sqrt(slope_ref[...]),
        rain_ref[...],
        dir_ref[...].astype(f32),
    )
    zeros = jnp.zeros((8, px), f32)
    for ref, image_ref, lo, strip in (
        (up_ref, last_ref, 16 - HALO_LINES, lambda x: jnp.transpose(x[:, cols - LANES :], (1, 0))[LANES - h :]),
        (down_ref, first_ref, 0, lambda x: jnp.transpose(x[:, 0:LANES], (1, 0))[0:h]),
    ):
        image = [image_ref[ch].astype(f32)[lo : lo + HALO_LINES] for ch in range(2)]
        strips = [strip(x) for x in fields]
        ref[...] = jnp.concatenate(
            [jnp.concatenate(strips[0:2], 1), jnp.concatenate(strips[2:4], 1), *image, zeros], 0
        ).astype(bf16)


def strips_of(ref, keep):
    both = jnp.where(keep, ref[0:16, :].astype(f32), 0.0)
    cols = both.shape[1] // 2
    return [both[0:8, 0:cols], both[0:8, cols:], both[8:16, 0:cols], both[8:16, cols:]]


def inner_kernel(
    devices, capacity,
    k1_ref, k2_ref, k3_ref, k4_ref, tile_ref, row_ref, sar_ref, gw_ref, cell_ref,
    w1_ref, w2_ref, w3_ref, w4_ref, perm_ref, extra_ref, frac_ref, slots_ref, e1_ref, e2_ref, e3_ref,
    t1_ref, t4_ref, s_ref, xa_ref, xb_ref, x3_ref, logit_ref, wnd_ref,
):
    rows = OUT_LINES * CH
    cols = IN_LINES * CH

    out_of = quo(iota((CH, OUT_LINES * cols), 1), cols)
    in_of = rem(iota((CH, OUT_LINES * cols), 1), cols) - iota((CH, OUT_LINES * cols), 0)
    spread = [(in_of == CH * (out_of + ky)).astype(bf16) for ky in range(3)]
    n1 = OUT_LINES * LANES
    group1 = quo(rem(iota((8, n1), 1), LANES), IN_LINES) == iota((8, n1), 0)
    line1 = rem(iota((8, n1), 1), IN_LINES) - quo(iota((8, n1), 1), LANES)
    spread1 = [(group1 & (line1 == ky)).astype(bf16) for ky in range(3)]
    tile4 = (rem(iota((CH, cols), 1), CH) == iota((CH, cols), 0)).astype(bf16)
    t1_ref[...] = jnp.zeros(t1_ref.shape, f32)
    t4_ref[...] = jnp.zeros(t4_ref.shape, f32)
    for ky in range(3):
        for kx in range(3):
            t1_ref[ky * 8 + 2 * kx : ky * 8 + 2 * kx + 2, :] = k1_ref[ky, kx].astype(f32)
        t4_ref[ky * 3 : ky * 3 + 3, :] = k4_ref[ky].astype(f32)
    wide1 = sum(dot_0(t1_ref[ky * 8 : ky * 8 + 8, :].astype(bf16), spread1[ky]) for ky in range(3))
    for i in range(OUT_LINES):
        w1_ref[i * CH : (i + 1) * CH, :] = wide1[:, i * LANES : (i + 1) * LANES].astype(bf16)
    for k_ref, w_ref in ((k2_ref, w2_ref), (k3_ref, w3_ref)):
        wide = sum(dot(k_ref[ky * 3 * CH : (ky + 1) * 3 * CH, :], spread[ky]) for ky in range(3))
        for kx in range(3):
            for i in range(OUT_LINES):
                w_ref[i * CH : (i + 1) * CH, kx * cols : (kx + 1) * cols] = wide[
                    kx * CH : (kx + 1) * CH, i * cols : (i + 1) * cols
                ].astype(bf16)
    wide4 = dot(t4_ref[...].astype(bf16), tile4)
    w4_ref[...] = jnp.concatenate(
        [
            band_weights(
                [jnp.broadcast_to(wide4[ky * 3 + kx : ky * 3 + kx + 1], (CH, cols)) for ky in range(3)],
                CH, cols, 1, lambda k: quo(k, CH),
            )
            for kx in range(3)
        ],
        0,
    )

    lines = tile_ref.shape[1]
    tile = tile_ref[...].astype(f32)
    same = iota((lines, lines), 0) == iota((lines, lines), 1)
    tile_sub = jnp.sum(jnp.where(same, jnp.broadcast_to(tile, (lines, lines)), 0.0), 1, keepdims=True)
    rival = (tile_sub == tile) & (iota((lines, lines), 0) < iota((lines, lines), 1))
    slot = tile * capacity + jnp.sum(jnp.where(rival, 1.0, 0.0), 0, keepdims=True)
    slots = slots_ref.shape[0]
    wnd_rows = CH * lines
    per_line = CH
    widen = (quo(iota((lines, wnd_rows), 1), per_line) == iota((lines, wnd_rows), 0)).astype(bf16)
    slot_wide = dot(jnp.broadcast_to(slot, (8, lines)).astype(bf16), widen)[0:1]
    place = slot_wide.astype(jnp.int32) * 4 + rem(quo(iota((1, wnd_rows), 1), 4), 4)
    perm = jnp.where(iota((slots, wnd_rows), 0) == place, 1.0, 0.0).astype(bf16)
    end = END_LINES * CH
    perm_ref[...] = jnp.concatenate([perm[:, 0:end], perm[:, wnd_rows - end :]], 1)

    row_of = dot(
        jnp.where(same, jnp.broadcast_to(row_ref[...].astype(f32), (lines, lines)), 0.0).astype(bf16),
        jnp.ones((lines, LANES), bf16),
    )
    perm_line = jnp.where(quo(iota((slots, lines), 0), 4) == slot.astype(jnp.int32), 1.0, 0.0).astype(bf16)
    row_own = dot(perm_line, row_of.astype(bf16))
    per_tile = 4 * capacity
    lane = iota((slots, LANES), 1)
    entry = rem(iota((slots, LANES), 0), per_tile)
    info = jnp.zeros((slots, LANES), f32)
    for turn, value in enumerate((row_own, of_right(row_own, per_tile), of_left(row_own, per_tile))):
        info = jnp.where(lane == turn * per_tile + entry, value, info)
    info = jnp.sum(info.reshape(devices, per_tile, LANES), 1, keepdims=True)
    at = iota((devices, 8, LANES), 1)
    extra_ref[...] = jnp.where(at == 2, info, 0.0).reshape(8 * devices, LANES)


    px = sar_ref.shape[2]
    for ch in range(2):
        s_ref[ch, 0:lines, :] = sar_ref[ch].astype(f32)
        s_ref[ch, lines:, :] = jnp.zeros((s_ref.shape[1] - lines, px), f32)
    total = xa_ref.shape[1] // CH
    xa_ref[:, (total - 2) * CH :, :] = jnp.zeros((3, 2 * CH, px), bf16)

    def put(ref, line, acc):
        feat = jnp.maximum(acc, 0.0).astype(bf16)
        at = slice(line * CH, line * CH + rows)
        if len(ref.shape) == 2:
            ref[at, :] = feat
            return
        before, after = pixel_shifts(feat)
        ref[0, at, :] = before
        ref[1, at, :] = feat
        ref[2, at, :] = after

    full = (lines + 4) // OUT_LINES + 1
    for b in range(full):
        at = b * OUT_LINES
        x = jnp.concatenate([s_ref[0, at : at + IN_LINES, :], s_ref[1, at : at + IN_LINES, :]], 0)
        put(xa_ref, 1 + at, dot(w1_ref[...], image_columns(x)))
    for w_ref, src, dst, line, blocks in ((w2_ref, xa_ref, xb_ref, 2, full), (w3_ref, xb_ref, x3_ref, 3, full - 1)):
        for b in range(blocks):
            at = line + b * OUT_LINES
            x = src[:, (at - 1) * CH : (at - 1) * CH + cols, :].reshape(3 * cols, px)
            put(dst, at, dot(w_ref[...], x))

    def ends_of(lo, center):
        hi = lines - lo - 2
        return jnp.concatenate([center[at * CH : (at + 2) * CH, :] for at in (lo, hi)], 0)

    e1_ref[...] = ends_of(3, xa_ref.at[1])
    e2_ref[...] = ends_of(4, xb_ref.at[1])
    e3_ref[...] = ends_of(5, x3_ref)
    logit_ref[0:END_LINES, :] = jnp.zeros((END_LINES, px), f32)
    starts = [3 + b * OUT_LINES for b in range(full - 2)] + [lines - 5 - IN_LINES]
    for at in starts:
        sums = dot(w4_ref[...], x3_ref[at * CH : at * CH + cols, :])
        logit_ref[at + 1 : at + 1 + CH, :] = merged(sums, CH)
    frac_ref[...] = sigmoid(logit_ref[0:lines, :])
    quarter = wnd_ref.shape[1]
    group = 16

    def window_group(g, carry):
        at = pl.ds(pl.multiple_of(g * group + END_LINES, END_LINES), group)
        cov = gw_ref[at, :]
        obs = sigmoid(logit_ref[at, :]).astype(f32) * cov
        for i, sums in enumerate(line_windows(cell_ref[at, :], obs, cov, quarter)):
            wnd_ref[pl.ds(pl.multiple_of(g * (CH * group) + CH * i, CH), CH), :] = sums
        return carry

    lax.fori_loop(0, (lines - 2 * END_LINES) // group, window_group, 0)
    slots_ref[...] = dot(perm[:, end : wnd_rows - end], window_goods(wnd_ref[...]))


def of_right(x, per_tile):
    return jnp.concatenate([x[per_tile:], jnp.zeros((per_tile, x.shape[1]), x.dtype)], 0)


def of_left(x, per_tile):
    return jnp.concatenate([jnp.zeros((per_tile, x.shape[1]), x.dtype), x[: x.shape[0] - per_tile]], 0)


def ends_kernel(
    devices, capacity,
    above_ref, below_ref, w1_ref, w2_ref, w3_ref, w4_ref, perm_ref, extra_ref, frac_in, slots_in, e1_ref, e2_ref, e3_ref,
    sar_ref, gw_ref, cell_ref,
    frac_ref, send_ref,
    f_ref,
):
    lines, px = gw_ref.shape
    n_ty = lax.axis_size("ty")
    me = lax.axis_index("tx") * n_ty + lax.axis_index("ty")
    rows = OUT_LINES * CH
    above = above_ref[16:32, :].astype(f32)
    below = below_ref[16:32, :].astype(f32)
    n = HALO_LINES

    pieces = []
    for ch in range(2):
        own = sar_ref[ch].astype(f32)
        pieces += [above[ch * n : (ch + 1) * n], own[0:n], own[lines - n :], below[ch * n : (ch + 1) * n]]
    x = image_columns(jnp.concatenate(pieces, 0))
    out_line = quo(iota((rows, px), 0), CH)
    low = jnp.where(me == 0, n, 0)
    high = jnp.where(me == devices - 1, OUT_LINES - n, 2 * OUT_LINES)
    for layer, (w_ref, e_ref) in enumerate(((w1_ref, e1_ref), (w2_ref, e2_ref), (w3_ref, e3_ref)), 1):
        acc = jnp.maximum(dot(w_ref[...], x), 0.0)
        inside = (out_line >= low - layer) & (out_line < high + layer)
        feat = jnp.where(inside, acc, 0.0).astype(bf16)
        block = jnp.concatenate([feat[0 : 6 * CH], e_ref[...], feat[8 * CH :]], 0)
        if layer < 3:
            before, after = pixel_shifts(block)
            x = jnp.concatenate([before, block, after], 0)
    frac = sigmoid(merged(dot(w4_ref[...], block), CH)).astype(f32)
    f_ref[...] = frac_in[...].astype(f32)
    f_ref[0:6, :] = frac[0:6]
    f_ref[lines - 6 :, :] = frac[8:14]
    frac_ref[...] = f_ref[...].astype(bf16)
    quarter = slots_in.shape[1] // 4
    sums = []
    for at in (slice(0, END_LINES), slice(lines - END_LINES, lines)):
        cov = gw_ref[at, :]
        sums += line_windows(cell_ref[at, :], f_ref[at, :] * cov, cov, quarter)
    by_slot = slots_in[...] + dot(perm_ref[...], window_goods(jnp.concatenate(sums, 0)))

    per_tile = 4 * capacity
    slots, tile_cols = by_slot.shape
    h = SUBSTEPS
    entry = rem(iota((slots, LANES), 0), per_tile)
    here = quo(iota((slots, LANES), 1), h) == entry
    column = rem(quo(iota((slots, LANES), 0), per_tile), n_ty)
    source = iota((LANES, LANES), 0)
    spot = rem(iota((LANES, LANES), 1), h)

    def strip(x, first_lane, keep):
        take = ((spot + first_lane == source) & (source - first_lane < h)).astype(bf16)
        x = jnp.where(here & keep, dot(x.astype(bf16), take), 0.0)
        return jnp.sum(x.reshape(devices, per_tile, LANES), 1, keepdims=True)

    right_strip = strip(of_right(by_slot[:, 0:LANES], per_tile), 0, column < n_ty - 1)
    left_strip = strip(of_left(by_slot[:, tile_cols - LANES :], per_tile), LANES - h, column > 0)
    at = iota((devices, 8, LANES), 1)
    extra = extra_ref[...].reshape(devices, 8, LANES)
    extra = jnp.where(at == 0, right_strip, jnp.where(at == 1, left_strip, extra))
    halves = [by_slot[:, at : at + LANES].reshape(devices, per_tile, LANES) for at in range(0, tile_cols, LANES)]
    packed = jnp.concatenate([*halves, extra], 1)
    send_ref[...] = packed.reshape(send_ref.shape).astype(bf16)


def transposed(x):
    return jnp.transpose(x, (1, 0))


def level_kernel(
    devices,
    got_ref, from_left_ref, from_right_ref, depth_ref, slope_ref, rain_ref, dir_ref,
    level_ref, side_ref, top_ref, bot_ref,
):
    tile_rows, tile_cols = depth_ref.shape
    h = SUBSTEPS
    halves = tile_cols // LANES
    n = (got_ref.shape[0] // devices - 8) // halves
    k = devices * n
    packed = got_ref[...].astype(f32).reshape(devices, halves * n + 8, LANES)
    main = jnp.concatenate([packed[:, i * n : (i + 1) * n].reshape(k, LANES) for i in range(halves)], 1)
    extra = packed[:, halves * n :]

    entry = rem(iota((k, LANES), 0), n)
    spread = quo(iota((k, LANES), 1), h) == entry

    def strip(r, first):
        rows = jnp.broadcast_to(extra[:, r : r + 1], (devices, n, LANES)).reshape(k, LANES)
        take = rem(iota((LANES, LANES), 0), h) + first == iota((LANES, LANES), 1)
        return dot(jnp.where(spread, rows, 0.0).astype(bf16), take.astype(bf16)).astype(bf16)

    lane = iota((1, k), 1)
    offset = rem(lane, 2) + tile_rows * rem(quo(lane, 2), 2)
    info = jnp.broadcast_to(extra[:, 2:3], (devices, n, LANES)).reshape(k, LANES)
    info = jnp.where(rem(iota((k, LANES), 1), n) == entry, info, 0.0).astype(bf16)
    turns = (quo(iota((LANES, LANES), 0), n) == iota((LANES, LANES), 1)).astype(bf16)
    lines = transposed(dot(info, turns))

    def placer(turn):
        target = lines[turn : turn + 1].astype(jnp.int32) + offset
        return jnp.where(iota((2 * tile_rows, k), 0) == target, 1.0, 0.0).astype(bf16)

    summed = dot(placer(0), main.astype(bf16))
    summed_side = dot(placer(1), strip(0, 0)) + dot(placer(2), strip(1, LANES - h))

    ty = lax.axis_index("ty")
    left = strips_of(from_left_ref, ty > 0)
    right = strips_of(from_right_ref, ty < lax.axis_size("ty") - 1)
    gap = jnp.zeros((LANES - 2 * h, tile_rows), f32)
    depth_side, conv_side, rain_side, code_side = [
        transposed(jnp.concatenate([r, gap, l], 0)) for r, l in zip(right, left)
    ]

    def analysed(sums, depth):
        observed = sums[0:tile_rows]
        covered = sums[tile_rows:]
        wet = depth / (depth + wet_depth)
        innovation = (observed - covered * wet) / (covered + 1.0)
        return depth * jnp.exp(innovation)

    level = analysed(summed, depth_ref[...])
    level_ref[...] = level
    sides = (analysed(summed_side, depth_side), rain_side, conv_side, code_side)
    owns = (level, rain_ref, slope_ref, dir_ref)

    def end_rows(at):
        own = [x[at, :] for x in owns]
        own[2] = runoff_coef * jnp.sqrt(own[2])
        own[3] = own[3].astype(f32)
        return jnp.concatenate([jnp.concatenate([o, x[at]], 1) for o, x in zip(own, sides)], 0).astype(bf16)

    for i, x in enumerate(sides):
        side_ref[i] = x
    top_ref[...] = end_rows(slice(0, h))
    bot_ref[...] = end_rows(slice(tile_rows - h, tile_rows))


def substeps(level, rain, conv, code, rain_s, conv_s, m_ref, part_ref, up_ref, down_ref, chunk):
    rows, cols = level.shape
    h = SUBSTEPS
    for ref in (up_ref, down_ref):
        ref[0] = jnp.zeros(ref.shape[1:], f32)
        ref[1, 0:h, :] = jnp.zeros((h, cols), f32)
        ref[1, h + rows :, :] = jnp.zeros((h, cols), f32)
    part_ref[0] = level
    rain_s[...] = rain
    conv_s[...] = conv
    sides = (-1, 0, 1, -1, 1, -1, 0, 1)
    for direction, side in enumerate(sides):
        share = jnp.where(code == direction, conv, 0.0)
        m_ref[direction] = pltpu.roll(share, side % cols, 1) if side else share

    def level_at(buf, r, n):
        level = part_ref[buf, r : r + n, :]
        return level + up_ref[buf, h + r + 1 : h + r + 1 + n, :] + down_ref[buf, h + r - 1 : h + r - 1 + n, :]

    def substep(buf, new):
        for r in range(0, rows, chunk):
            level = level_at(buf, r, chunk)
            power = level * jnp.exp((2.0 / 3.0) * jnp.log(jnp.maximum(jnp.abs(level), 1e-30)))
            from_right = pltpu.roll(power, cols - 1, 1)
            from_left = pltpu.roll(power, 1, 1)
            m = [m_ref[d, r : r + chunk, :] for d in range(8)]
            up_ref[new, h + r : h + r + chunk, :] = m[0] * from_right + m[1] * power + m[2] * from_left
            down_ref[new, h + r : h + r + chunk, :] = m[5] * from_right + m[6] * power + m[7] * from_left
            part_ref[new, r : r + chunk, :] = (
                level + rain_s[r : r + chunk, :] - conv_s[r : r + chunk, :] * power
                + (m[3] * from_right + m[4] * from_left)
            )

    def substep_pair(i, carry):
        substep(0, 1)
        substep(1, 0)
        return carry

    lax.fori_loop(0, SUBSTEPS // 2, substep_pair, 0)
    return level_at


def flow_inner_kernel(level_ref, side_ref, slope_ref, dir_ref, rain_ref, out_ref, *scratch):
    rows, cols = level_ref.shape
    own = (level_ref[...], rain_ref[...], runoff_coef * jnp.sqrt(slope_ref[...]), dir_ref[...].astype(f32))
    level_at = substeps(*[jnp.concatenate([x, side_ref[i]], 1) for i, x in enumerate(own)], *scratch, 16)
    out_ref[...] = level_at(0, 0, rows)[:, 0:cols]


def flow_ends_kernel(inner_ref, level_ref, side_ref, slope_ref, dir_ref, rain_ref, above_ref, below_ref, out_ref, *scratch):
    rows, cols = level_ref.shape
    h = SUBSTEPS
    above = above_ref[...].astype(f32)
    below = below_ref[...].astype(f32)
    fields = []
    for i, ref in enumerate((level_ref, rain_ref, slope_ref, dir_ref)):
        ends = []
        for at in (slice(0, 2 * h), slice(rows - 2 * h, rows)):
            own = ref[at, :].astype(f32)
            if i == 2:
                own = runoff_coef * jnp.sqrt(own)
            ends.append(jnp.concatenate([own, side_ref[i, at, :]], 1))
        fields.append(jnp.concatenate([above[i * h : (i + 1) * h], *ends, below[i * h : (i + 1) * h]], 0))
    level_at = substeps(*fields, *scratch, 16)
    out_ref[h : rows - h, :] = inner_ref[h : rows - h, :]
    out_ref[0:h, :] = level_at(0, h, h)[:, 0:cols]
    out_ref[rows - h :, :] = level_at(0, 4 * h, h)[:, 0:cols]


def flow_scratch(rows, cols):
    return [
        pltpu.VMEM((rows, cols), f32),
        pltpu.VMEM((rows, cols), f32),
        pltpu.VMEM((8, rows, cols), f32),
        pltpu.VMEM((2, rows, cols), f32),
        pltpu.VMEM((2, rows + 2 * SUBSTEPS, cols), f32),
        pltpu.VMEM((2, rows + 2 * SUBSTEPS, cols), f32),
    ]


def hbm_specs(n):
    return [pl.BlockSpec(memory_space=pltpu.HBM)] * n


def vmem_specs(n):
    return [pl.BlockSpec(memory_space=pltpu.VMEM)] * n


def per_device(
    sar_image, kernel_first, kernel_second, kernel_third, kernel_last,
    geo_weight, cell_index, block_tile, block_row, depth, slope, flow_dir, rain,
):
    both = ("tx", "ty")
    devices = lax.axis_size(both)
    az_lines, range_px = geo_weight.shape
    tile_rows, tile_cols = depth.shape
    capacity = max(2, 2 * az_lines // devices)

    def steps(axis):
        size = lax.axis_size(axis)
        up = [(i, i + 1) for i in range(size - 1)]
        return up, [(j, i) for i, j in up]

    params = pltpu.CompilerParams(vmem_limit_bytes=VMEM_LIMIT)
    up, down = steps(both)
    message = jax.ShapeDtypeStruct((32, range_px), bf16)
    to_next, to_previous = pl.pallas_call(
        edge_kernel,
        out_shape=(message, message),
        in_specs=hbm_specs(5),
        out_specs=tuple(vmem_specs(2)),
        scratch_shapes=[
            pltpu.VMEM((2, 16, range_px), bf16),
            pltpu.VMEM((2, 16, range_px), bf16),
            *[pltpu.VMEM(x.shape, x.dtype) for x in (depth, slope, rain, flow_dir)],
            pltpu.SemaphoreType.DMA((6,)),
        ],
        compiler_params=pltpu.CompilerParams(vmem_limit_bytes=VMEM_MOST),
        name="edges",
    )(sar_image, depth, slope, rain, flow_dir)
    from_previous = lax.ppermute(to_next, both, up)
    from_next = lax.ppermute(to_previous, both, down)

    rows, cols = OUT_LINES * CH, IN_LINES * CH
    slots = devices * capacity * 4
    send_rows = tile_cols // LANES * 4 * capacity + 8
    full = (az_lines + 4) // OUT_LINES + 1
    feats = (full * OUT_LINES + 3) * CH
    blocks_in = (az_lines + IN_LINES, range_px)

    def cost(flops):
        return pl.CostEstimate(flops=flops, bytes_accessed=4_000_000, transcendentals=0)

    prepared = pl.pallas_call(
        functools.partial(inner_kernel, devices, capacity),
        out_shape=(
            jax.ShapeDtypeStruct((rows, LANES), bf16),
            jax.ShapeDtypeStruct((rows, 3 * cols), bf16),
            jax.ShapeDtypeStruct((rows, 3 * cols), bf16),
            jax.ShapeDtypeStruct((3 * CH, cols), bf16),
            jax.ShapeDtypeStruct((slots, 2 * END_LINES * CH), bf16),
            jax.ShapeDtypeStruct((8 * devices, LANES), f32),
            jax.ShapeDtypeStruct((az_lines, range_px), bf16),
            jax.ShapeDtypeStruct((slots, tile_cols), f32),
            *[jax.ShapeDtypeStruct((4 * CH, range_px), bf16)] * 3,
        ),
        in_specs=vmem_specs(9),
        out_specs=tuple(vmem_specs(11)),
        scratch_shapes=[
            pltpu.VMEM((24, CH), f32),
            pltpu.VMEM((16, CH), f32),
            pltpu.VMEM((2, *blocks_in), f32),
            pltpu.VMEM((3, feats, range_px), bf16),
            pltpu.VMEM((3, feats, range_px), bf16),
            pltpu.VMEM((feats, range_px), bf16),
            pltpu.VMEM(blocks_in, f32),
            pltpu.VMEM(((az_lines - 2 * END_LINES) * CH, tile_cols // 4), f32),
        ],
        compiler_params=params,
        cost_estimate=cost(8_000_000_000),
        name="inner",
    )(
        jnp.transpose(kernel_first, (2, 3, 1, 0)),
        jnp.transpose(kernel_second, (2, 3, 0, 1)).reshape(9 * CH, CH),
        jnp.transpose(kernel_third, (2, 3, 0, 1)).reshape(9 * CH, CH),
        jnp.transpose(kernel_last[0], (1, 2, 0)),
        block_tile.reshape(1, az_lines), block_row.reshape(1, az_lines),
        sar_image, geo_weight, cell_index,
    )
    fraction, send = pl.pallas_call(
        functools.partial(ends_kernel, devices, capacity),
        out_shape=(
            jax.ShapeDtypeStruct((az_lines, range_px), bf16),
            jax.ShapeDtypeStruct((devices * send_rows, LANES), bf16),
        ),
        in_specs=vmem_specs(16),
        out_specs=tuple(vmem_specs(2)),
        scratch_shapes=[pltpu.VMEM((az_lines, range_px), f32)],
        compiler_params=params,
        name="ends",
    )(from_previous, from_next, *prepared, sar_image, geo_weight, cell_index)

    got = lax.all_to_all(
        send.reshape(devices, send_rows, LANES), both, split_axis=0, concat_axis=0, tiled=True
    ).reshape(devices * send_rows, LANES)

    wide_cols = tile_cols + LANES
    edge = jax.ShapeDtypeStruct((4 * SUBSTEPS, wide_cols), bf16)
    level, side, top_rows, bot_rows = pl.pallas_call(
        functools.partial(level_kernel, devices),
        out_shape=(
            jax.ShapeDtypeStruct((tile_rows, tile_cols), f32),
            jax.ShapeDtypeStruct((4, tile_rows, LANES), f32),
            edge,
            edge,
        ),
        in_specs=vmem_specs(7),
        out_specs=tuple(vmem_specs(4)),
        compiler_params=params,
        name="level",
    )(got, from_previous, from_next, depth, slope, rain, flow_dir)

    up, down = steps("tx")
    above = lax.ppermute(bot_rows, "tx", up)
    below = lax.ppermute(top_rows, "tx", down)

    inner = pl.pallas_call(
        flow_inner_kernel,
        out_shape=jax.ShapeDtypeStruct((tile_rows, tile_cols), f32),
        in_specs=vmem_specs(5),
        out_specs=vmem_specs(1)[0],
        scratch_shapes=flow_scratch(tile_rows, wide_cols),
        compiler_params=params,
        cost_estimate=cost(5_000_000_000),
        name="flow_inner",
    )(level, side, slope, flow_dir, rain)
    level = pl.pallas_call(
        flow_ends_kernel,
        out_shape=jax.ShapeDtypeStruct((tile_rows, tile_cols), f32),
        in_specs=vmem_specs(8),
        out_specs=vmem_specs(1)[0],
        scratch_shapes=flow_scratch(6 * SUBSTEPS, wide_cols),
        compiler_params=params,
        name="flow_ends",
    )(inner, level, side, slope, flow_dir, rain, above, below)
    return (fraction, level)


def solution(mesh):
    placed = (
        P(None, ("tx", "ty"), None),
        P(),
        P(),
        P(),
        P(),
        P(("tx", "ty"), None),
        P(("tx", "ty"), None),
        P(("tx", "ty"), None),
        P(("tx", "ty"), None),
        P("tx", "ty"),
        P("tx", "ty"),
        P("tx", "ty"),
        P("tx", "ty"),
    )
    return jax.shard_map(
        per_device,
        mesh=mesh,
        in_specs=placed,
        out_specs=(P(("tx", "ty"), None), P("tx", "ty")),
        check_vma=False,
    )
```

```python
import functools

import jax
import jax.numpy as jnp
from jax import lax
from jax.experimental import pallas as pl
from jax.experimental.pallas import tpu as pltpu
from jax.sharding import PartitionSpec as P

WIN_ROWS = 2
SUBSTEPS = 8
CH = 16
OUT_LINES = 14
IN_LINES = OUT_LINES + 2
HALO_LINES = 4
END_LINES = 8
LANES = 128
VMEM_LIMIT = 48 * 1024 * 1024
VMEM_MOST = 61880 * 1024

wet_depth = 0.5
runoff_coef = 0.25
bf16 = jnp.bfloat16
f32 = jnp.float32


def iota(shape, dim):
    return lax.broadcasted_iota(jnp.int32, shape, dim)


def quo(x, n):
    assert n & (n - 1) == 0
    return lax.shift_right_logical(x, jnp.int32(n.bit_length() - 1)) if n > 1 else x


def rem(x, n):
    assert n & (n - 1) == 0
    return x & (n - 1)


def dot(a, b):
    return lax.dot_general(a, b, (((1,), (0,)), ((), ())), preferred_element_type=f32)


def dot_0(a, b):
    return lax.dot_general(a, b, (((0,), (0,)), ((), ())), preferred_element_type=f32)


def dot_t(a, b):
    return lax.dot_general(a, b, (((1,), (1,)), ((), ())), preferred_element_type=f32)


def pixel_shifts(x):
    width = x.shape[1]
    pix = iota(x.shape, 1).astype(f32).astype(x.dtype)
    end = (width - 1 - iota(x.shape, 1)).astype(f32).astype(x.dtype)
    zero = jnp.zeros(x.shape, x.dtype)
    before = jnp.where(pix == 0, zero, pltpu.roll(x, 1, 1))
    after = jnp.where(end == 0, zero, pltpu.roll(x, width - 1, 1))
    return before, after


def merged(sums, n):
    before, _ = pixel_shifts(sums[0:n])
    _, after = pixel_shifts(sums[2 * n : 3 * n])
    return before + sums[n : 2 * n] + after


def image_columns(x):
    before, after = pixel_shifts(x)
    pad = jnp.zeros((LANES - 3 * x.shape[0], x.shape[1]), f32)
    return jnp.concatenate([before, x, after, pad], 0).astype(bf16)


def sigmoid(x):
    return (1.0 / (1.0 + jnp.exp(-x))).astype(bf16)


def line_windows(cell, obs, cov, quarter):
    px = cell.shape[1]
    kind = iota((CH, px), 0)
    is_obs = kind < CH // 2
    kind_part = rem(kind, CH // 2).astype(f32).astype(bf16)
    sub = kind.astype(f32).astype(bf16)
    one = jnp.ones((CH, px), bf16)
    nil = jnp.zeros((CH, px), bf16)
    part = quo(cell, quarter).astype(f32)
    col = rem(cell, quarter).astype(f32)

    def spread_row(x, i):
        return jnp.broadcast_to(x[i : i + 1], (CH, px)).astype(bf16)

    out = []
    for i in range(cell.shape[0]):
        value = jnp.where(is_obs, obs[i : i + 1], cov[i : i + 1]).astype(bf16)
        left = jnp.where(kind_part == spread_row(part, i), value, nil)
        where_col = spread_row(col, i)
        hot = jnp.concatenate([jnp.where(sub + g * CH == where_col, one, nil) for g in range(quarter // CH)], 0)
        out.append(dot_t(left, hot))
    return out


def window_goods(sums):
    rows, quarter = sums.shape
    cols = 4 * quarter
    repeat = (rem(iota((quarter, cols), 1), quarter) == iota((quarter, cols), 0)).astype(bf16)
    tiled = dot(sums.astype(bf16), repeat)
    mine = rem(iota((rows, cols), 0), 4) == quo(iota((rows, cols), 1), quarter)
    return jnp.where(mine, tiled, 0.0).astype(bf16)


def band_weights(tiled, rows, cols, per_row, line_of):
    out_line = quo(iota((rows, cols), 0), per_row)
    off = line_of(iota((rows, cols), 1)) - out_line
    out = jnp.zeros((rows, cols), f32)
    for ky in range(3):
        out = jnp.where(off == ky, tiled[ky], out)
    return out.astype(bf16)


def edge_kernel(
    sar_hbm, depth_hbm, slope_hbm, rain_hbm, dir_hbm, k1_hbm, k4_hbm, tile_hbm, row_hbm,
    first_swap_ref, second_swap_ref, k1_ref, k4_ref, tile_ref, row_ref,
    last_ref, first_ref, depth_ref, slope_ref, rain_ref, dir_ref, sems,
):
    even = rem(lax.axis_index("tx") * lax.axis_size("ty") + lax.axis_index("ty"), 2) == 0
    lines, px = sar_hbm.shape[1:]
    cols = depth_hbm.shape[1]
    h = SUBSTEPS
    copies = [
        pltpu.make_async_copy(src, dst, sems.at[i])
        for i, (src, dst) in enumerate(
            (
                (depth_hbm, depth_ref), (slope_hbm, slope_ref), (rain_hbm, rain_ref), (dir_hbm, dir_ref),
                (sar_hbm.at[:, lines - 16 : lines, :], last_ref), (sar_hbm.at[:, 0:16, :], first_ref),
                (k1_hbm, k1_ref), (k4_hbm, k4_ref), (tile_hbm, tile_ref), (row_hbm, row_ref),
            )
        )
    ]
    for copy in copies:
        copy.start()
    for copy in copies:
        copy.wait()
    fields = (
        depth_ref[...],
        runoff_coef * jnp.sqrt(slope_ref[...]),
        rain_ref[...],
        dir_ref[...].astype(f32),
    )
    zeros = jnp.zeros((8, px), f32)
    messages = []
    for image_ref, lo, strip in (
        (last_ref, 16 - HALO_LINES, lambda x: jnp.transpose(x[:, cols - LANES :], (1, 0))[LANES - h :]),
        (first_ref, 0, lambda x: jnp.transpose(x[:, 0:LANES], (1, 0))[0:h]),
    ):
        image = [image_ref[ch].astype(f32)[lo : lo + HALO_LINES] for ch in range(2)]
        strips = [strip(x) for x in fields]
        messages.append(
            jnp.concatenate([jnp.concatenate(strips[0:2], 1), jnp.concatenate(strips[2:4], 1), *image, zeros], 0)
        )
    first, second = in_turn(even, *messages)
    first_swap_ref[...] = first.astype(bf16)
    second_swap_ref[...] = second.astype(bf16)


def in_turn(even, to_next, to_previous):
    return jnp.where(even, to_next, to_previous), jnp.where(even, to_previous, to_next)


def from_turns(even, first, second):
    return jnp.where(even, second, first), jnp.where(even, first, second)


def strips_of(message, keep):
    both = jnp.where(keep, message, 0.0)
    cols = both.shape[1] // 2
    return [both[0:8, 0:cols], both[0:8, cols:], both[8:16, 0:cols], both[8:16, cols:]]


def inner_kernel(
    devices, capacity,
    k1_ref, k2_ref, k3_ref, k4_ref, tile_ref, row_ref, sar_ref, gw_ref, cell_ref,
    w1_ref, w2_ref, w3_ref, w4_ref, perm_ref, extra_ref, frac_ref, slots_ref, e1_ref, e2_ref, e3_ref,
    t1_ref, t4_ref, s_ref, xa_ref, xb_ref, x3_ref, logit_ref, wnd_ref,
):
    rows = OUT_LINES * CH
    cols = IN_LINES * CH

    out_of = quo(iota((CH, OUT_LINES * cols), 1), cols)
    in_of = rem(iota((CH, OUT_LINES * cols), 1), cols) - iota((CH, OUT_LINES * cols), 0)
    spread = [(in_of == CH * (out_of + ky)).astype(bf16) for ky in range(3)]
    n1 = OUT_LINES * LANES
    group1 = quo(rem(iota((8, n1), 1), LANES), IN_LINES) == iota((8, n1), 0)
    line1 = rem(iota((8, n1), 1), IN_LINES) - quo(iota((8, n1), 1), LANES)
    spread1 = [(group1 & (line1 == ky)).astype(bf16) for ky in range(3)]
    tile4 = (rem(iota((CH, cols), 1), CH) == iota((CH, cols), 0)).astype(bf16)
    t1_ref[...] = jnp.zeros(t1_ref.shape, f32)
    t4_ref[...] = jnp.zeros(t4_ref.shape, f32)
    for ky in range(3):
        for kx in range(3):
            t1_ref[ky * 8 + 2 * kx : ky * 8 + 2 * kx + 2, :] = k1_ref[ky, kx].astype(f32)
        t4_ref[ky * 3 : ky * 3 + 3, :] = k4_ref[ky].astype(f32)
    wide1 = sum(dot_0(t1_ref[ky * 8 : ky * 8 + 8, :].astype(bf16), spread1[ky]) for ky in range(3))
    for i in range(OUT_LINES):
        w1_ref[i * CH : (i + 1) * CH, :] = wide1[:, i * LANES : (i + 1) * LANES].astype(bf16)
    for k_ref, w_ref in ((k2_ref, w2_ref), (k3_ref, w3_ref)):
        wide = sum(dot(k_ref[ky * 3 * CH : (ky + 1) * 3 * CH, :], spread[ky]) for ky in range(3))
        for kx in range(3):
            for i in range(OUT_LINES):
                w_ref[i * CH : (i + 1) * CH, kx * cols : (kx + 1) * cols] = wide[
                    kx * CH : (kx + 1) * CH, i * cols : (i + 1) * cols
                ].astype(bf16)
    wide4 = dot(t4_ref[...].astype(bf16), tile4)
    w4_ref[...] = jnp.concatenate(
        [
            band_weights(
                [jnp.broadcast_to(wide4[ky * 3 + kx : ky * 3 + kx + 1], (CH, cols)) for ky in range(3)],
                CH, cols, 1, lambda k: quo(k, CH),
            )
            for kx in range(3)
        ],
        0,
    )

    lines = tile_ref.shape[1]
    tile = tile_ref[...].astype(f32)
    same = iota((lines, lines), 0) == iota((lines, lines), 1)
    tile_sub = jnp.sum(jnp.where(same, jnp.broadcast_to(tile, (lines, lines)), 0.0), 1, keepdims=True)
    rival = (tile_sub == tile) & (iota((lines, lines), 0) < iota((lines, lines), 1))
    slot = tile * capacity + jnp.sum(jnp.where(rival, 1.0, 0.0), 0, keepdims=True)
    slots = slots_ref.shape[0]
    wnd_rows = CH * lines
    per_line = CH
    widen = (quo(iota((lines, wnd_rows), 1), per_line) == iota((lines, wnd_rows), 0)).astype(bf16)
    slot_wide = dot(jnp.broadcast_to(slot, (8, lines)).astype(bf16), widen)[0:1]
    place = slot_wide.astype(jnp.int32) * 4 + rem(quo(iota((1, wnd_rows), 1), 4), 4)
    perm = jnp.where(iota((slots, wnd_rows), 0) == place, 1.0, 0.0).astype(bf16)
    end = END_LINES * CH
    perm_ref[...] = jnp.concatenate([perm[:, 0:end], perm[:, wnd_rows - end :]], 1)

    row_of = dot(
        jnp.where(same, jnp.broadcast_to(row_ref[...].astype(f32), (lines, lines)), 0.0).astype(bf16),
        jnp.ones((lines, LANES), bf16),
    )
    perm_line = jnp.where(quo(iota((slots, lines), 0), 4) == slot.astype(jnp.int32), 1.0, 0.0).astype(bf16)
    row_own = dot(perm_line, row_of.astype(bf16))
    per_tile = 4 * capacity
    lane = iota((slots, LANES), 1)
    entry = rem(iota((slots, LANES), 0), per_tile)
    info = jnp.zeros((slots, LANES), f32)
    for turn, value in enumerate((row_own, of_right(row_own, per_tile), of_left(row_own, per_tile))):
        info = jnp.where(lane == turn * per_tile + entry, value, info)
    info = jnp.sum(info.reshape(devices, per_tile, LANES), 1, keepdims=True)
    at = iota((devices, 8, LANES), 1)
    extra_ref[...] = jnp.where(at == 2, info, 0.0).reshape(8 * devices, LANES)


    px = sar_ref.shape[2]
    for ch in range(2):
        s_ref[ch, 0:lines, :] = sar_ref[ch].astype(f32)
        s_ref[ch, lines:, :] = jnp.zeros((s_ref.shape[1] - lines, px), f32)
    total = xa_ref.shape[1] // CH
    xa_ref[:, (total - 2) * CH :, :] = jnp.zeros((3, 2 * CH, px), bf16)

    def put(ref, line, acc):
        feat = jnp.maximum(acc, 0.0).astype(bf16)
        at = slice(line * CH, line * CH + rows)
        if len(ref.shape) == 2:
            ref[at, :] = feat
            return
        before, after = pixel_shifts(feat)
        ref[0, at, :] = before
        ref[1, at, :] = feat
        ref[2, at, :] = after

    full = (lines + 4) // OUT_LINES + 1
    for b in range(full):
        at = b * OUT_LINES
        x = jnp.concatenate([s_ref[0, at : at + IN_LINES, :], s_ref[1, at : at + IN_LINES, :]], 0)
        put(xa_ref, 1 + at, dot(w1_ref[...], image_columns(x)))
    for w_ref, src, dst, line, blocks in ((w2_ref, xa_ref, xb_ref, 2, full), (w3_ref, xb_ref, x3_ref, 3, full - 1)):
        for b in range(blocks):
            at = line + b * OUT_LINES
            x = src[:, (at - 1) * CH : (at - 1) * CH + cols, :].reshape(3 * cols, px)
            put(dst, at, dot(w_ref[...], x))

    def ends_of(lo, center):
        hi = lines - lo - 2
        return jnp.concatenate([center[at * CH : (at + 2) * CH, :] for at in (lo, hi)], 0)

    e1_ref[...] = ends_of(3, xa_ref.at[1])
    e2_ref[...] = ends_of(4, xb_ref.at[1])
    e3_ref[...] = ends_of(5, x3_ref)
    logit_ref[0:END_LINES, :] = jnp.zeros((END_LINES, px), f32)
    starts = [3 + b * OUT_LINES for b in range(full - 2)] + [lines - 5 - IN_LINES]
    for at in starts:
        sums = dot(w4_ref[...], x3_ref[at * CH : at * CH + cols, :])
        logit_ref[at + 1 : at + 1 + CH, :] = merged(sums, CH)
    frac_ref[...] = sigmoid(logit_ref[0:lines, :])
    quarter = wnd_ref.shape[1]
    group = 16

    def window_group(g, carry):
        at = pl.ds(pl.multiple_of(g * group + END_LINES, END_LINES), group)
        cov = gw_ref[at, :]
        obs = sigmoid(logit_ref[at, :]).astype(f32) * cov
        for i, sums in enumerate(line_windows(cell_ref[at, :], obs, cov, quarter)):
            wnd_ref[pl.ds(pl.multiple_of(g * (CH * group) + CH * i, CH), CH), :] = sums
        return carry

    lax.fori_loop(0, (lines - 2 * END_LINES) // group, window_group, 0)
    slots_ref[...] = dot(perm[:, end : wnd_rows - end], window_goods(wnd_ref[...]))


def of_right(x, per_tile):
    return jnp.concatenate([x[per_tile:], jnp.zeros((per_tile, x.shape[1]), x.dtype)], 0)


def of_left(x, per_tile):
    return jnp.concatenate([jnp.zeros((per_tile, x.shape[1]), x.dtype), x[: x.shape[0] - per_tile]], 0)


def ends_kernel(
    devices, capacity,
    first_swap_ref, second_swap_ref, w1_ref, w2_ref, w3_ref, w4_ref, perm_ref, extra_ref, frac_in, slots_in, e1_ref, e2_ref, e3_ref,
    sar_ref, gw_ref, cell_ref,
    frac_ref, send_ref,
    f_ref,
):
    lines, px = gw_ref.shape
    n_ty = lax.axis_size("ty")
    me = lax.axis_index("tx") * n_ty + lax.axis_index("ty")
    rows = OUT_LINES * CH
    above, below = from_turns(
        rem(me, 2) == 0, first_swap_ref[16:32, :].astype(f32), second_swap_ref[16:32, :].astype(f32)
    )
    n = HALO_LINES

    pieces = []
    for ch in range(2):
        own = sar_ref[ch].astype(f32)
        pieces += [above[ch * n : (ch + 1) * n], own[0:n], own[lines - n :], below[ch * n : (ch + 1) * n]]
    x = image_columns(jnp.concatenate(pieces, 0))
    out_line = quo(iota((rows, px), 0), CH)
    low = jnp.where(me == 0, n, 0)
    high = jnp.where(me == devices - 1, OUT_LINES - n, 2 * OUT_LINES)
    for layer, (w_ref, e_ref) in enumerate(((w1_ref, e1_ref), (w2_ref, e2_ref), (w3_ref, e3_ref)), 1):
        acc = jnp.maximum(dot(w_ref[...], x), 0.0)
        inside = (out_line >= low - layer) & (out_line < high + layer)
        feat = jnp.where(inside, acc, 0.0).astype(bf16)
        block = jnp.concatenate([feat[0 : 6 * CH], e_ref[...], feat[8 * CH :]], 0)
        if layer < 3:
            before, after = pixel_shifts(block)
            x = jnp.concatenate([before, block, after], 0)
    frac = sigmoid(merged(dot(w4_ref[...], block), CH)).astype(f32)
    f_ref[...] = frac_in[...].astype(f32)
    f_ref[0:6, :] = frac[0:6]
    f_ref[lines - 6 :, :] = frac[8:14]
    frac_ref[...] = f_ref[...].astype(bf16)
    quarter = slots_in.shape[1] // 4
    sums = []
    for at in (slice(0, END_LINES), slice(lines - END_LINES, lines)):
        cov = gw_ref[at, :]
        sums += line_windows(cell_ref[at, :], f_ref[at, :] * cov, cov, quarter)
    by_slot = slots_in[...] + dot(perm_ref[...], window_goods(jnp.concatenate(sums, 0)))

    per_tile = 4 * capacity
    slots, tile_cols = by_slot.shape
    h = SUBSTEPS
    entry = rem(iota((slots, LANES), 0), per_tile)
    here = quo(iota((slots, LANES), 1), h) == entry
    column = rem(quo(iota((slots, LANES), 0), per_tile), n_ty)
    source = iota((LANES, LANES), 0)
    spot = rem(iota((LANES, LANES), 1), h)

    def strip(x, first_lane, keep):
        take = ((spot + first_lane == source) & (source - first_lane < h)).astype(bf16)
        x = jnp.where(here & keep, dot(x.astype(bf16), take), 0.0)
        return jnp.sum(x.reshape(devices, per_tile, LANES), 1, keepdims=True)

    right_strip = strip(of_right(by_slot[:, 0:LANES], per_tile), 0, column < n_ty - 1)
    left_strip = strip(of_left(by_slot[:, tile_cols - LANES :], per_tile), LANES - h, column > 0)
    at = iota((devices, 8, LANES), 1)
    extra = extra_ref[...].reshape(devices, 8, LANES)
    extra = jnp.where(at == 0, right_strip, jnp.where(at == 1, left_strip, extra))
    halves = [by_slot[:, at : at + LANES].reshape(devices, per_tile, LANES) for at in range(0, tile_cols, LANES)]
    packed = jnp.concatenate([*halves, extra], 1)
    send_ref[...] = packed.reshape(send_ref.shape).astype(bf16)


def transposed(x):
    return jnp.transpose(x, (1, 0))


def level_kernel(
    devices,
    got_ref, first_swap_ref, second_swap_ref, depth_ref, slope_ref, rain_ref, dir_ref,
    level_ref, side_ref, first_ref, second_ref,
):
    tile_rows, tile_cols = depth_ref.shape
    h = SUBSTEPS
    halves = tile_cols // LANES
    n = (got_ref.shape[0] // devices - 8) // halves
    k = devices * n
    packed = got_ref[...].astype(f32).reshape(devices, halves * n + 8, LANES)
    main = jnp.concatenate([packed[:, i * n : (i + 1) * n].reshape(k, LANES) for i in range(halves)], 1)
    extra = packed[:, halves * n :]

    entry = rem(iota((k, LANES), 0), n)
    spread = quo(iota((k, LANES), 1), h) == entry

    def strip(r, first):
        rows = jnp.broadcast_to(extra[:, r : r + 1], (devices, n, LANES)).reshape(k, LANES)
        take = rem(iota((LANES, LANES), 0), h) + first == iota((LANES, LANES), 1)
        return dot(jnp.where(spread, rows, 0.0).astype(bf16), take.astype(bf16)).astype(bf16)

    lane = iota((1, k), 1)
    offset = rem(lane, 2) + tile_rows * rem(quo(lane, 2), 2)
    info = jnp.broadcast_to(extra[:, 2:3], (devices, n, LANES)).reshape(k, LANES)
    info = jnp.where(rem(iota((k, LANES), 1), n) == entry, info, 0.0).astype(bf16)
    turns = (quo(iota((LANES, LANES), 0), n) == iota((LANES, LANES), 1)).astype(bf16)
    lines = transposed(dot(info, turns))

    def placer(turn):
        target = lines[turn : turn + 1].astype(jnp.int32) + offset
        return jnp.where(iota((2 * tile_rows, k), 0) == target, 1.0, 0.0).astype(bf16)

    summed = dot(placer(0), main.astype(bf16))
    summed_side = dot(placer(1), strip(0, 0)) + dot(placer(2), strip(1, LANES - h))

    ty = lax.axis_index("ty")
    tx = lax.axis_index("tx")
    previous, following = from_turns(
        rem(tx * lax.axis_size("ty") + ty, 2) == 0,
        first_swap_ref[0:16, :].astype(f32), second_swap_ref[0:16, :].astype(f32),
    )
    left = strips_of(previous, ty > 0)
    right = strips_of(following, ty < lax.axis_size("ty") - 1)
    gap = jnp.zeros((LANES - 2 * h, tile_rows), f32)
    depth_side, conv_side, rain_side, code_side = [
        transposed(jnp.concatenate([r, gap, l], 0)) for r, l in zip(right, left)
    ]

    def analysed(sums, depth):
        observed = sums[0:tile_rows]
        covered = sums[tile_rows:]
        wet = depth / (depth + wet_depth)
        innovation = (observed - covered * wet) / (covered + 1.0)
        return depth * jnp.exp(innovation)

    level = analysed(summed, depth_ref[...])
    level_ref[...] = level
    sides = (analysed(summed_side, depth_side), rain_side, conv_side, code_side)
    owns = (level, rain_ref, slope_ref, dir_ref)

    def end_rows(at):
        own = [x[at, :] for x in owns]
        own[2] = runoff_coef * jnp.sqrt(own[2])
        own[3] = own[3].astype(f32)
        return jnp.concatenate([jnp.concatenate([o, x[at]], 1) for o, x in zip(own, sides)], 0)

    for i, x in enumerate(sides):
        side_ref[i] = x
    first, second = in_turn(rem(tx, 2) == 0, end_rows(slice(tile_rows - h, tile_rows)), end_rows(slice(0, h)))
    first_ref[...] = first.astype(bf16)
    second_ref[...] = second.astype(bf16)


def substeps(level, rain, conv, code, rain_s, conv_s, m_ref, part_ref, up_ref, down_ref, chunk):
    rows, cols = level.shape
    h = SUBSTEPS
    for ref in (up_ref, down_ref):
        ref[0] = jnp.zeros(ref.shape[1:], f32)
        ref[1, 0:h, :] = jnp.zeros((h, cols), f32)
        ref[1, h + rows :, :] = jnp.zeros((h, cols), f32)
    part_ref[0] = level
    rain_s[...] = rain
    conv_s[...] = conv
    sides = (-1, 0, 1, -1, 1, -1, 0, 1)
    for direction, side in enumerate(sides):
        share = jnp.where(code == direction, conv, 0.0)
        m_ref[direction] = pltpu.roll(share, side % cols, 1) if side else share

    def level_at(buf, r, n):
        level = part_ref[buf, r : r + n, :]
        return level + up_ref[buf, h + r + 1 : h + r + 1 + n, :] + down_ref[buf, h + r - 1 : h + r - 1 + n, :]

    def substep(buf, new):
        for r in range(0, rows, chunk):
            level = level_at(buf, r, chunk)
            power = level * jnp.exp((2.0 / 3.0) * jnp.log(jnp.maximum(jnp.abs(level), 1e-30)))
            from_right = pltpu.roll(power, cols - 1, 1)
            from_left = pltpu.roll(power, 1, 1)
            m = [m_ref[d, r : r + chunk, :] for d in range(8)]
            up_ref[new, h + r : h + r + chunk, :] = m[0] * from_right + m[1] * power + m[2] * from_left
            down_ref[new, h + r : h + r + chunk, :] = m[5] * from_right + m[6] * power + m[7] * from_left
            part_ref[new, r : r + chunk, :] = (
                level + rain_s[r : r + chunk, :] - conv_s[r : r + chunk, :] * power
                + (m[3] * from_right + m[4] * from_left)
            )

    def substep_pair(i, carry):
        substep(0, 1)
        substep(1, 0)
        return carry

    lax.fori_loop(0, SUBSTEPS // 2, substep_pair, 0)
    return level_at


def flow_inner_kernel(level_ref, side_ref, slope_ref, dir_ref, rain_ref, out_ref, *scratch):
    rows, cols = level_ref.shape
    own = (level_ref[...], rain_ref[...], runoff_coef * jnp.sqrt(slope_ref[...]), dir_ref[...].astype(f32))
    level_at = substeps(*[jnp.concatenate([x, side_ref[i]], 1) for i, x in enumerate(own)], *scratch, 16)
    out_ref[...] = level_at(0, 0, rows)[:, 0:cols]


def flow_ends_kernel(inner_ref, level_ref, side_ref, slope_ref, dir_ref, rain_ref, first_swap_ref, second_swap_ref, out_ref, *scratch):
    rows, cols = level_ref.shape
    h = SUBSTEPS
    above, below = from_turns(
        rem(lax.axis_index("tx"), 2) == 0, first_swap_ref[...].astype(f32), second_swap_ref[...].astype(f32)
    )
    fields = []
    for i, ref in enumerate((level_ref, rain_ref, slope_ref, dir_ref)):
        ends = []
        for at in (slice(0, 2 * h), slice(rows - 2 * h, rows)):
            own = ref[at, :].astype(f32)
            if i == 2:
                own = runoff_coef * jnp.sqrt(own)
            ends.append(jnp.concatenate([own, side_ref[i, at, :]], 1))
        fields.append(jnp.concatenate([above[i * h : (i + 1) * h], *ends, below[i * h : (i + 1) * h]], 0))
    level_at = substeps(*fields, *scratch, 16)
    out_ref[h : rows - h, :] = inner_ref[h : rows - h, :]
    out_ref[0:h, :] = level_at(0, h, h)[:, 0:cols]
    out_ref[rows - h :, :] = level_at(0, 4 * h, h)[:, 0:cols]


def flow_scratch(rows, cols):
    return [
        pltpu.VMEM((rows, cols), f32),
        pltpu.VMEM((rows, cols), f32),
        pltpu.VMEM((8, rows, cols), f32),
        pltpu.VMEM((2, rows, cols), f32),
        pltpu.VMEM((2, rows + 2 * SUBSTEPS, cols), f32),
        pltpu.VMEM((2, rows + 2 * SUBSTEPS, cols), f32),
    ]


def hbm_specs(n):
    return [pl.BlockSpec(memory_space=pltpu.HBM)] * n


def vmem_specs(n):
    return [pl.BlockSpec(memory_space=pltpu.VMEM)] * n


def per_device(
    sar_image, kernel_first, kernel_second, kernel_third, kernel_last,
    geo_weight, cell_index, block_tile, block_row, depth, slope, flow_dir, rain,
):
    both = ("tx", "ty")
    devices = lax.axis_size(both)
    az_lines, range_px = geo_weight.shape
    tile_rows, tile_cols = depth.shape
    capacity = max(2, 2 * az_lines // devices)

    def swaps(axis, first, second):
        out = []
        for start, x in enumerate((first, second)):
            pairs = [(i, i + 1) for i in range(start, lax.axis_size(axis) - 1, 2)]
            out.append(lax.ppermute(x, axis, pairs + [(j, i) for i, j in pairs]))
        return out

    params = pltpu.CompilerParams(vmem_limit_bytes=VMEM_LIMIT)
    message = pltpu.VMEM((32, range_px), bf16)
    small = (
        jnp.transpose(kernel_first, (2, 3, 1, 0)),
        jnp.transpose(kernel_last[0], (1, 2, 0)),
        block_tile.reshape(1, az_lines),
        block_row.reshape(1, az_lines),
    )
    first, second, *small = pl.pallas_call(
        edge_kernel,
        out_shape=(message, message, *[pltpu.VMEM(x.shape, x.dtype) for x in small]),
        in_specs=hbm_specs(9),
        out_specs=tuple(vmem_specs(6)),
        scratch_shapes=[
            pltpu.VMEM((2, 16, range_px), bf16),
            pltpu.VMEM((2, 16, range_px), bf16),
            *[pltpu.VMEM(x.shape, x.dtype) for x in (depth, slope, rain, flow_dir)],
            pltpu.SemaphoreType.DMA((10,)),
        ],
        compiler_params=pltpu.CompilerParams(vmem_limit_bytes=VMEM_MOST),
        name="edges",
    )(sar_image, depth, slope, rain, flow_dir, *small)
    halo = swaps(both, first, second)

    rows, cols = OUT_LINES * CH, IN_LINES * CH
    slots = devices * capacity * 4
    send_rows = tile_cols // LANES * 4 * capacity + 8
    full = (az_lines + 4) // OUT_LINES + 1
    feats = (full * OUT_LINES + 3) * CH
    blocks_in = (az_lines + IN_LINES, range_px)

    def cost(flops):
        return pl.CostEstimate(flops=flops, bytes_accessed=4_000_000, transcendentals=0)

    prepared = pl.pallas_call(
        functools.partial(inner_kernel, devices, capacity),
        out_shape=(
            jax.ShapeDtypeStruct((rows, LANES), bf16),
            jax.ShapeDtypeStruct((rows, 3 * cols), bf16),
            jax.ShapeDtypeStruct((rows, 3 * cols), bf16),
            jax.ShapeDtypeStruct((3 * CH, cols), bf16),
            jax.ShapeDtypeStruct((slots, 2 * END_LINES * CH), bf16),
            jax.ShapeDtypeStruct((8 * devices, LANES), f32),
            jax.ShapeDtypeStruct((az_lines, range_px), bf16),
            jax.ShapeDtypeStruct((slots, tile_cols), f32),
            *[jax.ShapeDtypeStruct((4 * CH, range_px), bf16)] * 3,
        ),
        in_specs=vmem_specs(9),
        out_specs=tuple(vmem_specs(11)),
        scratch_shapes=[
            pltpu.VMEM((24, CH), f32),
            pltpu.VMEM((16, CH), f32),
            pltpu.VMEM((2, *blocks_in), f32),
            pltpu.VMEM((3, feats, range_px), bf16),
            pltpu.VMEM((3, feats, range_px), bf16),
            pltpu.VMEM((feats, range_px), bf16),
            pltpu.VMEM(blocks_in, f32),
            pltpu.VMEM(((az_lines - 2 * END_LINES) * CH, tile_cols // 4), f32),
        ],
        compiler_params=params,
        cost_estimate=cost(8_000_000_000),
        name="inner",
    )(
        small[0],
        jnp.transpose(kernel_second, (2, 3, 0, 1)).reshape(9 * CH, CH),
        jnp.transpose(kernel_third, (2, 3, 0, 1)).reshape(9 * CH, CH),
        *small[1:],
        sar_image, geo_weight, cell_index,
    )
    fraction, send = pl.pallas_call(
        functools.partial(ends_kernel, devices, capacity),
        out_shape=(
            jax.ShapeDtypeStruct((az_lines, range_px), bf16),
            jax.ShapeDtypeStruct((devices * send_rows, LANES), bf16),
        ),
        in_specs=vmem_specs(16),
        out_specs=tuple(vmem_specs(2)),
        scratch_shapes=[pltpu.VMEM((az_lines, range_px), f32)],
        compiler_params=params,
        name="ends",
    )(*halo, *prepared, sar_image, geo_weight, cell_index)

    got = lax.all_to_all(
        send.reshape(devices, send_rows, LANES), both, split_axis=0, concat_axis=0, tiled=True
    ).reshape(devices * send_rows, LANES)

    wide_cols = tile_cols + LANES
    edge = jax.ShapeDtypeStruct((4 * SUBSTEPS, wide_cols), bf16)
    level, side, first, second = pl.pallas_call(
        functools.partial(level_kernel, devices),
        out_shape=(
            jax.ShapeDtypeStruct((tile_rows, tile_cols), f32),
            jax.ShapeDtypeStruct((4, tile_rows, LANES), f32),
            edge,
            edge,
        ),
        in_specs=vmem_specs(7),
        out_specs=tuple(vmem_specs(4)),
        compiler_params=params,
        name="level",
    )(got, *halo, depth, slope, rain, flow_dir)

    row_halo = swaps("tx", first, second)

    inner = pl.pallas_call(
        flow_inner_kernel,
        out_shape=jax.ShapeDtypeStruct((tile_rows, tile_cols), f32),
        in_specs=vmem_specs(5),
        out_specs=vmem_specs(1)[0],
        scratch_shapes=flow_scratch(tile_rows, wide_cols),
        compiler_params=params,
        cost_estimate=cost(5_000_000_000),
        name="flow_inner",
    )(level, side, slope, flow_dir, rain)
    level = pl.pallas_call(
        flow_ends_kernel,
        out_shape=jax.ShapeDtypeStruct((tile_rows, tile_cols), f32),
        in_specs=vmem_specs(8),
        out_specs=vmem_specs(1)[0],
        scratch_shapes=flow_scratch(6 * SUBSTEPS, wide_cols),
        compiler_params=params,
        name="flow_ends",
    )(inner, level, side, slope, flow_dir, rain, *row_halo)
    return (fraction, level)


def solution(mesh):
    placed = (
        P(None, ("tx", "ty"), None),
        P(),
        P(),
        P(),
        P(),
        P(("tx", "ty"), None),
        P(("tx", "ty"), None),
        P(("tx", "ty"), None),
        P(("tx", "ty"), None),
        P("tx", "ty"),
        P("tx", "ty"),
        P("tx", "ty"),
        P("tx", "ty"),
    )
    return jax.shard_map(
        per_device,
        mesh=mesh,
        in_specs=placed,
        out_specs=(P(("tx", "ty"), None), P("tx", "ty")),
        check_vma=False,
    )
```

```python
import functools
import math

import jax
import jax.numpy as jnp
from jax import lax
from jax.experimental import pallas as pl
from jax.experimental.pallas import tpu as pltpu
from jax.sharding import PartitionSpec as P

WIN_ROWS = 2
SUBSTEPS = 8
CH = 16
OUT_LINES = 14
IN_LINES = OUT_LINES + 2
HALO_LINES = 4
END_LINES = 8
LANES = 128
VMEM_LIMIT = 48 * 1024 * 1024
VMEM_MOST = 61880 * 1024

wet_depth = 0.5
runoff_coef = 0.25
bf16 = jnp.bfloat16
f32 = jnp.float32


def iota(shape, dim):
    return lax.broadcasted_iota(jnp.int32, shape, dim)


def quo(x, n):
    assert n & (n - 1) == 0
    return lax.shift_right_logical(x, jnp.int32(n.bit_length() - 1)) if n > 1 else x


def rem(x, n):
    assert n & (n - 1) == 0
    return x & (n - 1)


def dot(a, b):
    return lax.dot_general(a, b, (((1,), (0,)), ((), ())), preferred_element_type=f32)


def dot_0(a, b):
    return lax.dot_general(a, b, (((0,), (0,)), ((), ())), preferred_element_type=f32)


def dot_t(a, b):
    return lax.dot_general(a, b, (((1,), (1,)), ((), ())), preferred_element_type=f32)


def pixel_shifts(x):
    width = x.shape[1]
    pix = iota(x.shape, 1).astype(f32).astype(x.dtype)
    end = (width - 1 - iota(x.shape, 1)).astype(f32).astype(x.dtype)
    zero = jnp.zeros(x.shape, x.dtype)
    before = jnp.where(pix == 0, zero, pltpu.roll(x, 1, 1))
    after = jnp.where(end == 0, zero, pltpu.roll(x, width - 1, 1))
    return before, after


def merged(sums, n):
    before, _ = pixel_shifts(sums[0:n])
    _, after = pixel_shifts(sums[2 * n : 3 * n])
    return before + sums[n : 2 * n] + after


def image_columns(x):
    before, after = pixel_shifts(x)
    pad = jnp.zeros((LANES - 3 * x.shape[0], x.shape[1]), f32)
    return jnp.concatenate([before, x, after, pad], 0).astype(bf16)


def sigmoid(x):
    return (1.0 / (1.0 + jnp.exp(-x))).astype(bf16)


def line_windows(cell, obs, cov, quarter):
    px = cell.shape[1]
    kind = iota((CH, px), 0)
    is_obs = kind < CH // 2
    kind_part = rem(kind, CH // 2).astype(f32).astype(bf16)
    sub = kind.astype(f32).astype(bf16)
    one = jnp.ones((CH, px), bf16)
    nil = jnp.zeros((CH, px), bf16)
    part = quo(cell, quarter).astype(f32)
    col = rem(cell, quarter).astype(f32)

    def spread_row(x, i):
        return jnp.broadcast_to(x[i : i + 1], (CH, px)).astype(bf16)

    out = []
    for i in range(cell.shape[0]):
        value = jnp.where(is_obs, obs[i : i + 1], cov[i : i + 1]).astype(bf16)
        left = jnp.where(kind_part == spread_row(part, i), value, nil)
        where_col = spread_row(col, i)
        hot = jnp.concatenate([jnp.where(sub + g * CH == where_col, one, nil) for g in range(quarter // CH)], 0)
        out.append(dot_t(left, hot))
    return out


def window_goods(sums):
    rows, quarter = sums.shape
    cols = 4 * quarter
    repeat = (rem(iota((quarter, cols), 1), quarter) == iota((quarter, cols), 0)).astype(bf16)
    tiled = dot(sums.astype(bf16), repeat)
    mine = rem(iota((rows, cols), 0), 4) == quo(iota((rows, cols), 1), quarter)
    return jnp.where(mine, tiled, 0.0).astype(bf16)


def band_weights(tiled, rows, cols, per_row, line_of):
    out_line = quo(iota((rows, cols), 0), per_row)
    off = line_of(iota((rows, cols), 1)) - out_line
    out = jnp.zeros((rows, cols), f32)
    for ky in range(3):
        out = jnp.where(off == ky, tiled[ky], out)
    return out.astype(bf16)


def edge_kernel(
    sar_hbm, depth_hbm, slope_hbm, rain_hbm, dir_hbm, k1_hbm, k4_hbm, tile_hbm, row_hbm,
    first_swap_ref, second_swap_ref, k1_ref, k4_ref, tile_ref, row_ref,
    last_ref, first_ref, depth_ref, slope_ref, rain_ref, dir_ref, sems,
):
    even = rem(lax.axis_index("tx") * lax.axis_size("ty") + lax.axis_index("ty"), 2) == 0
    lines, px = sar_hbm.shape[1:]
    cols = depth_hbm.shape[1]
    h = SUBSTEPS
    copies = [
        pltpu.make_async_copy(src, dst, sems.at[i])
        for i, (src, dst) in enumerate(
            (
                (depth_hbm, depth_ref), (slope_hbm, slope_ref), (rain_hbm, rain_ref), (dir_hbm, dir_ref),
                (sar_hbm.at[:, lines - 16 : lines, :], last_ref), (sar_hbm.at[:, 0:16, :], first_ref),
                (k1_hbm, k1_ref), (k4_hbm, k4_ref), (tile_hbm, tile_ref), (row_hbm, row_ref),
            )
        )
    ]
    for copy in copies:
        copy.start()
    for copy in copies:
        copy.wait()
    fields = (
        depth_ref[...],
        runoff_coef * jnp.sqrt(slope_ref[...]),
        rain_ref[...],
        dir_ref[...].astype(f32),
    )
    zeros = jnp.zeros((8, px), f32)
    messages = []
    for image_ref, lo, strip in (
        (last_ref, 16 - HALO_LINES, lambda x: jnp.transpose(x[:, cols - LANES :], (1, 0))[LANES - h :]),
        (first_ref, 0, lambda x: jnp.transpose(x[:, 0:LANES], (1, 0))[0:h]),
    ):
        image = [image_ref[ch].astype(f32)[lo : lo + HALO_LINES] for ch in range(2)]
        strips = [strip(x) for x in fields]
        messages.append(
            jnp.concatenate([jnp.concatenate(strips[0:2], 1), jnp.concatenate(strips[2:4], 1), *image, zeros], 0)
        )
    first, second = in_turn(even, *messages)
    first_swap_ref[...] = first.astype(bf16)
    second_swap_ref[...] = second.astype(bf16)


def in_turn(even, to_next, to_previous):
    return jnp.where(even, to_next, to_previous), jnp.where(even, to_previous, to_next)


def from_turns(even, first, second):
    return jnp.where(even, second, first), jnp.where(even, first, second)


def strips_of(message, keep):
    both = jnp.where(keep, message, 0.0)
    cols = both.shape[1] // 2
    return [both[0:8, 0:cols], both[0:8, cols:], both[8:16, 0:cols], both[8:16, cols:]]


def inner_kernel(
    devices, capacity,
    k1_ref, k2_ref, k3_ref, k4_ref, tile_ref, row_ref, sar_ref, gw_ref, cell_ref,
    w1_ref, w2_ref, w3_ref, w4_ref, perm_ref, extra_ref, frac_ref, slots_ref, e1_ref, e2_ref, e3_ref,
    t1_ref, t4_ref, s_ref, xa_ref, xb_ref, x3_ref, logit_ref, wnd_ref,
):
    rows = OUT_LINES * CH
    cols = IN_LINES * CH

    out_of = quo(iota((CH, OUT_LINES * cols), 1), cols)
    in_of = rem(iota((CH, OUT_LINES * cols), 1), cols) - iota((CH, OUT_LINES * cols), 0)
    spread = [(in_of == CH * (out_of + ky)).astype(bf16) for ky in range(3)]
    n1 = OUT_LINES * LANES
    group1 = quo(rem(iota((8, n1), 1), LANES), IN_LINES) == iota((8, n1), 0)
    line1 = rem(iota((8, n1), 1), IN_LINES) - quo(iota((8, n1), 1), LANES)
    spread1 = [(group1 & (line1 == ky)).astype(bf16) for ky in range(3)]
    tile4 = (rem(iota((CH, cols), 1), CH) == iota((CH, cols), 0)).astype(bf16)
    t1_ref[...] = jnp.zeros(t1_ref.shape, f32)
    t4_ref[...] = jnp.zeros(t4_ref.shape, f32)
    for ky in range(3):
        for kx in range(3):
            t1_ref[ky * 8 + 2 * kx : ky * 8 + 2 * kx + 2, :] = k1_ref[ky, kx].astype(f32)
        t4_ref[ky * 3 : ky * 3 + 3, :] = k4_ref[ky].astype(f32)
    wide1 = sum(dot_0(t1_ref[ky * 8 : ky * 8 + 8, :].astype(bf16), spread1[ky]) for ky in range(3))
    for i in range(OUT_LINES):
        w1_ref[i * CH : (i + 1) * CH, :] = wide1[:, i * LANES : (i + 1) * LANES].astype(bf16)
    for k_ref, w_ref in ((k2_ref, w2_ref), (k3_ref, w3_ref)):
        wide = sum(dot(k_ref[ky * 3 * CH : (ky + 1) * 3 * CH, :], spread[ky]) for ky in range(3))
        for kx in range(3):
            for i in range(OUT_LINES):
                w_ref[i * CH : (i + 1) * CH, kx * cols : (kx + 1) * cols] = wide[
                    kx * CH : (kx + 1) * CH, i * cols : (i + 1) * cols
                ].astype(bf16)
    wide4 = dot(t4_ref[...].astype(bf16), tile4)
    w4_ref[...] = jnp.concatenate(
        [
            band_weights(
                [jnp.broadcast_to(wide4[ky * 3 + kx : ky * 3 + kx + 1], (CH, cols)) for ky in range(3)],
                CH, cols, 1, lambda k: quo(k, CH),
            )
            for kx in range(3)
        ],
        0,
    )

    lines = tile_ref.shape[1]
    tile = tile_ref[...].astype(f32)
    same = iota((lines, lines), 0) == iota((lines, lines), 1)
    tile_sub = jnp.sum(jnp.where(same, jnp.broadcast_to(tile, (lines, lines)), 0.0), 1, keepdims=True)
    rival = (tile_sub == tile) & (iota((lines, lines), 0) < iota((lines, lines), 1))
    slot = tile * capacity + jnp.sum(jnp.where(rival, 1.0, 0.0), 0, keepdims=True)
    slots = slots_ref.shape[0]
    wnd_rows = CH * lines
    per_line = CH
    widen = (quo(iota((lines, wnd_rows), 1), per_line) == iota((lines, wnd_rows), 0)).astype(bf16)
    slot_wide = dot(jnp.broadcast_to(slot, (8, lines)).astype(bf16), widen)[0:1]
    place = slot_wide.astype(jnp.int32) * 4 + rem(quo(iota((1, wnd_rows), 1), 4), 4)
    perm = jnp.where(iota((slots, wnd_rows), 0) == place, 1.0, 0.0).astype(bf16)
    end = END_LINES * CH
    perm_ref[...] = jnp.concatenate([perm[:, 0:end], perm[:, wnd_rows - end :]], 1)

    row_of = dot(
        jnp.where(same, jnp.broadcast_to(row_ref[...].astype(f32), (lines, lines)), 0.0).astype(bf16),
        jnp.ones((lines, LANES), bf16),
    )
    perm_line = jnp.where(quo(iota((slots, lines), 0), 4) == slot.astype(jnp.int32), 1.0, 0.0).astype(bf16)
    row_own = dot(perm_line, row_of.astype(bf16))
    per_tile = 4 * capacity
    lane = iota((slots, LANES), 1)
    entry = rem(iota((slots, LANES), 0), per_tile)
    info = jnp.zeros((slots, LANES), f32)
    for turn, value in enumerate((row_own, of_right(row_own, per_tile), of_left(row_own, per_tile))):
        info = jnp.where(lane == turn * per_tile + entry, value, info)
    info = jnp.sum(info.reshape(devices, per_tile, LANES), 1, keepdims=True)
    at = iota((devices, 8, LANES), 1)
    extra_ref[...] = jnp.where(at == 2, info, 0.0).reshape(8 * devices, LANES)


    px = sar_ref.shape[2]
    for ch in range(2):
        s_ref[ch, 0:lines, :] = sar_ref[ch].astype(f32)
        s_ref[ch, lines:, :] = jnp.zeros((s_ref.shape[1] - lines, px), f32)
    total = xa_ref.shape[1] // CH
    xa_ref[:, (total - 2) * CH :, :] = jnp.zeros((3, 2 * CH, px), bf16)

    def put(ref, line, acc):
        feat = jnp.maximum(acc, 0.0).astype(bf16)
        at = slice(line * CH, line * CH + rows)
        if len(ref.shape) == 2:
            ref[at, :] = feat
            return
        before, after = pixel_shifts(feat)
        ref[0, at, :] = before
        ref[1, at, :] = feat
        ref[2, at, :] = after

    full = (lines + 4) // OUT_LINES + 1
    for b in range(full):
        at = b * OUT_LINES
        x = jnp.concatenate([s_ref[0, at : at + IN_LINES, :], s_ref[1, at : at + IN_LINES, :]], 0)
        put(xa_ref, 1 + at, dot(w1_ref[...], image_columns(x)))
    for w_ref, src, dst, line, blocks in ((w2_ref, xa_ref, xb_ref, 2, full), (w3_ref, xb_ref, x3_ref, 3, full - 1)):
        for b in range(blocks):
            at = line + b * OUT_LINES
            x = src[:, (at - 1) * CH : (at - 1) * CH + cols, :].reshape(3 * cols, px)
            put(dst, at, dot(w_ref[...], x))

    def ends_of(lo, center):
        hi = lines - lo - 2
        return jnp.concatenate([center[at * CH : (at + 2) * CH, :] for at in (lo, hi)], 0)

    e1_ref[...] = ends_of(3, xa_ref.at[1])
    e2_ref[...] = ends_of(4, xb_ref.at[1])
    e3_ref[...] = ends_of(5, x3_ref)
    logit_ref[0:END_LINES, :] = jnp.zeros((END_LINES, px), f32)
    starts = [3 + b * OUT_LINES for b in range(full - 2)] + [lines - 5 - IN_LINES]
    for at in starts:
        sums = dot(w4_ref[...], x3_ref[at * CH : at * CH + cols, :])
        logit_ref[at + 1 : at + 1 + CH, :] = merged(sums, CH)
    frac_ref[...] = sigmoid(logit_ref[0:lines, :])
    quarter = wnd_ref.shape[1]
    group = 16

    def window_group(g, carry):
        at = pl.ds(pl.multiple_of(g * group + END_LINES, END_LINES), group)
        cov = gw_ref[at, :]
        obs = sigmoid(logit_ref[at, :]).astype(f32) * cov
        for i, sums in enumerate(line_windows(cell_ref[at, :], obs, cov, quarter)):
            wnd_ref[pl.ds(pl.multiple_of(g * (CH * group) + CH * i, CH), CH), :] = sums
        return carry

    lax.fori_loop(0, (lines - 2 * END_LINES) // group, window_group, 0)
    slots_ref[...] = dot(perm[:, end : wnd_rows - end], window_goods(wnd_ref[...]))


def of_right(x, per_tile):
    return jnp.concatenate([x[per_tile:], jnp.zeros((per_tile, x.shape[1]), x.dtype)], 0)


def of_left(x, per_tile):
    return jnp.concatenate([jnp.zeros((per_tile, x.shape[1]), x.dtype), x[: x.shape[0] - per_tile]], 0)


def ends_kernel(
    devices, capacity,
    first_swap_ref, second_swap_ref, w1_ref, w2_ref, w3_ref, w4_ref, perm_ref, extra_ref, frac_in, slots_in, e1_ref, e2_ref, e3_ref,
    sar_ref, gw_ref, cell_ref,
    frac_hbm, send_ref,
    f_ref, frac_ref, sem,
):
    lines, px = gw_ref.shape
    n_ty = lax.axis_size("ty")
    me = lax.axis_index("tx") * n_ty + lax.axis_index("ty")
    rows = OUT_LINES * CH
    above, below = from_turns(
        rem(me, 2) == 0, first_swap_ref[16:32, :].astype(f32), second_swap_ref[16:32, :].astype(f32)
    )
    n = HALO_LINES

    pieces = []
    for ch in range(2):
        own = sar_ref[ch].astype(f32)
        pieces += [above[ch * n : (ch + 1) * n], own[0:n], own[lines - n :], below[ch * n : (ch + 1) * n]]
    x = image_columns(jnp.concatenate(pieces, 0))
    out_line = quo(iota((rows, px), 0), CH)
    low = jnp.where(me == 0, n, 0)
    high = jnp.where(me == devices - 1, OUT_LINES - n, 2 * OUT_LINES)
    for layer, (w_ref, e_ref) in enumerate(((w1_ref, e1_ref), (w2_ref, e2_ref), (w3_ref, e3_ref)), 1):
        acc = jnp.maximum(dot(w_ref[...], x), 0.0)
        inside = (out_line >= low - layer) & (out_line < high + layer)
        feat = jnp.where(inside, acc, 0.0).astype(bf16)
        block = jnp.concatenate([feat[0 : 6 * CH], e_ref[...], feat[8 * CH :]], 0)
        if layer < 3:
            before, after = pixel_shifts(block)
            x = jnp.concatenate([before, block, after], 0)
    frac = sigmoid(merged(dot(w4_ref[...], block), CH)).astype(f32)
    f_ref[...] = frac_in[...].astype(f32)
    f_ref[0:6, :] = frac[0:6]
    f_ref[lines - 6 :, :] = frac[8:14]
    frac_ref[...] = f_ref[...].astype(bf16)
    copy = pltpu.make_async_copy(frac_ref, frac_hbm, sem)
    copy.start()
    quarter = slots_in.shape[1] // 4
    sums = []
    for at in (slice(0, END_LINES), slice(lines - END_LINES, lines)):
        cov = gw_ref[at, :]
        sums += line_windows(cell_ref[at, :], f_ref[at, :] * cov, cov, quarter)
    by_slot = slots_in[...] + dot(perm_ref[...], window_goods(jnp.concatenate(sums, 0)))

    per_tile = 4 * capacity
    slots, tile_cols = by_slot.shape
    h = SUBSTEPS
    entry = rem(iota((slots, LANES), 0), per_tile)
    here = quo(iota((slots, LANES), 1), h) == entry
    column = rem(quo(iota((slots, LANES), 0), per_tile), n_ty)
    source = iota((LANES, LANES), 0)
    spot = rem(iota((LANES, LANES), 1), h)

    def strip(x, first_lane, keep):
        take = ((spot + first_lane == source) & (source - first_lane < h)).astype(bf16)
        x = jnp.where(here & keep, dot(x.astype(bf16), take), 0.0)
        return jnp.sum(x.reshape(devices, per_tile, LANES), 1, keepdims=True)

    right_strip = strip(of_right(by_slot[:, 0:LANES], per_tile), 0, column < n_ty - 1)
    left_strip = strip(of_left(by_slot[:, tile_cols - LANES :], per_tile), LANES - h, column > 0)
    at = iota((devices, 8, LANES), 1)
    extra = extra_ref[...].reshape(devices, 8, LANES)
    extra = jnp.where(at == 0, right_strip, jnp.where(at == 1, left_strip, extra))
    halves = [by_slot[:, at : at + LANES].reshape(devices, per_tile, LANES) for at in range(0, tile_cols, LANES)]
    packed = jnp.concatenate([*halves, extra], 1)
    send_ref[...] = packed.reshape(send_ref.shape).astype(bf16)
    copy.wait()


def transposed(x):
    return jnp.transpose(x, (1, 0))


def level_kernel(
    devices,
    got_ref, first_swap_ref, second_swap_ref, depth_ref, slope_ref, rain_ref, dir_ref,
    level_ref, side_ref, first_ref, second_ref,
):
    tile_rows, tile_cols = depth_ref.shape
    h = SUBSTEPS
    halves = tile_cols // LANES
    n = (got_ref.shape[0] // devices - 8) // halves
    k = devices * n
    packed = got_ref[...].astype(f32).reshape(devices, halves * n + 8, LANES)
    main = jnp.concatenate([packed[:, i * n : (i + 1) * n].reshape(k, LANES) for i in range(halves)], 1)
    extra = packed[:, halves * n :]

    entry = rem(iota((k, LANES), 0), n)
    spread = quo(iota((k, LANES), 1), h) == entry

    def strip(r, first):
        rows = jnp.broadcast_to(extra[:, r : r + 1], (devices, n, LANES)).reshape(k, LANES)
        take = rem(iota((LANES, LANES), 0), h) + first == iota((LANES, LANES), 1)
        return dot(jnp.where(spread, rows, 0.0).astype(bf16), take.astype(bf16)).astype(bf16)

    lane = iota((1, k), 1)
    offset = rem(lane, 2) + tile_rows * rem(quo(lane, 2), 2)
    info = jnp.broadcast_to(extra[:, 2:3], (devices, n, LANES)).reshape(k, LANES)
    info = jnp.where(rem(iota((k, LANES), 1), n) == entry, info, 0.0).astype(bf16)
    turns = (quo(iota((LANES, LANES), 0), n) == iota((LANES, LANES), 1)).astype(bf16)
    lines = transposed(dot(info, turns))

    def placer(turn):
        target = lines[turn : turn + 1].astype(jnp.int32) + offset
        return jnp.where(iota((2 * tile_rows, k), 0) == target, 1.0, 0.0).astype(bf16)

    summed = dot(placer(0), main.astype(bf16))
    summed_side = dot(placer(1), strip(0, 0)) + dot(placer(2), strip(1, LANES - h))

    ty = lax.axis_index("ty")
    tx = lax.axis_index("tx")
    previous, following = from_turns(
        rem(tx * lax.axis_size("ty") + ty, 2) == 0,
        first_swap_ref[0:16, :].astype(f32), second_swap_ref[0:16, :].astype(f32),
    )
    left = strips_of(previous, ty > 0)
    right = strips_of(following, ty < lax.axis_size("ty") - 1)
    gap = jnp.zeros((LANES - 2 * h, tile_rows), f32)
    depth_side, conv_side, rain_side, code_side = [
        transposed(jnp.concatenate([r, gap, l], 0)) for r, l in zip(right, left)
    ]

    def analysed(sums, depth):
        observed = sums[0:tile_rows]
        covered = sums[tile_rows:]
        wet = depth / (depth + wet_depth)
        innovation = (observed - covered * wet) / (covered + 1.0)
        return depth * jnp.exp(innovation)

    level = analysed(summed, depth_ref[...])
    level_ref[...] = level
    sides = (analysed(summed_side, depth_side), rain_side, conv_side, code_side)
    owns = (level, rain_ref, slope_ref, dir_ref)

    def end_rows(at):
        own = [x[at, :] for x in owns]
        own[2] = runoff_coef * jnp.sqrt(own[2])
        own[3] = own[3].astype(f32)
        return jnp.concatenate([jnp.concatenate([o, x[at]], 1) for o, x in zip(own, sides)], 0)

    for i, x in enumerate(sides):
        side_ref[i] = x
    first, second = in_turn(rem(tx, 2) == 0, end_rows(slice(tile_rows - h, tile_rows)), end_rows(slice(0, h)))
    first_ref[...] = first.astype(bf16)
    second_ref[...] = second.astype(bf16)


def substeps(field, n, conv_s, rain_s, m_ref, part_ref, up_ref, down_ref):
    cols = conv_s.shape[2]
    sides = (-1, 0, 1, -1, 1, -1, 0, 1)
    up_ref[0] = jnp.zeros(up_ref.shape[1:], f32)
    down_ref[0] = jnp.zeros(down_ref.shape[1:], f32)
    for i in range(n):
        conv = field(2, i)
        code = field(3, i)
        part_ref[0, i] = field(0, i)
        rain_s[i] = field(1, i)
        conv_s[i] = conv
        for direction, side in enumerate(sides):
            share = jnp.where(code == direction, conv, 0.0)
            m_ref[direction, i] = pltpu.roll(share, side % cols, 1) if side else share

    def level_at(buf, i):
        return part_ref[buf, i] + up_ref[buf, i + 1] + down_ref[buf, i]

    def substep(buf, new):
        for i in range(n):
            level = level_at(buf, i)
            power = level * jnp.exp2((2.0 / 3.0 / math.log(2.0)) * jnp.log(jnp.maximum(jnp.abs(level), 1e-30)))
            from_right = pltpu.roll(power, cols - 1, 1)
            from_left = pltpu.roll(power, 1, 1)
            m = [m_ref[d, i] for d in range(8)]
            up = m[0] * from_right + m[1] * power + m[2] * from_left
            down = m[5] * from_right + m[6] * power + m[7] * from_left
            up_ref[new, i] = up
            down_ref[new, i + 1] = down
            if i == 0:
                up_ref[new, n] = pltpu.roll(up, 7, 0)
            if i == n - 1:
                down_ref[new, 0] = pltpu.roll(down, 1, 0)
            part_ref[new, i] = level + rain_s[i] - conv_s[i] * power + (m[3] * from_right + m[4] * from_left)

    def substep_pair(i, carry):
        substep(0, 1)
        substep(1, 0)
        return carry

    lax.fori_loop(0, SUBSTEPS // 2, substep_pair, 0)
    return functools.partial(level_at, 0)


def staged(ref, n):
    def field(f, i):
        return jnp.concatenate([ref[f, t, pl.ds(i, 8, stride=n), :] for t in range(ref.shape[1])], 1)

    return field


def flow_inner_kernel(level_ref, side_ref, slope_ref, dir_ref, rain_ref, out_ref, wide_ref, *scratch):
    rows, cols = level_ref.shape
    n = rows // 8
    tiles = cols // LANES
    for f, ref in enumerate((level_ref, rain_ref, slope_ref, dir_ref)):
        for t in range(tiles):
            own = ref[:, t * LANES : (t + 1) * LANES].astype(f32)
            wide_ref[f, t] = runoff_coef * jnp.sqrt(own) if f == 2 else own
        wide_ref[f, tiles] = side_ref[f]
    level = substeps(staged(wide_ref, n), n, *scratch)
    for i in range(n):
        x = level(i)
        for t in range(tiles):
            out_ref[t, pl.ds(i, 8, stride=n), :] = x[:, t * LANES : (t + 1) * LANES]


def flow_ends_kernel(
    inner_ref, level_ref, side_ref, slope_ref, dir_ref, rain_ref, first_swap_ref, second_swap_ref,
    out_hbm, wide_ref, sems, *scratch,
):
    rows, cols = level_ref.shape
    h = SUBSTEPS
    tiles = cols // LANES

    def copy_out(src, to, sem):
        return pltpu.make_async_copy(src, out_hbm.at[to[0], to[1]], sem)

    copies = []
    for t in range(tiles):
        lanes = slice(t * LANES, (t + 1) * LANES)
        copies.append(copy_out(inner_ref.at[t, h : rows - h, :], (slice(h, rows - h), lanes), sems.at[t]))
        copies[-1].start()
    above, below = from_turns(
        rem(lax.axis_index("tx"), 2) == 0, first_swap_ref[...].astype(f32), second_swap_ref[...].astype(f32)
    )
    for f, ref in enumerate((level_ref, rain_ref, slope_ref, dir_ref)):
        for t in range(tiles + 1):
            lanes = slice(t * LANES, (t + 1) * LANES)
            wide_ref[f, t, 0:h, :] = above[f * h : (f + 1) * h, lanes]
            wide_ref[f, t, 5 * h :, :] = below[f * h : (f + 1) * h, lanes]
            for to, at in ((h, slice(0, 2 * h)), (3 * h, slice(rows - 2 * h, rows))):
                if t < tiles:
                    own = ref[at, lanes].astype(f32)
                    own = runoff_coef * jnp.sqrt(own) if f == 2 else own
                else:
                    own = side_ref[f, at, :]
                wide_ref[f, t, to : to + 2 * h, :] = own
    n = 6 * h // 8
    level = substeps(staged(wide_ref, n), n, *scratch)
    for i in range(n):
        x = level(i)
        for t in range(tiles):
            wide_ref[0, t, pl.ds(i, 8, stride=n), :] = x[:, t * LANES : (t + 1) * LANES]
    for t in range(tiles):
        lanes = slice(t * LANES, (t + 1) * LANES)
        for k, (at, to) in enumerate(((h, 0), (4 * h, rows - h))):
            copies.append(
                copy_out(wide_ref.at[0, t, at : at + h, :], (slice(to, to + h), lanes), sems.at[tiles + 2 * t + k])
            )
            copies[-1].start()
    for copy in copies:
        copy.wait()


def flow_scratch(rows, cols):
    n = rows // 8
    return [
        pltpu.VMEM((n, 8, cols), f32),
        pltpu.VMEM((n, 8, cols), f32),
        pltpu.VMEM((8, n, 8, cols), f32),
        pltpu.VMEM((2, n, 8, cols), f32),
        pltpu.VMEM((2, n + 1, 8, cols), f32),
        pltpu.VMEM((2, n + 1, 8, cols), f32),
    ]


def hbm_specs(n):
    return [pl.BlockSpec(memory_space=pltpu.HBM)] * n


def vmem_specs(n):
    return [pl.BlockSpec(memory_space=pltpu.VMEM)] * n


def per_device(
    sar_image, kernel_first, kernel_second, kernel_third, kernel_last,
    geo_weight, cell_index, block_tile, block_row, depth, slope, flow_dir, rain,
):
    both = ("tx", "ty")
    devices = lax.axis_size(both)
    az_lines, range_px = geo_weight.shape
    tile_rows, tile_cols = depth.shape
    capacity = max(2, 2 * az_lines // devices)

    def swaps(axis, first, second):
        out = []
        for start, x in enumerate((first, second)):
            pairs = [(i, i + 1) for i in range(start, lax.axis_size(axis) - 1, 2)]
            out.append(lax.ppermute(x, axis, pairs + [(j, i) for i, j in pairs]))
        return out

    params = pltpu.CompilerParams(vmem_limit_bytes=VMEM_LIMIT)
    message = pltpu.VMEM((32, range_px), bf16)
    small = (
        jnp.transpose(kernel_first, (2, 3, 1, 0)),
        jnp.transpose(kernel_last[0], (1, 2, 0)),
        block_tile.reshape(1, az_lines),
        block_row.reshape(1, az_lines),
    )
    first, second, *small = pl.pallas_call(
        edge_kernel,
        out_shape=(message, message, *[pltpu.VMEM(x.shape, x.dtype) for x in small]),
        in_specs=hbm_specs(9),
        out_specs=tuple(vmem_specs(6)),
        scratch_shapes=[
            pltpu.VMEM((2, 16, range_px), bf16),
            pltpu.VMEM((2, 16, range_px), bf16),
            *[pltpu.VMEM(x.shape, x.dtype) for x in (depth, slope, rain, flow_dir)],
            pltpu.SemaphoreType.DMA((10,)),
        ],
        compiler_params=pltpu.CompilerParams(vmem_limit_bytes=VMEM_MOST),
        name="edges",
    )(sar_image, depth, slope, rain, flow_dir, *small)
    halo = swaps(both, first, second)

    rows, cols = OUT_LINES * CH, IN_LINES * CH
    slots = devices * capacity * 4
    send_rows = tile_cols // LANES * 4 * capacity + 8
    full = (az_lines + 4) // OUT_LINES + 1
    feats = (full * OUT_LINES + 3) * CH
    blocks_in = (az_lines + IN_LINES, range_px)

    def cost(flops):
        return pl.CostEstimate(flops=flops, bytes_accessed=4_000_000, transcendentals=0)

    prepared = pl.pallas_call(
        functools.partial(inner_kernel, devices, capacity),
        out_shape=(
            jax.ShapeDtypeStruct((rows, LANES), bf16),
            jax.ShapeDtypeStruct((rows, 3 * cols), bf16),
            jax.ShapeDtypeStruct((rows, 3 * cols), bf16),
            jax.ShapeDtypeStruct((3 * CH, cols), bf16),
            jax.ShapeDtypeStruct((slots, 2 * END_LINES * CH), bf16),
            jax.ShapeDtypeStruct((8 * devices, LANES), f32),
            jax.ShapeDtypeStruct((az_lines, range_px), bf16),
            jax.ShapeDtypeStruct((slots, tile_cols), f32),
            *[jax.ShapeDtypeStruct((4 * CH, range_px), bf16)] * 3,
        ),
        in_specs=vmem_specs(9),
        out_specs=tuple(vmem_specs(11)),
        scratch_shapes=[
            pltpu.VMEM((24, CH), f32),
            pltpu.VMEM((16, CH), f32),
            pltpu.VMEM((2, *blocks_in), f32),
            pltpu.VMEM((3, feats, range_px), bf16),
            pltpu.VMEM((3, feats, range_px), bf16),
            pltpu.VMEM((feats, range_px), bf16),
            pltpu.VMEM(blocks_in, f32),
            pltpu.VMEM(((az_lines - 2 * END_LINES) * CH, tile_cols // 4), f32),
        ],
        compiler_params=params,
        cost_estimate=cost(8_000_000_000),
        name="inner",
    )(
        small[0],
        jnp.transpose(kernel_second, (2, 3, 0, 1)).reshape(9 * CH, CH),
        jnp.transpose(kernel_third, (2, 3, 0, 1)).reshape(9 * CH, CH),
        *small[1:],
        sar_image, geo_weight, cell_index,
    )
    fraction, send = pl.pallas_call(
        functools.partial(ends_kernel, devices, capacity),
        out_shape=(
            jax.ShapeDtypeStruct((az_lines, range_px), bf16),
            jax.ShapeDtypeStruct((devices * send_rows, LANES), bf16),
        ),
        in_specs=vmem_specs(16),
        out_specs=(hbm_specs(1)[0], vmem_specs(1)[0]),
        scratch_shapes=[
            pltpu.VMEM((az_lines, range_px), f32),
            pltpu.VMEM((az_lines, range_px), bf16),
            pltpu.SemaphoreType.DMA(()),
        ],
        compiler_params=params,
        name="ends",
    )(*halo, *prepared, sar_image, geo_weight, cell_index)

    got = lax.all_to_all(
        send.reshape(devices, send_rows, LANES), both, split_axis=0, concat_axis=0, tiled=True
    ).reshape(devices * send_rows, LANES)

    wide_cols = tile_cols + LANES
    edge = jax.ShapeDtypeStruct((4 * SUBSTEPS, wide_cols), bf16)
    level, side, first, second = pl.pallas_call(
        functools.partial(level_kernel, devices),
        out_shape=(
            jax.ShapeDtypeStruct((tile_rows, tile_cols), f32),
            jax.ShapeDtypeStruct((4, tile_rows, LANES), f32),
            edge,
            edge,
        ),
        in_specs=vmem_specs(7),
        out_specs=tuple(vmem_specs(4)),
        compiler_params=params,
        name="level",
    )(got, *halo, depth, slope, rain, flow_dir)

    row_halo = swaps("tx", first, second)

    tiles = tile_cols // LANES
    inner = pl.pallas_call(
        flow_inner_kernel,
        out_shape=jax.ShapeDtypeStruct((tiles, tile_rows, LANES), f32),
        in_specs=vmem_specs(5),
        out_specs=vmem_specs(1)[0],
        scratch_shapes=[
            pltpu.VMEM((4, tiles + 1, tile_rows, LANES), f32),
            *flow_scratch(tile_rows, wide_cols),
        ],
        compiler_params=params,
        cost_estimate=cost(5_000_000_000),
        name="flow_inner",
    )(level, side, slope, flow_dir, rain)
    level = pl.pallas_call(
        flow_ends_kernel,
        out_shape=jax.ShapeDtypeStruct((tile_rows, tile_cols), f32),
        in_specs=vmem_specs(8),
        out_specs=hbm_specs(1)[0],
        scratch_shapes=[
            pltpu.VMEM((4, tiles + 1, 6 * SUBSTEPS, LANES), f32),
            pltpu.SemaphoreType.DMA((3 * tiles,)),
            *flow_scratch(6 * SUBSTEPS, wide_cols),
        ],
        compiler_params=params,
        name="flow_ends",
    )(inner, level, side, slope, flow_dir, rain, *row_halo)
    return (fraction, level)


def solution(mesh):
    placed = (
        P(None, ("tx", "ty"), None),
        P(),
        P(),
        P(),
        P(),
        P(("tx", "ty"), None),
        P(("tx", "ty"), None),
        P(("tx", "ty"), None),
        P(("tx", "ty"), None),
        P("tx", "ty"),
        P("tx", "ty"),
        P("tx", "ty"),
        P("tx", "ty"),
    )
    return jax.shard_map(
        per_device,
        mesh=mesh,
        in_specs=placed,
        out_specs=(P(("tx", "ty"), None), P("tx", "ty")),
        check_vma=False,
    )
```

```python
import functools

import jax
import jax.numpy as jnp
from jax import lax
from jax.experimental import pallas as pl
from jax.experimental.pallas import tpu as pltpu
from jax.sharding import PartitionSpec as P

WIN_ROWS = 2
SUBSTEPS = 8
CH = 16
OUT_LINES = 14
IN_LINES = OUT_LINES + 2
HALO_LINES = 4
END_LINES = 8
LANES = 128
VMEM_LIMIT = 48 * 1024 * 1024
VMEM_MOST = 61880 * 1024

wet_depth = 0.5
runoff_coef = 0.25
bf16 = jnp.bfloat16
f32 = jnp.float32


def iota(shape, dim):
    return lax.broadcasted_iota(jnp.int32, shape, dim)


def quo(x, n):
    assert n & (n - 1) == 0
    return lax.shift_right_logical(x, jnp.int32(n.bit_length() - 1)) if n > 1 else x


def rem(x, n):
    assert n & (n - 1) == 0
    return x & (n - 1)


def dot(a, b):
    return lax.dot_general(a, b, (((1,), (0,)), ((), ())), preferred_element_type=f32)


def dot_0(a, b):
    return lax.dot_general(a, b, (((0,), (0,)), ((), ())), preferred_element_type=f32)


def dot_t(a, b):
    return lax.dot_general(a, b, (((1,), (1,)), ((), ())), preferred_element_type=f32)


def pixel_shifts(x):
    width = x.shape[1]
    pix = iota(x.shape, 1).astype(f32).astype(x.dtype)
    end = (width - 1 - iota(x.shape, 1)).astype(f32).astype(x.dtype)
    zero = jnp.zeros(x.shape, x.dtype)
    before = jnp.where(pix == 0, zero, pltpu.roll(x, 1, 1))
    after = jnp.where(end == 0, zero, pltpu.roll(x, width - 1, 1))
    return before, after


def merged(sums, n):
    before, _ = pixel_shifts(sums[0:n])
    _, after = pixel_shifts(sums[2 * n : 3 * n])
    return before + sums[n : 2 * n] + after


def image_columns(x):
    before, after = pixel_shifts(x)
    pad = jnp.zeros((LANES - 3 * x.shape[0], x.shape[1]), f32)
    return jnp.concatenate([before, x, after, pad], 0).astype(bf16)


def sigmoid(x):
    return (1.0 / (1.0 + jnp.exp(-x))).astype(bf16)


def line_windows(cell, obs, cov, quarter):
    px = cell.shape[1]
    kind = iota((CH, px), 0)
    is_obs = kind < CH // 2
    kind_part = rem(kind, CH // 2).astype(f32).astype(bf16)
    sub = kind.astype(f32).astype(bf16)
    one = jnp.ones((CH, px), bf16)
    nil = jnp.zeros((CH, px), bf16)
    part = quo(cell, quarter).astype(f32)
    col = rem(cell, quarter).astype(f32)

    def spread_row(x, i):
        return jnp.broadcast_to(x[i : i + 1], (CH, px)).astype(bf16)

    out = []
    for i in range(cell.shape[0]):
        value = jnp.where(is_obs, obs[i : i + 1], cov[i : i + 1]).astype(bf16)
        left = jnp.where(kind_part == spread_row(part, i), value, nil)
        where_col = spread_row(col, i)
        hot = jnp.concatenate([jnp.where(sub + g * CH == where_col, one, nil) for g in range(quarter // CH)], 0)
        out.append(dot_t(left, hot))
    return out


def window_goods(sums):
    rows, quarter = sums.shape
    cols = 4 * quarter
    repeat = (rem(iota((quarter, cols), 1), quarter) == iota((quarter, cols), 0)).astype(bf16)
    tiled = dot(sums.astype(bf16), repeat)
    mine = rem(iota((rows, cols), 0), 4) == quo(iota((rows, cols), 1), quarter)
    return jnp.where(mine, tiled, 0.0).astype(bf16)


def band_weights(tiled, rows, cols, per_row, line_of):
    out_line = quo(iota((rows, cols), 0), per_row)
    off = line_of(iota((rows, cols), 1)) - out_line
    out = jnp.zeros((rows, cols), f32)
    for ky in range(3):
        out = jnp.where(off == ky, tiled[ky], out)
    return out.astype(bf16)


def edge_kernel(
    sar_hbm, depth_hbm, slope_hbm, rain_hbm, dir_hbm, k1_hbm, k4_hbm, tile_hbm, row_hbm,
    first_swap_ref, second_swap_ref, k1_ref, k4_ref, tile_ref, row_ref,
    last_ref, first_ref, depth_ref, slope_ref, rain_ref, dir_ref, sems,
):
    even = rem(lax.axis_index("tx") * lax.axis_size("ty") + lax.axis_index("ty"), 2) == 0
    lines, px = sar_hbm.shape[1:]
    cols = depth_hbm.shape[1]
    h = SUBSTEPS
    copies = [
        pltpu.make_async_copy(src, dst, sems.at[i])
        for i, (src, dst) in enumerate(
            (
                (depth_hbm, depth_ref), (slope_hbm, slope_ref), (rain_hbm, rain_ref), (dir_hbm, dir_ref),
                (sar_hbm.at[:, lines - 16 : lines, :], last_ref), (sar_hbm.at[:, 0:16, :], first_ref),
                (k1_hbm, k1_ref), (k4_hbm, k4_ref), (tile_hbm, tile_ref), (row_hbm, row_ref),
            )
        )
    ]
    for copy in copies:
        copy.start()
    for copy in copies:
        copy.wait()
    fields = (
        depth_ref[...],
        runoff_coef * jnp.sqrt(slope_ref[...]),
        rain_ref[...],
        dir_ref[...].astype(f32),
    )
    zeros = jnp.zeros((8, px), f32)
    messages = []
    for image_ref, lo, strip in (
        (last_ref, 16 - HALO_LINES, lambda x: jnp.transpose(x[:, cols - LANES :], (1, 0))[LANES - h :]),
        (first_ref, 0, lambda x: jnp.transpose(x[:, 0:LANES], (1, 0))[0:h]),
    ):
        image = [image_ref[ch].astype(f32)[lo : lo + HALO_LINES] for ch in range(2)]
        strips = [strip(x) for x in fields]
        messages.append(
            jnp.concatenate([jnp.concatenate(strips[0:2], 1), jnp.concatenate(strips[2:4], 1), *image, zeros], 0)
        )
    first, second = in_turn(even, *messages)
    first_swap_ref[...] = first.astype(bf16)
    second_swap_ref[...] = second.astype(bf16)


def in_turn(even, to_next, to_previous):
    return jnp.where(even, to_next, to_previous), jnp.where(even, to_previous, to_next)


def from_turns(place, size, first, second):
    even = rem(place, 2) == 0
    previous = jnp.where(even, second, first)
    following = jnp.where(even, first, second)
    return jnp.where(place > 0, previous, 0.0), jnp.where(place < size - 1, following, 0.0)


def strips_of(message, keep):
    both = jnp.where(keep, message, 0.0)
    cols = both.shape[1] // 2
    return [both[0:8, 0:cols], both[0:8, cols:], both[8:16, 0:cols], both[8:16, cols:]]


def inner_kernel(
    devices, capacity,
    k1_ref, k2_ref, k3_ref, k4_ref, tile_ref, row_ref, sar_ref, gw_ref, cell_ref,
    w1_ref, w2_ref, w3_ref, w4_ref, perm_ref, extra_ref, frac_ref, slots_ref, e1_ref, e2_ref, e3_ref,
    t1_ref, t4_ref, s_ref, xa_ref, xb_ref, x3_ref, logit_ref, wnd_ref,
):
    rows = OUT_LINES * CH
    cols = IN_LINES * CH

    out_of = quo(iota((CH, OUT_LINES * cols), 1), cols)
    in_of = rem(iota((CH, OUT_LINES * cols), 1), cols) - iota((CH, OUT_LINES * cols), 0)
    spread = [(in_of == CH * (out_of + ky)).astype(bf16) for ky in range(3)]
    n1 = OUT_LINES * LANES
    group1 = quo(rem(iota((8, n1), 1), LANES), IN_LINES) == iota((8, n1), 0)
    line1 = rem(iota((8, n1), 1), IN_LINES) - quo(iota((8, n1), 1), LANES)
    spread1 = [(group1 & (line1 == ky)).astype(bf16) for ky in range(3)]
    tile4 = (rem(iota((CH, cols), 1), CH) == iota((CH, cols), 0)).astype(bf16)
    t1_ref[...] = jnp.zeros(t1_ref.shape, f32)
    t4_ref[...] = jnp.zeros(t4_ref.shape, f32)
    for ky in range(3):
        for kx in range(3):
            t1_ref[ky * 8 + 2 * kx : ky * 8 + 2 * kx + 2, :] = k1_ref[ky, kx].astype(f32)
        t4_ref[ky * 3 : ky * 3 + 3, :] = k4_ref[ky].astype(f32)
    wide1 = sum(dot_0(t1_ref[ky * 8 : ky * 8 + 8, :].astype(bf16), spread1[ky]) for ky in range(3))
    for i in range(OUT_LINES):
        w1_ref[i * CH : (i + 1) * CH, :] = wide1[:, i * LANES : (i + 1) * LANES].astype(bf16)
    for k_ref, w_ref in ((k2_ref, w2_ref), (k3_ref, w3_ref)):
        wide = sum(dot(k_ref[ky * 3 * CH : (ky + 1) * 3 * CH, :], spread[ky]) for ky in range(3))
        for kx in range(3):
            for i in range(OUT_LINES):
                w_ref[i * CH : (i + 1) * CH, kx * cols : (kx + 1) * cols] = wide[
                    kx * CH : (kx + 1) * CH, i * cols : (i + 1) * cols
                ].astype(bf16)
    wide4 = dot(t4_ref[...].astype(bf16), tile4)
    w4_ref[...] = jnp.concatenate(
        [
            band_weights(
                [jnp.broadcast_to(wide4[ky * 3 + kx : ky * 3 + kx + 1], (CH, cols)) for ky in range(3)],
                CH, cols, 1, lambda k: quo(k, CH),
            )
            for kx in range(3)
        ],
        0,
    )

    lines = tile_ref.shape[1]
    tile = tile_ref[...].astype(f32)
    same = iota((lines, lines), 0) == iota((lines, lines), 1)
    tile_sub = jnp.sum(jnp.where(same, jnp.broadcast_to(tile, (lines, lines)), 0.0), 1, keepdims=True)
    rival = (tile_sub == tile) & (iota((lines, lines), 0) < iota((lines, lines), 1))
    slot = tile * capacity + jnp.sum(jnp.where(rival, 1.0, 0.0), 0, keepdims=True)
    slots = slots_ref.shape[0]
    wnd_rows = CH * lines
    per_line = CH
    widen = (quo(iota((lines, wnd_rows), 1), per_line) == iota((lines, wnd_rows), 0)).astype(bf16)
    slot_wide = dot(jnp.broadcast_to(slot, (8, lines)).astype(bf16), widen)[0:1]
    place = slot_wide.astype(jnp.int32) * 4 + rem(quo(iota((1, wnd_rows), 1), 4), 4)
    perm = jnp.where(iota((slots, wnd_rows), 0) == place, 1.0, 0.0).astype(bf16)
    end = END_LINES * CH
    perm_ref[...] = jnp.concatenate([perm[:, 0:end], perm[:, wnd_rows - end :]], 1)

    row_of = dot(
        jnp.where(same, jnp.broadcast_to(row_ref[...].astype(f32), (lines, lines)), 0.0).astype(bf16),
        jnp.ones((lines, LANES), bf16),
    )
    perm_line = jnp.where(quo(iota((slots, lines), 0), 4) == slot.astype(jnp.int32), 1.0, 0.0).astype(bf16)
    row_own = dot(perm_line, row_of.astype(bf16))
    per_tile = 4 * capacity
    lane = iota((slots, LANES), 1)
    entry = rem(iota((slots, LANES), 0), per_tile)
    info = jnp.zeros((slots, LANES), f32)
    for turn, value in enumerate((row_own, of_right(row_own, per_tile), of_left(row_own, per_tile))):
        info = jnp.where(lane == turn * per_tile + entry, value, info)
    info = jnp.sum(info.reshape(devices, per_tile, LANES), 1, keepdims=True)
    at = iota((devices, 8, LANES), 1)
    extra_ref[...] = jnp.where(at == 2, info, 0.0).reshape(8 * devices, LANES)


    px = sar_ref.shape[2]
    for ch in range(2):
        s_ref[ch, 0:lines, :] = sar_ref[ch].astype(f32)
        s_ref[ch, lines:, :] = jnp.zeros((s_ref.shape[1] - lines, px), f32)
    total = xa_ref.shape[1] // CH
    xa_ref[:, (total - 2) * CH :, :] = jnp.zeros((3, 2 * CH, px), bf16)

    def put(ref, line, acc):
        feat = jnp.maximum(acc, 0.0).astype(bf16)
        at = slice(line * CH, line * CH + rows)
        if len(ref.shape) == 2:
            ref[at, :] = feat
            return
        before, after = pixel_shifts(feat)
        ref[0, at, :] = before
        ref[1, at, :] = feat
        ref[2, at, :] = after

    full = (lines + 4) // OUT_LINES + 1
    for b in range(full):
        at = b * OUT_LINES
        x = jnp.concatenate([s_ref[0, at : at + IN_LINES, :], s_ref[1, at : at + IN_LINES, :]], 0)
        put(xa_ref, 1 + at, dot(w1_ref[...], image_columns(x)))
    for w_ref, src, dst, line, blocks in ((w2_ref, xa_ref, xb_ref, 2, full), (w3_ref, xb_ref, x3_ref, 3, full - 1)):
        for b in range(blocks):
            at = line + b * OUT_LINES
            x = src[:, (at - 1) * CH : (at - 1) * CH + cols, :].reshape(3 * cols, px)
            put(dst, at, dot(w_ref[...], x))

    def ends_of(lo, center):
        hi = lines - lo - 2
        return jnp.concatenate([center[at * CH : (at + 2) * CH, :] for at in (lo, hi)], 0)

    e1_ref[...] = ends_of(3, xa_ref.at[1])
    e2_ref[...] = ends_of(4, xb_ref.at[1])
    e3_ref[...] = ends_of(5, x3_ref)
    logit_ref[0:END_LINES, :] = jnp.zeros((END_LINES, px), f32)
    starts = [3 + b * OUT_LINES for b in range(full - 2)] + [lines - 5 - IN_LINES]
    for at in starts:
        sums = dot(w4_ref[...], x3_ref[at * CH : at * CH + cols, :])
        logit_ref[at + 1 : at + 1 + CH, :] = merged(sums, CH)
    frac_ref[...] = sigmoid(logit_ref[0:lines, :])
    quarter = wnd_ref.shape[1]
    group = 16

    def window_group(g, carry):
        at = pl.ds(pl.multiple_of(g * group + END_LINES, END_LINES), group)
        cov = gw_ref[at, :]
        obs = sigmoid(logit_ref[at, :]).astype(f32) * cov
        for i, sums in enumerate(line_windows(cell_ref[at, :], obs, cov, quarter)):
            wnd_ref[pl.ds(pl.multiple_of(g * (CH * group) + CH * i, CH), CH), :] = sums
        return carry

    lax.fori_loop(0, (lines - 2 * END_LINES) // group, window_group, 0)
    slots_ref[...] = dot(perm[:, end : wnd_rows - end], window_goods(wnd_ref[...]))


def of_right(x, per_tile):
    return jnp.concatenate([x[per_tile:], jnp.zeros((per_tile, x.shape[1]), x.dtype)], 0)


def of_left(x, per_tile):
    return jnp.concatenate([jnp.zeros((per_tile, x.shape[1]), x.dtype), x[: x.shape[0] - per_tile]], 0)


def ends_kernel(
    devices, capacity,
    first_swap_ref, second_swap_ref, w1_ref, w2_ref, w3_ref, w4_ref, perm_ref, extra_ref, frac_in, slots_in, e1_ref, e2_ref, e3_ref,
    sar_ref, gw_ref, cell_ref,
    frac_ref, send_ref,
    f_ref,
):
    lines, px = gw_ref.shape
    n_ty = lax.axis_size("ty")
    me = lax.axis_index("tx") * n_ty + lax.axis_index("ty")
    rows = OUT_LINES * CH
    above, below = from_turns(
        me, devices, first_swap_ref[16:32, :].astype(f32), second_swap_ref[16:32, :].astype(f32)
    )
    n = HALO_LINES

    pieces = []
    for ch in range(2):
        own = sar_ref[ch].astype(f32)
        pieces += [above[ch * n : (ch + 1) * n], own[0:n], own[lines - n :], below[ch * n : (ch + 1) * n]]
    x = image_columns(jnp.concatenate(pieces, 0))
    out_line = quo(iota((rows, px), 0), CH)
    low = jnp.where(me == 0, n, 0)
    high = jnp.where(me == devices - 1, OUT_LINES - n, 2 * OUT_LINES)
    for layer, (w_ref, e_ref) in enumerate(((w1_ref, e1_ref), (w2_ref, e2_ref), (w3_ref, e3_ref)), 1):
        acc = jnp.maximum(dot(w_ref[...], x), 0.0)
        inside = (out_line >= low - layer) & (out_line < high + layer)
        feat = jnp.where(inside, acc, 0.0).astype(bf16)
        block = jnp.concatenate([feat[0 : 6 * CH], e_ref[...], feat[8 * CH :]], 0)
        if layer < 3:
            before, after = pixel_shifts(block)
            x = jnp.concatenate([before, block, after], 0)
    frac = sigmoid(merged(dot(w4_ref[...], block), CH)).astype(f32)
    f_ref[...] = frac_in[...].astype(f32)
    f_ref[0:6, :] = frac[0:6]
    f_ref[lines - 6 :, :] = frac[8:14]
    frac_ref[...] = f_ref[...].astype(bf16)
    quarter = slots_in.shape[1] // 4
    sums = []
    for at in (slice(0, END_LINES), slice(lines - END_LINES, lines)):
        cov = gw_ref[at, :]
        sums += line_windows(cell_ref[at, :], f_ref[at, :] * cov, cov, quarter)
    by_slot = slots_in[...] + dot(perm_ref[...], window_goods(jnp.concatenate(sums, 0)))

    per_tile = 4 * capacity
    slots, tile_cols = by_slot.shape
    h = SUBSTEPS
    entry = rem(iota((slots, LANES), 0), per_tile)
    here = quo(iota((slots, LANES), 1), h) == entry
    column = rem(quo(iota((slots, LANES), 0), per_tile), n_ty)
    source = iota((LANES, LANES), 0)
    spot = rem(iota((LANES, LANES), 1), h)

    def strip(x, first_lane, keep):
        take = ((spot + first_lane == source) & (source - first_lane < h)).astype(bf16)
        x = jnp.where(here & keep, dot(x.astype(bf16), take), 0.0)
        return jnp.sum(x.reshape(devices, per_tile, LANES), 1, keepdims=True)

    right_strip = strip(of_right(by_slot[:, 0:LANES], per_tile), 0, column < n_ty - 1)
    left_strip = strip(of_left(by_slot[:, tile_cols - LANES :], per_tile), LANES - h, column > 0)
    at = iota((devices, 8, LANES), 1)
    extra = extra_ref[...].reshape(devices, 8, LANES)
    extra = jnp.where(at == 0, right_strip, jnp.where(at == 1, left_strip, extra))
    halves = [by_slot[:, at : at + LANES].reshape(devices, per_tile, LANES) for at in range(0, tile_cols, LANES)]
    packed = jnp.concatenate([*halves, extra], 1)
    send_ref[...] = packed.reshape(send_ref.shape).astype(bf16)


def transposed(x):
    return jnp.transpose(x, (1, 0))


def level_kernel(
    devices,
    got_ref, first_swap_ref, second_swap_ref, depth_ref, slope_ref, rain_ref, dir_ref,
    level_ref, side_ref, first_ref, second_ref,
):
    tile_rows, tile_cols = depth_ref.shape
    h = SUBSTEPS
    halves = tile_cols // LANES
    n = (got_ref.shape[0] // devices - 8) // halves
    k = devices * n
    packed = got_ref[...].astype(f32).reshape(devices, halves * n + 8, LANES)
    main = jnp.concatenate([packed[:, i * n : (i + 1) * n].reshape(k, LANES) for i in range(halves)], 1)
    extra = packed[:, halves * n :]

    entry = rem(iota((k, LANES), 0), n)
    spread = quo(iota((k, LANES), 1), h) == entry

    def strip(r, first):
        rows = jnp.broadcast_to(extra[:, r : r + 1], (devices, n, LANES)).reshape(k, LANES)
        take = rem(iota((LANES, LANES), 0), h) + first == iota((LANES, LANES), 1)
        return dot(jnp.where(spread, rows, 0.0).astype(bf16), take.astype(bf16)).astype(bf16)

    lane = iota((1, k), 1)
    offset = rem(lane, 2) + tile_rows * rem(quo(lane, 2), 2)
    info = jnp.broadcast_to(extra[:, 2:3], (devices, n, LANES)).reshape(k, LANES)
    info = jnp.where(rem(iota((k, LANES), 1), n) == entry, info, 0.0).astype(bf16)
    turns = (quo(iota((LANES, LANES), 0), n) == iota((LANES, LANES), 1)).astype(bf16)
    lines = transposed(dot(info, turns))

    def placer(turn):
        target = lines[turn : turn + 1].astype(jnp.int32) + offset
        return jnp.where(iota((2 * tile_rows, k), 0) == target, 1.0, 0.0).astype(bf16)

    summed = dot(placer(0), main.astype(bf16))
    summed_side = dot(placer(1), strip(0, 0)) + dot(placer(2), strip(1, LANES - h))

    ty = lax.axis_index("ty")
    tx = lax.axis_index("tx")
    previous, following = from_turns(
        tx * lax.axis_size("ty") + ty, devices,
        first_swap_ref[0:16, :].astype(f32), second_swap_ref[0:16, :].astype(f32),
    )
    left = strips_of(previous, ty > 0)
    right = strips_of(following, ty < lax.axis_size("ty") - 1)
    gap = jnp.zeros((LANES - 2 * h, tile_rows), f32)
    depth_side, conv_side, rain_side, code_side = [
        transposed(jnp.concatenate([r, gap, l], 0)) for r, l in zip(right, left)
    ]

    def analysed(sums, depth):
        observed = sums[0:tile_rows]
        covered = sums[tile_rows:]
        wet = depth / (depth + wet_depth)
        innovation = (observed - covered * wet) / (covered + 1.0)
        return depth * jnp.exp(innovation)

    level = analysed(summed, depth_ref[...])
    level_ref[...] = level
    sides = (analysed(summed_side, depth_side), rain_side, conv_side, code_side)
    owns = (level, rain_ref, slope_ref, dir_ref)

    def end_rows(at):
        own = [x[at, :] for x in owns]
        own[2] = runoff_coef * jnp.sqrt(own[2])
        own[3] = own[3].astype(f32)
        return jnp.concatenate([jnp.concatenate([o, x[at]], 1) for o, x in zip(own, sides)], 0)

    for i, x in enumerate(sides):
        side_ref[i] = x
    first, second = in_turn(rem(tx, 2) == 0, end_rows(slice(tile_rows - h, tile_rows)), end_rows(slice(0, h)))
    first_ref[...] = first.astype(bf16)
    second_ref[...] = second.astype(bf16)


def substeps(level, rain, conv, code, rain_s, conv_s, m_ref, part_ref, up_ref, down_ref, chunk):
    rows, cols = level.shape
    h = SUBSTEPS
    for ref in (up_ref, down_ref):
        ref[0] = jnp.zeros(ref.shape[1:], f32)
        ref[1, 0:h, :] = jnp.zeros((h, cols), f32)
        ref[1, h + rows :, :] = jnp.zeros((h, cols), f32)
    part_ref[0] = level
    rain_s[...] = rain
    conv_s[...] = conv
    sides = (-1, 0, 1, -1, 1, -1, 0, 1)
    for direction, side in enumerate(sides):
        share = jnp.where(code == direction, conv, 0.0)
        m_ref[direction] = pltpu.roll(share, side % cols, 1) if side else share

    def level_at(buf, r, n):
        level = part_ref[buf, r : r + n, :]
        return level + up_ref[buf, h + r + 1 : h + r + 1 + n, :] + down_ref[buf, h + r - 1 : h + r - 1 + n, :]

    def substep(buf, new):
        for r in range(0, rows, chunk):
            level = level_at(buf, r, chunk)
            power = level * jnp.exp((2.0 / 3.0) * jnp.log(jnp.maximum(jnp.abs(level), 1e-30)))
            from_right = pltpu.roll(power, cols - 1, 1)
            from_left = pltpu.roll(power, 1, 1)
            m = [m_ref[d, r : r + chunk, :] for d in range(8)]
            up_ref[new, h + r : h + r + chunk, :] = m[0] * from_right + m[1] * power + m[2] * from_left
            down_ref[new, h + r : h + r + chunk, :] = m[5] * from_right + m[6] * power + m[7] * from_left
            part_ref[new, r : r + chunk, :] = (
                level + rain_s[r : r + chunk, :] - conv_s[r : r + chunk, :] * power
                + (m[3] * from_right + m[4] * from_left)
            )

    def substep_pair(i, carry):
        substep(0, 1)
        substep(1, 0)
        return carry

    lax.fori_loop(0, SUBSTEPS // 2, substep_pair, 0)
    return level_at


def flow_inner_kernel(level_ref, side_ref, slope_ref, dir_ref, rain_ref, out_ref, *scratch):
    rows, cols = level_ref.shape
    own = (level_ref[...], rain_ref[...], runoff_coef * jnp.sqrt(slope_ref[...]), dir_ref[...].astype(f32))
    level_at = substeps(*[jnp.concatenate([x, side_ref[i]], 1) for i, x in enumerate(own)], *scratch, 16)
    out_ref[...] = level_at(0, 0, rows)[:, 0:cols]


def flow_ends_kernel(inner_ref, level_ref, side_ref, slope_ref, dir_ref, rain_ref, first_swap_ref, second_swap_ref, out_ref, *scratch):
    rows, cols = level_ref.shape
    h = SUBSTEPS
    above, below = from_turns(
        lax.axis_index("tx"), lax.axis_size("tx"),
        first_swap_ref[...].astype(f32), second_swap_ref[...].astype(f32),
    )
    fields = []
    for i, ref in enumerate((level_ref, rain_ref, slope_ref, dir_ref)):
        ends = []
        for at in (slice(0, 2 * h), slice(rows - 2 * h, rows)):
            own = ref[at, :].astype(f32)
            if i == 2:
                own = runoff_coef * jnp.sqrt(own)
            ends.append(jnp.concatenate([own, side_ref[i, at, :]], 1))
        fields.append(jnp.concatenate([above[i * h : (i + 1) * h], *ends, below[i * h : (i + 1) * h]], 0))
    level_at = substeps(*fields, *scratch, 16)
    out_ref[h : rows - h, :] = inner_ref[h : rows - h, :]
    out_ref[0:h, :] = level_at(0, h, h)[:, 0:cols]
    out_ref[rows - h :, :] = level_at(0, 4 * h, h)[:, 0:cols]


def flow_scratch(rows, cols):
    return [
        pltpu.VMEM((rows, cols), f32),
        pltpu.VMEM((rows, cols), f32),
        pltpu.VMEM((8, rows, cols), f32),
        pltpu.VMEM((2, rows, cols), f32),
        pltpu.VMEM((2, rows + 2 * SUBSTEPS, cols), f32),
        pltpu.VMEM((2, rows + 2 * SUBSTEPS, cols), f32),
    ]


def hbm_specs(n):
    return [pl.BlockSpec(memory_space=pltpu.HBM)] * n


def vmem_specs(n):
    return [pl.BlockSpec(memory_space=pltpu.VMEM)] * n


def per_device(
    sar_image, kernel_first, kernel_second, kernel_third, kernel_last,
    geo_weight, cell_index, block_tile, block_row, depth, slope, flow_dir, rain,
):
    both = ("tx", "ty")
    devices = lax.axis_size(both)
    az_lines, range_px = geo_weight.shape
    tile_rows, tile_cols = depth.shape
    capacity = max(2, 2 * az_lines // devices)

    def swaps(axis, first, second):
        size = lax.axis_size(axis)
        out = []
        for start, x in enumerate((first, second)):
            pairs = [(i, (i + 1) % size) for i in range(start, size, 2)]
            out.append(lax.ppermute(x, axis, pairs + [(j, i) for i, j in pairs]))
        return out

    params = pltpu.CompilerParams(vmem_limit_bytes=VMEM_LIMIT)
    message = pltpu.VMEM((32, range_px), bf16)
    small = (
        jnp.transpose(kernel_first, (2, 3, 1, 0)),
        jnp.transpose(kernel_last[0], (1, 2, 0)),
        block_tile.reshape(1, az_lines),
        block_row.reshape(1, az_lines),
    )
    first, second, *small = pl.pallas_call(
        edge_kernel,
        out_shape=(message, message, *[pltpu.VMEM(x.shape, x.dtype) for x in small]),
        in_specs=hbm_specs(9),
        out_specs=tuple(vmem_specs(6)),
        scratch_shapes=[
            pltpu.VMEM((2, 16, range_px), bf16),
            pltpu.VMEM((2, 16, range_px), bf16),
            *[pltpu.VMEM(x.shape, x.dtype) for x in (depth, slope, rain, flow_dir)],
            pltpu.SemaphoreType.DMA((10,)),
        ],
        compiler_params=pltpu.CompilerParams(vmem_limit_bytes=VMEM_MOST),
        name="edges",
    )(sar_image, depth, slope, rain, flow_dir, *small)
    halo = swaps(both, first, second)

    rows, cols = OUT_LINES * CH, IN_LINES * CH
    slots = devices * capacity * 4
    send_rows = tile_cols // LANES * 4 * capacity + 8
    full = (az_lines + 4) // OUT_LINES + 1
    feats = (full * OUT_LINES + 3) * CH
    blocks_in = (az_lines + IN_LINES, range_px)

    def cost(flops):
        return pl.CostEstimate(flops=flops, bytes_accessed=4_000_000, transcendentals=0)

    prepared = pl.pallas_call(
        functools.partial(inner_kernel, devices, capacity),
        out_shape=(
            jax.ShapeDtypeStruct((rows, LANES), bf16),
            jax.ShapeDtypeStruct((rows, 3 * cols), bf16),
            jax.ShapeDtypeStruct((rows, 3 * cols), bf16),
            jax.ShapeDtypeStruct((3 * CH, cols), bf16),
            jax.ShapeDtypeStruct((slots, 2 * END_LINES * CH), bf16),
            jax.ShapeDtypeStruct((8 * devices, LANES), f32),
            jax.ShapeDtypeStruct((az_lines, range_px), bf16),
            jax.ShapeDtypeStruct((slots, tile_cols), f32),
            *[jax.ShapeDtypeStruct((4 * CH, range_px), bf16)] * 3,
        ),
        in_specs=vmem_specs(9),
        out_specs=tuple(vmem_specs(11)),
        scratch_shapes=[
            pltpu.VMEM((24, CH), f32),
            pltpu.VMEM((16, CH), f32),
            pltpu.VMEM((2, *blocks_in), f32),
            pltpu.VMEM((3, feats, range_px), bf16),
            pltpu.VMEM((3, feats, range_px), bf16),
            pltpu.VMEM((feats, range_px), bf16),
            pltpu.VMEM(blocks_in, f32),
            pltpu.VMEM(((az_lines - 2 * END_LINES) * CH, tile_cols // 4), f32),
        ],
        compiler_params=params,
        cost_estimate=cost(8_000_000_000),
        name="inner",
    )(
        small[0],
        jnp.transpose(kernel_second, (2, 3, 0, 1)).reshape(9 * CH, CH),
        jnp.transpose(kernel_third, (2, 3, 0, 1)).reshape(9 * CH, CH),
        *small[1:],
        sar_image, geo_weight, cell_index,
    )
    fraction, send = pl.pallas_call(
        functools.partial(ends_kernel, devices, capacity),
        out_shape=(
            jax.ShapeDtypeStruct((az_lines, range_px), bf16),
            jax.ShapeDtypeStruct((devices * send_rows, LANES), bf16),
        ),
        in_specs=vmem_specs(16),
        out_specs=tuple(vmem_specs(2)),
        scratch_shapes=[pltpu.VMEM((az_lines, range_px), f32)],
        compiler_params=params,
        name="ends",
    )(*halo, *prepared, sar_image, geo_weight, cell_index)

    got = lax.all_to_all(
        send.reshape(devices, send_rows, LANES), both, split_axis=0, concat_axis=0, tiled=True
    ).reshape(devices * send_rows, LANES)

    wide_cols = tile_cols + LANES
    edge = jax.ShapeDtypeStruct((4 * SUBSTEPS, wide_cols), bf16)
    level, side, first, second = pl.pallas_call(
        functools.partial(level_kernel, devices),
        out_shape=(
            jax.ShapeDtypeStruct((tile_rows, tile_cols), f32),
            jax.ShapeDtypeStruct((4, tile_rows, LANES), f32),
            edge,
            edge,
        ),
        in_specs=vmem_specs(7),
        out_specs=tuple(vmem_specs(4)),
        compiler_params=params,
        name="level",
    )(got, *halo, depth, slope, rain, flow_dir)

    row_halo = swaps("tx", first, second)

    inner = pl.pallas_call(
        flow_inner_kernel,
        out_shape=jax.ShapeDtypeStruct((tile_rows, tile_cols), f32),
        in_specs=vmem_specs(5),
        out_specs=vmem_specs(1)[0],
        scratch_shapes=flow_scratch(tile_rows, wide_cols),
        compiler_params=params,
        cost_estimate=cost(5_000_000_000),
        name="flow_inner",
    )(level, side, slope, flow_dir, rain)
    level = pl.pallas_call(
        flow_ends_kernel,
        out_shape=jax.ShapeDtypeStruct((tile_rows, tile_cols), f32),
        in_specs=vmem_specs(8),
        out_specs=vmem_specs(1)[0],
        scratch_shapes=flow_scratch(6 * SUBSTEPS, wide_cols),
        compiler_params=params,
        name="flow_ends",
    )(inner, level, side, slope, flow_dir, rain, *row_halo)
    return (fraction, level)


def solution(mesh):
    placed = (
        P(None, ("tx", "ty"), None),
        P(),
        P(),
        P(),
        P(),
        P(("tx", "ty"), None),
        P(("tx", "ty"), None),
        P(("tx", "ty"), None),
        P(("tx", "ty"), None),
        P("tx", "ty"),
        P("tx", "ty"),
        P("tx", "ty"),
        P("tx", "ty"),
    )
    return jax.shard_map(
        per_device,
        mesh=mesh,
        in_specs=placed,
        out_specs=(P(("tx", "ty"), None), P("tx", "ty")),
        check_vma=False,
    )
```

```python
import functools

import jax
import jax.numpy as jnp
from jax import lax
from jax.experimental import pallas as pl
from jax.experimental.pallas import tpu as pltpu
from jax.sharding import PartitionSpec as P

WIN_ROWS = 2
SUBSTEPS = 8
CH = 16
OUT_LINES = 14
IN_LINES = OUT_LINES + 2
HALO_LINES = 4
END_LINES = 8
LANES = 128
VMEM_LIMIT = 48 * 1024 * 1024
VMEM_MOST = 61880 * 1024

wet_depth = 0.5
runoff_coef = 0.25
bf16 = jnp.bfloat16
f32 = jnp.float32


def iota(shape, dim):
    return lax.broadcasted_iota(jnp.int32, shape, dim)


def quo(x, n):
    assert n & (n - 1) == 0
    return lax.shift_right_logical(x, jnp.int32(n.bit_length() - 1)) if n > 1 else x


def rem(x, n):
    assert n & (n - 1) == 0
    return x & (n - 1)


def dot(a, b):
    return lax.dot_general(a, b, (((1,), (0,)), ((), ())), preferred_element_type=f32)


def dot_0(a, b):
    return lax.dot_general(a, b, (((0,), (0,)), ((), ())), preferred_element_type=f32)


def dot_t(a, b):
    return lax.dot_general(a, b, (((1,), (1,)), ((), ())), preferred_element_type=f32)


def pixel_shifts(x):
    width = x.shape[1]
    pix = iota(x.shape, 1).astype(f32).astype(x.dtype)
    end = (width - 1 - iota(x.shape, 1)).astype(f32).astype(x.dtype)
    zero = jnp.zeros(x.shape, x.dtype)
    before = jnp.where(pix == 0, zero, pltpu.roll(x, 1, 1))
    after = jnp.where(end == 0, zero, pltpu.roll(x, width - 1, 1))
    return before, after


def merged(sums, n):
    before, _ = pixel_shifts(sums[0:n])
    _, after = pixel_shifts(sums[2 * n : 3 * n])
    return before + sums[n : 2 * n] + after


def image_columns(x):
    before, after = pixel_shifts(x)
    pad = jnp.zeros((LANES - 3 * x.shape[0], x.shape[1]), f32)
    return jnp.concatenate([before, x, after, pad], 0).astype(bf16)


def sigmoid(x):
    return (1.0 / (1.0 + jnp.exp(-x))).astype(bf16)


def line_windows(cell, obs, cov, quarter):
    px = cell.shape[1]
    kind = iota((CH, px), 0)
    is_obs = kind < CH // 2
    kind_part = rem(kind, CH // 2).astype(f32).astype(bf16)
    sub = kind.astype(f32).astype(bf16)
    one = jnp.ones((CH, px), bf16)
    nil = jnp.zeros((CH, px), bf16)
    part = quo(cell, quarter).astype(f32)
    col = rem(cell, quarter).astype(f32)

    def spread_row(x, i):
        return jnp.broadcast_to(x[i : i + 1], (CH, px)).astype(bf16)

    out = []
    for i in range(cell.shape[0]):
        value = jnp.where(is_obs, obs[i : i + 1], cov[i : i + 1]).astype(bf16)
        left = jnp.where(kind_part == spread_row(part, i), value, nil)
        where_col = spread_row(col, i)
        hot = jnp.concatenate([jnp.where(sub + g * CH == where_col, one, nil) for g in range(quarter // CH)], 0)
        out.append(dot_t(left, hot))
    return out


def window_goods(sums):
    rows, quarter = sums.shape
    cols = 4 * quarter
    repeat = (rem(iota((quarter, cols), 1), quarter) == iota((quarter, cols), 0)).astype(bf16)
    tiled = dot(sums.astype(bf16), repeat)
    mine = rem(iota((rows, cols), 0), 4) == quo(iota((rows, cols), 1), quarter)
    return jnp.where(mine, tiled, 0.0).astype(bf16)


def band_weights(tiled, rows, cols, per_row, line_of):
    out_line = quo(iota((rows, cols), 0), per_row)
    off = line_of(iota((rows, cols), 1)) - out_line
    out = jnp.zeros((rows, cols), f32)
    for ky in range(3):
        out = jnp.where(off == ky, tiled[ky], out)
    return out.astype(bf16)


def edge_kernel(
    sar_hbm, depth_hbm, slope_hbm, rain_hbm, dir_hbm, k1_hbm, k4_hbm, tile_hbm, row_hbm,
    first_swap_ref, second_swap_ref, k1_ref, k4_ref, tile_ref, row_ref,
    last_ref, first_ref, depth_ref, slope_ref, rain_ref, dir_ref, sems,
):
    even = rem(lax.axis_index("tx") * lax.axis_size("ty") + lax.axis_index("ty"), 2) == 0
    lines, px = sar_hbm.shape[1:]
    cols = depth_hbm.shape[1]
    h = SUBSTEPS
    copies = [
        pltpu.make_async_copy(src, dst, sems.at[i])
        for i, (src, dst) in enumerate(
            (
                (depth_hbm, depth_ref), (slope_hbm, slope_ref), (rain_hbm, rain_ref), (dir_hbm, dir_ref),
                (sar_hbm.at[:, lines - 16 : lines, :], last_ref), (sar_hbm.at[:, 0:16, :], first_ref),
                (k1_hbm, k1_ref), (k4_hbm, k4_ref), (tile_hbm, tile_ref), (row_hbm, row_ref),
            )
        )
    ]
    for copy in copies:
        copy.start()
    for copy in copies:
        copy.wait()
    fields = (
        depth_ref[...],
        runoff_coef * jnp.sqrt(slope_ref[...]),
        rain_ref[...],
        dir_ref[...].astype(f32),
    )
    zeros = jnp.zeros((8, px), f32)
    messages = []
    for image_ref, lo, strip in (
        (last_ref, 16 - HALO_LINES, lambda x: jnp.transpose(x[:, cols - LANES :], (1, 0))[LANES - h :]),
        (first_ref, 0, lambda x: jnp.transpose(x[:, 0:LANES], (1, 0))[0:h]),
    ):
        image = [image_ref[ch].astype(f32)[lo : lo + HALO_LINES] for ch in range(2)]
        strips = [strip(x) for x in fields]
        messages.append(
            jnp.concatenate([jnp.concatenate(strips[0:2], 1), jnp.concatenate(strips[2:4], 1), *image, zeros], 0)
        )
    first, second = in_turn(even, *messages)
    first_swap_ref[...] = first.astype(bf16)
    second_swap_ref[...] = second.astype(bf16)


def in_turn(even, to_next, to_previous):
    return jnp.where(even, to_next, to_previous), jnp.where(even, to_previous, to_next)


def from_turns(place, size, first, second):
    even = rem(place, 2) == 0
    previous = jnp.where(even, second, first)
    following = jnp.where(even, first, second)
    return jnp.where(place > 0, previous, 0.0), jnp.where(place < size - 1, following, 0.0)


def strips_of(message, keep):
    both = jnp.where(keep, message, 0.0)
    cols = both.shape[1] // 2
    return [both[0:8, 0:cols], both[0:8, cols:], both[8:16, 0:cols], both[8:16, cols:]]


def inner_kernel(
    devices, capacity,
    k1_ref, k2_ref, k3_ref, k4_ref, tile_ref, row_ref, sar_ref, gw_ref, cell_ref,
    w1_ref, w2_ref, w3_ref, w4_ref, perm_ref, extra_ref, frac_ref, slots_ref, e1_ref, e2_ref, e3_ref,
    t1_ref, t4_ref, s_ref, xa_ref, xb_ref, x3_ref, logit_ref, wnd_ref,
):
    rows = OUT_LINES * CH
    cols = IN_LINES * CH

    out_of = quo(iota((CH, OUT_LINES * cols), 1), cols)
    in_of = rem(iota((CH, OUT_LINES * cols), 1), cols) - iota((CH, OUT_LINES * cols), 0)
    spread = [(in_of == CH * (out_of + ky)).astype(bf16) for ky in range(3)]
    n1 = OUT_LINES * LANES
    group1 = quo(rem(iota((8, n1), 1), LANES), IN_LINES) == iota((8, n1), 0)
    line1 = rem(iota((8, n1), 1), IN_LINES) - quo(iota((8, n1), 1), LANES)
    spread1 = [(group1 & (line1 == ky)).astype(bf16) for ky in range(3)]
    tile4 = (rem(iota((CH, cols), 1), CH) == iota((CH, cols), 0)).astype(bf16)
    t1_ref[...] = jnp.zeros(t1_ref.shape, f32)
    t4_ref[...] = jnp.zeros(t4_ref.shape, f32)
    for ky in range(3):
        for kx in range(3):
            t1_ref[ky * 8 + 2 * kx : ky * 8 + 2 * kx + 2, :] = k1_ref[ky, kx].astype(f32)
        t4_ref[ky * 3 : ky * 3 + 3, :] = k4_ref[ky].astype(f32)
    wide1 = sum(dot_0(t1_ref[ky * 8 : ky * 8 + 8, :].astype(bf16), spread1[ky]) for ky in range(3))
    for i in range(OUT_LINES):
        w1_ref[i * CH : (i + 1) * CH, :] = wide1[:, i * LANES : (i + 1) * LANES].astype(bf16)
    for k_ref, w_ref in ((k2_ref, w2_ref), (k3_ref, w3_ref)):
        wide = sum(dot(k_ref[ky * 3 * CH : (ky + 1) * 3 * CH, :], spread[ky]) for ky in range(3))
        for kx in range(3):
            for i in range(OUT_LINES):
                w_ref[i * CH : (i + 1) * CH, kx * cols : (kx + 1) * cols] = wide[
                    kx * CH : (kx + 1) * CH, i * cols : (i + 1) * cols
                ].astype(bf16)
    wide4 = dot(t4_ref[...].astype(bf16), tile4)
    w4_ref[...] = jnp.concatenate(
        [
            band_weights(
                [jnp.broadcast_to(wide4[ky * 3 + kx : ky * 3 + kx + 1], (CH, cols)) for ky in range(3)],
                CH, cols, 1, lambda k: quo(k, CH),
            )
            for kx in range(3)
        ],
        0,
    )

    lines = tile_ref.shape[1]
    tile = tile_ref[...].astype(f32)
    same = iota((lines, lines), 0) == iota((lines, lines), 1)
    tile_sub = jnp.sum(jnp.where(same, jnp.broadcast_to(tile, (lines, lines)), 0.0), 1, keepdims=True)
    rival = (tile_sub == tile) & (iota((lines, lines), 0) < iota((lines, lines), 1))
    slot = tile * capacity + jnp.sum(jnp.where(rival, 1.0, 0.0), 0, keepdims=True)
    slots = slots_ref.shape[0]
    wnd_rows = CH * lines
    per_line = CH
    widen = (quo(iota((lines, wnd_rows), 1), per_line) == iota((lines, wnd_rows), 0)).astype(bf16)
    slot_wide = dot(jnp.broadcast_to(slot, (8, lines)).astype(bf16), widen)[0:1]
    place = slot_wide.astype(jnp.int32) * 4 + rem(quo(iota((1, wnd_rows), 1), 4), 4)
    perm = jnp.where(iota((slots, wnd_rows), 0) == place, 1.0, 0.0).astype(bf16)
    end = END_LINES * CH
    perm_ref[...] = jnp.concatenate([perm[:, 0:end], perm[:, wnd_rows - end :]], 1)

    row_of = dot(
        jnp.where(same, jnp.broadcast_to(row_ref[...].astype(f32), (lines, lines)), 0.0).astype(bf16),
        jnp.ones((lines, LANES), bf16),
    )
    perm_line = jnp.where(quo(iota((slots, lines), 0), 4) == slot.astype(jnp.int32), 1.0, 0.0).astype(bf16)
    row_own = dot(perm_line, row_of.astype(bf16))
    per_tile = 4 * capacity
    lane = iota((slots, LANES), 1)
    entry = rem(iota((slots, LANES), 0), per_tile)
    info = jnp.zeros((slots, LANES), f32)
    for turn, value in enumerate((row_own, of_right(row_own, per_tile), of_left(row_own, per_tile))):
        info = jnp.where(lane == turn * per_tile + entry, value, info)
    info = jnp.sum(info.reshape(devices, per_tile, LANES), 1, keepdims=True)
    at = iota((devices, 8, LANES), 1)
    extra_ref[...] = jnp.where(at == 2, info, 0.0).reshape(8 * devices, LANES)


    px = sar_ref.shape[2]
    for ch in range(2):
        s_ref[ch, 0:lines, :] = sar_ref[ch].astype(f32)
        s_ref[ch, lines:, :] = jnp.zeros((s_ref.shape[1] - lines, px), f32)
    total = xa_ref.shape[1] // CH
    xa_ref[:, (total - 2) * CH :, :] = jnp.zeros((3, 2 * CH, px), bf16)

    def put(ref, line, acc):
        feat = jnp.maximum(acc, 0.0).astype(bf16)
        at = slice(line * CH, line * CH + rows)
        if len(ref.shape) == 2:
            ref[at, :] = feat
            return
        before, after = pixel_shifts(feat)
        ref[0, at, :] = before
        ref[1, at, :] = feat
        ref[2, at, :] = after

    full = (lines + 4) // OUT_LINES + 1
    for b in range(full):
        at = b * OUT_LINES
        x = jnp.concatenate([s_ref[0, at : at + IN_LINES, :], s_ref[1, at : at + IN_LINES, :]], 0)
        put(xa_ref, 1 + at, dot(w1_ref[...], image_columns(x)))
    for w_ref, src, dst, line, blocks in ((w2_ref, xa_ref, xb_ref, 2, full), (w3_ref, xb_ref, x3_ref, 3, full - 1)):
        for b in range(blocks):
            at = line + b * OUT_LINES
            x = src[:, (at - 1) * CH : (at - 1) * CH + cols, :].reshape(3 * cols, px)
            put(dst, at, dot(w_ref[...], x))

    def ends_of(lo, center):
        hi = lines - lo - 2
        return jnp.concatenate([center[at * CH : (at + 2) * CH, :] for at in (lo, hi)], 0)

    e1_ref[...] = ends_of(3, xa_ref.at[1])
    e2_ref[...] = ends_of(4, xb_ref.at[1])
    e3_ref[...] = ends_of(5, x3_ref)
    logit_ref[0:END_LINES, :] = jnp.zeros((END_LINES, px), f32)
    starts = [3 + b * OUT_LINES for b in range(full - 2)] + [lines - 5 - IN_LINES]
    for at in starts:
        sums = dot(w4_ref[...], x3_ref[at * CH : at * CH + cols, :])
        logit_ref[at + 1 : at + 1 + CH, :] = merged(sums, CH)
    frac_ref[...] = sigmoid(logit_ref[0:lines, :])
    quarter = wnd_ref.shape[1]
    group = 16

    def window_group(g, carry):
        at = pl.ds(pl.multiple_of(g * group + END_LINES, END_LINES), group)
        cov = gw_ref[at, :]
        obs = sigmoid(logit_ref[at, :]).astype(f32) * cov
        for i, sums in enumerate(line_windows(cell_ref[at, :], obs, cov, quarter)):
            wnd_ref[pl.ds(pl.multiple_of(g * (CH * group) + CH * i, CH), CH), :] = sums
        return carry

    lax.fori_loop(0, (lines - 2 * END_LINES) // group, window_group, 0)
    slots_ref[...] = dot(perm[:, end : wnd_rows - end], window_goods(wnd_ref[...]))


def of_right(x, per_tile):
    return jnp.concatenate([x[per_tile:], jnp.zeros((per_tile, x.shape[1]), x.dtype)], 0)


def of_left(x, per_tile):
    return jnp.concatenate([jnp.zeros((per_tile, x.shape[1]), x.dtype), x[: x.shape[0] - per_tile]], 0)


def ends_kernel(
    devices, capacity,
    first_swap_ref, second_swap_ref, w1_ref, w2_ref, w3_ref, w4_ref, perm_ref, extra_ref, frac_in, slots_in, e1_ref, e2_ref, e3_ref,
    sar_ref, gw_ref, cell_ref,
    frac_ref, send_ref,
    f_ref,
):
    lines, px = gw_ref.shape
    n_ty = lax.axis_size("ty")
    me = lax.axis_index("tx") * n_ty + lax.axis_index("ty")
    rows = OUT_LINES * CH
    above, below = from_turns(
        me, devices, first_swap_ref[16:32, :].astype(f32), second_swap_ref[16:32, :].astype(f32)
    )
    n = HALO_LINES

    pieces = []
    for ch in range(2):
        own = sar_ref[ch].astype(f32)
        pieces += [above[ch * n : (ch + 1) * n], own[0:n], own[lines - n :], below[ch * n : (ch + 1) * n]]
    x = image_columns(jnp.concatenate(pieces, 0))
    out_line = quo(iota((rows, px), 0), CH)
    low = jnp.where(me == 0, n, 0)
    high = jnp.where(me == devices - 1, OUT_LINES - n, 2 * OUT_LINES)
    for layer, (w_ref, e_ref) in enumerate(((w1_ref, e1_ref), (w2_ref, e2_ref), (w3_ref, e3_ref)), 1):
        acc = jnp.maximum(dot(w_ref[...], x), 0.0)
        inside = (out_line >= low - layer) & (out_line < high + layer)
        feat = jnp.where(inside, acc, 0.0).astype(bf16)
        block = jnp.concatenate([feat[0 : 6 * CH], e_ref[...], feat[8 * CH :]], 0)
        if layer < 3:
            before, after = pixel_shifts(block)
            x = jnp.concatenate([before, block, after], 0)
    frac = sigmoid(merged(dot(w4_ref[...], block), CH)).astype(f32)
    f_ref[...] = frac_in[...].astype(f32)
    f_ref[0:6, :] = frac[0:6]
    f_ref[lines - 6 :, :] = frac[8:14]
    frac_ref[...] = f_ref[...].astype(bf16)
    quarter = slots_in.shape[1] // 4
    sums = []
    for at in (slice(0, END_LINES), slice(lines - END_LINES, lines)):
        cov = gw_ref[at, :]
        sums += line_windows(cell_ref[at, :], f_ref[at, :] * cov, cov, quarter)
    by_slot = slots_in[...] + dot(perm_ref[...], window_goods(jnp.concatenate(sums, 0)))

    per_tile = 4 * capacity
    slots, tile_cols = by_slot.shape
    h = SUBSTEPS
    entry = rem(iota((slots, LANES), 0), per_tile)
    here = quo(iota((slots, LANES), 1), h) == entry
    column = rem(quo(iota((slots, LANES), 0), per_tile), n_ty)
    source = iota((LANES, LANES), 0)
    spot = rem(iota((LANES, LANES), 1), h)

    def strip(x, first_lane, keep):
        take = ((spot + first_lane == source) & (source - first_lane < h)).astype(bf16)
        x = jnp.where(here & keep, dot(x.astype(bf16), take), 0.0)
        return jnp.sum(x.reshape(devices, per_tile, LANES), 1, keepdims=True)

    right_strip = strip(of_right(by_slot[:, 0:LANES], per_tile), 0, column < n_ty - 1)
    left_strip = strip(of_left(by_slot[:, tile_cols - LANES :], per_tile), LANES - h, column > 0)
    at = iota((devices, 8, LANES), 1)
    extra = extra_ref[...].reshape(devices, 8, LANES)
    extra = jnp.where(at == 0, right_strip, jnp.where(at == 1, left_strip, extra))
    halves = [by_slot[:, at : at + LANES].reshape(devices, per_tile, LANES) for at in range(0, tile_cols, LANES)]
    packed = jnp.concatenate([*halves, extra], 1)
    send_ref[...] = packed.reshape(send_ref.shape).astype(bf16)


def transposed(x):
    return jnp.transpose(x, (1, 0))


def level_kernel(
    devices,
    got_ref, first_swap_ref, second_swap_ref, depth_ref, slope_ref, rain_ref, dir_ref,
    level_ref, side_ref, first_ref, second_ref,
):
    tile_rows, tile_cols = depth_ref.shape
    h = SUBSTEPS
    halves = tile_cols // LANES
    n = (got_ref.shape[0] // devices - 8) // halves
    k = devices * n
    packed = got_ref[...].astype(f32).reshape(devices, halves * n + 8, LANES)
    main = jnp.concatenate([packed[:, i * n : (i + 1) * n].reshape(k, LANES) for i in range(halves)], 1)
    extra = packed[:, halves * n :]

    entry = rem(iota((k, LANES), 0), n)
    spread = quo(iota((k, LANES), 1), h) == entry

    def strip(r, first):
        rows = jnp.broadcast_to(extra[:, r : r + 1], (devices, n, LANES)).reshape(k, LANES)
        take = rem(iota((LANES, LANES), 0), h) + first == iota((LANES, LANES), 1)
        return dot(jnp.where(spread, rows, 0.0).astype(bf16), take.astype(bf16)).astype(bf16)

    lane = iota((1, k), 1)
    offset = rem(lane, 2) + tile_rows * rem(quo(lane, 2), 2)
    info = jnp.broadcast_to(extra[:, 2:3], (devices, n, LANES)).reshape(k, LANES)
    info = jnp.where(rem(iota((k, LANES), 1), n) == entry, info, 0.0).astype(bf16)
    turns = (quo(iota((LANES, LANES), 0), n) == iota((LANES, LANES), 1)).astype(bf16)
    lines = transposed(dot(info, turns))

    def placer(turn):
        target = lines[turn : turn + 1].astype(jnp.int32) + offset
        return jnp.where(iota((2 * tile_rows, k), 0) == target, 1.0, 0.0).astype(bf16)

    summed = dot(placer(0), main.astype(bf16))
    summed_side = dot(placer(1), strip(0, 0)) + dot(placer(2), strip(1, LANES - h))

    ty = lax.axis_index("ty")
    tx = lax.axis_index("tx")
    previous, following = from_turns(
        tx * lax.axis_size("ty") + ty, devices,
        first_swap_ref[0:16, :].astype(f32), second_swap_ref[0:16, :].astype(f32),
    )
    left = strips_of(previous, ty > 0)
    right = strips_of(following, ty < lax.axis_size("ty") - 1)
    gap = jnp.zeros((LANES - 2 * h, tile_rows), f32)
    depth_side, conv_side, rain_side, code_side = [
        transposed(jnp.concatenate([r, gap, l], 0)) for r, l in zip(right, left)
    ]

    def analysed(sums, depth):
        observed = sums[0:tile_rows]
        covered = sums[tile_rows:]
        wet = depth / (depth + wet_depth)
        innovation = (observed - covered * wet) / (covered + 1.0)
        return depth * jnp.exp(innovation)

    level = analysed(summed, depth_ref[...])
    level_ref[...] = level
    sides = (analysed(summed_side, depth_side), rain_side, conv_side, code_side)
    owns = (level, rain_ref, slope_ref, dir_ref)

    def end_rows(at):
        own = [x[at, :] for x in owns]
        own[2] = runoff_coef * jnp.sqrt(own[2])
        own[3] = own[3].astype(f32)
        return jnp.concatenate([jnp.concatenate([o, x[at]], 1) for o, x in zip(own, sides)], 0)

    for i, x in enumerate(sides):
        side_ref[i] = x
    first, second = in_turn(rem(tx, 2) == 0, end_rows(slice(tile_rows - h, tile_rows)), end_rows(slice(0, h)))
    first_ref[...] = first.astype(bf16)
    second_ref[...] = second.astype(bf16)


def substeps(level, rain, conv, code, rain_s, conv_s, m_ref, part_ref, up_ref, down_ref, chunk):
    rows, cols = level.shape
    h = SUBSTEPS
    for ref in (up_ref, down_ref):
        ref[0] = jnp.zeros(ref.shape[1:], f32)
        ref[1, 0:h, :] = jnp.zeros((h, cols), f32)
        ref[1, h + rows :, :] = jnp.zeros((h, cols), f32)
    part_ref[0] = level
    rain_s[...] = rain
    conv_s[...] = conv
    sides = (-1, 0, 1, -1, 1, -1, 0, 1)
    for direction, side in enumerate(sides):
        share = jnp.where(code == direction, conv, 0.0)
        m_ref[direction] = pltpu.roll(share, side % cols, 1) if side else share

    def level_at(buf, r, n):
        level = part_ref[buf, r : r + n, :]
        return level + up_ref[buf, h + r + 1 : h + r + 1 + n, :] + down_ref[buf, h + r - 1 : h + r - 1 + n, :]

    def substep(buf, new):
        for r in range(0, rows, chunk):
            level = level_at(buf, r, chunk)
            power = level * jnp.exp((2.0 / 3.0) * jnp.log(jnp.maximum(jnp.abs(level), 1e-30)))
            from_right = pltpu.roll(power, cols - 1, 1)
            from_left = pltpu.roll(power, 1, 1)
            m = [m_ref[d, r : r + chunk, :] for d in range(8)]
            up_ref[new, h + r : h + r + chunk, :] = m[0] * from_right + m[1] * power + m[2] * from_left
            down_ref[new, h + r : h + r + chunk, :] = m[5] * from_right + m[6] * power + m[7] * from_left
            part_ref[new, r : r + chunk, :] = (
                level + rain_s[r : r + chunk, :] - conv_s[r : r + chunk, :] * power
                + (m[3] * from_right + m[4] * from_left)
            )

    def substep_pair(i, carry):
        substep(0, 1)
        substep(1, 0)
        return carry

    lax.fori_loop(0, SUBSTEPS // 2, substep_pair, 0)
    return level_at


def flow_inner_kernel(level_ref, side_ref, slope_ref, dir_ref, rain_ref, out_ref, *scratch):
    rows, cols = level_ref.shape
    own = (level_ref[...], rain_ref[...], runoff_coef * jnp.sqrt(slope_ref[...]), dir_ref[...].astype(f32))
    level_at = substeps(*[jnp.concatenate([x, side_ref[i]], 1) for i, x in enumerate(own)], *scratch, 16)
    out_ref[...] = level_at(0, 0, rows)[:, 0:cols]


def flow_ends_kernel(inner_ref, level_ref, side_ref, slope_ref, dir_ref, rain_ref, first_swap_ref, second_swap_ref, out_ref, *scratch):
    rows, cols = level_ref.shape
    h = SUBSTEPS
    above, below = from_turns(
        lax.axis_index("tx"), lax.axis_size("tx"),
        first_swap_ref[...].astype(f32), second_swap_ref[...].astype(f32),
    )
    fields = []
    for i, ref in enumerate((level_ref, rain_ref, slope_ref, dir_ref)):
        ends = []
        for at in (slice(0, 2 * h), slice(rows - 2 * h, rows)):
            own = ref[at, :].astype(f32)
            if i == 2:
                own = runoff_coef * jnp.sqrt(own)
            ends.append(jnp.concatenate([own, side_ref[i, at, :]], 1))
        fields.append(jnp.concatenate([above[i * h : (i + 1) * h], *ends, below[i * h : (i + 1) * h]], 0))
    level_at = substeps(*fields, *scratch, 16)
    out_ref[h : rows - h, :] = inner_ref[h : rows - h, :]
    out_ref[0:h, :] = level_at(0, h, h)[:, 0:cols]
    out_ref[rows - h :, :] = level_at(0, 4 * h, h)[:, 0:cols]


def flow_scratch(rows, cols):
    return [
        pltpu.VMEM((rows, cols), f32),
        pltpu.VMEM((rows, cols), f32),
        pltpu.VMEM((8, rows, cols), f32),
        pltpu.VMEM((2, rows, cols), f32),
        pltpu.VMEM((2, rows + 2 * SUBSTEPS, cols), f32),
        pltpu.VMEM((2, rows + 2 * SUBSTEPS, cols), f32),
    ]


def hbm_specs(n):
    return [pl.BlockSpec(memory_space=pltpu.HBM)] * n


def vmem_specs(n):
    return [pl.BlockSpec(memory_space=pltpu.VMEM)] * n


def per_device(
    sar_image, kernel_first, kernel_second, kernel_third, kernel_last,
    geo_weight, cell_index, block_tile, block_row, depth, slope, flow_dir, rain,
):
    both = ("tx", "ty")
    devices = lax.axis_size(both)
    az_lines, range_px = geo_weight.shape
    tile_rows, tile_cols = depth.shape
    capacity = max(2, 2 * az_lines // devices)

    def swaps(axis, first, second):
        size = lax.axis_size(axis)
        out = []
        for start, x in enumerate((first, second)):
            to = list(range(size))
            for i in range(start, size - 1, 2):
                to[i], to[i + 1] = i + 1, i
            out.append(lax.ppermute(x, axis, list(enumerate(to))))
        return out

    params = pltpu.CompilerParams(vmem_limit_bytes=VMEM_LIMIT)
    message = pltpu.VMEM((32, range_px), bf16)
    small = (
        jnp.transpose(kernel_first, (2, 3, 1, 0)),
        jnp.transpose(kernel_last[0], (1, 2, 0)),
        block_tile.reshape(1, az_lines),
        block_row.reshape(1, az_lines),
    )
    first, second, *small = pl.pallas_call(
        edge_kernel,
        out_shape=(message, message, *[pltpu.VMEM(x.shape, x.dtype) for x in small]),
        in_specs=hbm_specs(9),
        out_specs=tuple(vmem_specs(6)),
        scratch_shapes=[
            pltpu.VMEM((2, 16, range_px), bf16),
            pltpu.VMEM((2, 16, range_px), bf16),
            *[pltpu.VMEM(x.shape, x.dtype) for x in (depth, slope, rain, flow_dir)],
            pltpu.SemaphoreType.DMA((10,)),
        ],
        compiler_params=pltpu.CompilerParams(vmem_limit_bytes=VMEM_MOST),
        name="edges",
    )(sar_image, depth, slope, rain, flow_dir, *small)
    halo = swaps(both, first, second)

    rows, cols = OUT_LINES * CH, IN_LINES * CH
    slots = devices * capacity * 4
    send_rows = tile_cols // LANES * 4 * capacity + 8
    full = (az_lines + 4) // OUT_LINES + 1
    feats = (full * OUT_LINES + 3) * CH
    blocks_in = (az_lines + IN_LINES, range_px)

    def cost(flops):
        return pl.CostEstimate(flops=flops, bytes_accessed=4_000_000, transcendentals=0)

    prepared = pl.pallas_call(
        functools.partial(inner_kernel, devices, capacity),
        out_shape=(
            jax.ShapeDtypeStruct((rows, LANES), bf16),
            jax.ShapeDtypeStruct((rows, 3 * cols), bf16),
            jax.ShapeDtypeStruct((rows, 3 * cols), bf16),
            jax.ShapeDtypeStruct((3 * CH, cols), bf16),
            jax.ShapeDtypeStruct((slots, 2 * END_LINES * CH), bf16),
            jax.ShapeDtypeStruct((8 * devices, LANES), f32),
            jax.ShapeDtypeStruct((az_lines, range_px), bf16),
            jax.ShapeDtypeStruct((slots, tile_cols), f32),
            *[jax.ShapeDtypeStruct((4 * CH, range_px), bf16)] * 3,
        ),
        in_specs=vmem_specs(9),
        out_specs=tuple(vmem_specs(11)),
        scratch_shapes=[
            pltpu.VMEM((24, CH), f32),
            pltpu.VMEM((16, CH), f32),
            pltpu.VMEM((2, *blocks_in), f32),
            pltpu.VMEM((3, feats, range_px), bf16),
            pltpu.VMEM((3, feats, range_px), bf16),
            pltpu.VMEM((feats, range_px), bf16),
            pltpu.VMEM(blocks_in, f32),
            pltpu.VMEM(((az_lines - 2 * END_LINES) * CH, tile_cols // 4), f32),
        ],
        compiler_params=params,
        cost_estimate=cost(8_000_000_000),
        name="inner",
    )(
        small[0],
        jnp.transpose(kernel_second, (2, 3, 0, 1)).reshape(9 * CH, CH),
        jnp.transpose(kernel_third, (2, 3, 0, 1)).reshape(9 * CH, CH),
        *small[1:],
        sar_image, geo_weight, cell_index,
    )
    fraction, send = pl.pallas_call(
        functools.partial(ends_kernel, devices, capacity),
        out_shape=(
            jax.ShapeDtypeStruct((az_lines, range_px), bf16),
            jax.ShapeDtypeStruct((devices * send_rows, LANES), bf16),
        ),
        in_specs=vmem_specs(16),
        out_specs=tuple(vmem_specs(2)),
        scratch_shapes=[pltpu.VMEM((az_lines, range_px), f32)],
        compiler_params=params,
        name="ends",
    )(*halo, *prepared, sar_image, geo_weight, cell_index)

    got = lax.all_to_all(
        send.reshape(devices, send_rows, LANES), both, split_axis=0, concat_axis=0, tiled=True
    ).reshape(devices * send_rows, LANES)

    wide_cols = tile_cols + LANES
    edge = jax.ShapeDtypeStruct((4 * SUBSTEPS, wide_cols), bf16)
    level, side, first, second = pl.pallas_call(
        functools.partial(level_kernel, devices),
        out_shape=(
            jax.ShapeDtypeStruct((tile_rows, tile_cols), f32),
            jax.ShapeDtypeStruct((4, tile_rows, LANES), f32),
            edge,
            edge,
        ),
        in_specs=vmem_specs(7),
        out_specs=tuple(vmem_specs(4)),
        compiler_params=params,
        name="level",
    )(got, *halo, depth, slope, rain, flow_dir)

    row_halo = swaps("tx", first, second)

    inner = pl.pallas_call(
        flow_inner_kernel,
        out_shape=jax.ShapeDtypeStruct((tile_rows, tile_cols), f32),
        in_specs=vmem_specs(5),
        out_specs=vmem_specs(1)[0],
        scratch_shapes=flow_scratch(tile_rows, wide_cols),
        compiler_params=params,
        cost_estimate=cost(5_000_000_000),
        name="flow_inner",
    )(level, side, slope, flow_dir, rain)
    level = pl.pallas_call(
        flow_ends_kernel,
        out_shape=jax.ShapeDtypeStruct((tile_rows, tile_cols), f32),
        in_specs=vmem_specs(8),
        out_specs=vmem_specs(1)[0],
        scratch_shapes=flow_scratch(6 * SUBSTEPS, wide_cols),
        compiler_params=params,
        name="flow_ends",
    )(inner, level, side, slope, flow_dir, rain, *row_halo)
    return (fraction, level)


def solution(mesh):
    placed = (
        P(None, ("tx", "ty"), None),
        P(),
        P(),
        P(),
        P(),
        P(("tx", "ty"), None),
        P(("tx", "ty"), None),
        P(("tx", "ty"), None),
        P(("tx", "ty"), None),
        P("tx", "ty"),
        P("tx", "ty"),
        P("tx", "ty"),
        P("tx", "ty"),
    )
    return jax.shard_map(
        per_device,
        mesh=mesh,
        in_specs=placed,
        out_specs=(P(("tx", "ty"), None), P("tx", "ty")),
        check_vma=False,
    )
```

```python
import functools

import jax
import jax.numpy as jnp
from jax import lax
from jax.experimental import pallas as pl
from jax.experimental.pallas import tpu as pltpu
from jax.sharding import PartitionSpec as P

WIN_ROWS = 2
SUBSTEPS = 8
CH = 16
OUT_LINES = 14
IN_LINES = OUT_LINES + 2
HALO_LINES = 4
END_LINES = 8
LANES = 128
VMEM_LIMIT = 48 * 1024 * 1024
VMEM_MOST = 60160 * 1024

wet_depth = 0.5
runoff_coef = 0.25
bf16 = jnp.bfloat16
f32 = jnp.float32


def iota(shape, dim):
    return lax.broadcasted_iota(jnp.int32, shape, dim)


def quo(x, n):
    assert n & (n - 1) == 0
    return lax.shift_right_logical(x, jnp.int32(n.bit_length() - 1)) if n > 1 else x


def rem(x, n):
    assert n & (n - 1) == 0
    return x & (n - 1)


def dot(a, b):
    return lax.dot_general(a, b, (((1,), (0,)), ((), ())), preferred_element_type=f32)


def dot_0(a, b):
    return lax.dot_general(a, b, (((0,), (0,)), ((), ())), preferred_element_type=f32)


def dot_t(a, b):
    return lax.dot_general(a, b, (((1,), (1,)), ((), ())), preferred_element_type=f32)


def pixel_shifts(x):
    width = x.shape[1]
    pix = iota(x.shape, 1).astype(f32).astype(x.dtype)
    end = (width - 1 - iota(x.shape, 1)).astype(f32).astype(x.dtype)
    zero = jnp.zeros(x.shape, x.dtype)
    before = jnp.where(pix == 0, zero, pltpu.roll(x, 1, 1))
    after = jnp.where(end == 0, zero, pltpu.roll(x, width - 1, 1))
    return before, after


def merged(sums, n):
    before, _ = pixel_shifts(sums[0:n])
    _, after = pixel_shifts(sums[2 * n : 3 * n])
    return before + sums[n : 2 * n] + after


def image_columns(x):
    before, after = pixel_shifts(x)
    pad = jnp.zeros((LANES - 3 * x.shape[0], x.shape[1]), f32)
    return jnp.concatenate([before, x, after, pad], 0).astype(bf16)


def sigmoid(x):
    return (1.0 / (1.0 + jnp.exp(-x))).astype(bf16)


def line_windows(cell, obs, cov, quarter):
    px = cell.shape[1]
    kind = iota((CH, px), 0)
    is_obs = kind < CH // 2
    kind_part = rem(kind, CH // 2).astype(f32).astype(bf16)
    sub = kind.astype(f32).astype(bf16)
    one = jnp.ones((CH, px), bf16)
    nil = jnp.zeros((CH, px), bf16)
    part = quo(cell, quarter).astype(f32)
    col = rem(cell, quarter).astype(f32)

    def spread_row(x, i):
        return jnp.broadcast_to(x[i : i + 1], (CH, px)).astype(bf16)

    out = []
    for i in range(cell.shape[0]):
        value = jnp.where(is_obs, obs[i : i + 1], cov[i : i + 1]).astype(bf16)
        left = jnp.where(kind_part == spread_row(part, i), value, nil)
        where_col = spread_row(col, i)
        hot = jnp.concatenate([jnp.where(sub + g * CH == where_col, one, nil) for g in range(quarter // CH)], 0)
        out.append(dot_t(left, hot))
    return out


def window_goods(sums):
    rows, quarter = sums.shape
    cols = 4 * quarter
    repeat = (rem(iota((quarter, cols), 1), quarter) == iota((quarter, cols), 0)).astype(bf16)
    tiled = dot(sums.astype(bf16), repeat)
    mine = rem(iota((rows, cols), 0), 4) == quo(iota((rows, cols), 1), quarter)
    return jnp.where(mine, tiled, 0.0).astype(bf16)


def band_weights(tiled, rows, cols, per_row, line_of):
    out_line = quo(iota((rows, cols), 0), per_row)
    off = line_of(iota((rows, cols), 1)) - out_line
    out = jnp.zeros((rows, cols), f32)
    for ky in range(3):
        out = jnp.where(off == ky, tiled[ky], out)
    return out.astype(bf16)


def edge_kernel(
    depth_hbm, slope_hbm, rain_hbm, dir_hbm, sar_hbm, *refs
):
    n_on = (len(refs) - 8) // 2
    on_hbm = refs[:n_on]
    first_swap_ref, second_swap_ref, sar_ref, *on_refs = refs[n_on : 2 * n_on + 3]
    depth_ref, slope_ref, rain_ref, dir_ref, sems = refs[2 * n_on + 3 :]
    even = rem(lax.axis_index("tx") * lax.axis_size("ty") + lax.axis_index("ty"), 2) == 0
    lines, px = sar_hbm.shape[1:]
    cols = depth_hbm.shape[1]
    h = SUBSTEPS
    pairs = (
        (depth_hbm, depth_ref), (slope_hbm, slope_ref), (rain_hbm, rain_ref), (dir_hbm, dir_ref),
        (sar_hbm, sar_ref), *zip(on_hbm, on_refs),
    )
    copies = [pltpu.make_async_copy(src, dst, sems.at[i]) for i, (src, dst) in enumerate(pairs)]
    for copy in copies:
        copy.start()
    for copy in copies[0:5]:
        copy.wait()
    fields = (
        depth_ref[...],
        runoff_coef * jnp.sqrt(slope_ref[...]),
        rain_ref[...],
        dir_ref[...].astype(f32),
    )
    zeros = jnp.zeros((8, px), f32)
    messages = []
    for at, lo, strip in (
        (lines - 16, 16 - HALO_LINES, lambda x: jnp.transpose(x[:, cols - LANES :], (1, 0))[LANES - h :]),
        (0, 0, lambda x: jnp.transpose(x[:, 0:LANES], (1, 0))[0:h]),
    ):
        image = [sar_ref[ch, at : at + 16, :].astype(f32)[lo : lo + HALO_LINES] for ch in range(2)]
        strips = [strip(x) for x in fields]
        messages.append(
            jnp.concatenate([jnp.concatenate(strips[0:2], 1), jnp.concatenate(strips[2:4], 1), *image, zeros], 0)
        )
    first, second = in_turn(even, *messages)
    first_swap_ref[...] = first.astype(bf16)
    second_swap_ref[...] = second.astype(bf16)
    for copy in copies[5:]:
        copy.wait()


def in_turn(even, to_next, to_previous):
    return jnp.where(even, to_next, to_previous), jnp.where(even, to_previous, to_next)


def from_turns(place, size, first, second):
    even = rem(place, 2) == 0
    previous = jnp.where(even, second, first)
    following = jnp.where(even, first, second)
    return jnp.where(place > 0, previous, 0.0), jnp.where(place < size - 1, following, 0.0)


def strips_of(message, keep):
    both = jnp.where(keep, message, 0.0)
    cols = both.shape[1] // 2
    return [both[0:8, 0:cols], both[0:8, cols:], both[8:16, 0:cols], both[8:16, cols:]]


def inner_kernel(
    devices, capacity,
    k1_ref, k2_ref, k3_ref, k4_ref, tile_ref, row_ref, sar_ref, gw_ref, cell_ref,
    w1_ref, w2_ref, w3_ref, w4_ref, perm_ref, extra_ref, frac_ref, slots_ref, e1_ref, e2_ref, e3_ref,
    t1_ref, t4_ref, s_ref, xa_ref, xb_ref, x3_ref, logit_ref, wnd_ref,
):
    rows = OUT_LINES * CH
    cols = IN_LINES * CH

    out_of = quo(iota((CH, OUT_LINES * cols), 1), cols)
    in_of = rem(iota((CH, OUT_LINES * cols), 1), cols) - iota((CH, OUT_LINES * cols), 0)
    spread = [(in_of == CH * (out_of + ky)).astype(bf16) for ky in range(3)]
    n1 = OUT_LINES * LANES
    group1 = quo(rem(iota((8, n1), 1), LANES), IN_LINES) == iota((8, n1), 0)
    line1 = rem(iota((8, n1), 1), IN_LINES) - quo(iota((8, n1), 1), LANES)
    spread1 = [(group1 & (line1 == ky)).astype(bf16) for ky in range(3)]
    tile4 = (rem(iota((CH, cols), 1), CH) == iota((CH, cols), 0)).astype(bf16)
    t1_ref[...] = jnp.zeros(t1_ref.shape, f32)
    t4_ref[...] = jnp.zeros(t4_ref.shape, f32)
    for ky in range(3):
        for kx in range(3):
            t1_ref[ky * 8 + 2 * kx : ky * 8 + 2 * kx + 2, :] = k1_ref[ky, kx].astype(f32)
        t4_ref[ky * 3 : ky * 3 + 3, :] = k4_ref[ky].astype(f32)
    wide1 = sum(dot_0(t1_ref[ky * 8 : ky * 8 + 8, :].astype(bf16), spread1[ky]) for ky in range(3))
    for i in range(OUT_LINES):
        w1_ref[i * CH : (i + 1) * CH, :] = wide1[:, i * LANES : (i + 1) * LANES].astype(bf16)
    for k_ref, w_ref in ((k2_ref, w2_ref), (k3_ref, w3_ref)):
        wide = sum(dot(k_ref[ky * 3 * CH : (ky + 1) * 3 * CH, :], spread[ky]) for ky in range(3))
        for kx in range(3):
            for i in range(OUT_LINES):
                w_ref[i * CH : (i + 1) * CH, kx * cols : (kx + 1) * cols] = wide[
                    kx * CH : (kx + 1) * CH, i * cols : (i + 1) * cols
                ].astype(bf16)
    wide4 = dot(t4_ref[...].astype(bf16), tile4)
    w4_ref[...] = jnp.concatenate(
        [
            band_weights(
                [jnp.broadcast_to(wide4[ky * 3 + kx : ky * 3 + kx + 1], (CH, cols)) for ky in range(3)],
                CH, cols, 1, lambda k: quo(k, CH),
            )
            for kx in range(3)
        ],
        0,
    )

    lines = tile_ref.shape[1]
    tile = tile_ref[...].astype(f32)
    same = iota((lines, lines), 0) == iota((lines, lines), 1)
    tile_sub = jnp.sum(jnp.where(same, jnp.broadcast_to(tile, (lines, lines)), 0.0), 1, keepdims=True)
    rival = (tile_sub == tile) & (iota((lines, lines), 0) < iota((lines, lines), 1))
    slot = tile * capacity + jnp.sum(jnp.where(rival, 1.0, 0.0), 0, keepdims=True)
    slots = slots_ref.shape[0]
    wnd_rows = CH * lines
    per_line = CH
    widen = (quo(iota((lines, wnd_rows), 1), per_line) == iota((lines, wnd_rows), 0)).astype(bf16)
    slot_wide = dot(jnp.broadcast_to(slot, (8, lines)).astype(bf16), widen)[0:1]
    place = slot_wide.astype(jnp.int32) * 4 + rem(quo(iota((1, wnd_rows), 1), 4), 4)
    perm = jnp.where(iota((slots, wnd_rows), 0) == place, 1.0, 0.0).astype(bf16)
    end = END_LINES * CH
    perm_ref[...] = jnp.concatenate([perm[:, 0:end], perm[:, wnd_rows - end :]], 1)

    row_of = dot(
        jnp.where(same, jnp.broadcast_to(row_ref[...].astype(f32), (lines, lines)), 0.0).astype(bf16),
        jnp.ones((lines, LANES), bf16),
    )
    perm_line = jnp.where(quo(iota((slots, lines), 0), 4) == slot.astype(jnp.int32), 1.0, 0.0).astype(bf16)
    row_own = dot(perm_line, row_of.astype(bf16))
    per_tile = 4 * capacity
    lane = iota((slots, LANES), 1)
    entry = rem(iota((slots, LANES), 0), per_tile)
    info = jnp.zeros((slots, LANES), f32)
    for turn, value in enumerate((row_own, of_right(row_own, per_tile), of_left(row_own, per_tile))):
        info = jnp.where(lane == turn * per_tile + entry, value, info)
    info = jnp.sum(info.reshape(devices, per_tile, LANES), 1, keepdims=True)
    at = iota((devices, 8, LANES), 1)
    extra_ref[...] = jnp.where(at == 2, info, 0.0).reshape(8 * devices, LANES)


    px = sar_ref.shape[2]
    for ch in range(2):
        s_ref[ch, 0:lines, :] = sar_ref[ch].astype(f32)
        s_ref[ch, lines:, :] = jnp.zeros((s_ref.shape[1] - lines, px), f32)
    total = xa_ref.shape[1] // CH
    xa_ref[:, (total - 2) * CH :, :] = jnp.zeros((3, 2 * CH, px), bf16)

    def put(ref, line, acc):
        feat = jnp.maximum(acc, 0.0).astype(bf16)
        at = slice(line * CH, line * CH + rows)
        if len(ref.shape) == 2:
            ref[at, :] = feat
            return
        before, after = pixel_shifts(feat)
        ref[0, at, :] = before
        ref[1, at, :] = feat
        ref[2, at, :] = after

    full = (lines + 4) // OUT_LINES + 1
    for b in range(full):
        at = b * OUT_LINES
        x = jnp.concatenate([s_ref[0, at : at + IN_LINES, :], s_ref[1, at : at + IN_LINES, :]], 0)
        put(xa_ref, 1 + at, dot(w1_ref[...], image_columns(x)))
    for w_ref, src, dst, line, blocks in ((w2_ref, xa_ref, xb_ref, 2, full), (w3_ref, xb_ref, x3_ref, 3, full - 1)):
        for b in range(blocks):
            at = line + b * OUT_LINES
            x = src[:, (at - 1) * CH : (at - 1) * CH + cols, :].reshape(3 * cols, px)
            put(dst, at, dot(w_ref[...], x))

    def ends_of(lo, center):
        hi = lines - lo - 2
        return jnp.concatenate([center[at * CH : (at + 2) * CH, :] for at in (lo, hi)], 0)

    e1_ref[...] = ends_of(3, xa_ref.at[1])
    e2_ref[...] = ends_of(4, xb_ref.at[1])
    e3_ref[...] = ends_of(5, x3_ref)
    logit_ref[0:END_LINES, :] = jnp.zeros((END_LINES, px), f32)
    starts = [3 + b * OUT_LINES for b in range(full - 2)] + [lines - 5 - IN_LINES]
    for at in starts:
        sums = dot(w4_ref[...], x3_ref[at * CH : at * CH + cols, :])
        logit_ref[at + 1 : at + 1 + CH, :] = merged(sums, CH)
    frac_ref[...] = sigmoid(logit_ref[0:lines, :])
    quarter = wnd_ref.shape[1]
    group = 16

    def window_group(g, carry):
        at = pl.ds(pl.multiple_of(g * group + END_LINES, END_LINES), group)
        cov = gw_ref[at, :]
        obs = sigmoid(logit_ref[at, :]).astype(f32) * cov
        for i, sums in enumerate(line_windows(cell_ref[at, :], obs, cov, quarter)):
            wnd_ref[pl.ds(pl.multiple_of(g * (CH * group) + CH * i, CH), CH), :] = sums
        return carry

    lax.fori_loop(0, (lines - 2 * END_LINES) // group, window_group, 0)
    slots_ref[...] = dot(perm[:, end : wnd_rows - end], window_goods(wnd_ref[...]))


def of_right(x, per_tile):
    return jnp.concatenate([x[per_tile:], jnp.zeros((per_tile, x.shape[1]), x.dtype)], 0)


def of_left(x, per_tile):
    return jnp.concatenate([jnp.zeros((per_tile, x.shape[1]), x.dtype), x[: x.shape[0] - per_tile]], 0)


def ends_kernel(
    devices, capacity,
    first_swap_ref, second_swap_ref, w1_ref, w2_ref, w3_ref, w4_ref, perm_ref, extra_ref, frac_in, slots_in, e1_ref, e2_ref, e3_ref,
    sar_ref, gw_ref, cell_ref,
    frac_ref, send_ref,
    f_ref,
):
    lines, px = gw_ref.shape
    n_ty = lax.axis_size("ty")
    me = lax.axis_index("tx") * n_ty + lax.axis_index("ty")
    rows = OUT_LINES * CH
    above, below = from_turns(
        me, devices, first_swap_ref[16:32, :].astype(f32), second_swap_ref[16:32, :].astype(f32)
    )
    n = HALO_LINES

    pieces = []
    for ch in range(2):
        own = sar_ref[ch].astype(f32)
        pieces += [above[ch * n : (ch + 1) * n], own[0:n], own[lines - n :], below[ch * n : (ch + 1) * n]]
    x = image_columns(jnp.concatenate(pieces, 0))
    out_line = quo(iota((rows, px), 0), CH)
    low = jnp.where(me == 0, n, 0)
    high = jnp.where(me == devices - 1, OUT_LINES - n, 2 * OUT_LINES)
    for layer, (w_ref, e_ref) in enumerate(((w1_ref, e1_ref), (w2_ref, e2_ref), (w3_ref, e3_ref)), 1):
        acc = jnp.maximum(dot(w_ref[...], x), 0.0)
        inside = (out_line >= low - layer) & (out_line < high + layer)
        feat = jnp.where(inside, acc, 0.0).astype(bf16)
        block = jnp.concatenate([feat[0 : 6 * CH], e_ref[...], feat[8 * CH :]], 0)
        if layer < 3:
            before, after = pixel_shifts(block)
            x = jnp.concatenate([before, block, after], 0)
    frac = sigmoid(merged(dot(w4_ref[...], block), CH)).astype(f32)
    f_ref[...] = frac_in[...].astype(f32)
    f_ref[0:6, :] = frac[0:6]
    f_ref[lines - 6 :, :] = frac[8:14]
    frac_ref[...] = f_ref[...].astype(bf16)
    quarter = slots_in.shape[1] // 4
    sums = []
    for at in (slice(0, END_LINES), slice(lines - END_LINES, lines)):
        cov = gw_ref[at, :]
        sums += line_windows(cell_ref[at, :], f_ref[at, :] * cov, cov, quarter)
    by_slot = slots_in[...] + dot(perm_ref[...], window_goods(jnp.concatenate(sums, 0)))

    per_tile = 4 * capacity
    slots, tile_cols = by_slot.shape
    h = SUBSTEPS
    entry = rem(iota((slots, LANES), 0), per_tile)
    here = quo(iota((slots, LANES), 1), h) == entry
    column = rem(quo(iota((slots, LANES), 0), per_tile), n_ty)
    source = iota((LANES, LANES), 0)
    spot = rem(iota((LANES, LANES), 1), h)

    def strip(x, first_lane, keep):
        take = ((spot + first_lane == source) & (source - first_lane < h)).astype(bf16)
        x = jnp.where(here & keep, dot(x.astype(bf16), take), 0.0)
        return jnp.sum(x.reshape(devices, per_tile, LANES), 1, keepdims=True)

    right_strip = strip(of_right(by_slot[:, 0:LANES], per_tile), 0, column < n_ty - 1)
    left_strip = strip(of_left(by_slot[:, tile_cols - LANES :], per_tile), LANES - h, column > 0)
    at = iota((devices, 8, LANES), 1)
    extra = extra_ref[...].reshape(devices, 8, LANES)
    extra = jnp.where(at == 0, right_strip, jnp.where(at == 1, left_strip, extra))
    halves = [by_slot[:, at : at + LANES].reshape(devices, per_tile, LANES) for at in range(0, tile_cols, LANES)]
    packed = jnp.concatenate([*halves, extra], 1)
    send_ref[...] = packed.reshape(send_ref.shape).astype(bf16)


def transposed(x):
    return jnp.transpose(x, (1, 0))


def shares_by_direction(code, conv):
    cols = conv.shape[1]
    for direction, side in enumerate((-1, 0, 1, -1, 1, -1, 0, 1)):
        share = jnp.where(code == direction, conv, 0.0)
        yield direction, pltpu.roll(share, side % cols, 1) if side else share


def static_kernel(side_ref, slope_ref, rain_ref, dir_ref, rain_wide_ref, conv_wide_ref, m_ref):
    conv = jnp.concatenate([runoff_coef * jnp.sqrt(slope_ref[...]), side_ref[1]], 1)
    code = jnp.concatenate([dir_ref[...].astype(f32), side_ref[2]], 1)
    conv_wide_ref[...] = conv
    rain_wide_ref[...] = jnp.concatenate([rain_ref[...], side_ref[0]], 1)
    for direction, share in shares_by_direction(code, conv):
        m_ref[direction] = share


def level_kernel(
    devices,
    got_ref, first_swap_ref, second_swap_ref, depth_ref, slope_ref, rain_ref, dir_ref,
    level_ref, side_ref, first_ref, second_ref,
):
    tile_rows, tile_cols = depth_ref.shape
    h = SUBSTEPS
    halves = tile_cols // LANES
    n = (got_ref.shape[0] // devices - 8) // halves
    k = devices * n
    packed = got_ref[...].astype(f32).reshape(devices, halves * n + 8, LANES)
    main = jnp.concatenate([packed[:, i * n : (i + 1) * n].reshape(k, LANES) for i in range(halves)], 1)
    extra = packed[:, halves * n :]

    entry = rem(iota((k, LANES), 0), n)
    spread = quo(iota((k, LANES), 1), h) == entry

    def strip(r, first):
        rows = jnp.broadcast_to(extra[:, r : r + 1], (devices, n, LANES)).reshape(k, LANES)
        take = rem(iota((LANES, LANES), 0), h) + first == iota((LANES, LANES), 1)
        return dot(jnp.where(spread, rows, 0.0).astype(bf16), take.astype(bf16)).astype(bf16)

    lane = iota((1, k), 1)
    offset = rem(lane, 2) + tile_rows * rem(quo(lane, 2), 2)
    info = jnp.broadcast_to(extra[:, 2:3], (devices, n, LANES)).reshape(k, LANES)
    info = jnp.where(rem(iota((k, LANES), 1), n) == entry, info, 0.0).astype(bf16)
    turns = (quo(iota((LANES, LANES), 0), n) == iota((LANES, LANES), 1)).astype(bf16)
    lines = transposed(dot(info, turns))

    def placer(turn):
        target = lines[turn : turn + 1].astype(jnp.int32) + offset
        return jnp.where(iota((2 * tile_rows, k), 0) == target, 1.0, 0.0).astype(bf16)

    summed = dot(placer(0), main.astype(bf16))
    summed_side = dot(placer(1), strip(0, 0)) + dot(placer(2), strip(1, LANES - h))

    tx, ty = lax.axis_index("tx"), lax.axis_index("ty")
    previous, following = from_turns(
        tx * lax.axis_size("ty") + ty, devices,
        first_swap_ref[0:16, :].astype(f32), second_swap_ref[0:16, :].astype(f32),
    )
    left = strips_of(previous, ty > 0)
    right = strips_of(following, ty < lax.axis_size("ty") - 1)
    gap = jnp.zeros((LANES - 2 * h, tile_rows), f32)
    depth_side, conv_side, rain_side, code_side = [
        transposed(jnp.concatenate([r, gap, l], 0)) for r, l in zip(right, left)
    ]

    def analysed(sums, depth):
        observed = sums[0:tile_rows]
        covered = sums[tile_rows:]
        wet = depth / (depth + wet_depth)
        innovation = (observed - covered * wet) / (covered + 1.0)
        return depth * jnp.exp(innovation)

    level = jnp.concatenate([analysed(summed, depth_ref[...]), analysed(summed_side, depth_side)], 1)
    level_ref[...] = level
    sides = (rain_side, conv_side, code_side)
    for i, x in enumerate(sides):
        side_ref[i] = x

    def end_rows(at):
        own = (rain_ref[at, :], runoff_coef * jnp.sqrt(slope_ref[at, :]), dir_ref[at, :].astype(f32))
        return jnp.concatenate([level[at], *[jnp.concatenate([o, x[at]], 1) for o, x in zip(own, sides)]], 0)

    first, second = in_turn(rem(tx, 2) == 0, end_rows(slice(tile_rows - h, tile_rows)), end_rows(slice(0, h)))
    first_ref[...] = first.astype(bf16)
    second_ref[...] = second.astype(bf16)


def flow_kernel(
    level_ref, rain_ref, conv_ref, m_ref, first_swap_ref, second_swap_ref,
    out_ref,
    end_ref, end_m_ref, part_ref, up_ref, down_ref,
):
    rows, cols = level_ref.shape
    h = SUBSTEPS
    for ref in (up_ref, down_ref):
        ref[0] = jnp.zeros(ref.shape[1:], f32)
        ref[1, 0:h, :] = jnp.zeros((h, cols), f32)
        ref[1, h + rows + 2 * h :, :] = jnp.zeros((h, cols), f32)
    part_ref[0, h : h + rows, :] = level_ref[...]
    ends = from_turns(
        lax.axis_index("tx"), lax.axis_size("tx"),
        first_swap_ref[...].astype(f32), second_swap_ref[...].astype(f32),
    )
    for k, (end, at) in enumerate(zip(ends, (0, h + rows))):
        part_ref[0, at : at + h, :] = end[0:h]
        end_ref[0, k * h : (k + 1) * h, :] = end[h : 2 * h]
        end_ref[1, k * h : (k + 1) * h, :] = end[2 * h : 3 * h]
        for direction, share in shares_by_direction(end[3 * h : 4 * h], end[2 * h : 3 * h]):
            end_m_ref[direction, k * h : (k + 1) * h, :] = share

    def level_at(buf, r, n):
        level = part_ref[buf, r : r + n, :]
        return level + up_ref[buf, h + r + 1 : h + r + 1 + n, :] + down_ref[buf, h + r - 1 : h + r - 1 + n, :]

    chunk = 16
    chunks = [(0, h, end_ref.at[0], end_ref.at[1], end_m_ref, 0)]
    chunks += [(h + r, chunk, rain_ref, conv_ref, m_ref, r) for r in range(0, rows, chunk)]
    chunks += [(h + rows, h, end_ref.at[0], end_ref.at[1], end_m_ref, h)]

    def substep(buf, new):
        for r, n, rain, conv, shares, at in chunks:
            level = level_at(buf, r, n)
            power = level * jnp.exp((2.0 / 3.0) * jnp.log(jnp.maximum(jnp.abs(level), 1e-30)))
            from_right = pltpu.roll(power, cols - 1, 1)
            from_left = pltpu.roll(power, 1, 1)
            at = slice(at, at + n)
            m = [shares[d, at, :] for d in range(8)]
            up_ref[new, h + r : h + r + n, :] = m[0] * from_right + m[1] * power + m[2] * from_left
            down_ref[new, h + r : h + r + n, :] = m[5] * from_right + m[6] * power + m[7] * from_left
            part_ref[new, r : r + n, :] = (
                level + rain[at, :] - conv[at, :] * power + (m[3] * from_right + m[4] * from_left)
            )

    def substep_pair(i, carry):
        substep(0, 1)
        substep(1, 0)
        return carry

    lax.fori_loop(0, SUBSTEPS // 2, substep_pair, 0)
    out_ref[...] = level_at(0, h, rows)[:, 0 : out_ref.shape[1]]


def hbm_specs(n):
    return [pl.BlockSpec(memory_space=pltpu.HBM)] * n


def vmem_specs(n):
    return [pl.BlockSpec(memory_space=pltpu.VMEM)] * n


def per_device(
    sar_image, kernel_first, kernel_second, kernel_third, kernel_last,
    geo_weight, cell_index, block_tile, block_row, depth, slope, flow_dir, rain,
):
    both = ("tx", "ty")
    devices = lax.axis_size(both)
    az_lines, range_px = geo_weight.shape
    tile_rows, tile_cols = depth.shape
    capacity = max(2, 2 * az_lines // devices)

    n_tx, n_ty = lax.axis_size("tx"), lax.axis_size("ty")

    def swaps(first, second, stride):
        size = devices // stride
        out = []
        for start, x in enumerate((first, second)):
            to = {}
            for place in range(start, size, 2):
                for k in range(stride):
                    i, j = place * stride + k, (place + 1) % size * stride + k
                    if place == size - 1 and stride > 1:
                        ends = (i, i ^ 1), (j, j ^ 1)
                    else:
                        ends = (i, j), (j, i)
                    to.update(ends)
            out.append(lax.ppermute(x, both, sorted(to.items())))
        return out

    params = pltpu.CompilerParams(vmem_limit_bytes=VMEM_LIMIT)
    message = pltpu.VMEM((32, range_px), bf16)
    handed = (
        sar_image,
        jnp.transpose(kernel_first, (2, 3, 1, 0)),
        jnp.transpose(kernel_second, (2, 3, 0, 1)).reshape(9 * CH, CH),
        jnp.transpose(kernel_third, (2, 3, 0, 1)).reshape(9 * CH, CH),
        jnp.transpose(kernel_last[0], (1, 2, 0)),
        block_tile.reshape(1, az_lines),
        block_row.reshape(1, az_lines),
        geo_weight,
        cell_index,
    )
    first, second, sar_image, *handed = pl.pallas_call(
        edge_kernel,
        out_shape=(message, message, *[pltpu.VMEM(x.shape, x.dtype) for x in handed]),
        in_specs=hbm_specs(4 + len(handed)),
        out_specs=tuple(vmem_specs(2 + len(handed))),
        scratch_shapes=[
            *[pltpu.VMEM(x.shape, x.dtype) for x in (depth, slope, rain, flow_dir)],
            pltpu.SemaphoreType.DMA((4 + len(handed),)),
        ],
        compiler_params=pltpu.CompilerParams(vmem_limit_bytes=VMEM_MOST),
        name="edges",
    )(depth, slope, rain, flow_dir, *handed)
    geo_weight, cell_index = handed[-2:]
    halo = swaps(first, second, 1)

    rows, cols = OUT_LINES * CH, IN_LINES * CH
    slots = devices * capacity * 4
    send_rows = tile_cols // LANES * 4 * capacity + 8
    full = (az_lines + 4) // OUT_LINES + 1
    feats = (full * OUT_LINES + 3) * CH
    blocks_in = (az_lines + IN_LINES, range_px)

    def cost(flops):
        return pl.CostEstimate(flops=flops, bytes_accessed=4_000_000, transcendentals=0)

    prepared = pl.pallas_call(
        functools.partial(inner_kernel, devices, capacity),
        out_shape=(
            jax.ShapeDtypeStruct((rows, LANES), bf16),
            jax.ShapeDtypeStruct((rows, 3 * cols), bf16),
            jax.ShapeDtypeStruct((rows, 3 * cols), bf16),
            jax.ShapeDtypeStruct((3 * CH, cols), bf16),
            jax.ShapeDtypeStruct((slots, 2 * END_LINES * CH), bf16),
            jax.ShapeDtypeStruct((8 * devices, LANES), f32),
            jax.ShapeDtypeStruct((az_lines, range_px), bf16),
            jax.ShapeDtypeStruct((slots, tile_cols), f32),
            *[jax.ShapeDtypeStruct((4 * CH, range_px), bf16)] * 3,
        ),
        in_specs=vmem_specs(9),
        out_specs=tuple(vmem_specs(11)),
        scratch_shapes=[
            pltpu.VMEM((24, CH), f32),
            pltpu.VMEM((16, CH), f32),
            pltpu.VMEM((2, *blocks_in), f32),
            pltpu.VMEM((3, feats, range_px), bf16),
            pltpu.VMEM((3, feats, range_px), bf16),
            pltpu.VMEM((feats, range_px), bf16),
            pltpu.VMEM(blocks_in, f32),
            pltpu.VMEM(((az_lines - 2 * END_LINES) * CH, tile_cols // 4), f32),
        ],
        compiler_params=params,
        cost_estimate=cost(8_000_000_000),
        name="inner",
    )(
        *handed[:-2], sar_image, geo_weight, cell_index,
    )
    fraction, send = pl.pallas_call(
        functools.partial(ends_kernel, devices, capacity),
        out_shape=(
            jax.ShapeDtypeStruct((az_lines, range_px), bf16),
            jax.ShapeDtypeStruct((devices * send_rows, LANES), bf16),
        ),
        in_specs=vmem_specs(16),
        out_specs=tuple(vmem_specs(2)),
        scratch_shapes=[pltpu.VMEM((az_lines, range_px), f32)],
        compiler_params=params,
        name="ends",
    )(*halo, *prepared, sar_image, geo_weight, cell_index)

    got = lax.all_to_all(
        send.reshape(devices, send_rows, LANES), both, split_axis=0, concat_axis=0, tiled=True
    ).reshape(devices * send_rows, LANES)

    wide_cols = tile_cols + LANES
    wide = jax.ShapeDtypeStruct((tile_rows, wide_cols), f32)
    edge = jax.ShapeDtypeStruct((4 * SUBSTEPS, wide_cols), bf16)
    level, side, first, second = pl.pallas_call(
        functools.partial(level_kernel, devices),
        out_shape=(wide, jax.ShapeDtypeStruct((3, tile_rows, LANES), f32), edge, edge),
        in_specs=vmem_specs(7),
        out_specs=tuple(vmem_specs(4)),
        compiler_params=params,
        name="level",
    )(got, *halo, depth, slope, rain, flow_dir)

    row_halo = swaps(first, second, n_ty)

    rain_wide, conv_wide, shares = pl.pallas_call(
        static_kernel,
        out_shape=(wide, wide, jax.ShapeDtypeStruct((8, tile_rows, wide_cols), f32)),
        in_specs=vmem_specs(4),
        out_specs=tuple(vmem_specs(3)),
        compiler_params=params,
        cost_estimate=cost(2_000_000_000),
        name="static",
    )(side, slope, rain, flow_dir)
    flow_rows = tile_rows + 2 * SUBSTEPS
    level = pl.pallas_call(
        flow_kernel,
        out_shape=jax.ShapeDtypeStruct((tile_rows, tile_cols), f32),
        in_specs=vmem_specs(6),
        out_specs=vmem_specs(1)[0],
        scratch_shapes=[
            pltpu.VMEM((2, 2 * SUBSTEPS, wide_cols), f32),
            pltpu.VMEM((8, 2 * SUBSTEPS, wide_cols), f32),
            pltpu.VMEM((2, flow_rows, wide_cols), f32),
            pltpu.VMEM((2, flow_rows + 2 * SUBSTEPS, wide_cols), f32),
            pltpu.VMEM((2, flow_rows + 2 * SUBSTEPS, wide_cols), f32),
        ],
        compiler_params=params,
        name="flow",
    )(level, rain_wide, conv_wide, shares, *row_halo)
    return (fraction, level)


def solution(mesh):
    placed = (
        P(None, ("tx", "ty"), None),
        P(),
        P(),
        P(),
        P(),
        P(("tx", "ty"), None),
        P(("tx", "ty"), None),
        P(("tx", "ty"), None),
        P(("tx", "ty"), None),
        P("tx", "ty"),
        P("tx", "ty"),
        P("tx", "ty"),
        P("tx", "ty"),
    )
    return jax.shard_map(
        per_device,
        mesh=mesh,
        in_specs=placed,
        out_specs=(P(("tx", "ty"), None), P("tx", "ty")),
        check_vma=False,
    )
```

```python
import functools

import jax
import jax.numpy as jnp
from jax import lax
from jax.experimental import pallas as pl
from jax.experimental.pallas import tpu as pltpu
from jax.sharding import PartitionSpec as P

WIN_ROWS = 2
SUBSTEPS = 8
CH = 16
OUT_LINES = 14
IN_LINES = OUT_LINES + 2
HALO_LINES = 4
END_LINES = 8
LANES = 128
VMEM_LIMIT = 48 * 1024 * 1024
VMEM_MOST = 60160 * 1024

wet_depth = 0.5
runoff_coef = 0.25
bf16 = jnp.bfloat16
f32 = jnp.float32


def iota(shape, dim):
    return lax.broadcasted_iota(jnp.int32, shape, dim)


def quo(x, n):
    assert n & (n - 1) == 0
    return lax.shift_right_logical(x, jnp.int32(n.bit_length() - 1)) if n > 1 else x


def rem(x, n):
    assert n & (n - 1) == 0
    return x & (n - 1)


def dot(a, b):
    return lax.dot_general(a, b, (((1,), (0,)), ((), ())), preferred_element_type=f32)


def dot_0(a, b):
    return lax.dot_general(a, b, (((0,), (0,)), ((), ())), preferred_element_type=f32)


def dot_t(a, b):
    return lax.dot_general(a, b, (((1,), (1,)), ((), ())), preferred_element_type=f32)


def pixel_shifts(x):
    width = x.shape[1]
    pix = iota(x.shape, 1).astype(f32).astype(x.dtype)
    end = (width - 1 - iota(x.shape, 1)).astype(f32).astype(x.dtype)
    zero = jnp.zeros(x.shape, x.dtype)
    before = jnp.where(pix == 0, zero, pltpu.roll(x, 1, 1))
    after = jnp.where(end == 0, zero, pltpu.roll(x, width - 1, 1))
    return before, after


def merged(sums, n):
    before, _ = pixel_shifts(sums[0:n])
    _, after = pixel_shifts(sums[2 * n : 3 * n])
    return before + sums[n : 2 * n] + after


def image_columns(x):
    before, after = pixel_shifts(x)
    pad = jnp.zeros((LANES - 3 * x.shape[0], x.shape[1]), f32)
    return jnp.concatenate([before, x, after, pad], 0).astype(bf16)


def sigmoid(x):
    return (1.0 / (1.0 + jnp.exp(-x))).astype(bf16)


def line_windows(cell, obs, cov, quarter):
    px = cell.shape[1]
    kind = iota((CH, px), 0)
    is_obs = kind < CH // 2
    kind_part = rem(kind, CH // 2).astype(f32).astype(bf16)
    sub = kind.astype(f32).astype(bf16)
    one = jnp.ones((CH, px), bf16)
    nil = jnp.zeros((CH, px), bf16)
    part = quo(cell, quarter).astype(f32)
    col = rem(cell, quarter).astype(f32)

    def spread_row(x, i):
        return jnp.broadcast_to(x[i : i + 1], (CH, px)).astype(bf16)

    out = []
    for i in range(cell.shape[0]):
        value = jnp.where(is_obs, obs[i : i + 1], cov[i : i + 1]).astype(bf16)
        left = jnp.where(kind_part == spread_row(part, i), value, nil)
        where_col = spread_row(col, i)
        hot = jnp.concatenate([jnp.where(sub + g * CH == where_col, one, nil) for g in range(quarter // CH)], 0)
        out.append(dot_t(left, hot))
    return out


def window_goods(sums):
    rows, quarter = sums.shape
    cols = 4 * quarter
    repeat = (rem(iota((quarter, cols), 1), quarter) == iota((quarter, cols), 0)).astype(bf16)
    tiled = dot(sums.astype(bf16), repeat)
    mine = rem(iota((rows, cols), 0), 4) == quo(iota((rows, cols), 1), quarter)
    return jnp.where(mine, tiled, 0.0).astype(bf16)


def band_weights(tiled, rows, cols, per_row, line_of):
    out_line = quo(iota((rows, cols), 0), per_row)
    off = line_of(iota((rows, cols), 1)) - out_line
    out = jnp.zeros((rows, cols), f32)
    for ky in range(3):
        out = jnp.where(off == ky, tiled[ky], out)
    return out.astype(bf16)


def edge_kernel(
    depth_hbm, slope_hbm, rain_hbm, dir_hbm, sar_hbm, *refs
):
    n_on = (len(refs) - 8) // 2
    on_hbm = refs[:n_on]
    first_swap_ref, second_swap_ref, sar_ref, *on_refs = refs[n_on : 2 * n_on + 3]
    depth_ref, slope_ref, rain_ref, dir_ref, sems = refs[2 * n_on + 3 :]
    even = rem(lax.axis_index("tx") * lax.axis_size("ty") + lax.axis_index("ty"), 2) == 0
    lines, px = sar_hbm.shape[1:]
    cols = depth_hbm.shape[1]
    h = SUBSTEPS
    pairs = (
        (depth_hbm, depth_ref), (slope_hbm, slope_ref), (rain_hbm, rain_ref), (dir_hbm, dir_ref),
        (sar_hbm, sar_ref), *zip(on_hbm, on_refs),
    )
    copies = [pltpu.make_async_copy(src, dst, sems.at[i]) for i, (src, dst) in enumerate(pairs)]
    for copy in copies:
        copy.start()
    for copy in copies[0:5]:
        copy.wait()
    fields = (
        depth_ref[...],
        runoff_coef * jnp.sqrt(slope_ref[...]),
        rain_ref[...],
        dir_ref[...].astype(f32),
    )
    zeros = jnp.zeros((8, px), f32)
    messages = []
    for at, lo, strip in (
        (lines - 16, 16 - HALO_LINES, lambda x: jnp.transpose(x[:, cols - LANES :], (1, 0))[LANES - h :]),
        (0, 0, lambda x: jnp.transpose(x[:, 0:LANES], (1, 0))[0:h]),
    ):
        image = [sar_ref[ch, at : at + 16, :].astype(f32)[lo : lo + HALO_LINES] for ch in range(2)]
        strips = [strip(x) for x in fields]
        messages.append(
            jnp.concatenate([jnp.concatenate(strips[0:2], 1), jnp.concatenate(strips[2:4], 1), *image, zeros], 0)
        )
    first, second = in_turn(even, *messages)
    first_swap_ref[...] = first.astype(bf16)
    second_swap_ref[...] = second.astype(bf16)
    for copy in copies[5:]:
        copy.wait()


def in_turn(even, to_next, to_previous):
    return jnp.where(even, to_next, to_previous), jnp.where(even, to_previous, to_next)


def from_turns(place, size, first, second):
    even = rem(place, 2) == 0
    previous = jnp.where(even, second, first)
    following = jnp.where(even, first, second)
    return jnp.where(place > 0, previous, 0.0), jnp.where(place < size - 1, following, 0.0)


def strips_of(message, keep):
    both = jnp.where(keep, message, 0.0)
    cols = both.shape[1] // 2
    return [both[0:8, 0:cols], both[0:8, cols:], both[8:16, 0:cols], both[8:16, cols:]]


def inner_kernel(
    devices, capacity,
    k1_ref, k2_ref, k3_ref, k4_ref, tile_ref, row_ref, sar_ref, gw_ref, cell_ref,
    w1_ref, w2_ref, w3_ref, w4_ref, perm_ref, extra_ref, frac_ref, slots_ref, e1_ref, e2_ref, e3_ref,
    t1_ref, t4_ref, s_ref, xa_ref, xb_ref, x3_ref, logit_ref, wnd_ref,
):
    rows = OUT_LINES * CH
    cols = IN_LINES * CH

    out_of = quo(iota((CH, OUT_LINES * cols), 1), cols)
    in_of = rem(iota((CH, OUT_LINES * cols), 1), cols) - iota((CH, OUT_LINES * cols), 0)
    spread = [(in_of == CH * (out_of + ky)).astype(bf16) for ky in range(3)]
    n1 = OUT_LINES * LANES
    group1 = quo(rem(iota((8, n1), 1), LANES), IN_LINES) == iota((8, n1), 0)
    line1 = rem(iota((8, n1), 1), IN_LINES) - quo(iota((8, n1), 1), LANES)
    spread1 = [(group1 & (line1 == ky)).astype(bf16) for ky in range(3)]
    tile4 = (rem(iota((CH, cols), 1), CH) == iota((CH, cols), 0)).astype(bf16)
    t1_ref[...] = jnp.zeros(t1_ref.shape, f32)
    t4_ref[...] = jnp.zeros(t4_ref.shape, f32)
    for ky in range(3):
        for kx in range(3):
            t1_ref[ky * 8 + 2 * kx : ky * 8 + 2 * kx + 2, :] = k1_ref[ky, kx].astype(f32)
        t4_ref[ky * 3 : ky * 3 + 3, :] = k4_ref[ky].astype(f32)
    wide1 = sum(dot_0(t1_ref[ky * 8 : ky * 8 + 8, :].astype(bf16), spread1[ky]) for ky in range(3))
    for i in range(OUT_LINES):
        w1_ref[i * CH : (i + 1) * CH, :] = wide1[:, i * LANES : (i + 1) * LANES].astype(bf16)
    for k_ref, w_ref in ((k2_ref, w2_ref), (k3_ref, w3_ref)):
        wide = sum(dot(k_ref[ky * 3 * CH : (ky + 1) * 3 * CH, :], spread[ky]) for ky in range(3))
        for kx in range(3):
            for i in range(OUT_LINES):
                w_ref[i * CH : (i + 1) * CH, kx * cols : (kx + 1) * cols] = wide[
                    kx * CH : (kx + 1) * CH, i * cols : (i + 1) * cols
                ].astype(bf16)
    wide4 = dot(t4_ref[...].astype(bf16), tile4)
    w4_ref[...] = jnp.concatenate(
        [
            band_weights(
                [jnp.broadcast_to(wide4[ky * 3 + kx : ky * 3 + kx + 1], (CH, cols)) for ky in range(3)],
                CH, cols, 1, lambda k: quo(k, CH),
            )
            for kx in range(3)
        ],
        0,
    )

    lines = tile_ref.shape[1]
    tile = tile_ref[...].astype(f32)
    same = iota((lines, lines), 0) == iota((lines, lines), 1)
    tile_sub = jnp.sum(jnp.where(same, jnp.broadcast_to(tile, (lines, lines)), 0.0), 1, keepdims=True)
    rival = (tile_sub == tile) & (iota((lines, lines), 0) < iota((lines, lines), 1))
    slot = tile * capacity + jnp.sum(jnp.where(rival, 1.0, 0.0), 0, keepdims=True)
    slots = slots_ref.shape[0]
    wnd_rows = CH * lines
    per_line = CH
    widen = (quo(iota((lines, wnd_rows), 1), per_line) == iota((lines, wnd_rows), 0)).astype(bf16)
    slot_wide = dot(jnp.broadcast_to(slot, (8, lines)).astype(bf16), widen)[0:1]
    place = slot_wide.astype(jnp.int32) * 4 + rem(quo(iota((1, wnd_rows), 1), 4), 4)
    perm = jnp.where(iota((slots, wnd_rows), 0) == place, 1.0, 0.0).astype(bf16)
    end = END_LINES * CH
    perm_ref[...] = jnp.concatenate([perm[:, 0:end], perm[:, wnd_rows - end :]], 1)

    row_of = dot(
        jnp.where(same, jnp.broadcast_to(row_ref[...].astype(f32), (lines, lines)), 0.0).astype(bf16),
        jnp.ones((lines, LANES), bf16),
    )
    perm_line = jnp.where(quo(iota((slots, lines), 0), 4) == slot.astype(jnp.int32), 1.0, 0.0).astype(bf16)
    row_own = dot(perm_line, row_of.astype(bf16))
    per_tile = 4 * capacity
    lane = iota((slots, LANES), 1)
    entry = rem(iota((slots, LANES), 0), per_tile)
    info = jnp.zeros((slots, LANES), f32)
    for turn, value in enumerate((row_own, of_right(row_own, per_tile), of_left(row_own, per_tile))):
        info = jnp.where(lane == turn * per_tile + entry, value, info)
    info = jnp.sum(info.reshape(devices, per_tile, LANES), 1, keepdims=True)
    at = iota((devices, 8, LANES), 1)
    extra_ref[...] = jnp.where(at == 2, info, 0.0).reshape(8 * devices, LANES)


    px = sar_ref.shape[2]
    for ch in range(2):
        s_ref[ch, 0:lines, :] = sar_ref[ch].astype(f32)
        s_ref[ch, lines:, :] = jnp.zeros((s_ref.shape[1] - lines, px), f32)
    total = xa_ref.shape[1] // CH
    xa_ref[:, (total - 2) * CH :, :] = jnp.zeros((3, 2 * CH, px), bf16)

    def put(ref, line, acc):
        feat = jnp.maximum(acc, 0.0).astype(bf16)
        at = slice(line * CH, line * CH + rows)
        if len(ref.shape) == 2:
            ref[at, :] = feat
            return
        before, after = pixel_shifts(feat)
        ref[0, at, :] = before
        ref[1, at, :] = feat
        ref[2, at, :] = after

    full = (lines + 4) // OUT_LINES + 1
    for b in range(full):
        at = b * OUT_LINES
        x = jnp.concatenate([s_ref[0, at : at + IN_LINES, :], s_ref[1, at : at + IN_LINES, :]], 0)
        put(xa_ref, 1 + at, dot(w1_ref[...], image_columns(x)))
    for w_ref, src, dst, line, blocks in ((w2_ref, xa_ref, xb_ref, 2, full), (w3_ref, xb_ref, x3_ref, 3, full - 1)):
        for b in range(blocks):
            at = line + b * OUT_LINES
            x = src[:, (at - 1) * CH : (at - 1) * CH + cols, :].reshape(3 * cols, px)
            put(dst, at, dot(w_ref[...], x))

    def ends_of(lo, center):
        hi = lines - lo - 2
        return jnp.concatenate([center[at * CH : (at + 2) * CH, :] for at in (lo, hi)], 0)

    e1_ref[...] = ends_of(3, xa_ref.at[1])
    e2_ref[...] = ends_of(4, xb_ref.at[1])
    e3_ref[...] = ends_of(5, x3_ref)
    logit_ref[0:END_LINES, :] = jnp.zeros((END_LINES, px), f32)
    starts = [3 + b * OUT_LINES for b in range(full - 2)] + [lines - 5 - IN_LINES]
    for at in starts:
        sums = dot(w4_ref[...], x3_ref[at * CH : at * CH + cols, :])
        logit_ref[at + 1 : at + 1 + CH, :] = merged(sums, CH)
    frac_ref[...] = sigmoid(logit_ref[0:lines, :])
    quarter = wnd_ref.shape[1]
    group = 16

    def window_group(g, carry):
        at = pl.ds(pl.multiple_of(g * group + END_LINES, END_LINES), group)
        cov = gw_ref[at, :]
        obs = sigmoid(logit_ref[at, :]).astype(f32) * cov
        for i, sums in enumerate(line_windows(cell_ref[at, :], obs, cov, quarter)):
            wnd_ref[pl.ds(pl.multiple_of(g * (CH * group) + CH * i, CH), CH), :] = sums
        return carry

    lax.fori_loop(0, (lines - 2 * END_LINES) // group, window_group, 0)
    slots_ref[...] = dot(perm[:, end : wnd_rows - end], window_goods(wnd_ref[...]))


def of_right(x, per_tile):
    return jnp.concatenate([x[per_tile:], jnp.zeros((per_tile, x.shape[1]), x.dtype)], 0)


def of_left(x, per_tile):
    return jnp.concatenate([jnp.zeros((per_tile, x.shape[1]), x.dtype), x[: x.shape[0] - per_tile]], 0)


def ends_kernel(
    devices, capacity,
    first_swap_ref, second_swap_ref, w1_ref, w2_ref, w3_ref, w4_ref, perm_ref, extra_ref, frac_in, slots_in, e1_ref, e2_ref, e3_ref,
    sar_ref, gw_ref, cell_ref,
    frac_ref, send_ref,
    f_ref,
):
    lines, px = gw_ref.shape
    n_ty = lax.axis_size("ty")
    me = lax.axis_index("tx") * n_ty + lax.axis_index("ty")
    rows = OUT_LINES * CH
    above, below = from_turns(
        me, devices, first_swap_ref[16:32, :].astype(f32), second_swap_ref[16:32, :].astype(f32)
    )
    n = HALO_LINES

    pieces = []
    for ch in range(2):
        own = sar_ref[ch].astype(f32)
        pieces += [above[ch * n : (ch + 1) * n], own[0:n], own[lines - n :], below[ch * n : (ch + 1) * n]]
    x = image_columns(jnp.concatenate(pieces, 0))
    out_line = quo(iota((rows, px), 0), CH)
    low = jnp.where(me == 0, n, 0)
    high = jnp.where(me == devices - 1, OUT_LINES - n, 2 * OUT_LINES)
    for layer, (w_ref, e_ref) in enumerate(((w1_ref, e1_ref), (w2_ref, e2_ref), (w3_ref, e3_ref)), 1):
        acc = jnp.maximum(dot(w_ref[...], x), 0.0)
        inside = (out_line >= low - layer) & (out_line < high + layer)
        feat = jnp.where(inside, acc, 0.0).astype(bf16)
        block = jnp.concatenate([feat[0 : 6 * CH], e_ref[...], feat[8 * CH :]], 0)
        if layer < 3:
            before, after = pixel_shifts(block)
            x = jnp.concatenate([before, block, after], 0)
    frac = sigmoid(merged(dot(w4_ref[...], block), CH)).astype(f32)
    f_ref[...] = frac_in[...].astype(f32)
    f_ref[0:6, :] = frac[0:6]
    f_ref[lines - 6 :, :] = frac[8:14]
    frac_ref[...] = f_ref[...].astype(bf16)
    quarter = slots_in.shape[1] // 4
    sums = []
    for at in (slice(0, END_LINES), slice(lines - END_LINES, lines)):
        cov = gw_ref[at, :]
        sums += line_windows(cell_ref[at, :], f_ref[at, :] * cov, cov, quarter)
    by_slot = slots_in[...] + dot(perm_ref[...], window_goods(jnp.concatenate(sums, 0)))

    per_tile = 4 * capacity
    slots, tile_cols = by_slot.shape
    h = SUBSTEPS
    entry = rem(iota((slots, LANES), 0), per_tile)
    here = quo(iota((slots, LANES), 1), h) == entry
    column = rem(quo(iota((slots, LANES), 0), per_tile), n_ty)
    source = iota((LANES, LANES), 0)
    spot = rem(iota((LANES, LANES), 1), h)

    def strip(x, first_lane, keep):
        take = ((spot + first_lane == source) & (source - first_lane < h)).astype(bf16)
        x = jnp.where(here & keep, dot(x.astype(bf16), take), 0.0)
        return jnp.sum(x.reshape(devices, per_tile, LANES), 1, keepdims=True)

    right_strip = strip(of_right(by_slot[:, 0:LANES], per_tile), 0, column < n_ty - 1)
    left_strip = strip(of_left(by_slot[:, tile_cols - LANES :], per_tile), LANES - h, column > 0)
    at = iota((devices, 8, LANES), 1)
    extra = extra_ref[...].reshape(devices, 8, LANES)
    extra = jnp.where(at == 0, right_strip, jnp.where(at == 1, left_strip, extra))
    halves = [by_slot[:, at : at + LANES].reshape(devices, per_tile, LANES) for at in range(0, tile_cols, LANES)]
    packed = jnp.concatenate([*halves, extra], 1)
    send_ref[...] = packed.reshape(send_ref.shape).astype(bf16)


def transposed(x):
    return jnp.transpose(x, (1, 0))


def level_kernel(
    devices,
    got_ref, first_swap_ref, second_swap_ref, depth_ref, slope_ref, rain_ref, dir_ref,
    level_ref, side_ref, first_ref, second_ref,
):
    tile_rows, tile_cols = depth_ref.shape
    h = SUBSTEPS
    halves = tile_cols // LANES
    n = (got_ref.shape[0] // devices - 8) // halves
    k = devices * n
    packed = got_ref[...].astype(f32).reshape(devices, halves * n + 8, LANES)
    main = jnp.concatenate([packed[:, i * n : (i + 1) * n].reshape(k, LANES) for i in range(halves)], 1)
    extra = packed[:, halves * n :]

    entry = rem(iota((k, LANES), 0), n)
    spread = quo(iota((k, LANES), 1), h) == entry

    def strip(r, first):
        rows = jnp.broadcast_to(extra[:, r : r + 1], (devices, n, LANES)).reshape(k, LANES)
        take = rem(iota((LANES, LANES), 0), h) + first == iota((LANES, LANES), 1)
        return dot(jnp.where(spread, rows, 0.0).astype(bf16), take.astype(bf16)).astype(bf16)

    lane = iota((1, k), 1)
    offset = rem(lane, 2) + tile_rows * rem(quo(lane, 2), 2)
    info = jnp.broadcast_to(extra[:, 2:3], (devices, n, LANES)).reshape(k, LANES)
    info = jnp.where(rem(iota((k, LANES), 1), n) == entry, info, 0.0).astype(bf16)
    turns = (quo(iota((LANES, LANES), 0), n) == iota((LANES, LANES), 1)).astype(bf16)
    lines = transposed(dot(info, turns))

    def placer(turn):
        target = lines[turn : turn + 1].astype(jnp.int32) + offset
        return jnp.where(iota((2 * tile_rows, k), 0) == target, 1.0, 0.0).astype(bf16)

    summed = dot(placer(0), main.astype(bf16))
    summed_side = dot(placer(1), strip(0, 0)) + dot(placer(2), strip(1, LANES - h))

    ty = lax.axis_index("ty")
    tx = lax.axis_index("tx")
    previous, following = from_turns(
        tx * lax.axis_size("ty") + ty, devices,
        first_swap_ref[0:16, :].astype(f32), second_swap_ref[0:16, :].astype(f32),
    )
    left = strips_of(previous, ty > 0)
    right = strips_of(following, ty < lax.axis_size("ty") - 1)
    gap = jnp.zeros((LANES - 2 * h, tile_rows), f32)
    depth_side, conv_side, rain_side, code_side = [
        transposed(jnp.concatenate([r, gap, l], 0)) for r, l in zip(right, left)
    ]

    def analysed(sums, depth):
        observed = sums[0:tile_rows]
        covered = sums[tile_rows:]
        wet = depth / (depth + wet_depth)
        innovation = (observed - covered * wet) / (covered + 1.0)
        return depth * jnp.exp(innovation)

    level = analysed(summed, depth_ref[...])
    level_ref[...] = level
    sides = (analysed(summed_side, depth_side), rain_side, conv_side, code_side)
    owns = (level, rain_ref, slope_ref, dir_ref)

    def end_rows(at):
        own = [x[at, :] for x in owns]
        own[2] = runoff_coef * jnp.sqrt(own[2])
        own[3] = own[3].astype(f32)
        return jnp.concatenate([jnp.concatenate([o, x[at]], 1) for o, x in zip(own, sides)], 0)

    for i, x in enumerate(sides):
        side_ref[i] = x
    first, second = in_turn(rem(tx, 2) == 0, end_rows(slice(tile_rows - h, tile_rows)), end_rows(slice(0, h)))
    first_ref[...] = first.astype(bf16)
    second_ref[...] = second.astype(bf16)


def substeps(level, rain, conv, code, rain_s, conv_s, m_ref, part_ref, up_ref, down_ref, chunk):
    rows, cols = level.shape
    h = SUBSTEPS
    for ref in (up_ref, down_ref):
        ref[0] = jnp.zeros(ref.shape[1:], f32)
        ref[1, 0:h, :] = jnp.zeros((h, cols), f32)
        ref[1, h + rows :, :] = jnp.zeros((h, cols), f32)
    part_ref[0] = level
    rain_s[...] = rain
    conv_s[...] = conv
    sides = (-1, 0, 1, -1, 1, -1, 0, 1)
    for direction, side in enumerate(sides):
        share = jnp.where(code == direction, conv, 0.0)
        m_ref[direction] = pltpu.roll(share, side % cols, 1) if side else share

    def level_at(buf, r, n):
        level = part_ref[buf, r : r + n, :]
        return level + up_ref[buf, h + r + 1 : h + r + 1 + n, :] + down_ref[buf, h + r - 1 : h + r - 1 + n, :]

    def substep(buf, new):
        for r in range(0, rows, chunk):
            level = level_at(buf, r, chunk)
            power = level * jnp.exp((2.0 / 3.0) * jnp.log(jnp.maximum(jnp.abs(level), 1e-30)))
            from_right = pltpu.roll(power, cols - 1, 1)
            from_left = pltpu.roll(power, 1, 1)
            m = [m_ref[d, r : r + chunk, :] for d in range(8)]
            up_ref[new, h + r : h + r + chunk, :] = m[0] * from_right + m[1] * power + m[2] * from_left
            down_ref[new, h + r : h + r + chunk, :] = m[5] * from_right + m[6] * power + m[7] * from_left
            part_ref[new, r : r + chunk, :] = (
                level + rain_s[r : r + chunk, :] - conv_s[r : r + chunk, :] * power
                + (m[3] * from_right + m[4] * from_left)
            )

    def substep_pair(i, carry):
        substep(0, 1)
        substep(1, 0)
        return carry

    lax.fori_loop(0, SUBSTEPS // 2, substep_pair, 0)
    return level_at


def flow_inner_kernel(level_ref, side_ref, slope_ref, dir_ref, rain_ref, out_ref, *scratch):
    rows, cols = level_ref.shape
    own = (level_ref[...], rain_ref[...], runoff_coef * jnp.sqrt(slope_ref[...]), dir_ref[...].astype(f32))
    level_at = substeps(*[jnp.concatenate([x, side_ref[i]], 1) for i, x in enumerate(own)], *scratch, 16)
    out_ref[...] = level_at(0, 0, rows)[:, 0:cols]


def flow_ends_kernel(inner_ref, level_ref, side_ref, slope_ref, dir_ref, rain_ref, first_swap_ref, second_swap_ref, out_ref, *scratch):
    rows, cols = level_ref.shape
    h = SUBSTEPS
    above, below = from_turns(
        lax.axis_index("tx"), lax.axis_size("tx"),
        first_swap_ref[...].astype(f32), second_swap_ref[...].astype(f32),
    )
    fields = []
    for i, ref in enumerate((level_ref, rain_ref, slope_ref, dir_ref)):
        ends = []
        for at in (slice(0, 2 * h), slice(rows - 2 * h, rows)):
            own = ref[at, :].astype(f32)
            if i == 2:
                own = runoff_coef * jnp.sqrt(own)
            ends.append(jnp.concatenate([own, side_ref[i, at, :]], 1))
        fields.append(jnp.concatenate([above[i * h : (i + 1) * h], *ends, below[i * h : (i + 1) * h]], 0))
    level_at = substeps(*fields, *scratch, 16)
    out_ref[h : rows - h, :] = inner_ref[h : rows - h, :]
    out_ref[0:h, :] = level_at(0, h, h)[:, 0:cols]
    out_ref[rows - h :, :] = level_at(0, 4 * h, h)[:, 0:cols]


def flow_scratch(rows, cols):
    return [
        pltpu.VMEM((rows, cols), f32),
        pltpu.VMEM((rows, cols), f32),
        pltpu.VMEM((8, rows, cols), f32),
        pltpu.VMEM((2, rows, cols), f32),
        pltpu.VMEM((2, rows + 2 * SUBSTEPS, cols), f32),
        pltpu.VMEM((2, rows + 2 * SUBSTEPS, cols), f32),
    ]


def hbm_specs(n):
    return [pl.BlockSpec(memory_space=pltpu.HBM)] * n


def vmem_specs(n):
    return [pl.BlockSpec(memory_space=pltpu.VMEM)] * n


def per_device(
    sar_image, kernel_first, kernel_second, kernel_third, kernel_last,
    geo_weight, cell_index, block_tile, block_row, depth, slope, flow_dir, rain,
):
    both = ("tx", "ty")
    devices = lax.axis_size(both)
    az_lines, range_px = geo_weight.shape
    tile_rows, tile_cols = depth.shape
    capacity = max(2, 2 * az_lines // devices)

    n_tx, n_ty = lax.axis_size("tx"), lax.axis_size("ty")

    def swaps(first, second, stride):
        size = devices // stride
        out = []
        for start, x in enumerate((first, second)):
            to = {}
            for place in range(start, size, 2):
                for k in range(stride):
                    i, j = place * stride + k, (place + 1) % size * stride + k
                    if place == size - 1 and stride > 1:
                        ends = (i, i ^ 1), (j, j ^ 1)
                    else:
                        ends = (i, j), (j, i)
                    to.update(ends)
            out.append(lax.ppermute(x, both, sorted(to.items())))
        return out

    params = pltpu.CompilerParams(vmem_limit_bytes=VMEM_LIMIT)
    message = pltpu.VMEM((32, range_px), bf16)
    handed = (
        sar_image,
        jnp.transpose(kernel_first, (2, 3, 1, 0)),
        jnp.transpose(kernel_second, (2, 3, 0, 1)).reshape(9 * CH, CH),
        jnp.transpose(kernel_third, (2, 3, 0, 1)).reshape(9 * CH, CH),
        jnp.transpose(kernel_last[0], (1, 2, 0)),
        block_tile.reshape(1, az_lines),
        block_row.reshape(1, az_lines),
        geo_weight,
        cell_index,
    )
    first, second, sar_image, *handed = pl.pallas_call(
        edge_kernel,
        out_shape=(message, message, *[pltpu.VMEM(x.shape, x.dtype) for x in handed]),
        in_specs=hbm_specs(4 + len(handed)),
        out_specs=tuple(vmem_specs(2 + len(handed))),
        scratch_shapes=[
            *[pltpu.VMEM(x.shape, x.dtype) for x in (depth, slope, rain, flow_dir)],
            pltpu.SemaphoreType.DMA((4 + len(handed),)),
        ],
        compiler_params=pltpu.CompilerParams(vmem_limit_bytes=VMEM_MOST),
        name="edges",
    )(depth, slope, rain, flow_dir, *handed)
    geo_weight, cell_index = handed[-2:]
    halo = swaps(first, second, 1)

    rows, cols = OUT_LINES * CH, IN_LINES * CH
    slots = devices * capacity * 4
    send_rows = tile_cols // LANES * 4 * capacity + 8
    full = (az_lines + 4) // OUT_LINES + 1
    feats = (full * OUT_LINES + 3) * CH
    blocks_in = (az_lines + IN_LINES, range_px)

    def cost(flops):
        return pl.CostEstimate(flops=flops, bytes_accessed=4_000_000, transcendentals=0)

    prepared = pl.pallas_call(
        functools.partial(inner_kernel, devices, capacity),
        out_shape=(
            jax.ShapeDtypeStruct((rows, LANES), bf16),
            jax.ShapeDtypeStruct((rows, 3 * cols), bf16),
            jax.ShapeDtypeStruct((rows, 3 * cols), bf16),
            jax.ShapeDtypeStruct((3 * CH, cols), bf16),
            jax.ShapeDtypeStruct((slots, 2 * END_LINES * CH), bf16),
            jax.ShapeDtypeStruct((8 * devices, LANES), f32),
            jax.ShapeDtypeStruct((az_lines, range_px), bf16),
            jax.ShapeDtypeStruct((slots, tile_cols), f32),
            *[jax.ShapeDtypeStruct((4 * CH, range_px), bf16)] * 3,
        ),
        in_specs=vmem_specs(9),
        out_specs=tuple(vmem_specs(11)),
        scratch_shapes=[
            pltpu.VMEM((24, CH), f32),
            pltpu.VMEM((16, CH), f32),
            pltpu.VMEM((2, *blocks_in), f32),
            pltpu.VMEM((3, feats, range_px), bf16),
            pltpu.VMEM((3, feats, range_px), bf16),
            pltpu.VMEM((feats, range_px), bf16),
            pltpu.VMEM(blocks_in, f32),
            pltpu.VMEM(((az_lines - 2 * END_LINES) * CH, tile_cols // 4), f32),
        ],
        compiler_params=params,
        cost_estimate=cost(8_000_000_000),
        name="inner",
    )(
        *handed[:-2], sar_image, geo_weight, cell_index,
    )
    fraction, send = pl.pallas_call(
        functools.partial(ends_kernel, devices, capacity),
        out_shape=(
            jax.ShapeDtypeStruct((az_lines, range_px), bf16),
            jax.ShapeDtypeStruct((devices * send_rows, LANES), bf16),
        ),
        in_specs=vmem_specs(16),
        out_specs=tuple(vmem_specs(2)),
        scratch_shapes=[pltpu.VMEM((az_lines, range_px), f32)],
        compiler_params=params,
        name="ends",
    )(*halo, *prepared, sar_image, geo_weight, cell_index)

    got = lax.all_to_all(
        send.reshape(devices, send_rows, LANES), both, split_axis=0, concat_axis=0, tiled=True
    ).reshape(devices * send_rows, LANES)

    wide_cols = tile_cols + LANES
    edge = jax.ShapeDtypeStruct((4 * SUBSTEPS, wide_cols), bf16)
    level, side, first, second = pl.pallas_call(
        functools.partial(level_kernel, devices),
        out_shape=(
            jax.ShapeDtypeStruct((tile_rows, tile_cols), f32),
            jax.ShapeDtypeStruct((4, tile_rows, LANES), f32),
            edge,
            edge,
        ),
        in_specs=vmem_specs(7),
        out_specs=tuple(vmem_specs(4)),
        compiler_params=params,
        name="level",
    )(got, *halo, depth, slope, rain, flow_dir)

    row_halo = swaps(first, second, n_ty)

    inner = pl.pallas_call(
        flow_inner_kernel,
        out_shape=jax.ShapeDtypeStruct((tile_rows, tile_cols), f32),
        in_specs=vmem_specs(5),
        out_specs=vmem_specs(1)[0],
        scratch_shapes=flow_scratch(tile_rows, wide_cols),
        compiler_params=params,
        cost_estimate=cost(5_000_000_000),
        name="flow_inner",
    )(level, side, slope, flow_dir, rain)
    level = pl.pallas_call(
        flow_ends_kernel,
        out_shape=jax.ShapeDtypeStruct((tile_rows, tile_cols), f32),
        in_specs=vmem_specs(8),
        out_specs=vmem_specs(1)[0],
        scratch_shapes=flow_scratch(6 * SUBSTEPS, wide_cols),
        compiler_params=params,
        name="flow_ends",
    )(inner, level, side, slope, flow_dir, rain, *row_halo)
    return (fraction, level)


def solution(mesh):
    placed = (
        P(None, ("tx", "ty"), None),
        P(),
        P(),
        P(),
        P(),
        P(("tx", "ty"), None),
        P(("tx", "ty"), None),
        P(("tx", "ty"), None),
        P(("tx", "ty"), None),
        P("tx", "ty"),
        P("tx", "ty"),
        P("tx", "ty"),
        P("tx", "ty"),
    )
    return jax.shard_map(
        per_device,
        mesh=mesh,
        in_specs=placed,
        out_specs=(P(("tx", "ty"), None), P("tx", "ty")),
        check_vma=False,
    )
```

```python
import functools

import jax
import jax.numpy as jnp
from jax import lax
from jax.experimental import pallas as pl
from jax.experimental.pallas import tpu as pltpu
from jax.sharding import PartitionSpec as P

WIN_ROWS = 2
SUBSTEPS = 8
CH = 16
OUT_LINES = 14
IN_LINES = OUT_LINES + 2
HALO_LINES = 4
END_LINES = 8
LANES = 128
VMEM_LIMIT = 48 * 1024 * 1024
VMEM_MOST = 60160 * 1024

wet_depth = 0.5
runoff_coef = 0.25
bf16 = jnp.bfloat16
f32 = jnp.float32


def iota(shape, dim):
    return lax.broadcasted_iota(jnp.int32, shape, dim)


def quo(x, n):
    assert n & (n - 1) == 0
    return lax.shift_right_logical(x, jnp.int32(n.bit_length() - 1)) if n > 1 else x


def rem(x, n):
    assert n & (n - 1) == 0
    return x & (n - 1)


def dot(a, b):
    return lax.dot_general(a, b, (((1,), (0,)), ((), ())), preferred_element_type=f32)


def dot_0(a, b):
    return lax.dot_general(a, b, (((0,), (0,)), ((), ())), preferred_element_type=f32)


def dot_t(a, b):
    return lax.dot_general(a, b, (((1,), (1,)), ((), ())), preferred_element_type=f32)


def pixel_shifts(x):
    width = x.shape[1]
    pix = iota(x.shape, 1).astype(f32).astype(x.dtype)
    end = (width - 1 - iota(x.shape, 1)).astype(f32).astype(x.dtype)
    zero = jnp.zeros(x.shape, x.dtype)
    before = jnp.where(pix == 0, zero, pltpu.roll(x, 1, 1))
    after = jnp.where(end == 0, zero, pltpu.roll(x, width - 1, 1))
    return before, after


def merged(sums, n):
    before, _ = pixel_shifts(sums[0:n])
    _, after = pixel_shifts(sums[2 * n : 3 * n])
    return before + sums[n : 2 * n] + after


def image_columns(x):
    before, after = pixel_shifts(x)
    pad = jnp.zeros((LANES - 3 * x.shape[0], x.shape[1]), f32)
    return jnp.concatenate([before, x, after, pad], 0).astype(bf16)


def sigmoid(x):
    return (1.0 / (1.0 + jnp.exp(-x))).astype(bf16)


def line_windows(cell, obs, cov, quarter):
    px = cell.shape[1]
    kind = iota((CH, px), 0)
    is_obs = kind < CH // 2
    kind_part = rem(kind, CH // 2).astype(f32).astype(bf16)
    sub = kind.astype(f32).astype(bf16)
    one = jnp.ones((CH, px), bf16)
    nil = jnp.zeros((CH, px), bf16)
    part = quo(cell, quarter).astype(f32)
    col = rem(cell, quarter).astype(f32)

    def spread_row(x, i):
        return jnp.broadcast_to(x[i : i + 1], (CH, px)).astype(bf16)

    out = []
    for i in range(cell.shape[0]):
        value = jnp.where(is_obs, obs[i : i + 1], cov[i : i + 1]).astype(bf16)
        left = jnp.where(kind_part == spread_row(part, i), value, nil)
        where_col = spread_row(col, i)
        hot = jnp.concatenate([jnp.where(sub + g * CH == where_col, one, nil) for g in range(quarter // CH)], 0)
        out.append(dot_t(left, hot))
    return out


def window_goods(sums):
    rows, quarter = sums.shape
    cols = 4 * quarter
    repeat = (rem(iota((quarter, cols), 1), quarter) == iota((quarter, cols), 0)).astype(bf16)
    tiled = dot(sums.astype(bf16), repeat)
    mine = rem(iota((rows, cols), 0), 4) == quo(iota((rows, cols), 1), quarter)
    return jnp.where(mine, tiled, 0.0).astype(bf16)


def band_weights(tiled, rows, cols, per_row, line_of):
    out_line = quo(iota((rows, cols), 0), per_row)
    off = line_of(iota((rows, cols), 1)) - out_line
    out = jnp.zeros((rows, cols), f32)
    for ky in range(3):
        out = jnp.where(off == ky, tiled[ky], out)
    return out.astype(bf16)


def edge_kernel(
    depth_hbm, slope_hbm, rain_hbm, dir_hbm, sar_hbm, *refs
):
    n_on = (len(refs) - 8) // 2
    on_hbm = refs[:n_on]
    first_swap_ref, second_swap_ref, sar_ref, *on_refs = refs[n_on : 2 * n_on + 3]
    depth_ref, slope_ref, rain_ref, dir_ref, sems = refs[2 * n_on + 3 :]
    even = rem(lax.axis_index("tx") * lax.axis_size("ty") + lax.axis_index("ty"), 2) == 0
    lines, px = sar_hbm.shape[1:]
    cols = depth_hbm.shape[1]
    h = SUBSTEPS
    pairs = (
        (depth_hbm, depth_ref), (slope_hbm, slope_ref), (rain_hbm, rain_ref), (dir_hbm, dir_ref),
        (sar_hbm, sar_ref), *zip(on_hbm, on_refs),
    )
    copies = [pltpu.make_async_copy(src, dst, sems.at[i]) for i, (src, dst) in enumerate(pairs)]
    for copy in copies:
        copy.start()
    for copy in copies[0:5]:
        copy.wait()
    fields = (
        depth_ref[...],
        runoff_coef * jnp.sqrt(slope_ref[...]),
        rain_ref[...],
        dir_ref[...].astype(f32),
    )
    zeros = jnp.zeros((8, px), f32)
    messages = []
    for at, lo, strip in (
        (lines - 16, 16 - HALO_LINES, lambda x: jnp.transpose(x[:, cols - LANES :], (1, 0))[LANES - h :]),
        (0, 0, lambda x: jnp.transpose(x[:, 0:LANES], (1, 0))[0:h]),
    ):
        image = [sar_ref[ch, at : at + 16, :].astype(f32)[lo : lo + HALO_LINES] for ch in range(2)]
        strips = [strip(x) for x in fields]
        messages.append(
            jnp.concatenate([jnp.concatenate(strips[0:2], 1), jnp.concatenate(strips[2:4], 1), *image, zeros], 0)
        )
    first, second = in_turn(even, *messages)
    first_swap_ref[...] = first.astype(bf16)
    second_swap_ref[...] = second.astype(bf16)
    for copy in copies[5:]:
        copy.wait()


def in_turn(even, to_next, to_previous):
    return jnp.where(even, to_next, to_previous), jnp.where(even, to_previous, to_next)


def from_turns(place, size, first, second):
    even = rem(place, 2) == 0
    previous = jnp.where(even, second, first)
    following = jnp.where(even, first, second)
    return jnp.where(place > 0, previous, 0.0), jnp.where(place < size - 1, following, 0.0)


def strips_of(message, keep):
    both = jnp.where(keep, message, 0.0)
    cols = both.shape[1] // 2
    return [both[0:8, 0:cols], both[0:8, cols:], both[8:16, 0:cols], both[8:16, cols:]]


def inner_kernel(
    devices, capacity,
    k1_ref, k2_ref, k3_ref, k4_ref, tile_ref, row_ref, sar_ref, gw_ref, cell_ref,
    w1_ref, w2_ref, w3_ref, w4_ref, perm_ref, extra_ref, frac_ref, slots_ref, e1_ref, e2_ref, e3_ref,
    t1_ref, t4_ref, s_ref, xa_ref, xb_ref, x3_ref, logit_ref, wnd_ref,
):
    rows = OUT_LINES * CH
    cols = IN_LINES * CH

    out_of = quo(iota((CH, OUT_LINES * cols), 1), cols)
    in_of = rem(iota((CH, OUT_LINES * cols), 1), cols) - iota((CH, OUT_LINES * cols), 0)
    spread = [(in_of == CH * (out_of + ky)).astype(bf16) for ky in range(3)]
    n1 = OUT_LINES * LANES
    group1 = quo(rem(iota((8, n1), 1), LANES), IN_LINES) == iota((8, n1), 0)
    line1 = rem(iota((8, n1), 1), IN_LINES) - quo(iota((8, n1), 1), LANES)
    spread1 = [(group1 & (line1 == ky)).astype(bf16) for ky in range(3)]
    tile4 = (rem(iota((CH, cols), 1), CH) == iota((CH, cols), 0)).astype(bf16)
    t1_ref[...] = jnp.zeros(t1_ref.shape, f32)
    t4_ref[...] = jnp.zeros(t4_ref.shape, f32)
    for ky in range(3):
        for kx in range(3):
            t1_ref[ky * 8 + 2 * kx : ky * 8 + 2 * kx + 2, :] = k1_ref[ky, kx].astype(f32)
        t4_ref[ky * 3 : ky * 3 + 3, :] = k4_ref[ky].astype(f32)
    wide1 = sum(dot_0(t1_ref[ky * 8 : ky * 8 + 8, :].astype(bf16), spread1[ky]) for ky in range(3))
    for i in range(OUT_LINES):
        w1_ref[i * CH : (i + 1) * CH, :] = wide1[:, i * LANES : (i + 1) * LANES].astype(bf16)
    for k_ref, w_ref in ((k2_ref, w2_ref), (k3_ref, w3_ref)):
        wide = sum(dot(k_ref[ky * 3 * CH : (ky + 1) * 3 * CH, :], spread[ky]) for ky in range(3))
        for kx in range(3):
            for i in range(OUT_LINES):
                w_ref[kx * rows + i * CH : kx * rows + (i + 1) * CH, :] = wide[
                    kx * CH : (kx + 1) * CH, i * cols : (i + 1) * cols
                ].astype(bf16)
    wide4 = dot(t4_ref[...].astype(bf16), tile4)
    w4_ref[...] = jnp.concatenate(
        [
            band_weights(
                [jnp.broadcast_to(wide4[ky * 3 + kx : ky * 3 + kx + 1], (CH, cols)) for ky in range(3)],
                CH, cols, 1, lambda k: quo(k, CH),
            )
            for kx in range(3)
        ],
        0,
    )

    lines = tile_ref.shape[1]
    tile = tile_ref[...].astype(f32)
    same = iota((lines, lines), 0) == iota((lines, lines), 1)
    tile_sub = jnp.sum(jnp.where(same, jnp.broadcast_to(tile, (lines, lines)), 0.0), 1, keepdims=True)
    rival = (tile_sub == tile) & (iota((lines, lines), 0) < iota((lines, lines), 1))
    slot = tile * capacity + jnp.sum(jnp.where(rival, 1.0, 0.0), 0, keepdims=True)
    slots = slots_ref.shape[0]
    wnd_rows = CH * lines
    per_line = CH
    widen = (quo(iota((lines, wnd_rows), 1), per_line) == iota((lines, wnd_rows), 0)).astype(bf16)
    slot_wide = dot(jnp.broadcast_to(slot, (8, lines)).astype(bf16), widen)[0:1]
    place = slot_wide.astype(jnp.int32) * 4 + rem(quo(iota((1, wnd_rows), 1), 4), 4)
    perm = jnp.where(iota((slots, wnd_rows), 0) == place, 1.0, 0.0).astype(bf16)
    end = END_LINES * CH
    perm_ref[...] = jnp.concatenate([perm[:, 0:end], perm[:, wnd_rows - end :]], 1)

    row_of = dot(
        jnp.where(same, jnp.broadcast_to(row_ref[...].astype(f32), (lines, lines)), 0.0).astype(bf16),
        jnp.ones((lines, LANES), bf16),
    )
    perm_line = jnp.where(quo(iota((slots, lines), 0), 4) == slot.astype(jnp.int32), 1.0, 0.0).astype(bf16)
    row_own = dot(perm_line, row_of.astype(bf16))
    per_tile = 4 * capacity
    lane = iota((slots, LANES), 1)
    entry = rem(iota((slots, LANES), 0), per_tile)
    info = jnp.zeros((slots, LANES), f32)
    for turn, value in enumerate((row_own, of_right(row_own, per_tile), of_left(row_own, per_tile))):
        info = jnp.where(lane == turn * per_tile + entry, value, info)
    info = jnp.sum(info.reshape(devices, per_tile, LANES), 1, keepdims=True)
    at = iota((devices, 8, LANES), 1)
    extra_ref[...] = jnp.where(at == 2, info, 0.0).reshape(8 * devices, LANES)


    px = sar_ref.shape[2]
    for ch in range(2):
        s_ref[ch, 0:lines, :] = sar_ref[ch].astype(f32)
        s_ref[ch, lines:, :] = jnp.zeros((s_ref.shape[1] - lines, px), f32)
    total = xa_ref.shape[0] // CH
    xa_ref[(total - 2) * CH :, :] = jnp.zeros((2 * CH, px), bf16)

    def put(ref, line, acc):
        ref[line * CH : line * CH + rows, :] = jnp.maximum(acc, 0.0).astype(bf16)

    full = (lines + 4) // OUT_LINES + 1
    for b in range(full):
        at = b * OUT_LINES
        x = jnp.concatenate([s_ref[0, at : at + IN_LINES, :], s_ref[1, at : at + IN_LINES, :]], 0)
        put(xa_ref, 1 + at, dot(w1_ref[...], image_columns(x)))
    for w_ref, src, dst, line, blocks in ((w2_ref, xa_ref, xb_ref, 2, full), (w3_ref, xb_ref, x3_ref, 3, full - 1)):
        for b in range(blocks):
            at = line + b * OUT_LINES
            sums = dot(w_ref[...], src[(at - 1) * CH : (at - 1) * CH + cols, :])
            put(dst, at, merged(sums, rows))

    def ends_of(lo, center):
        hi = lines - lo - 2
        return jnp.concatenate([center[at * CH : (at + 2) * CH, :] for at in (lo, hi)], 0)

    e1_ref[...] = ends_of(3, xa_ref)
    e2_ref[...] = ends_of(4, xb_ref)
    e3_ref[...] = ends_of(5, x3_ref)
    logit_ref[0:END_LINES, :] = jnp.zeros((END_LINES, px), f32)
    starts = [3 + b * OUT_LINES for b in range(full - 2)] + [lines - 5 - IN_LINES]
    for at in starts:
        sums = dot(w4_ref[...], x3_ref[at * CH : at * CH + cols, :])
        logit_ref[at + 1 : at + 1 + CH, :] = merged(sums, CH)
    frac_ref[...] = sigmoid(logit_ref[0:lines, :])
    quarter = wnd_ref.shape[1]
    group = 16

    def window_group(g, carry):
        at = pl.ds(pl.multiple_of(g * group + END_LINES, END_LINES), group)
        cov = gw_ref[at, :]
        obs = sigmoid(logit_ref[at, :]).astype(f32) * cov
        for i, sums in enumerate(line_windows(cell_ref[at, :], obs, cov, quarter)):
            wnd_ref[pl.ds(pl.multiple_of(g * (CH * group) + CH * i, CH), CH), :] = sums
        return carry

    lax.fori_loop(0, (lines - 2 * END_LINES) // group, window_group, 0)
    slots_ref[...] = dot(perm[:, end : wnd_rows - end], window_goods(wnd_ref[...]))


def of_right(x, per_tile):
    return jnp.concatenate([x[per_tile:], jnp.zeros((per_tile, x.shape[1]), x.dtype)], 0)


def of_left(x, per_tile):
    return jnp.concatenate([jnp.zeros((per_tile, x.shape[1]), x.dtype), x[: x.shape[0] - per_tile]], 0)


def ends_kernel(
    devices, capacity,
    first_swap_ref, second_swap_ref, w1_ref, w2_ref, w3_ref, w4_ref, perm_ref, extra_ref, frac_in, slots_in, e1_ref, e2_ref, e3_ref,
    sar_ref, gw_ref, cell_ref,
    frac_ref, send_ref,
    f_ref,
):
    lines, px = gw_ref.shape
    n_ty = lax.axis_size("ty")
    me = lax.axis_index("tx") * n_ty + lax.axis_index("ty")
    rows = OUT_LINES * CH
    above, below = from_turns(
        me, devices, first_swap_ref[16:32, :].astype(f32), second_swap_ref[16:32, :].astype(f32)
    )
    n = HALO_LINES

    pieces = []
    for ch in range(2):
        own = sar_ref[ch].astype(f32)
        pieces += [above[ch * n : (ch + 1) * n], own[0:n], own[lines - n :], below[ch * n : (ch + 1) * n]]
    x = image_columns(jnp.concatenate(pieces, 0))
    out_line = quo(iota((rows, px), 0), CH)
    low = jnp.where(me == 0, n, 0)
    high = jnp.where(me == devices - 1, OUT_LINES - n, 2 * OUT_LINES)
    for layer, (w_ref, e_ref) in enumerate(((w1_ref, e1_ref), (w2_ref, e2_ref), (w3_ref, e3_ref)), 1):
        acc = dot(w_ref[...], x)
        acc = jnp.maximum(acc if layer == 1 else merged(acc, rows), 0.0)
        inside = (out_line >= low - layer) & (out_line < high + layer)
        feat = jnp.where(inside, acc, 0.0).astype(bf16)
        block = jnp.concatenate([feat[0 : 6 * CH], e_ref[...], feat[8 * CH :]], 0)
        x = block
    frac = sigmoid(merged(dot(w4_ref[...], x), CH)).astype(f32)
    f_ref[...] = frac_in[...].astype(f32)
    f_ref[0:6, :] = frac[0:6]
    f_ref[lines - 6 :, :] = frac[8:14]
    frac_ref[...] = f_ref[...].astype(bf16)
    quarter = slots_in.shape[1] // 4
    sums = []
    for at in (slice(0, END_LINES), slice(lines - END_LINES, lines)):
        cov = gw_ref[at, :]
        sums += line_windows(cell_ref[at, :], f_ref[at, :] * cov, cov, quarter)
    by_slot = slots_in[...] + dot(perm_ref[...], window_goods(jnp.concatenate(sums, 0)))

    per_tile = 4 * capacity
    slots, tile_cols = by_slot.shape
    h = SUBSTEPS
    entry = rem(iota((slots, LANES), 0), per_tile)
    here = quo(iota((slots, LANES), 1), h) == entry
    column = rem(quo(iota((slots, LANES), 0), per_tile), n_ty)
    source = iota((LANES, LANES), 0)
    spot = rem(iota((LANES, LANES), 1), h)

    def strip(x, first_lane, keep):
        take = ((spot + first_lane == source) & (source - first_lane < h)).astype(bf16)
        x = jnp.where(here & keep, dot(x.astype(bf16), take), 0.0)
        return jnp.sum(x.reshape(devices, per_tile, LANES), 1, keepdims=True)

    right_strip = strip(of_right(by_slot[:, 0:LANES], per_tile), 0, column < n_ty - 1)
    left_strip = strip(of_left(by_slot[:, tile_cols - LANES :], per_tile), LANES - h, column > 0)
    at = iota((devices, 8, LANES), 1)
    extra = extra_ref[...].reshape(devices, 8, LANES)
    extra = jnp.where(at == 0, right_strip, jnp.where(at == 1, left_strip, extra))
    halves = [by_slot[:, at : at + LANES].reshape(devices, per_tile, LANES) for at in range(0, tile_cols, LANES)]
    packed = jnp.concatenate([*halves, extra], 1)
    send_ref[...] = packed.reshape(send_ref.shape).astype(bf16)


def transposed(x):
    return jnp.transpose(x, (1, 0))


def level_kernel(
    devices,
    got_ref, first_swap_ref, second_swap_ref, depth_ref, slope_ref, rain_ref, dir_ref,
    level_ref, side_ref, first_ref, second_ref,
):
    tile_rows, tile_cols = depth_ref.shape
    h = SUBSTEPS
    halves = tile_cols // LANES
    n = (got_ref.shape[0] // devices - 8) // halves
    k = devices * n
    packed = got_ref[...].astype(f32).reshape(devices, halves * n + 8, LANES)
    main = jnp.concatenate([packed[:, i * n : (i + 1) * n].reshape(k, LANES) for i in range(halves)], 1)
    extra = packed[:, halves * n :]

    entry = rem(iota((k, LANES), 0), n)
    spread = quo(iota((k, LANES), 1), h) == entry

    def strip(r, first):
        rows = jnp.broadcast_to(extra[:, r : r + 1], (devices, n, LANES)).reshape(k, LANES)
        take = rem(iota((LANES, LANES), 0), h) + first == iota((LANES, LANES), 1)
        return dot(jnp.where(spread, rows, 0.0).astype(bf16), take.astype(bf16)).astype(bf16)

    lane = iota((1, k), 1)
    offset = rem(lane, 2) + tile_rows * rem(quo(lane, 2), 2)
    info = jnp.broadcast_to(extra[:, 2:3], (devices, n, LANES)).reshape(k, LANES)
    info = jnp.where(rem(iota((k, LANES), 1), n) == entry, info, 0.0).astype(bf16)
    turns = (quo(iota((LANES, LANES), 0), n) == iota((LANES, LANES), 1)).astype(bf16)
    lines = transposed(dot(info, turns))

    def placer(turn):
        target = lines[turn : turn + 1].astype(jnp.int32) + offset
        return jnp.where(iota((2 * tile_rows, k), 0) == target, 1.0, 0.0).astype(bf16)

    summed = dot(placer(0), main.astype(bf16))
    summed_side = dot(placer(1), strip(0, 0)) + dot(placer(2), strip(1, LANES - h))

    ty = lax.axis_index("ty")
    tx = lax.axis_index("tx")
    previous, following = from_turns(
        tx * lax.axis_size("ty") + ty, devices,
        first_swap_ref[0:16, :].astype(f32), second_swap_ref[0:16, :].astype(f32),
    )
    left = strips_of(previous, ty > 0)
    right = strips_of(following, ty < lax.axis_size("ty") - 1)
    gap = jnp.zeros((LANES - 2 * h, tile_rows), f32)
    depth_side, conv_side, rain_side, code_side = [
        transposed(jnp.concatenate([r, gap, l], 0)) for r, l in zip(right, left)
    ]

    def analysed(sums, depth):
        observed = sums[0:tile_rows]
        covered = sums[tile_rows:]
        wet = depth / (depth + wet_depth)
        innovation = (observed - covered * wet) / (covered + 1.0)
        return depth * jnp.exp(innovation)

    level = analysed(summed, depth_ref[...])
    level_ref[...] = level
    sides = (analysed(summed_side, depth_side), rain_side, conv_side, code_side)
    owns = (level, rain_ref, slope_ref, dir_ref)

    def end_rows(at):
        own = [x[at, :] for x in owns]
        own[2] = runoff_coef * jnp.sqrt(own[2])
        own[3] = own[3].astype(f32)
        return jnp.concatenate([jnp.concatenate([o, x[at]], 1) for o, x in zip(own, sides)], 0)

    for i, x in enumerate(sides):
        side_ref[i] = x
    first, second = in_turn(rem(tx, 2) == 0, end_rows(slice(tile_rows - h, tile_rows)), end_rows(slice(0, h)))
    first_ref[...] = first.astype(bf16)
    second_ref[...] = second.astype(bf16)


def substeps(level, rain, conv, code, rain_s, conv_s, m_ref, part_ref, up_ref, down_ref, chunk):
    rows, cols = level.shape
    h = SUBSTEPS
    for ref in (up_ref, down_ref):
        ref[0] = jnp.zeros(ref.shape[1:], f32)
        ref[1, 0:h, :] = jnp.zeros((h, cols), f32)
        ref[1, h + rows :, :] = jnp.zeros((h, cols), f32)
    part_ref[0] = level
    rain_s[...] = rain
    conv_s[...] = conv
    sides = (-1, 0, 1, -1, 1, -1, 0, 1)
    for direction, side in enumerate(sides):
        share = jnp.where(code == direction, conv, 0.0)
        m_ref[direction] = pltpu.roll(share, side % cols, 1) if side else share

    def level_at(buf, r, n):
        level = part_ref[buf, r : r + n, :]
        return level + up_ref[buf, h + r + 1 : h + r + 1 + n, :] + down_ref[buf, h + r - 1 : h + r - 1 + n, :]

    def substep(buf, new):
        for r in range(0, rows, chunk):
            level = level_at(buf, r, chunk)
            power = level * jnp.exp((2.0 / 3.0) * jnp.log(jnp.maximum(jnp.abs(level), 1e-30)))
            from_right = pltpu.roll(power, cols - 1, 1)
            from_left = pltpu.roll(power, 1, 1)
            m = [m_ref[d, r : r + chunk, :] for d in range(8)]
            up_ref[new, h + r : h + r + chunk, :] = m[0] * from_right + m[1] * power + m[2] * from_left
            down_ref[new, h + r : h + r + chunk, :] = m[5] * from_right + m[6] * power + m[7] * from_left
            part_ref[new, r : r + chunk, :] = (
                level + rain_s[r : r + chunk, :] - conv_s[r : r + chunk, :] * power
                + (m[3] * from_right + m[4] * from_left)
            )

    def substep_pair(i, carry):
        substep(0, 1)
        substep(1, 0)
        return carry

    lax.fori_loop(0, SUBSTEPS // 2, substep_pair, 0)
    return level_at


def flow_inner_kernel(level_ref, side_ref, slope_ref, dir_ref, rain_ref, out_ref, *scratch):
    rows, cols = level_ref.shape
    own = (level_ref[...], rain_ref[...], runoff_coef * jnp.sqrt(slope_ref[...]), dir_ref[...].astype(f32))
    level_at = substeps(*[jnp.concatenate([x, side_ref[i]], 1) for i, x in enumerate(own)], *scratch, 16)
    out_ref[...] = level_at(0, 0, rows)[:, 0:cols]


def flow_ends_kernel(inner_ref, level_ref, side_ref, slope_ref, dir_ref, rain_ref, first_swap_ref, second_swap_ref, out_ref, *scratch):
    rows, cols = level_ref.shape
    h = SUBSTEPS
    above, below = from_turns(
        lax.axis_index("tx"), lax.axis_size("tx"),
        first_swap_ref[...].astype(f32), second_swap_ref[...].astype(f32),
    )
    fields = []
    for i, ref in enumerate((level_ref, rain_ref, slope_ref, dir_ref)):
        ends = []
        for at in (slice(0, 2 * h), slice(rows - 2 * h, rows)):
            own = ref[at, :].astype(f32)
            if i == 2:
                own = runoff_coef * jnp.sqrt(own)
            ends.append(jnp.concatenate([own, side_ref[i, at, :]], 1))
        fields.append(jnp.concatenate([above[i * h : (i + 1) * h], *ends, below[i * h : (i + 1) * h]], 0))
    level_at = substeps(*fields, *scratch, 16)
    out_ref[h : rows - h, :] = inner_ref[h : rows - h, :]
    out_ref[0:h, :] = level_at(0, h, h)[:, 0:cols]
    out_ref[rows - h :, :] = level_at(0, 4 * h, h)[:, 0:cols]


def flow_scratch(rows, cols):
    return [
        pltpu.VMEM((rows, cols), f32),
        pltpu.VMEM((rows, cols), f32),
        pltpu.VMEM((8, rows, cols), f32),
        pltpu.VMEM((2, rows, cols), f32),
        pltpu.VMEM((2, rows + 2 * SUBSTEPS, cols), f32),
        pltpu.VMEM((2, rows + 2 * SUBSTEPS, cols), f32),
    ]


def hbm_specs(n):
    return [pl.BlockSpec(memory_space=pltpu.HBM)] * n


def vmem_specs(n):
    return [pl.BlockSpec(memory_space=pltpu.VMEM)] * n


def per_device(
    sar_image, kernel_first, kernel_second, kernel_third, kernel_last,
    geo_weight, cell_index, block_tile, block_row, depth, slope, flow_dir, rain,
):
    both = ("tx", "ty")
    devices = lax.axis_size(both)
    az_lines, range_px = geo_weight.shape
    tile_rows, tile_cols = depth.shape
    capacity = max(2, 2 * az_lines // devices)

    n_tx, n_ty = lax.axis_size("tx"), lax.axis_size("ty")

    def swaps(first, second, stride):
        size = devices // stride
        out = []
        for start, x in enumerate((first, second)):
            to = {}
            for place in range(start, size, 2):
                for k in range(stride):
                    i, j = place * stride + k, (place + 1) % size * stride + k
                    if place == size - 1 and stride > 1:
                        ends = (i, i ^ 1), (j, j ^ 1)
                    else:
                        ends = (i, j), (j, i)
                    to.update(ends)
            out.append(lax.ppermute(x, both, sorted(to.items())))
        return out

    params = pltpu.CompilerParams(vmem_limit_bytes=VMEM_LIMIT)
    message = pltpu.VMEM((32, range_px), bf16)
    handed = (
        sar_image,
        jnp.transpose(kernel_first, (2, 3, 1, 0)),
        jnp.transpose(kernel_second, (2, 3, 0, 1)).reshape(9 * CH, CH),
        jnp.transpose(kernel_third, (2, 3, 0, 1)).reshape(9 * CH, CH),
        jnp.transpose(kernel_last[0], (1, 2, 0)),
        block_tile.reshape(1, az_lines),
        block_row.reshape(1, az_lines),
        geo_weight,
        cell_index,
    )
    first, second, sar_image, *handed = pl.pallas_call(
        edge_kernel,
        out_shape=(message, message, *[pltpu.VMEM(x.shape, x.dtype) for x in handed]),
        in_specs=hbm_specs(4 + len(handed)),
        out_specs=tuple(vmem_specs(2 + len(handed))),
        scratch_shapes=[
            *[pltpu.VMEM(x.shape, x.dtype) for x in (depth, slope, rain, flow_dir)],
            pltpu.SemaphoreType.DMA((4 + len(handed),)),
        ],
        compiler_params=pltpu.CompilerParams(vmem_limit_bytes=VMEM_MOST),
        name="edges",
    )(depth, slope, rain, flow_dir, *handed)
    geo_weight, cell_index = handed[-2:]
    halo = swaps(first, second, 1)

    rows, cols = OUT_LINES * CH, IN_LINES * CH
    slots = devices * capacity * 4
    send_rows = tile_cols // LANES * 4 * capacity + 8
    full = (az_lines + 4) // OUT_LINES + 1
    feats = (full * OUT_LINES + 3) * CH
    blocks_in = (az_lines + IN_LINES, range_px)

    def cost(flops):
        return pl.CostEstimate(flops=flops, bytes_accessed=4_000_000, transcendentals=0)

    prepared = pl.pallas_call(
        functools.partial(inner_kernel, devices, capacity),
        out_shape=(
            jax.ShapeDtypeStruct((rows, LANES), bf16),
            jax.ShapeDtypeStruct((3 * rows, cols), bf16),
            jax.ShapeDtypeStruct((3 * rows, cols), bf16),
            jax.ShapeDtypeStruct((3 * CH, cols), bf16),
            jax.ShapeDtypeStruct((slots, 2 * END_LINES * CH), bf16),
            jax.ShapeDtypeStruct((8 * devices, LANES), f32),
            jax.ShapeDtypeStruct((az_lines, range_px), bf16),
            jax.ShapeDtypeStruct((slots, tile_cols), f32),
            *[jax.ShapeDtypeStruct((4 * CH, range_px), bf16)] * 3,
        ),
        in_specs=vmem_specs(9),
        out_specs=tuple(vmem_specs(11)),
        scratch_shapes=[
            pltpu.VMEM((24, CH), f32),
            pltpu.VMEM((16, CH), f32),
            pltpu.VMEM((2, *blocks_in), f32),
            pltpu.VMEM((feats, range_px), bf16),
            pltpu.VMEM((feats, range_px), bf16),
            pltpu.VMEM((feats, range_px), bf16),
            pltpu.VMEM(blocks_in, f32),
            pltpu.VMEM(((az_lines - 2 * END_LINES) * CH, tile_cols // 4), f32),
        ],
        compiler_params=params,
        cost_estimate=cost(8_000_000_000),
        name="inner",
    )(
        *handed[:-2], sar_image, geo_weight, cell_index,
    )
    fraction, send = pl.pallas_call(
        functools.partial(ends_kernel, devices, capacity),
        out_shape=(
            jax.ShapeDtypeStruct((az_lines, range_px), bf16),
            jax.ShapeDtypeStruct((devices * send_rows, LANES), bf16),
        ),
        in_specs=vmem_specs(16),
        out_specs=tuple(vmem_specs(2)),
        scratch_shapes=[pltpu.VMEM((az_lines, range_px), f32)],
        compiler_params=params,
        name="ends",
    )(*halo, *prepared, sar_image, geo_weight, cell_index)

    got = lax.all_to_all(
        send.reshape(devices, send_rows, LANES), both, split_axis=0, concat_axis=0, tiled=True
    ).reshape(devices * send_rows, LANES)

    wide_cols = tile_cols + LANES
    edge = jax.ShapeDtypeStruct((4 * SUBSTEPS, wide_cols), bf16)
    level, side, first, second = pl.pallas_call(
        functools.partial(level_kernel, devices),
        out_shape=(
            jax.ShapeDtypeStruct((tile_rows, tile_cols), f32),
            jax.ShapeDtypeStruct((4, tile_rows, LANES), f32),
            edge,
            edge,
        ),
        in_specs=vmem_specs(7),
        out_specs=tuple(vmem_specs(4)),
        compiler_params=params,
        name="level",
    )(got, *halo, depth, slope, rain, flow_dir)

    row_halo = swaps(first, second, n_ty)

    inner = pl.pallas_call(
        flow_inner_kernel,
        out_shape=jax.ShapeDtypeStruct((tile_rows, tile_cols), f32),
        in_specs=vmem_specs(5),
        out_specs=vmem_specs(1)[0],
        scratch_shapes=flow_scratch(tile_rows, wide_cols),
        compiler_params=params,
        cost_estimate=cost(5_000_000_000),
        name="flow_inner",
    )(level, side, slope, flow_dir, rain)
    level = pl.pallas_call(
        flow_ends_kernel,
        out_shape=jax.ShapeDtypeStruct((tile_rows, tile_cols), f32),
        in_specs=vmem_specs(8),
        out_specs=vmem_specs(1)[0],
        scratch_shapes=flow_scratch(6 * SUBSTEPS, wide_cols),
        compiler_params=params,
        name="flow_ends",
    )(inner, level, side, slope, flow_dir, rain, *row_halo)
    return (fraction, level)


def solution(mesh):
    placed = (
        P(None, ("tx", "ty"), None),
        P(),
        P(),
        P(),
        P(),
        P(("tx", "ty"), None),
        P(("tx", "ty"), None),
        P(("tx", "ty"), None),
        P(("tx", "ty"), None),
        P("tx", "ty"),
        P("tx", "ty"),
        P("tx", "ty"),
        P("tx", "ty"),
    )
    return jax.shard_map(
        per_device,
        mesh=mesh,
        in_specs=placed,
        out_specs=(P(("tx", "ty"), None), P("tx", "ty")),
        check_vma=False,
    )
```

```python
import functools

import jax
import jax.numpy as jnp
from jax import lax
from jax.experimental import pallas as pl
from jax.experimental.pallas import tpu as pltpu
from jax.sharding import PartitionSpec as P

WIN_ROWS = 2
SUBSTEPS = 8
CH = 16
OUT_LINES = 14
IN_LINES = OUT_LINES + 2
HALO_LINES = 4
END_LINES = 8
LANES = 128
VMEM_LIMIT = 48 * 1024 * 1024
VMEM_MOST = 60160 * 1024

wet_depth = 0.5
runoff_coef = 0.25
bf16 = jnp.bfloat16
f32 = jnp.float32


def iota(shape, dim):
    return lax.broadcasted_iota(jnp.int32, shape, dim)


def quo(x, n):
    assert n & (n - 1) == 0
    return lax.shift_right_logical(x, jnp.int32(n.bit_length() - 1)) if n > 1 else x


def rem(x, n):
    assert n & (n - 1) == 0
    return x & (n - 1)


def dot(a, b):
    return lax.dot_general(a, b, (((1,), (0,)), ((), ())), preferred_element_type=f32)


def dot_0(a, b):
    return lax.dot_general(a, b, (((0,), (0,)), ((), ())), preferred_element_type=f32)


def dot_t(a, b):
    return lax.dot_general(a, b, (((1,), (1,)), ((), ())), preferred_element_type=f32)


def pixel_shifts(x):
    rows, width = x.shape
    lane = iota((rows, LANES), 1)
    zero = jnp.zeros((rows, LANES), x.dtype)
    first = lane.astype(f32).astype(x.dtype) == 0
    last = (LANES - 1 - lane).astype(f32).astype(x.dtype) == 0
    before = pltpu.roll(x, 1, 1)
    after = pltpu.roll(x, width - 1, 1)
    before = jnp.concatenate([jnp.where(first, zero, before[:, 0:LANES]), before[:, LANES:]], 1)
    after = jnp.concatenate([after[:, : width - LANES], jnp.where(last, zero, after[:, width - LANES :])], 1)
    return before, after


def merged(sums, n):
    before, _ = pixel_shifts(sums[0:n])
    _, after = pixel_shifts(sums[2 * n : 3 * n])
    return before + sums[n : 2 * n] + after


def image_columns(x):
    before, after = pixel_shifts(x)
    pad = jnp.zeros((LANES - 3 * x.shape[0], x.shape[1]), f32)
    return jnp.concatenate([before, x, after, pad], 0).astype(bf16)


def sigmoid(x):
    return (1.0 / (1.0 + jnp.exp(-x))).astype(bf16)


def line_windows(cell, obs, cov, quarter):
    px = cell.shape[1]
    kind = iota((CH, px), 0)
    kind_part = rem(kind, CH // 2).astype(f32).astype(bf16)
    sub = kind.astype(f32).astype(bf16)
    one = jnp.ones((CH, px), bf16)
    nil = jnp.zeros((CH, px), bf16)
    part = quo(cell, quarter).astype(f32)
    col = rem(cell, quarter).astype(f32)

    def spread_row(x, i):
        return jnp.broadcast_to(x[i : i + 1], (CH, px)).astype(bf16)

    out = []
    for i in range(cell.shape[0]):
        pair = [jnp.broadcast_to(x[i : i + 1], (CH // 2, px)) for x in (obs, cov)]
        value = jnp.concatenate(pair, 0).astype(bf16)
        left = jnp.where(kind_part == spread_row(part, i), value, nil)
        where_col = spread_row(col, i)
        hot = jnp.concatenate([jnp.where(sub + g * CH == where_col, one, nil) for g in range(quarter // CH)], 0)
        out.append(dot_t(left, hot))
    return out


def window_goods(sums):
    rows, quarter = sums.shape
    cols = 4 * quarter
    repeat = (rem(iota((quarter, cols), 1), quarter) == iota((quarter, cols), 0)).astype(bf16)
    tiled = dot(sums.astype(bf16), repeat)
    mine = rem(iota((rows, cols), 0), 4) == quo(iota((rows, cols), 1), quarter)
    return jnp.where(mine, tiled, 0.0).astype(bf16)


def band_weights(tiled, rows, cols, per_row, line_of):
    out_line = quo(iota((rows, cols), 0), per_row)
    off = line_of(iota((rows, cols), 1)) - out_line
    out = jnp.zeros((rows, cols), f32)
    for ky in range(3):
        out = jnp.where(off == ky, tiled[ky], out)
    return out.astype(bf16)


def edge_kernel(
    depth_hbm, slope_hbm, rain_hbm, dir_hbm, sar_hbm, *refs
):
    n_on = (len(refs) - 8) // 2
    on_hbm = refs[:n_on]
    first_swap_ref, second_swap_ref, sar_ref, *on_refs = refs[n_on : 2 * n_on + 3]
    depth_ref, slope_ref, rain_ref, dir_ref, sems = refs[2 * n_on + 3 :]
    even = rem(lax.axis_index("tx") * lax.axis_size("ty") + lax.axis_index("ty"), 2) == 0
    lines, px = sar_hbm.shape[1:]
    cols = depth_hbm.shape[1]
    h = SUBSTEPS
    pairs = (
        (depth_hbm, depth_ref), (slope_hbm, slope_ref), (rain_hbm, rain_ref), (dir_hbm, dir_ref),
        (sar_hbm, sar_ref), *zip(on_hbm, on_refs),
    )
    copies = [pltpu.make_async_copy(src, dst, sems.at[i]) for i, (src, dst) in enumerate(pairs)]
    for copy in copies:
        copy.start()
    for copy in copies[0:5]:
        copy.wait()
    fields = (
        depth_ref[...],
        runoff_coef * jnp.sqrt(slope_ref[...]),
        rain_ref[...],
        dir_ref[...].astype(f32),
    )
    zeros = jnp.zeros((8, px), f32)
    messages = []
    for at, lo, strip in (
        (lines - 16, 16 - HALO_LINES, lambda x: jnp.transpose(x[:, cols - LANES :], (1, 0))[LANES - h :]),
        (0, 0, lambda x: jnp.transpose(x[:, 0:LANES], (1, 0))[0:h]),
    ):
        image = [sar_ref[ch, at : at + 16, :].astype(f32)[lo : lo + HALO_LINES] for ch in range(2)]
        strips = [strip(x) for x in fields]
        messages.append(
            jnp.concatenate([jnp.concatenate(strips[0:2], 1), jnp.concatenate(strips[2:4], 1), *image, zeros], 0)
        )
    first, second = in_turn(even, *messages)
    first_swap_ref[...] = first.astype(bf16)
    second_swap_ref[...] = second.astype(bf16)
    for copy in copies[5:]:
        copy.wait()


def in_turn(even, to_next, to_previous):
    return jnp.where(even, to_next, to_previous), jnp.where(even, to_previous, to_next)


def from_turns(place, size, first, second):
    even = rem(place, 2) == 0
    previous = jnp.where(even, second, first)
    following = jnp.where(even, first, second)
    return jnp.where(place > 0, previous, 0.0), jnp.where(place < size - 1, following, 0.0)


def strips_of(message, keep):
    both = jnp.where(keep, message, 0.0)
    cols = both.shape[1] // 2
    return [both[0:8, 0:cols], both[0:8, cols:], both[8:16, 0:cols], both[8:16, cols:]]


def inner_kernel(
    devices, capacity,
    k1_ref, k2_ref, k3_ref, k4_ref, tile_ref, row_ref, sar_ref, gw_ref, cell_ref,
    w1_ref, w2_ref, w3_ref, w4_ref, perm_ref, extra_ref, frac_ref, slots_ref, e1_ref, e2_ref, e3_ref,
    t1_ref, t4_ref, s_ref, xa_ref, xb_ref, x3_ref, logit_ref, wnd_ref,
):
    rows = OUT_LINES * CH
    cols = IN_LINES * CH

    out_of = quo(iota((CH, OUT_LINES * cols), 1), cols)
    in_of = rem(iota((CH, OUT_LINES * cols), 1), cols) - iota((CH, OUT_LINES * cols), 0)
    spread = [(in_of == CH * (out_of + ky)).astype(bf16) for ky in range(3)]
    n1 = OUT_LINES * LANES
    group1 = quo(rem(iota((8, n1), 1), LANES), IN_LINES) == iota((8, n1), 0)
    line1 = rem(iota((8, n1), 1), IN_LINES) - quo(iota((8, n1), 1), LANES)
    spread1 = [(group1 & (line1 == ky)).astype(bf16) for ky in range(3)]
    tile4 = (rem(iota((CH, cols), 1), CH) == iota((CH, cols), 0)).astype(bf16)
    t1_ref[...] = jnp.zeros(t1_ref.shape, f32)
    t4_ref[...] = jnp.zeros(t4_ref.shape, f32)
    for ky in range(3):
        for kx in range(3):
            t1_ref[ky * 8 + 2 * kx : ky * 8 + 2 * kx + 2, :] = k1_ref[ky, kx].astype(f32)
        t4_ref[ky * 3 : ky * 3 + 3, :] = k4_ref[ky].astype(f32)
    wide1 = sum(dot_0(t1_ref[ky * 8 : ky * 8 + 8, :].astype(bf16), spread1[ky]) for ky in range(3))
    for i in range(OUT_LINES):
        w1_ref[i * CH : (i + 1) * CH, :] = wide1[:, i * LANES : (i + 1) * LANES].astype(bf16)
    for k_ref, w_ref in ((k2_ref, w2_ref), (k3_ref, w3_ref)):
        wide = sum(dot(k_ref[ky * 3 * CH : (ky + 1) * 3 * CH, :], spread[ky]) for ky in range(3))
        for kx in range(3):
            for i in range(OUT_LINES):
                w_ref[i * CH : (i + 1) * CH, kx * cols : (kx + 1) * cols] = wide[
                    kx * CH : (kx + 1) * CH, i * cols : (i + 1) * cols
                ].astype(bf16)
    wide4 = dot(t4_ref[...].astype(bf16), tile4)
    w4_ref[...] = jnp.concatenate(
        [
            band_weights(
                [jnp.broadcast_to(wide4[ky * 3 + kx : ky * 3 + kx + 1], (CH, cols)) for ky in range(3)],
                CH, cols, 1, lambda k: quo(k, CH),
            )
            for kx in range(3)
        ],
        0,
    )

    lines = tile_ref.shape[1]
    tile = tile_ref[...].astype(f32)
    same = iota((lines, lines), 0) == iota((lines, lines), 1)
    tile_sub = jnp.sum(jnp.where(same, jnp.broadcast_to(tile, (lines, lines)), 0.0), 1, keepdims=True)
    rival = (tile_sub == tile) & (iota((lines, lines), 0) < iota((lines, lines), 1))
    slot = tile * capacity + jnp.sum(jnp.where(rival, 1.0, 0.0), 0, keepdims=True)
    slots = slots_ref.shape[0]
    wnd_rows = CH * lines
    per_line = CH
    widen = (quo(iota((lines, wnd_rows), 1), per_line) == iota((lines, wnd_rows), 0)).astype(bf16)
    slot_wide = dot(jnp.broadcast_to(slot, (8, lines)).astype(bf16), widen)[0:1]
    place = slot_wide.astype(jnp.int32) * 4 + rem(quo(iota((1, wnd_rows), 1), 4), 4)
    perm = jnp.where(iota((slots, wnd_rows), 0) == place, 1.0, 0.0).astype(bf16)
    end = END_LINES * CH
    perm_ref[...] = jnp.concatenate([perm[:, 0:end], perm[:, wnd_rows - end :]], 1)

    row_of = dot(
        jnp.where(same, jnp.broadcast_to(row_ref[...].astype(f32), (lines, lines)), 0.0).astype(bf16),
        jnp.ones((lines, LANES), bf16),
    )
    perm_line = jnp.where(quo(iota((slots, lines), 0), 4) == slot.astype(jnp.int32), 1.0, 0.0).astype(bf16)
    row_own = dot(perm_line, row_of.astype(bf16))
    per_tile = 4 * capacity
    lane = iota((slots, LANES), 1)
    entry = rem(iota((slots, LANES), 0), per_tile)
    info = jnp.zeros((slots, LANES), f32)
    for turn, value in enumerate((row_own, of_right(row_own, per_tile), of_left(row_own, per_tile))):
        info = jnp.where(lane == turn * per_tile + entry, value, info)
    info = jnp.sum(info.reshape(devices, per_tile, LANES), 1, keepdims=True)
    at = iota((devices, 8, LANES), 1)
    extra_ref[...] = jnp.where(at == 2, info, 0.0).reshape(8 * devices, LANES)


    px = sar_ref.shape[2]
    for ch in range(2):
        s_ref[ch, 0:lines, :] = sar_ref[ch].astype(f32)
        s_ref[ch, lines:, :] = jnp.zeros((s_ref.shape[1] - lines, px), f32)
    total = xa_ref.shape[1] // CH
    xa_ref[:, (total - 2) * CH :, :] = jnp.zeros((3, 2 * CH, px), bf16)

    def put(ref, line, acc):
        feat = jnp.maximum(acc.astype(bf16), jnp.zeros(acc.shape, bf16))
        at = slice(line * CH, line * CH + rows)
        if len(ref.shape) == 2:
            ref[at, :] = feat
            return
        before, after = pixel_shifts(feat)
        ref[0, at, :] = before
        ref[1, at, :] = feat
        ref[2, at, :] = after

    full = (lines + 4) // OUT_LINES + 1
    for b in range(full):
        at = b * OUT_LINES
        x = jnp.concatenate([s_ref[0, at : at + IN_LINES, :], s_ref[1, at : at + IN_LINES, :]], 0)
        put(xa_ref, 1 + at, dot(w1_ref[...], image_columns(x)))
    for w_ref, src, dst, line, blocks in ((w2_ref, xa_ref, xb_ref, 2, full), (w3_ref, xb_ref, x3_ref, 3, full - 1)):
        for b in range(blocks):
            at = line + b * OUT_LINES
            x = src[:, (at - 1) * CH : (at - 1) * CH + cols, :].reshape(3 * cols, px)
            put(dst, at, dot(w_ref[...], x))

    def ends_of(lo, center):
        hi = lines - lo - 2
        return jnp.concatenate([center[at * CH : (at + 2) * CH, :] for at in (lo, hi)], 0)

    e1_ref[...] = ends_of(3, xa_ref.at[1])
    e2_ref[...] = ends_of(4, xb_ref.at[1])
    e3_ref[...] = ends_of(5, x3_ref)
    logit_ref[0:END_LINES, :] = jnp.zeros((END_LINES, px), f32)
    starts = [3 + b * OUT_LINES for b in range(full - 2)] + [lines - 5 - IN_LINES]
    for at in starts:
        sums = dot(w4_ref[...], x3_ref[at * CH : at * CH + cols, :])
        logit_ref[at + 1 : at + 1 + CH, :] = merged(sums, CH)
    frac_ref[...] = sigmoid(logit_ref[0:lines, :])
    quarter = wnd_ref.shape[1]
    group = 16

    def window_group(g, carry):
        at = pl.ds(pl.multiple_of(g * group + END_LINES, END_LINES), group)
        cov = gw_ref[at, :]
        obs = sigmoid(logit_ref[at, :]).astype(f32) * cov
        for i, sums in enumerate(line_windows(cell_ref[at, :], obs, cov, quarter)):
            wnd_ref[pl.ds(pl.multiple_of(g * (CH * group) + CH * i, CH), CH), :] = sums
        return carry

    lax.fori_loop(0, (lines - 2 * END_LINES) // group, window_group, 0)
    slots_ref[...] = dot(perm[:, end : wnd_rows - end], window_goods(wnd_ref[...]))


def of_right(x, per_tile):
    return jnp.concatenate([x[per_tile:], jnp.zeros((per_tile, x.shape[1]), x.dtype)], 0)


def of_left(x, per_tile):
    return jnp.concatenate([jnp.zeros((per_tile, x.shape[1]), x.dtype), x[: x.shape[0] - per_tile]], 0)


def ends_kernel(
    devices, capacity,
    first_swap_ref, second_swap_ref, w1_ref, w2_ref, w3_ref, w4_ref, perm_ref, extra_ref, frac_in, slots_in, e1_ref, e2_ref, e3_ref,
    sar_ref, gw_ref, cell_ref,
    frac_ref, send_ref,
    f_ref,
):
    lines, px = gw_ref.shape
    n_ty = lax.axis_size("ty")
    me = lax.axis_index("tx") * n_ty + lax.axis_index("ty")
    rows = OUT_LINES * CH
    above, below = from_turns(
        me, devices, first_swap_ref[16:32, :].astype(f32), second_swap_ref[16:32, :].astype(f32)
    )
    n = HALO_LINES

    pieces = []
    for ch in range(2):
        own = sar_ref[ch].astype(f32)
        pieces += [above[ch * n : (ch + 1) * n], own[0:n], own[lines - n :], below[ch * n : (ch + 1) * n]]
    x = image_columns(jnp.concatenate(pieces, 0))
    out_line = quo(iota((rows, px), 0), CH).astype(f32).astype(bf16)
    low = jnp.where(me == 0, n, 0)
    high = jnp.where(me == devices - 1, OUT_LINES - n, 2 * OUT_LINES)
    for layer, (w_ref, e_ref) in enumerate(((w1_ref, e1_ref), (w2_ref, e2_ref), (w3_ref, e3_ref)), 1):
        acc = dot(w_ref[...], x).astype(bf16)
        inside = (out_line >= (low - layer).astype(f32).astype(bf16)) & (out_line < (high + layer).astype(f32).astype(bf16))
        nil = jnp.zeros(acc.shape, bf16)
        feat = jnp.where(inside, jnp.maximum(acc, nil), nil)
        block = jnp.concatenate([feat[0 : 6 * CH], e_ref[...], feat[8 * CH :]], 0)
        if layer < 3:
            before, after = pixel_shifts(block)
            x = jnp.concatenate([before, block, after], 0)
    frac = sigmoid(merged(dot(w4_ref[...], block), CH)).astype(f32)
    f_ref[...] = frac_in[...].astype(f32)
    f_ref[0:6, :] = frac[0:6]
    f_ref[lines - 6 :, :] = frac[8:14]
    frac_ref[...] = f_ref[...].astype(bf16)
    quarter = slots_in.shape[1] // 4
    sums = []
    for at in (slice(0, END_LINES), slice(lines - END_LINES, lines)):
        cov = gw_ref[at, :]
        sums += line_windows(cell_ref[at, :], f_ref[at, :] * cov, cov, quarter)
    by_slot = slots_in[...] + dot(perm_ref[...], window_goods(jnp.concatenate(sums, 0)))

    per_tile = 4 * capacity
    slots, tile_cols = by_slot.shape
    h = SUBSTEPS
    entry = rem(iota((slots, LANES), 0), per_tile)
    here = quo(iota((slots, LANES), 1), h) == entry
    column = rem(quo(iota((slots, LANES), 0), per_tile), n_ty)
    source = iota((LANES, LANES), 0)
    spot = rem(iota((LANES, LANES), 1), h)

    def strip(x, first_lane, keep):
        take = ((spot + first_lane == source) & (source - first_lane < h)).astype(bf16)
        x = jnp.where(here & keep, dot(x.astype(bf16), take), 0.0)
        return jnp.sum(x.reshape(devices, per_tile, LANES), 1, keepdims=True)

    right_strip = strip(of_right(by_slot[:, 0:LANES], per_tile), 0, column < n_ty - 1)
    left_strip = strip(of_left(by_slot[:, tile_cols - LANES :], per_tile), LANES - h, column > 0)
    at = iota((devices, 8, LANES), 1)
    extra = extra_ref[...].reshape(devices, 8, LANES)
    extra = jnp.where(at == 0, right_strip, jnp.where(at == 1, left_strip, extra))
    halves = [by_slot[:, at : at + LANES].reshape(devices, per_tile, LANES) for at in range(0, tile_cols, LANES)]
    packed = jnp.concatenate([*halves, extra], 1)
    send_ref[...] = packed.reshape(send_ref.shape).astype(bf16)


def transposed(x):
    return jnp.transpose(x, (1, 0))


def level_kernel(
    devices,
    got_ref, first_swap_ref, second_swap_ref, depth_ref, slope_ref, rain_ref, dir_ref,
    level_ref, side_ref, first_ref, second_ref,
):
    tile_rows, tile_cols = depth_ref.shape
    h = SUBSTEPS
    halves = tile_cols // LANES
    n = (got_ref.shape[0] // devices - 8) // halves
    k = devices * n
    packed = got_ref[...].astype(f32).reshape(devices, halves * n + 8, LANES)
    main = jnp.concatenate([packed[:, i * n : (i + 1) * n].reshape(k, LANES) for i in range(halves)], 1)
    extra = packed[:, halves * n :]

    entry = rem(iota((k, LANES), 0), n)
    spread = quo(iota((k, LANES), 1), h) == entry

    def strip(r, first):
        rows = jnp.broadcast_to(extra[:, r : r + 1], (devices, n, LANES)).reshape(k, LANES)
        take = rem(iota((LANES, LANES), 0), h) + first == iota((LANES, LANES), 1)
        return dot(jnp.where(spread, rows, 0.0).astype(bf16), take.astype(bf16)).astype(bf16)

    lane = iota((1, k), 1)
    offset = rem(lane, 2) + tile_rows * rem(quo(lane, 2), 2)
    info = jnp.broadcast_to(extra[:, 2:3], (devices, n, LANES)).reshape(k, LANES)
    info = jnp.where(rem(iota((k, LANES), 1), n) == entry, info, 0.0).astype(bf16)
    turns = (quo(iota((LANES, LANES), 0), n) == iota((LANES, LANES), 1)).astype(bf16)
    lines = transposed(dot(info, turns))

    def placer(turn):
        target = lines[turn : turn + 1].astype(jnp.int32) + offset
        return jnp.where(iota((2 * tile_rows, k), 0) == target, 1.0, 0.0).astype(bf16)

    summed = dot(placer(0), main.astype(bf16))
    summed_side = dot(placer(1), strip(0, 0)) + dot(placer(2), strip(1, LANES - h))

    ty = lax.axis_index("ty")
    tx = lax.axis_index("tx")
    previous, following = from_turns(
        tx * lax.axis_size("ty") + ty, devices,
        first_swap_ref[0:16, :].astype(f32), second_swap_ref[0:16, :].astype(f32),
    )
    left = strips_of(previous, ty > 0)
    right = strips_of(following, ty < lax.axis_size("ty") - 1)
    gap = jnp.zeros((LANES - 2 * h, tile_rows), f32)
    depth_side, conv_side, rain_side, code_side = [
        transposed(jnp.concatenate([r, gap, l], 0)) for r, l in zip(right, left)
    ]

    def analysed(sums, depth):
        observed = sums[0:tile_rows]
        covered = sums[tile_rows:]
        wet = depth / (depth + wet_depth)
        innovation = (observed - covered * wet) / (covered + 1.0)
        return depth * jnp.exp(innovation)

    level = analysed(summed, depth_ref[...])
    level_ref[...] = level
    sides = (analysed(summed_side, depth_side), rain_side, conv_side, code_side)
    owns = (level, rain_ref, slope_ref, dir_ref)

    def end_rows(at):
        own = [x[at, :] for x in owns]
        own[2] = runoff_coef * jnp.sqrt(own[2])
        own[3] = own[3].astype(f32)
        return jnp.concatenate([jnp.concatenate([o, x[at]], 1) for o, x in zip(own, sides)], 0)

    for i, x in enumerate(sides):
        side_ref[i] = x
    first, second = in_turn(rem(tx, 2) == 0, end_rows(slice(tile_rows - h, tile_rows)), end_rows(slice(0, h)))
    first_ref[...] = first.astype(bf16)
    second_ref[...] = second.astype(bf16)


def substeps(level, rain, conv, code, rain_s, conv_s, m_ref, part_ref, up_ref, down_ref, chunk):
    rows, cols = level.shape
    h = SUBSTEPS
    for ref in (up_ref, down_ref):
        ref[0] = jnp.zeros(ref.shape[1:], f32)
        ref[1, 0:h, :] = jnp.zeros((h, cols), f32)
        ref[1, h + rows :, :] = jnp.zeros((h, cols), f32)
    part_ref[0] = level
    rain_s[...] = rain
    conv_s[...] = conv
    sides = (-1, 0, 1, -1, 1, -1, 0, 1)
    for direction, side in enumerate(sides):
        share = jnp.where(code == direction, conv, 0.0)
        m_ref[direction] = pltpu.roll(share, side % cols, 1) if side else share

    def level_at(buf, r, n):
        level = part_ref[buf, r : r + n, :]
        return level + up_ref[buf, h + r + 1 : h + r + 1 + n, :] + down_ref[buf, h + r - 1 : h + r - 1 + n, :]

    def substep(buf, new):
        for r in range(0, rows, chunk):
            level = level_at(buf, r, chunk)
            power = level * jnp.exp((2.0 / 3.0) * jnp.log(jnp.maximum(jnp.abs(level), 1e-30)))
            from_right = pltpu.roll(power, cols - 1, 1)
            from_left = pltpu.roll(power, 1, 1)
            m = [m_ref[d, r : r + chunk, :] for d in range(8)]
            up_ref[new, h + r : h + r + chunk, :] = m[0] * from_right + m[1] * power + m[2] * from_left
            down_ref[new, h + r : h + r + chunk, :] = m[5] * from_right + m[6] * power + m[7] * from_left
            part_ref[new, r : r + chunk, :] = (
                level + rain_s[r : r + chunk, :] - conv_s[r : r + chunk, :] * power
                + (m[3] * from_right + m[4] * from_left)
            )

    def substep_pair(i, carry):
        substep(0, 1)
        substep(1, 0)
        return carry

    lax.fori_loop(0, SUBSTEPS // 2, substep_pair, 0)
    return level_at


def flow_inner_kernel(level_ref, side_ref, slope_ref, dir_ref, rain_ref, out_ref, *scratch):
    rows, cols = level_ref.shape
    own = (level_ref[...], rain_ref[...], runoff_coef * jnp.sqrt(slope_ref[...]), dir_ref[...].astype(f32))
    level_at = substeps(*[jnp.concatenate([x, side_ref[i]], 1) for i, x in enumerate(own)], *scratch, 16)
    out_ref[...] = level_at(0, 0, rows)[:, 0:cols]


def flow_ends_kernel(inner_ref, level_ref, side_ref, slope_ref, dir_ref, rain_ref, first_swap_ref, second_swap_ref, out_ref, *scratch):
    rows, cols = level_ref.shape
    h = SUBSTEPS
    above, below = from_turns(
        lax.axis_index("tx"), lax.axis_size("tx"),
        first_swap_ref[...].astype(f32), second_swap_ref[...].astype(f32),
    )
    fields = []
    for i, ref in enumerate((level_ref, rain_ref, slope_ref, dir_ref)):
        ends = []
        for at in (slice(0, 2 * h), slice(rows - 2 * h, rows)):
            own = ref[at, :].astype(f32)
            if i == 2:
                own = runoff_coef * jnp.sqrt(own)
            ends.append(jnp.concatenate([own, side_ref[i, at, :]], 1))
        fields.append(jnp.concatenate([above[i * h : (i + 1) * h], *ends, below[i * h : (i + 1) * h]], 0))
    level_at = substeps(*fields, *scratch, 16)
    out_ref[h : rows - h, :] = inner_ref[h : rows - h, :]
    out_ref[0:h, :] = level_at(0, h, h)[:, 0:cols]
    out_ref[rows - h :, :] = level_at(0, 4 * h, h)[:, 0:cols]


def flow_scratch(rows, cols):
    return [
        pltpu.VMEM((rows, cols), f32),
        pltpu.VMEM((rows, cols), f32),
        pltpu.VMEM((8, rows, cols), f32),
        pltpu.VMEM((2, rows, cols), f32),
        pltpu.VMEM((2, rows + 2 * SUBSTEPS, cols), f32),
        pltpu.VMEM((2, rows + 2 * SUBSTEPS, cols), f32),
    ]


def hbm_specs(n):
    return [pl.BlockSpec(memory_space=pltpu.HBM)] * n


def vmem_specs(n):
    return [pl.BlockSpec(memory_space=pltpu.VMEM)] * n


def per_device(
    sar_image, kernel_first, kernel_second, kernel_third, kernel_last,
    geo_weight, cell_index, block_tile, block_row, depth, slope, flow_dir, rain,
):
    both = ("tx", "ty")
    devices = lax.axis_size(both)
    az_lines, range_px = geo_weight.shape
    tile_rows, tile_cols = depth.shape
    capacity = max(2, 2 * az_lines // devices)

    n_tx, n_ty = lax.axis_size("tx"), lax.axis_size("ty")

    def swaps(first, second, stride):
        size = devices // stride
        out = []
        for start, x in enumerate((first, second)):
            to = {}
            for place in range(start, size, 2):
                for k in range(stride):
                    i, j = place * stride + k, (place + 1) % size * stride + k
                    if place == size - 1 and stride > 1:
                        ends = (i, i ^ 1), (j, j ^ 1)
                    else:
                        ends = (i, j), (j, i)
                    to.update(ends)
            out.append(lax.ppermute(x, both, sorted(to.items())))
        return out

    params = pltpu.CompilerParams(vmem_limit_bytes=VMEM_LIMIT)
    message = pltpu.VMEM((32, range_px), bf16)
    handed = (
        sar_image,
        jnp.transpose(kernel_first, (2, 3, 1, 0)),
        jnp.transpose(kernel_second, (2, 3, 0, 1)).reshape(9 * CH, CH),
        jnp.transpose(kernel_third, (2, 3, 0, 1)).reshape(9 * CH, CH),
        jnp.transpose(kernel_last[0], (1, 2, 0)),
        block_tile.reshape(1, az_lines),
        block_row.reshape(1, az_lines),
        geo_weight,
        cell_index,
    )
    first, second, sar_image, *handed = pl.pallas_call(
        edge_kernel,
        out_shape=(message, message, *[pltpu.VMEM(x.shape, x.dtype) for x in handed]),
        in_specs=hbm_specs(4 + len(handed)),
        out_specs=tuple(vmem_specs(2 + len(handed))),
        scratch_shapes=[
            *[pltpu.VMEM(x.shape, x.dtype) for x in (depth, slope, rain, flow_dir)],
            pltpu.SemaphoreType.DMA((4 + len(handed),)),
        ],
        compiler_params=pltpu.CompilerParams(vmem_limit_bytes=VMEM_MOST),
        name="edges",
    )(depth, slope, rain, flow_dir, *handed)
    geo_weight, cell_index = handed[-2:]
    halo = swaps(first, second, 1)

    rows, cols = OUT_LINES * CH, IN_LINES * CH
    slots = devices * capacity * 4
    send_rows = tile_cols // LANES * 4 * capacity + 8
    full = (az_lines + 4) // OUT_LINES + 1
    feats = (full * OUT_LINES + 3) * CH
    blocks_in = (az_lines + IN_LINES, range_px)

    def cost(flops):
        return pl.CostEstimate(flops=flops, bytes_accessed=4_000_000, transcendentals=0)

    prepared = pl.pallas_call(
        functools.partial(inner_kernel, devices, capacity),
        out_shape=(
            jax.ShapeDtypeStruct((rows, LANES), bf16),
            jax.ShapeDtypeStruct((rows, 3 * cols), bf16),
            jax.ShapeDtypeStruct((rows, 3 * cols), bf16),
            jax.ShapeDtypeStruct((3 * CH, cols), bf16),
            jax.ShapeDtypeStruct((slots, 2 * END_LINES * CH), bf16),
            jax.ShapeDtypeStruct((8 * devices, LANES), f32),
            jax.ShapeDtypeStruct((az_lines, range_px), bf16),
            jax.ShapeDtypeStruct((slots, tile_cols), f32),
            *[jax.ShapeDtypeStruct((4 * CH, range_px), bf16)] * 3,
        ),
        in_specs=vmem_specs(9),
        out_specs=tuple(vmem_specs(11)),
        scratch_shapes=[
            pltpu.VMEM((24, CH), f32),
            pltpu.VMEM((16, CH), f32),
            pltpu.VMEM((2, *blocks_in), f32),
            pltpu.VMEM((3, feats, range_px), bf16),
            pltpu.VMEM((3, feats, range_px), bf16),
            pltpu.VMEM((feats, range_px), bf16),
            pltpu.VMEM(blocks_in, f32),
            pltpu.VMEM(((az_lines - 2 * END_LINES) * CH, tile_cols // 4), f32),
        ],
        compiler_params=params,
        cost_estimate=cost(8_000_000_000),
        name="inner",
    )(
        *handed[:-2], sar_image, geo_weight, cell_index,
    )
    fraction, send = pl.pallas_call(
        functools.partial(ends_kernel, devices, capacity),
        out_shape=(
            jax.ShapeDtypeStruct((az_lines, range_px), bf16),
            jax.ShapeDtypeStruct((devices * send_rows, LANES), bf16),
        ),
        in_specs=vmem_specs(16),
        out_specs=tuple(vmem_specs(2)),
        scratch_shapes=[pltpu.VMEM((az_lines, range_px), f32)],
        compiler_params=params,
        name="ends",
    )(*halo, *prepared, sar_image, geo_weight, cell_index)

    got = lax.all_to_all(
        send.reshape(devices, send_rows, LANES), both, split_axis=0, concat_axis=0, tiled=True
    ).reshape(devices * send_rows, LANES)

    wide_cols = tile_cols + LANES
    edge = jax.ShapeDtypeStruct((4 * SUBSTEPS, wide_cols), bf16)
    level, side, first, second = pl.pallas_call(
        functools.partial(level_kernel, devices),
        out_shape=(
            jax.ShapeDtypeStruct((tile_rows, tile_cols), f32),
            jax.ShapeDtypeStruct((4, tile_rows, LANES), f32),
            edge,
            edge,
        ),
        in_specs=vmem_specs(7),
        out_specs=tuple(vmem_specs(4)),
        compiler_params=params,
        name="level",
    )(got, *halo, depth, slope, rain, flow_dir)

    row_halo = swaps(first, second, n_ty)

    inner = pl.pallas_call(
        flow_inner_kernel,
        out_shape=jax.ShapeDtypeStruct((tile_rows, tile_cols), f32),
        in_specs=vmem_specs(5),
        out_specs=vmem_specs(1)[0],
        scratch_shapes=flow_scratch(tile_rows, wide_cols),
        compiler_params=params,
        cost_estimate=cost(5_000_000_000),
        name="flow_inner",
    )(level, side, slope, flow_dir, rain)
    level = pl.pallas_call(
        flow_ends_kernel,
        out_shape=jax.ShapeDtypeStruct((tile_rows, tile_cols), f32),
        in_specs=vmem_specs(8),
        out_specs=vmem_specs(1)[0],
        scratch_shapes=flow_scratch(6 * SUBSTEPS, wide_cols),
        compiler_params=params,
        name="flow_ends",
    )(inner, level, side, slope, flow_dir, rain, *row_halo)
    return (fraction, level)


def solution(mesh):
    placed = (
        P(None, ("tx", "ty"), None),
        P(),
        P(),
        P(),
        P(),
        P(("tx", "ty"), None),
        P(("tx", "ty"), None),
        P(("tx", "ty"), None),
        P(("tx", "ty"), None),
        P("tx", "ty"),
        P("tx", "ty"),
        P("tx", "ty"),
        P("tx", "ty"),
    )
    return jax.shard_map(
        per_device,
        mesh=mesh,
        in_specs=placed,
        out_specs=(P(("tx", "ty"), None), P("tx", "ty")),
        check_vma=False,
    )
```

```python
import functools

import jax
import jax.numpy as jnp
from jax import lax
from jax.experimental import pallas as pl
from jax.experimental.pallas import tpu as pltpu
from jax.sharding import PartitionSpec as P

WIN_ROWS = 2
SUBSTEPS = 8
CH = 16
OUT_LINES = 14
IN_LINES = OUT_LINES + 2
MID_LINES = 3
MID_IN = MID_LINES + 2
HALO_LINES = 4
END_LINES = 8
LANES = 128
VMEM_LIMIT = 48 * 1024 * 1024
VMEM_MOST = 60160 * 1024

wet_depth = 0.5
runoff_coef = 0.25
bf16 = jnp.bfloat16
f32 = jnp.float32


def iota(shape, dim):
    return lax.broadcasted_iota(jnp.int32, shape, dim)


def quo(x, n):
    assert n & (n - 1) == 0
    return lax.shift_right_logical(x, jnp.int32(n.bit_length() - 1)) if n > 1 else x


def rem(x, n):
    assert n & (n - 1) == 0
    return x & (n - 1)


def dot(a, b):
    return lax.dot_general(a, b, (((1,), (0,)), ((), ())), preferred_element_type=f32)


def dot_0(a, b):
    return lax.dot_general(a, b, (((0,), (0,)), ((), ())), preferred_element_type=f32)


def dot_t(a, b):
    return lax.dot_general(a, b, (((1,), (1,)), ((), ())), preferred_element_type=f32)


def pixel_shifts(x):
    rows, width = x.shape
    lane = iota((rows, LANES), 1)
    zero = jnp.zeros((rows, LANES), x.dtype)
    first = lane.astype(f32).astype(x.dtype) == 0
    last = (LANES - 1 - lane).astype(f32).astype(x.dtype) == 0
    before = pltpu.roll(x, 1, 1)
    after = pltpu.roll(x, width - 1, 1)
    before = jnp.concatenate([jnp.where(first, zero, before[:, 0:LANES]), before[:, LANES:]], 1)
    after = jnp.concatenate([after[:, : width - LANES], jnp.where(last, zero, after[:, width - LANES :])], 1)
    return before, after


def merged(sums, n):
    before, _ = pixel_shifts(sums[0:n])
    _, after = pixel_shifts(sums[2 * n : 3 * n])
    return before + sums[n : 2 * n] + after


def image_columns(x):
    before, after = pixel_shifts(x)
    pad = jnp.zeros((LANES - 3 * x.shape[0], x.shape[1]), f32)
    return jnp.concatenate([before, x, after, pad], 0).astype(bf16)


def mid_columns(before, x, after):
    return jnp.concatenate([before, x, after, x[0:CH]], 0)


def sigmoid(x):
    return (1.0 / (1.0 + jnp.exp(-x))).astype(bf16)


def line_windows(cell, obs, cov, quarter):
    px = cell.shape[1]
    kind = iota((CH, px), 0)
    kind_part = rem(kind, CH // 2).astype(f32).astype(bf16)
    sub = kind.astype(f32).astype(bf16)
    one = jnp.ones((CH, px), bf16)
    nil = jnp.zeros((CH, px), bf16)
    part = quo(cell, quarter).astype(f32)
    col = rem(cell, quarter).astype(f32)

    def spread_row(x, i):
        return jnp.broadcast_to(x[i : i + 1], (CH, px)).astype(bf16)

    out = []
    for i in range(cell.shape[0]):
        pair = [jnp.broadcast_to(x[i : i + 1], (CH // 2, px)) for x in (obs, cov)]
        value = jnp.concatenate(pair, 0).astype(bf16)
        left = jnp.where(kind_part == spread_row(part, i), value, nil)
        where_col = spread_row(col, i)
        hot = jnp.concatenate([jnp.where(sub + g * CH == where_col, one, nil) for g in range(quarter // CH)], 0)
        out.append(dot_t(left, hot))
    return out


def window_goods(sums):
    rows, quarter = sums.shape
    cols = 4 * quarter
    repeat = (rem(iota((quarter, cols), 1), quarter) == iota((quarter, cols), 0)).astype(bf16)
    tiled = dot(sums.astype(bf16), repeat)
    mine = rem(iota((rows, cols), 0), 4) == quo(iota((rows, cols), 1), quarter)
    return jnp.where(mine, tiled, 0.0).astype(bf16)


def band_weights(tiled, rows, cols, per_row, line_of):
    out_line = quo(iota((rows, cols), 0), per_row)
    off = line_of(iota((rows, cols), 1)) - out_line
    out = jnp.zeros((rows, cols), f32)
    for ky in range(3):
        out = jnp.where(off == ky, tiled[ky], out)
    return out.astype(bf16)


def edge_kernel(
    depth_hbm, slope_hbm, rain_hbm, dir_hbm, sar_hbm, *refs
):
    n_on = (len(refs) - 8) // 2
    on_hbm = refs[:n_on]
    first_swap_ref, second_swap_ref, sar_ref, *on_refs = refs[n_on : 2 * n_on + 3]
    depth_ref, slope_ref, rain_ref, dir_ref, sems = refs[2 * n_on + 3 :]
    even = rem(lax.axis_index("tx") * lax.axis_size("ty") + lax.axis_index("ty"), 2) == 0
    lines, px = sar_hbm.shape[1:]
    cols = depth_hbm.shape[1]
    h = SUBSTEPS
    pairs = (
        (depth_hbm, depth_ref), (slope_hbm, slope_ref), (rain_hbm, rain_ref), (dir_hbm, dir_ref),
        (sar_hbm, sar_ref), *zip(on_hbm, on_refs),
    )
    copies = [pltpu.make_async_copy(src, dst, sems.at[i]) for i, (src, dst) in enumerate(pairs)]
    for copy in copies:
        copy.start()
    for copy in copies[0:5]:
        copy.wait()
    fields = (
        depth_ref[...],
        runoff_coef * jnp.sqrt(slope_ref[...]),
        rain_ref[...],
        dir_ref[...].astype(f32),
    )
    zeros = jnp.zeros((8, px), f32)
    messages = []
    for at, lo, strip in (
        (lines - 16, 16 - HALO_LINES, lambda x: jnp.transpose(x[:, cols - LANES :], (1, 0))[LANES - h :]),
        (0, 0, lambda x: jnp.transpose(x[:, 0:LANES], (1, 0))[0:h]),
    ):
        image = [sar_ref[ch, at : at + 16, :].astype(f32)[lo : lo + HALO_LINES] for ch in range(2)]
        strips = [strip(x) for x in fields]
        messages.append(
            jnp.concatenate([jnp.concatenate(strips[0:2], 1), jnp.concatenate(strips[2:4], 1), *image, zeros], 0)
        )
    first, second = in_turn(even, *messages)
    first_swap_ref[...] = first.astype(bf16)
    second_swap_ref[...] = second.astype(bf16)
    for copy in copies[5:]:
        copy.wait()


def in_turn(even, to_next, to_previous):
    return jnp.where(even, to_next, to_previous), jnp.where(even, to_previous, to_next)


def from_turns(place, size, first, second):
    even = rem(place, 2) == 0
    previous = jnp.where(even, second, first)
    following = jnp.where(even, first, second)
    return jnp.where(place > 0, previous, 0.0), jnp.where(place < size - 1, following, 0.0)


def strips_of(message, keep):
    both = jnp.where(keep, message, 0.0)
    cols = both.shape[1] // 2
    return [both[0:8, 0:cols], both[0:8, cols:], both[8:16, 0:cols], both[8:16, cols:]]


def inner_kernel(
    devices, capacity,
    k1_ref, k2_ref, k3_ref, k4_ref, tile_ref, row_ref, sar_ref, gw_ref, cell_ref,
    w1_ref, w2_ref, w3_ref, w4_ref, perm_ref, extra_ref, frac_ref, slots_ref, e1_ref, e2_ref, e3_ref,
    t1_ref, t4_ref, s_ref, xa_ref, xb_ref, x3_ref, logit_ref, wnd_ref,
):
    rows = OUT_LINES * CH
    cols = IN_LINES * CH

    n2 = MID_LINES * cols
    spot2 = rem(iota((CH, n2), 1), cols) - iota((CH, n2), 0)
    line2 = quo(iota((CH, n2), 1), cols)
    n1 = OUT_LINES * LANES
    group1 = quo(rem(iota((8, n1), 1), LANES), IN_LINES) == iota((8, n1), 0)
    line1 = rem(iota((8, n1), 1), IN_LINES) - quo(iota((8, n1), 1), LANES)
    spread1 = [(group1 & (line1 == ky)).astype(bf16) for ky in range(3)]
    tile4 = (rem(iota((CH, cols), 1), CH) == iota((CH, cols), 0)).astype(bf16)
    t1_ref[...] = jnp.zeros(t1_ref.shape, f32)
    t4_ref[...] = jnp.zeros(t4_ref.shape, f32)
    for ky in range(3):
        for kx in range(3):
            t1_ref[ky * 8 + 2 * kx : ky * 8 + 2 * kx + 2, :] = k1_ref[ky, kx].astype(f32)
        t4_ref[ky * 3 : ky * 3 + 3, :] = k4_ref[ky].astype(f32)
    wide1 = sum(dot_0(t1_ref[ky * 8 : ky * 8 + 8, :].astype(bf16), spread1[ky]) for ky in range(3))
    for i in range(OUT_LINES):
        w1_ref[i * CH : (i + 1) * CH, :] = wide1[:, i * LANES : (i + 1) * LANES].astype(bf16)
    spread2 = [
        (spot2 == (kx * MID_IN + ky + line2) * CH).astype(bf16) for ky in range(3) for kx in range(3)
    ]
    for k_ref, w_ref in ((k2_ref, w2_ref), (k3_ref, w3_ref)):
        wide = sum(dot(k_ref[n * CH : (n + 1) * CH, :], spread2[n]) for n in range(9))
        for i in range(MID_LINES):
            w_ref[i * CH : (i + 1) * CH, :] = wide[:, i * cols : (i + 1) * cols].astype(bf16)
    wide4 = dot(t4_ref[...].astype(bf16), tile4)
    w4_ref[...] = jnp.concatenate(
        [
            band_weights(
                [jnp.broadcast_to(wide4[ky * 3 + kx : ky * 3 + kx + 1], (CH, cols)) for ky in range(3)],
                CH, cols, 1, lambda k: quo(k, CH),
            )
            for kx in range(3)
        ],
        0,
    )

    lines = tile_ref.shape[1]
    tile = tile_ref[...].astype(f32)
    same = iota((lines, lines), 0) == iota((lines, lines), 1)
    tile_sub = jnp.sum(jnp.where(same, jnp.broadcast_to(tile, (lines, lines)), 0.0), 1, keepdims=True)
    rival = (tile_sub == tile) & (iota((lines, lines), 0) < iota((lines, lines), 1))
    slot = tile * capacity + jnp.sum(jnp.where(rival, 1.0, 0.0), 0, keepdims=True)
    slots = slots_ref.shape[0]
    wnd_rows = CH * lines
    per_line = CH
    widen = (quo(iota((lines, wnd_rows), 1), per_line) == iota((lines, wnd_rows), 0)).astype(bf16)
    slot_wide = dot(jnp.broadcast_to(slot, (8, lines)).astype(bf16), widen)[0:1]
    place = slot_wide.astype(jnp.int32) * 4 + rem(quo(iota((1, wnd_rows), 1), 4), 4)
    perm = jnp.where(iota((slots, wnd_rows), 0) == place, 1.0, 0.0).astype(bf16)
    end = END_LINES * CH
    perm_ref[...] = jnp.concatenate([perm[:, 0:end], perm[:, wnd_rows - end :]], 1)

    row_of = dot(
        jnp.where(same, jnp.broadcast_to(row_ref[...].astype(f32), (lines, lines)), 0.0).astype(bf16),
        jnp.ones((lines, LANES), bf16),
    )
    perm_line = jnp.where(quo(iota((slots, lines), 0), 4) == slot.astype(jnp.int32), 1.0, 0.0).astype(bf16)
    row_own = dot(perm_line, row_of.astype(bf16))
    per_tile = 4 * capacity
    lane = iota((slots, LANES), 1)
    entry = rem(iota((slots, LANES), 0), per_tile)
    info = jnp.zeros((slots, LANES), f32)
    for turn, value in enumerate((row_own, of_right(row_own, per_tile), of_left(row_own, per_tile))):
        info = jnp.where(lane == turn * per_tile + entry, value, info)
    info = jnp.sum(info.reshape(devices, per_tile, LANES), 1, keepdims=True)
    at = iota((devices, 8, LANES), 1)
    extra_ref[...] = jnp.where(at == 2, info, 0.0).reshape(8 * devices, LANES)


    px = sar_ref.shape[2]
    for ch in range(2):
        s_ref[ch, 0:lines, :] = sar_ref[ch].astype(f32)
        s_ref[ch, lines:, :] = jnp.zeros((s_ref.shape[1] - lines, px), f32)
    total = xa_ref.shape[1] // CH
    xa_ref[:, (total - 2) * CH :, :] = jnp.zeros((3, 2 * CH, px), bf16)

    def put(ref, line, acc):
        rows = acc.shape[0]
        feat = jnp.maximum(acc.astype(bf16), jnp.zeros(acc.shape, bf16))
        at = slice(line * CH, line * CH + rows)
        if len(ref.shape) == 2:
            ref[at, :] = feat
            return
        before, after = pixel_shifts(feat)
        ref[0, at, :] = before
        ref[1, at, :] = feat
        ref[2, at, :] = after

    full = (lines + 4) // OUT_LINES + 1
    for b in range(full):
        at = b * OUT_LINES
        x = jnp.concatenate([s_ref[0, at : at + IN_LINES, :], s_ref[1, at : at + IN_LINES, :]], 0)
        put(xa_ref, 1 + at, dot(w1_ref[...], image_columns(x)))
    stop = lines - 4
    for w_ref, src, dst, line, end_line in ((w2_ref, xa_ref, xb_ref, 2, stop), (w3_ref, xb_ref, x3_ref, 3, stop - 1)):
        for at in range(line, end_line, MID_LINES):
            x = src[:, (at - 1) * CH : (at - 1 + MID_IN) * CH, :]
            put(dst, at, dot(w_ref[...], mid_columns(*[x[i] for i in range(3)])))

    def ends_of(lo, center):
        hi = lines - lo - 2
        return jnp.concatenate([center[at * CH : (at + 2) * CH, :] for at in (lo, hi)], 0)

    e1_ref[...] = ends_of(3, xa_ref.at[1])
    e2_ref[...] = ends_of(4, xb_ref.at[1])
    e3_ref[...] = ends_of(5, x3_ref)
    logit_ref[0:END_LINES, :] = jnp.zeros((END_LINES, px), f32)
    starts = [3 + b * OUT_LINES for b in range(full - 2)] + [lines - 5 - IN_LINES]
    for at in starts:
        sums = dot(w4_ref[...], x3_ref[at * CH : at * CH + cols, :])
        logit_ref[at + 1 : at + 1 + CH, :] = merged(sums, CH)
    frac_ref[...] = sigmoid(logit_ref[0:lines, :])
    quarter = wnd_ref.shape[1]
    group = 16

    def window_group(g, carry):
        at = pl.ds(pl.multiple_of(g * group + END_LINES, END_LINES), group)
        cov = gw_ref[at, :]
        obs = sigmoid(logit_ref[at, :]).astype(f32) * cov
        for i, sums in enumerate(line_windows(cell_ref[at, :], obs, cov, quarter)):
            wnd_ref[pl.ds(pl.multiple_of(g * (CH * group) + CH * i, CH), CH), :] = sums
        return carry

    lax.fori_loop(0, (lines - 2 * END_LINES) // group, window_group, 0)
    slots_ref[...] = dot(perm[:, end : wnd_rows - end], window_goods(wnd_ref[...]))


def of_right(x, per_tile):
    return jnp.concatenate([x[per_tile:], jnp.zeros((per_tile, x.shape[1]), x.dtype)], 0)


def of_left(x, per_tile):
    return jnp.concatenate([jnp.zeros((per_tile, x.shape[1]), x.dtype), x[: x.shape[0] - per_tile]], 0)


def ends_kernel(
    devices, capacity,
    first_swap_ref, second_swap_ref, w1_ref, w2_ref, w3_ref, w4_ref, perm_ref, extra_ref, frac_in, slots_in, e1_ref, e2_ref, e3_ref,
    sar_ref, gw_ref, cell_ref,
    frac_ref, send_ref,
    f_ref,
):
    lines, px = gw_ref.shape
    n_ty = lax.axis_size("ty")
    me = lax.axis_index("tx") * n_ty + lax.axis_index("ty")
    rows = OUT_LINES * CH
    above, below = from_turns(
        me, devices, first_swap_ref[16:32, :].astype(f32), second_swap_ref[16:32, :].astype(f32)
    )
    n = HALO_LINES

    pieces = []
    for ch in range(2):
        own = sar_ref[ch].astype(f32)
        pieces += [above[ch * n : (ch + 1) * n], own[0:n], own[lines - n :], below[ch * n : (ch + 1) * n]]
    x = image_columns(jnp.concatenate(pieces, 0))
    half = 6 * CH
    out_line = quo(iota((half, px), 0), CH).astype(f32).astype(bf16)
    nil = jnp.zeros((half, px), bf16)
    low = jnp.where(me == 0, n, 0)
    high = jnp.where(me == devices - 1, OUT_LINES - 8 - n, OUT_LINES)
    for layer, (w_ref, e_ref) in enumerate(((w1_ref, e1_ref), (w2_ref, e2_ref), (w3_ref, e3_ref)), 1):
        if layer == 1:
            acc = dot(w_ref[...], x).astype(bf16)
            top, bottom = acc[0:half], acc[8 * CH :]
        else:
            before, after = pixel_shifts(block)
            top, bottom = [
                jnp.concatenate(
                    [
                        dot(w_ref[...], mid_columns(*[y[at * CH : (at + MID_IN) * CH] for y in (before, block, after)]))
                        for at in (first, first + MID_LINES)
                    ],
                    0,
                ).astype(bf16)
                for first in (0, 8)
            ]
        top = jnp.where(out_line >= (low - layer).astype(f32).astype(bf16), jnp.maximum(top, nil), nil)
        bottom = jnp.where(out_line < (high + layer).astype(f32).astype(bf16), jnp.maximum(bottom, nil), nil)
        block = jnp.concatenate([top, e_ref[...], bottom], 0)
    frac = sigmoid(merged(dot(w4_ref[...], block), CH)).astype(f32)
    f_ref[...] = frac_in[...].astype(f32)
    f_ref[0:6, :] = frac[0:6]
    f_ref[lines - 6 :, :] = frac[8:14]
    frac_ref[...] = f_ref[...].astype(bf16)
    quarter = slots_in.shape[1] // 4
    sums = []
    for at in (slice(0, END_LINES), slice(lines - END_LINES, lines)):
        cov = gw_ref[at, :]
        sums += line_windows(cell_ref[at, :], f_ref[at, :] * cov, cov, quarter)
    by_slot = slots_in[...] + dot(perm_ref[...], window_goods(jnp.concatenate(sums, 0)))

    per_tile = 4 * capacity
    slots, tile_cols = by_slot.shape
    h = SUBSTEPS
    entry = rem(iota((slots, LANES), 0), per_tile)
    here = quo(iota((slots, LANES), 1), h) == entry
    column = rem(quo(iota((slots, LANES), 0), per_tile), n_ty)
    source = iota((LANES, LANES), 0)
    spot = rem(iota((LANES, LANES), 1), h)

    def strip(x, first_lane, keep):
        take = ((spot + first_lane == source) & (source - first_lane < h)).astype(bf16)
        x = jnp.where(here & keep, dot(x.astype(bf16), take), 0.0)
        return jnp.sum(x.reshape(devices, per_tile, LANES), 1, keepdims=True)

    right_strip = strip(of_right(by_slot[:, 0:LANES], per_tile), 0, column < n_ty - 1)
    left_strip = strip(of_left(by_slot[:, tile_cols - LANES :], per_tile), LANES - h, column > 0)
    at = iota((devices, 8, LANES), 1)
    extra = extra_ref[...].reshape(devices, 8, LANES)
    extra = jnp.where(at == 0, right_strip, jnp.where(at == 1, left_strip, extra))
    halves = [by_slot[:, at : at + LANES].reshape(devices, per_tile, LANES) for at in range(0, tile_cols, LANES)]
    packed = jnp.concatenate([*halves, extra], 1)
    send_ref[...] = packed.reshape(send_ref.shape).astype(bf16)


def transposed(x):
    return jnp.transpose(x, (1, 0))


def level_kernel(
    devices,
    got_ref, first_swap_ref, second_swap_ref, depth_ref, slope_ref, rain_ref, dir_ref,
    level_ref, side_ref, first_ref, second_ref,
):
    tile_rows, tile_cols = depth_ref.shape
    h = SUBSTEPS
    halves = tile_cols // LANES
    n = (got_ref.shape[0] // devices - 8) // halves
    k = devices * n
    packed = got_ref[...].astype(f32).reshape(devices, halves * n + 8, LANES)
    main = jnp.concatenate([packed[:, i * n : (i + 1) * n].reshape(k, LANES) for i in range(halves)], 1)
    extra = packed[:, halves * n :]

    entry = rem(iota((k, LANES), 0), n)
    spread = quo(iota((k, LANES), 1), h) == entry

    def strip(r, first):
        rows = jnp.broadcast_to(extra[:, r : r + 1], (devices, n, LANES)).reshape(k, LANES)
        take = rem(iota((LANES, LANES), 0), h) + first == iota((LANES, LANES), 1)
        return dot(jnp.where(spread, rows, 0.0).astype(bf16), take.astype(bf16)).astype(bf16)

    lane = iota((1, k), 1)
    offset = rem(lane, 2) + tile_rows * rem(quo(lane, 2), 2)
    info = jnp.broadcast_to(extra[:, 2:3], (devices, n, LANES)).reshape(k, LANES)
    info = jnp.where(rem(iota((k, LANES), 1), n) == entry, info, 0.0).astype(bf16)
    turns = (quo(iota((LANES, LANES), 0), n) == iota((LANES, LANES), 1)).astype(bf16)
    lines = transposed(dot(info, turns))

    def placer(turn):
        target = lines[turn : turn + 1].astype(jnp.int32) + offset
        return jnp.where(iota((2 * tile_rows, k), 0) == target, 1.0, 0.0).astype(bf16)

    summed = dot(placer(0), main.astype(bf16))
    summed_side = dot(placer(1), strip(0, 0)) + dot(placer(2), strip(1, LANES - h))

    ty = lax.axis_index("ty")
    tx = lax.axis_index("tx")
    previous, following = from_turns(
        tx * lax.axis_size("ty") + ty, devices,
        first_swap_ref[0:16, :].astype(f32), second_swap_ref[0:16, :].astype(f32),
    )
    left = strips_of(previous, ty > 0)
    right = strips_of(following, ty < lax.axis_size("ty") - 1)
    gap = jnp.zeros((LANES - 2 * h, tile_rows), f32)
    depth_side, conv_side, rain_side, code_side = [
        transposed(jnp.concatenate([r, gap, l], 0)) for r, l in zip(right, left)
    ]

    def analysed(sums, depth):
        observed = sums[0:tile_rows]
        covered = sums[tile_rows:]
        wet = depth / (depth + wet_depth)
        innovation = (observed - covered * wet) / (covered + 1.0)
        return depth * jnp.exp(innovation)

    level = analysed(summed, depth_ref[...])
    level_ref[...] = level
    sides = (analysed(summed_side, depth_side), rain_side, conv_side, code_side)
    owns = (level, rain_ref, slope_ref, dir_ref)

    def end_rows(at):
        own = [x[at, :] for x in owns]
        own[2] = runoff_coef * jnp.sqrt(own[2])
        own[3] = own[3].astype(f32)
        return jnp.concatenate([jnp.concatenate([o, x[at]], 1) for o, x in zip(own, sides)], 0)

    for i, x in enumerate(sides):
        side_ref[i] = x
    first, second = in_turn(rem(tx, 2) == 0, end_rows(slice(tile_rows - h, tile_rows)), end_rows(slice(0, h)))
    first_ref[...] = first.astype(bf16)
    second_ref[...] = second.astype(bf16)


def substeps(level, rain, conv, code, rain_s, conv_s, m_ref, part_ref, up_ref, down_ref, chunk):
    rows, cols = level.shape
    h = SUBSTEPS
    for ref in (up_ref, down_ref):
        ref[0] = jnp.zeros(ref.shape[1:], f32)
        ref[1, 0:h, :] = jnp.zeros((h, cols), f32)
        ref[1, h + rows :, :] = jnp.zeros((h, cols), f32)
    part_ref[0] = level
    rain_s[...] = rain
    conv_s[...] = conv
    sides = (-1, 0, 1, -1, 1, -1, 0, 1)
    for direction, side in enumerate(sides):
        share = jnp.where(code == direction, conv, 0.0)
        m_ref[direction] = pltpu.roll(share, side % cols, 1) if side else share

    def level_at(buf, r, n):
        level = part_ref[buf, r : r + n, :]
        return level + up_ref[buf, h + r + 1 : h + r + 1 + n, :] + down_ref[buf, h + r - 1 : h + r - 1 + n, :]

    def substep(buf, new):
        for r in range(0, rows, chunk):
            level = level_at(buf, r, chunk)
            power = level * jnp.exp((2.0 / 3.0) * jnp.log(jnp.maximum(jnp.abs(level), 1e-30)))
            from_right = pltpu.roll(power, cols - 1, 1)
            from_left = pltpu.roll(power, 1, 1)
            m = [m_ref[d, r : r + chunk, :] for d in range(8)]
            up_ref[new, h + r : h + r + chunk, :] = m[0] * from_right + m[1] * power + m[2] * from_left
            down_ref[new, h + r : h + r + chunk, :] = m[5] * from_right + m[6] * power + m[7] * from_left
            part_ref[new, r : r + chunk, :] = (
                level + rain_s[r : r + chunk, :] - conv_s[r : r + chunk, :] * power
                + (m[3] * from_right + m[4] * from_left)
            )

    def substep_pair(i, carry):
        substep(0, 1)
        substep(1, 0)
        return carry

    lax.fori_loop(0, SUBSTEPS // 2, substep_pair, 0)
    return level_at


def flow_inner_kernel(level_ref, side_ref, slope_ref, dir_ref, rain_ref, out_ref, *scratch):
    rows, cols = level_ref.shape
    own = (level_ref[...], rain_ref[...], runoff_coef * jnp.sqrt(slope_ref[...]), dir_ref[...].astype(f32))
    level_at = substeps(*[jnp.concatenate([x, side_ref[i]], 1) for i, x in enumerate(own)], *scratch, 16)
    out_ref[...] = level_at(0, 0, rows)[:, 0:cols]


def flow_ends_kernel(inner_ref, level_ref, side_ref, slope_ref, dir_ref, rain_ref, first_swap_ref, second_swap_ref, out_ref, *scratch):
    rows, cols = level_ref.shape
    h = SUBSTEPS
    above, below = from_turns(
        lax.axis_index("tx"), lax.axis_size("tx"),
        first_swap_ref[...].astype(f32), second_swap_ref[...].astype(f32),
    )
    fields = []
    for i, ref in enumerate((level_ref, rain_ref, slope_ref, dir_ref)):
        ends = []
        for at in (slice(0, 2 * h), slice(rows - 2 * h, rows)):
            own = ref[at, :].astype(f32)
            if i == 2:
                own = runoff_coef * jnp.sqrt(own)
            ends.append(jnp.concatenate([own, side_ref[i, at, :]], 1))
        fields.append(jnp.concatenate([above[i * h : (i + 1) * h], *ends, below[i * h : (i + 1) * h]], 0))
    level_at = substeps(*fields, *scratch, 16)
    out_ref[h : rows - h, :] = inner_ref[h : rows - h, :]
    out_ref[0:h, :] = level_at(0, h, h)[:, 0:cols]
    out_ref[rows - h :, :] = level_at(0, 4 * h, h)[:, 0:cols]


def flow_scratch(rows, cols):
    return [
        pltpu.VMEM((rows, cols), f32),
        pltpu.VMEM((rows, cols), f32),
        pltpu.VMEM((8, rows, cols), f32),
        pltpu.VMEM((2, rows, cols), f32),
        pltpu.VMEM((2, rows + 2 * SUBSTEPS, cols), f32),
        pltpu.VMEM((2, rows + 2 * SUBSTEPS, cols), f32),
    ]


def hbm_specs(n):
    return [pl.BlockSpec(memory_space=pltpu.HBM)] * n


def vmem_specs(n):
    return [pl.BlockSpec(memory_space=pltpu.VMEM)] * n


def per_device(
    sar_image, kernel_first, kernel_second, kernel_third, kernel_last,
    geo_weight, cell_index, block_tile, block_row, depth, slope, flow_dir, rain,
):
    both = ("tx", "ty")
    devices = lax.axis_size(both)
    az_lines, range_px = geo_weight.shape
    tile_rows, tile_cols = depth.shape
    capacity = max(2, 2 * az_lines // devices)

    n_tx, n_ty = lax.axis_size("tx"), lax.axis_size("ty")

    def swaps(first, second, stride):
        size = devices // stride
        out = []
        for start, x in enumerate((first, second)):
            to = {}
            for place in range(start, size, 2):
                for k in range(stride):
                    i, j = place * stride + k, (place + 1) % size * stride + k
                    if place == size - 1 and stride > 1:
                        ends = (i, i ^ 1), (j, j ^ 1)
                    else:
                        ends = (i, j), (j, i)
                    to.update(ends)
            out.append(lax.ppermute(x, both, sorted(to.items())))
        return out

    params = pltpu.CompilerParams(vmem_limit_bytes=VMEM_LIMIT)
    message = pltpu.VMEM((32, range_px), bf16)
    handed = (
        sar_image,
        jnp.transpose(kernel_first, (2, 3, 1, 0)),
        jnp.transpose(kernel_second, (2, 3, 0, 1)).reshape(9 * CH, CH),
        jnp.transpose(kernel_third, (2, 3, 0, 1)).reshape(9 * CH, CH),
        jnp.transpose(kernel_last[0], (1, 2, 0)),
        block_tile.reshape(1, az_lines),
        block_row.reshape(1, az_lines),
        geo_weight,
        cell_index,
    )
    first, second, sar_image, *handed = pl.pallas_call(
        edge_kernel,
        out_shape=(message, message, *[pltpu.VMEM(x.shape, x.dtype) for x in handed]),
        in_specs=hbm_specs(4 + len(handed)),
        out_specs=tuple(vmem_specs(2 + len(handed))),
        scratch_shapes=[
            *[pltpu.VMEM(x.shape, x.dtype) for x in (depth, slope, rain, flow_dir)],
            pltpu.SemaphoreType.DMA((4 + len(handed),)),
        ],
        compiler_params=pltpu.CompilerParams(vmem_limit_bytes=VMEM_MOST),
        name="edges",
    )(depth, slope, rain, flow_dir, *handed)
    geo_weight, cell_index = handed[-2:]
    halo = swaps(first, second, 1)

    rows, cols = OUT_LINES * CH, IN_LINES * CH
    slots = devices * capacity * 4
    send_rows = tile_cols // LANES * 4 * capacity + 8
    full = (az_lines + 4) // OUT_LINES + 1
    feats = (full * OUT_LINES + 3) * CH
    blocks_in = (az_lines + IN_LINES, range_px)

    def cost(flops):
        return pl.CostEstimate(flops=flops, bytes_accessed=4_000_000, transcendentals=0)

    prepared = pl.pallas_call(
        functools.partial(inner_kernel, devices, capacity),
        out_shape=(
            jax.ShapeDtypeStruct((rows, LANES), bf16),
            jax.ShapeDtypeStruct((MID_LINES * CH, cols), bf16),
            jax.ShapeDtypeStruct((MID_LINES * CH, cols), bf16),
            jax.ShapeDtypeStruct((3 * CH, cols), bf16),
            jax.ShapeDtypeStruct((slots, 2 * END_LINES * CH), bf16),
            jax.ShapeDtypeStruct((8 * devices, LANES), f32),
            jax.ShapeDtypeStruct((az_lines, range_px), bf16),
            jax.ShapeDtypeStruct((slots, tile_cols), f32),
            *[jax.ShapeDtypeStruct((4 * CH, range_px), bf16)] * 3,
        ),
        in_specs=vmem_specs(9),
        out_specs=tuple(vmem_specs(11)),
        scratch_shapes=[
            pltpu.VMEM((24, CH), f32),
            pltpu.VMEM((16, CH), f32),
            pltpu.VMEM((2, *blocks_in), f32),
            pltpu.VMEM((3, feats, range_px), bf16),
            pltpu.VMEM((3, feats, range_px), bf16),
            pltpu.VMEM((feats, range_px), bf16),
            pltpu.VMEM(blocks_in, f32),
            pltpu.VMEM(((az_lines - 2 * END_LINES) * CH, tile_cols // 4), f32),
        ],
        compiler_params=params,
        cost_estimate=cost(8_000_000_000),
        name="inner",
    )(
        *handed[:-2], sar_image, geo_weight, cell_index,
    )
    fraction, send = pl.pallas_call(
        functools.partial(ends_kernel, devices, capacity),
        out_shape=(
            jax.ShapeDtypeStruct((az_lines, range_px), bf16),
            jax.ShapeDtypeStruct((devices * send_rows, LANES), bf16),
        ),
        in_specs=vmem_specs(16),
        out_specs=tuple(vmem_specs(2)),
        scratch_shapes=[pltpu.VMEM((az_lines, range_px), f32)],
        compiler_params=params,
        name="ends",
    )(*halo, *prepared, sar_image, geo_weight, cell_index)

    got = lax.all_to_all(
        send.reshape(devices, send_rows, LANES), both, split_axis=0, concat_axis=0, tiled=True
    ).reshape(devices * send_rows, LANES)

    wide_cols = tile_cols + LANES
    edge = jax.ShapeDtypeStruct((4 * SUBSTEPS, wide_cols), bf16)
    level, side, first, second = pl.pallas_call(
        functools.partial(level_kernel, devices),
        out_shape=(
            jax.ShapeDtypeStruct((tile_rows, tile_cols), f32),
            jax.ShapeDtypeStruct((4, tile_rows, LANES), f32),
            edge,
            edge,
        ),
        in_specs=vmem_specs(7),
        out_specs=tuple(vmem_specs(4)),
        compiler_params=params,
        name="level",
    )(got, *halo, depth, slope, rain, flow_dir)

    row_halo = swaps(first, second, n_ty)

    inner = pl.pallas_call(
        flow_inner_kernel,
        out_shape=jax.ShapeDtypeStruct((tile_rows, tile_cols), f32),
        in_specs=vmem_specs(5),
        out_specs=vmem_specs(1)[0],
        scratch_shapes=flow_scratch(tile_rows, wide_cols),
        compiler_params=params,
        cost_estimate=cost(5_000_000_000),
        name="flow_inner",
    )(level, side, slope, flow_dir, rain)
    level = pl.pallas_call(
        flow_ends_kernel,
        out_shape=jax.ShapeDtypeStruct((tile_rows, tile_cols), f32),
        in_specs=vmem_specs(8),
        out_specs=vmem_specs(1)[0],
        scratch_shapes=flow_scratch(6 * SUBSTEPS, wide_cols),
        compiler_params=params,
        name="flow_ends",
    )(inner, level, side, slope, flow_dir, rain, *row_halo)
    return (fraction, level)


def solution(mesh):
    placed = (
        P(None, ("tx", "ty"), None),
        P(),
        P(),
        P(),
        P(),
        P(("tx", "ty"), None),
        P(("tx", "ty"), None),
        P(("tx", "ty"), None),
        P(("tx", "ty"), None),
        P("tx", "ty"),
        P("tx", "ty"),
        P("tx", "ty"),
        P("tx", "ty"),
    )
    return jax.shard_map(
        per_device,
        mesh=mesh,
        in_specs=placed,
        out_specs=(P(("tx", "ty"), None), P("tx", "ty")),
        check_vma=False,
    )
```

```python
import functools

import jax
import jax.numpy as jnp
from jax import lax
from jax.experimental import pallas as pl
from jax.experimental.pallas import tpu as pltpu
from jax.sharding import PartitionSpec as P

WIN_ROWS = 2
SUBSTEPS = 8
CH = 16
OUT_LINES = 14
IN_LINES = OUT_LINES + 2
MID_LINES = 3
MID_IN = MID_LINES + 2
HALO_LINES = 4
END_LINES = 8
LANES = 128
VMEM_LIMIT = 48 * 1024 * 1024
VMEM_MOST = 60160 * 1024

wet_depth = 0.5
runoff_coef = 0.25
bf16 = jnp.bfloat16
f32 = jnp.float32


def iota(shape, dim):
    return lax.broadcasted_iota(jnp.int32, shape, dim)


def quo(x, n):
    assert n & (n - 1) == 0
    return lax.shift_right_logical(x, jnp.int32(n.bit_length() - 1)) if n > 1 else x


def rem(x, n):
    assert n & (n - 1) == 0
    return x & (n - 1)


def dot(a, b):
    return lax.dot_general(a, b, (((1,), (0,)), ((), ())), preferred_element_type=f32)


def dot_0(a, b):
    return lax.dot_general(a, b, (((0,), (0,)), ((), ())), preferred_element_type=f32)


def dot_t(a, b):
    return lax.dot_general(a, b, (((1,), (1,)), ((), ())), preferred_element_type=f32)


def pixel_shifts(x):
    rows, width = x.shape
    lane = iota((rows, LANES), 1)
    zero = jnp.zeros((rows, LANES), x.dtype)
    first = lane.astype(f32).astype(x.dtype) == 0
    last = (LANES - 1 - lane).astype(f32).astype(x.dtype) == 0
    before = pltpu.roll(x, 1, 1)
    after = pltpu.roll(x, width - 1, 1)
    before = jnp.concatenate([jnp.where(first, zero, before[:, 0:LANES]), before[:, LANES:]], 1)
    after = jnp.concatenate([after[:, : width - LANES], jnp.where(last, zero, after[:, width - LANES :])], 1)
    return before, after


def merged(sums, n):
    before, _ = pixel_shifts(sums[0:n])
    _, after = pixel_shifts(sums[2 * n : 3 * n])
    return before + sums[n : 2 * n] + after


def image_columns(x):
    before, after = pixel_shifts(x)
    pad = jnp.zeros((LANES - 3 * x.shape[0], x.shape[1]), f32)
    return jnp.concatenate([before, x, after, pad], 0).astype(bf16)


def mid_columns(before, x, after):
    return jnp.concatenate([before, x, after, x[0:CH]], 0)


def sigmoid(x):
    return (1.0 / (1.0 + jnp.exp(-x))).astype(bf16)


def line_windows(cell, obs, cov, quarter):
    px = cell.shape[1]
    kind = iota((CH, px), 0)
    kind_part = rem(kind, CH // 2).astype(f32).astype(bf16)
    sub = kind.astype(f32).astype(bf16)
    one = jnp.ones((CH, px), bf16)
    nil = jnp.zeros((CH, px), bf16)
    part = quo(cell, quarter).astype(f32)
    col = rem(cell, quarter).astype(f32)

    def spread_row(x, i):
        return jnp.broadcast_to(x[i : i + 1], (CH, px)).astype(bf16)

    out = []
    for i in range(cell.shape[0]):
        pair = [jnp.broadcast_to(x[i : i + 1], (CH // 2, px)) for x in (obs, cov)]
        value = jnp.concatenate(pair, 0).astype(bf16)
        left = jnp.where(kind_part == spread_row(part, i), value, nil)
        where_col = spread_row(col, i)
        hot = jnp.concatenate([jnp.where(sub + g * CH == where_col, one, nil) for g in range(quarter // CH)], 0)
        out.append(dot_t(left, hot))
    return out


def window_goods(sums):
    rows, quarter = sums.shape
    cols = 4 * quarter
    repeat = (rem(iota((quarter, cols), 1), quarter) == iota((quarter, cols), 0)).astype(bf16)
    tiled = dot(sums.astype(bf16), repeat)
    mine = rem(iota((rows, cols), 0), 4) == quo(iota((rows, cols), 1), quarter)
    return jnp.where(mine, tiled, 0.0).astype(bf16)


def band_weights(tiled, rows, cols, per_row, line_of):
    out_line = quo(iota((rows, cols), 0), per_row)
    off = line_of(iota((rows, cols), 1)) - out_line
    out = jnp.zeros((rows, cols), f32)
    for ky in range(3):
        out = jnp.where(off == ky, tiled[ky], out)
    return out.astype(bf16)


def edge_kernel(
    depth_hbm, slope_hbm, rain_hbm, dir_hbm, sar_hbm, *refs
):
    n_on = (len(refs) - 8) // 2
    on_hbm = refs[:n_on]
    first_swap_ref, second_swap_ref, sar_ref, *on_refs = refs[n_on : 2 * n_on + 3]
    depth_ref, slope_ref, rain_ref, dir_ref, sems = refs[2 * n_on + 3 :]
    even = rem(lax.axis_index("tx") * lax.axis_size("ty") + lax.axis_index("ty"), 2) == 0
    lines, px = sar_hbm.shape[1:]
    cols = depth_hbm.shape[1]
    h = SUBSTEPS
    pairs = (
        (depth_hbm, depth_ref), (slope_hbm, slope_ref), (rain_hbm, rain_ref), (dir_hbm, dir_ref),
        (sar_hbm, sar_ref), *zip(on_hbm, on_refs),
    )
    copies = [pltpu.make_async_copy(src, dst, sems.at[i]) for i, (src, dst) in enumerate(pairs)]
    for copy in copies:
        copy.start()
    for copy in copies[0:5]:
        copy.wait()
    fields = (
        depth_ref[...],
        runoff_coef * jnp.sqrt(slope_ref[...]),
        rain_ref[...],
        dir_ref[...].astype(f32),
    )
    zeros = jnp.zeros((8, px), f32)
    messages = []
    for at, lo, strip in (
        (lines - 16, 16 - HALO_LINES, lambda x: jnp.transpose(x[:, cols - LANES :], (1, 0))[LANES - h :]),
        (0, 0, lambda x: jnp.transpose(x[:, 0:LANES], (1, 0))[0:h]),
    ):
        image = [sar_ref[ch, at : at + 16, :].astype(f32)[lo : lo + HALO_LINES] for ch in range(2)]
        strips = [strip(x) for x in fields]
        messages.append(
            jnp.concatenate([jnp.concatenate(strips[0:2], 1), jnp.concatenate(strips[2:4], 1), *image, zeros], 0)
        )
    first, second = in_turn(even, *messages)
    first_swap_ref[...] = first.astype(bf16)
    second_swap_ref[...] = second.astype(bf16)
    for copy in copies[5:]:
        copy.wait()


def in_turn(even, to_next, to_previous):
    return jnp.where(even, to_next, to_previous), jnp.where(even, to_previous, to_next)


def from_turns(place, size, first, second):
    even = rem(place, 2) == 0
    previous = jnp.where(even, second, first)
    following = jnp.where(even, first, second)
    return jnp.where(place > 0, previous, 0.0), jnp.where(place < size - 1, following, 0.0)


def strips_of(message, keep):
    both = jnp.where(keep, message, 0.0)
    cols = both.shape[1] // 2
    return [both[0:8, 0:cols], both[0:8, cols:], both[8:16, 0:cols], both[8:16, cols:]]


def inner_kernel(
    devices, capacity,
    k1_ref, k2_ref, k3_ref, k4_ref, tile_ref, row_ref, sar_ref, gw_ref, cell_ref,
    w1_ref, w2_ref, w3_ref, w4_ref, perm_ref, extra_ref, frac_ref, slots_ref, e1_ref, e2_ref, e3_ref,
    t1_ref, t4_ref, s_ref, xa_ref, xb_ref, x3_ref, logit_ref, wnd_ref,
):
    rows = OUT_LINES * CH
    cols = IN_LINES * CH

    n2 = MID_LINES * cols
    spot2 = rem(iota((CH, n2), 1), cols) - iota((CH, n2), 0)
    line2 = quo(iota((CH, n2), 1), cols)
    n1 = OUT_LINES * LANES
    group1 = quo(rem(iota((8, n1), 1), LANES), IN_LINES) == iota((8, n1), 0)
    line1 = rem(iota((8, n1), 1), IN_LINES) - quo(iota((8, n1), 1), LANES)
    spread1 = [(group1 & (line1 == ky)).astype(bf16) for ky in range(3)]
    tile4 = (rem(iota((CH, cols), 1), CH) == iota((CH, cols), 0)).astype(bf16)
    t1_ref[...] = jnp.zeros(t1_ref.shape, f32)
    t4_ref[...] = jnp.zeros(t4_ref.shape, f32)
    for ky in range(3):
        for kx in range(3):
            t1_ref[ky * 8 + 2 * kx : ky * 8 + 2 * kx + 2, :] = k1_ref[ky, kx].astype(f32)
        t4_ref[ky * 3 : ky * 3 + 3, :] = k4_ref[ky].astype(f32)
    wide1 = sum(dot_0(t1_ref[ky * 8 : ky * 8 + 8, :].astype(bf16), spread1[ky]) for ky in range(3))
    for i in range(OUT_LINES):
        w1_ref[i * CH : (i + 1) * CH, :] = wide1[:, i * LANES : (i + 1) * LANES].astype(bf16)
    spread2 = [
        (spot2 == (kx * MID_IN + ky + line2) * CH).astype(bf16) for ky in range(3) for kx in range(3)
    ]
    for k_ref, w_ref in ((k2_ref, w2_ref), (k3_ref, w3_ref)):
        wide = sum(dot(k_ref[n * CH : (n + 1) * CH, :], spread2[n]) for n in range(9))
        for i in range(MID_LINES):
            w_ref[i * CH : (i + 1) * CH, :] = wide[:, i * cols : (i + 1) * cols].astype(bf16)
    wide4 = dot(t4_ref[...].astype(bf16), tile4)
    w4_ref[...] = jnp.concatenate(
        [
            band_weights(
                [jnp.broadcast_to(wide4[ky * 3 + kx : ky * 3 + kx + 1], (CH, cols)) for ky in range(3)],
                CH, cols, 1, lambda k: quo(k, CH),
            )
            for kx in range(3)
        ],
        0,
    )

    lines = tile_ref.shape[1]
    tile = tile_ref[...].astype(f32)
    same = iota((lines, lines), 0) == iota((lines, lines), 1)
    tile_sub = jnp.sum(jnp.where(same, jnp.broadcast_to(tile, (lines, lines)), 0.0), 1, keepdims=True)
    rival = (tile_sub == tile) & (iota((lines, lines), 0) < iota((lines, lines), 1))
    slot = tile * capacity + jnp.sum(jnp.where(rival, 1.0, 0.0), 0, keepdims=True)
    slots = slots_ref.shape[0]
    wnd_rows = CH * lines
    per_line = CH
    widen = (quo(iota((lines, wnd_rows), 1), per_line) == iota((lines, wnd_rows), 0)).astype(bf16)
    slot_wide = dot(jnp.broadcast_to(slot, (8, lines)).astype(bf16), widen)[0:1]
    place = slot_wide.astype(jnp.int32) * 4 + rem(quo(iota((1, wnd_rows), 1), 4), 4)
    perm = jnp.where(iota((slots, wnd_rows), 0) == place, 1.0, 0.0).astype(bf16)
    end = END_LINES * CH
    perm_ref[...] = jnp.concatenate([perm[:, 0:end], perm[:, wnd_rows - end :]], 1)

    row_of = dot(
        jnp.where(same, jnp.broadcast_to(row_ref[...].astype(f32), (lines, lines)), 0.0).astype(bf16),
        jnp.ones((lines, LANES), bf16),
    )
    perm_line = jnp.where(quo(iota((slots, lines), 0), 4) == slot.astype(jnp.int32), 1.0, 0.0).astype(bf16)
    row_own = dot(perm_line, row_of.astype(bf16))
    per_tile = 4 * capacity
    lane = iota((slots, LANES), 1)
    entry = rem(iota((slots, LANES), 0), per_tile)
    info = jnp.zeros((slots, LANES), f32)
    for turn, value in enumerate((row_own, of_right(row_own, per_tile), of_left(row_own, per_tile))):
        info = jnp.where(lane == turn * per_tile + entry, value, info)
    info = jnp.sum(info.reshape(devices, per_tile, LANES), 1, keepdims=True)
    at = iota((devices, 8, LANES), 1)
    extra_ref[...] = jnp.where(at == 2, info, 0.0).reshape(8 * devices, LANES)


    px = sar_ref.shape[2]
    for ch in range(2):
        s_ref[ch, 0:lines, :] = sar_ref[ch].astype(f32)
        s_ref[ch, lines:, :] = jnp.zeros((s_ref.shape[1] - lines, px), f32)
    total = xa_ref.shape[1] // CH
    xa_ref[:, (total - 2) * CH :, :] = jnp.zeros((3, 2 * CH, px), bf16)

    def put(ref, line, acc):
        rows = acc.shape[0]
        feat = jnp.maximum(acc.astype(bf16), jnp.zeros(acc.shape, bf16))
        at = slice(line * CH, line * CH + rows)
        if len(ref.shape) == 2:
            ref[at, :] = feat
            return
        before, after = pixel_shifts(feat)
        ref[0, at, :] = before
        ref[1, at, :] = feat
        ref[2, at, :] = after

    full = (lines + 4) // OUT_LINES + 1
    for b in range(full):
        at = b * OUT_LINES
        x = jnp.concatenate([s_ref[0, at : at + IN_LINES, :], s_ref[1, at : at + IN_LINES, :]], 0)
        put(xa_ref, 1 + at, dot(w1_ref[...], image_columns(x)))
    stop = lines - 4
    for w_ref, src, dst, line, end_line in ((w2_ref, xa_ref, xb_ref, 2, stop), (w3_ref, xb_ref, x3_ref, 3, stop - 1)):
        for at in range(line, end_line, MID_LINES):
            x = src[:, (at - 1) * CH : (at - 1 + MID_IN) * CH, :]
            put(dst, at, dot(w_ref[...], mid_columns(*[x[i] for i in range(3)])))

    def ends_of(lo, center):
        hi = lines - lo - 2
        return jnp.concatenate([center[at * CH : (at + 2) * CH, :] for at in (lo, hi)], 0)

    e1_ref[...] = ends_of(3, xa_ref.at[1])
    e2_ref[...] = ends_of(4, xb_ref.at[1])
    e3_ref[...] = ends_of(5, x3_ref)
    logit_ref[0:END_LINES, :] = jnp.zeros((END_LINES, px), f32)
    starts = [3 + b * OUT_LINES for b in range(full - 2)] + [lines - 5 - IN_LINES]
    for at in starts:
        sums = dot(w4_ref[...], x3_ref[at * CH : at * CH + cols, :])
        logit_ref[at + 1 : at + 1 + CH, :] = merged(sums, CH)
    frac_ref[...] = sigmoid(logit_ref[0:lines, :])
    quarter = wnd_ref.shape[1]
    group = 16

    for g in range((lines - 2 * END_LINES) // group):
        at = slice(g * group + END_LINES, (g + 1) * group + END_LINES)
        cov = gw_ref[at, :]
        obs = sigmoid(logit_ref[at, :]).astype(f32) * cov
        for i, sums in enumerate(line_windows(cell_ref[at, :], obs, cov, quarter)):
            to = CH * (group * g + i)
            wnd_ref[to : to + CH, :] = sums
    slots_ref[...] = dot(perm[:, end : wnd_rows - end], window_goods(wnd_ref[...]))


def of_right(x, per_tile):
    return jnp.concatenate([x[per_tile:], jnp.zeros((per_tile, x.shape[1]), x.dtype)], 0)


def of_left(x, per_tile):
    return jnp.concatenate([jnp.zeros((per_tile, x.shape[1]), x.dtype), x[: x.shape[0] - per_tile]], 0)


def ends_kernel(
    devices, capacity,
    first_swap_ref, second_swap_ref, w1_ref, w2_ref, w3_ref, w4_ref, perm_ref, extra_ref, frac_in, slots_in, e1_ref, e2_ref, e3_ref,
    sar_ref, gw_ref, cell_ref,
    frac_ref, send_ref,
    f_ref,
):
    lines, px = gw_ref.shape
    n_ty = lax.axis_size("ty")
    me = lax.axis_index("tx") * n_ty + lax.axis_index("ty")
    rows = OUT_LINES * CH
    above, below = from_turns(
        me, devices, first_swap_ref[16:32, :].astype(f32), second_swap_ref[16:32, :].astype(f32)
    )
    n = HALO_LINES

    pieces = []
    for ch in range(2):
        own = sar_ref[ch].astype(f32)
        pieces += [above[ch * n : (ch + 1) * n], own[0:n], own[lines - n :], below[ch * n : (ch + 1) * n]]
    x = image_columns(jnp.concatenate(pieces, 0))
    half = 6 * CH
    out_line = quo(iota((half, px), 0), CH).astype(f32).astype(bf16)
    nil = jnp.zeros((half, px), bf16)
    low = jnp.where(me == 0, n, 0)
    high = jnp.where(me == devices - 1, OUT_LINES - 8 - n, OUT_LINES)
    for layer, (w_ref, e_ref) in enumerate(((w1_ref, e1_ref), (w2_ref, e2_ref), (w3_ref, e3_ref)), 1):
        if layer == 1:
            acc = dot(w_ref[...], x).astype(bf16)
            top, bottom = acc[0:half], acc[8 * CH :]
        else:
            before, after = pixel_shifts(block)
            top, bottom = [
                jnp.concatenate(
                    [
                        dot(w_ref[...], mid_columns(*[y[at * CH : (at + MID_IN) * CH] for y in (before, block, after)]))
                        for at in (first, first + MID_LINES)
                    ],
                    0,
                ).astype(bf16)
                for first in (0, 8)
            ]
        top = jnp.where(out_line >= (low - layer).astype(f32).astype(bf16), jnp.maximum(top, nil), nil)
        bottom = jnp.where(out_line < (high + layer).astype(f32).astype(bf16), jnp.maximum(bottom, nil), nil)
        block = jnp.concatenate([top, e_ref[...], bottom], 0)
    frac = sigmoid(merged(dot(w4_ref[...], block), CH)).astype(f32)
    f_ref[...] = frac_in[...].astype(f32)
    f_ref[0:6, :] = frac[0:6]
    f_ref[lines - 6 :, :] = frac[8:14]
    frac_ref[...] = f_ref[...].astype(bf16)
    quarter = slots_in.shape[1] // 4
    sums = []
    for at in (slice(0, END_LINES), slice(lines - END_LINES, lines)):
        cov = gw_ref[at, :]
        sums += line_windows(cell_ref[at, :], f_ref[at, :] * cov, cov, quarter)
    by_slot = slots_in[...] + dot(perm_ref[...], window_goods(jnp.concatenate(sums, 0)))

    per_tile = 4 * capacity
    slots, tile_cols = by_slot.shape
    h = SUBSTEPS
    entry = rem(iota((slots, LANES), 0), per_tile)
    here = quo(iota((slots, LANES), 1), h) == entry
    column = rem(quo(iota((slots, LANES), 0), per_tile), n_ty)
    source = iota((LANES, LANES), 0)
    spot = rem(iota((LANES, LANES), 1), h)

    def strip(x, first_lane, keep):
        take = ((spot + first_lane == source) & (source - first_lane < h)).astype(bf16)
        x = jnp.where(here & keep, dot(x.astype(bf16), take), 0.0)
        return jnp.sum(x.reshape(devices, per_tile, LANES), 1, keepdims=True)

    right_strip = strip(of_right(by_slot[:, 0:LANES], per_tile), 0, column < n_ty - 1)
    left_strip = strip(of_left(by_slot[:, tile_cols - LANES :], per_tile), LANES - h, column > 0)
    at = iota((devices, 8, LANES), 1)
    extra = extra_ref[...].reshape(devices, 8, LANES)
    extra = jnp.where(at == 0, right_strip, jnp.where(at == 1, left_strip, extra))
    halves = [by_slot[:, at : at + LANES].reshape(devices, per_tile, LANES) for at in range(0, tile_cols, LANES)]
    packed = jnp.concatenate([*halves, extra], 1)
    send_ref[...] = packed.reshape(send_ref.shape).astype(bf16)


def transposed(x):
    return jnp.transpose(x, (1, 0))


def level_kernel(
    devices,
    got_ref, first_swap_ref, second_swap_ref, depth_ref, slope_ref, rain_ref, dir_ref,
    level_ref, side_ref, first_ref, second_ref,
):
    tile_rows, tile_cols = depth_ref.shape
    h = SUBSTEPS
    halves = tile_cols // LANES
    n = (got_ref.shape[0] // devices - 8) // halves
    k = devices * n
    packed = got_ref[...].astype(f32).reshape(devices, halves * n + 8, LANES)
    main = jnp.concatenate([packed[:, i * n : (i + 1) * n].reshape(k, LANES) for i in range(halves)], 1)
    extra = packed[:, halves * n :]

    entry = rem(iota((k, LANES), 0), n)
    spread = quo(iota((k, LANES), 1), h) == entry

    def strip(r, first):
        rows = jnp.broadcast_to(extra[:, r : r + 1], (devices, n, LANES)).reshape(k, LANES)
        take = rem(iota((LANES, LANES), 0), h) + first == iota((LANES, LANES), 1)
        return dot(jnp.where(spread, rows, 0.0).astype(bf16), take.astype(bf16)).astype(bf16)

    lane = iota((1, k), 1)
    offset = rem(lane, 2) + tile_rows * rem(quo(lane, 2), 2)
    info = jnp.broadcast_to(extra[:, 2:3], (devices, n, LANES)).reshape(k, LANES)
    info = jnp.where(rem(iota((k, LANES), 1), n) == entry, info, 0.0).astype(bf16)
    turns = (quo(iota((LANES, LANES), 0), n) == iota((LANES, LANES), 1)).astype(bf16)
    lines = transposed(dot(info, turns))

    def placer(turn):
        target = lines[turn : turn + 1].astype(jnp.int32) + offset
        return jnp.where(iota((2 * tile_rows, k), 0) == target, 1.0, 0.0).astype(bf16)

    summed = dot(placer(0), main.astype(bf16))
    summed_side = dot(placer(1), strip(0, 0)) + dot(placer(2), strip(1, LANES - h))

    ty = lax.axis_index("ty")
    tx = lax.axis_index("tx")
    previous, following = from_turns(
        tx * lax.axis_size("ty") + ty, devices,
        first_swap_ref[0:16, :].astype(f32), second_swap_ref[0:16, :].astype(f32),
    )
    left = strips_of(previous, ty > 0)
    right = strips_of(following, ty < lax.axis_size("ty") - 1)
    gap = jnp.zeros((LANES - 2 * h, tile_rows), f32)
    depth_side, conv_side, rain_side, code_side = [
        transposed(jnp.concatenate([r, gap, l], 0)) for r, l in zip(right, left)
    ]

    def analysed(sums, depth):
        observed = sums[0:tile_rows]
        covered = sums[tile_rows:]
        wet = depth / (depth + wet_depth)
        innovation = (observed - covered * wet) / (covered + 1.0)
        return depth * jnp.exp(innovation)

    level = analysed(summed, depth_ref[...])
    level_ref[...] = level
    sides = (analysed(summed_side, depth_side), rain_side, conv_side, code_side)
    owns = (level, rain_ref, slope_ref, dir_ref)

    def end_rows(at):
        own = [x[at, :] for x in owns]
        own[2] = runoff_coef * jnp.sqrt(own[2])
        own[3] = own[3].astype(f32)
        return jnp.concatenate([jnp.concatenate([o, x[at]], 1) for o, x in zip(own, sides)], 0)

    for i, x in enumerate(sides):
        side_ref[i] = x
    first, second = in_turn(rem(tx, 2) == 0, end_rows(slice(tile_rows - h, tile_rows)), end_rows(slice(0, h)))
    first_ref[...] = first.astype(bf16)
    second_ref[...] = second.astype(bf16)


def substeps(level, rain, conv, code, rain_s, conv_s, m_ref, part_ref, up_ref, down_ref, chunk):
    rows, cols = level.shape
    h = SUBSTEPS
    for ref in (up_ref, down_ref):
        ref[0] = jnp.zeros(ref.shape[1:], f32)
        ref[1, 0:h, :] = jnp.zeros((h, cols), f32)
        ref[1, h + rows :, :] = jnp.zeros((h, cols), f32)
    part_ref[0] = level
    rain_s[...] = rain
    conv_s[...] = conv
    sides = (-1, 0, 1, -1, 1, -1, 0, 1)
    for direction, side in enumerate(sides):
        share = jnp.where(code == direction, conv, 0.0)
        m_ref[direction] = pltpu.roll(share, side % cols, 1) if side else share

    def level_at(buf, r, n):
        level = part_ref[buf, r : r + n, :]
        return level + up_ref[buf, h + r + 1 : h + r + 1 + n, :] + down_ref[buf, h + r - 1 : h + r - 1 + n, :]

    def substep(buf, new):
        for r in range(0, rows, chunk):
            level = level_at(buf, r, chunk)
            power = level * jnp.exp((2.0 / 3.0) * jnp.log(jnp.maximum(jnp.abs(level), 1e-30)))
            from_right = pltpu.roll(power, cols - 1, 1)
            from_left = pltpu.roll(power, 1, 1)
            m = [m_ref[d, r : r + chunk, :] for d in range(8)]
            up_ref[new, h + r : h + r + chunk, :] = m[0] * from_right + m[1] * power + m[2] * from_left
            down_ref[new, h + r : h + r + chunk, :] = m[5] * from_right + m[6] * power + m[7] * from_left
            part_ref[new, r : r + chunk, :] = (
                level + rain_s[r : r + chunk, :] - conv_s[r : r + chunk, :] * power
                + (m[3] * from_right + m[4] * from_left)
            )

    def substep_pair(i, carry):
        substep(0, 1)
        substep(1, 0)
        return carry

    lax.fori_loop(0, SUBSTEPS // 2, substep_pair, 0)
    return level_at


def flow_inner_kernel(level_ref, side_ref, slope_ref, dir_ref, rain_ref, out_ref, *scratch):
    rows, cols = level_ref.shape
    own = (level_ref[...], rain_ref[...], runoff_coef * jnp.sqrt(slope_ref[...]), dir_ref[...].astype(f32))
    level_at = substeps(*[jnp.concatenate([x, side_ref[i]], 1) for i, x in enumerate(own)], *scratch, 16)
    out_ref[...] = level_at(0, 0, rows)[:, 0:cols]


def flow_ends_kernel(inner_ref, level_ref, side_ref, slope_ref, dir_ref, rain_ref, first_swap_ref, second_swap_ref, out_ref, *scratch):
    rows, cols = level_ref.shape
    h = SUBSTEPS
    above, below = from_turns(
        lax.axis_index("tx"), lax.axis_size("tx"),
        first_swap_ref[...].astype(f32), second_swap_ref[...].astype(f32),
    )
    fields = []
    for i, ref in enumerate((level_ref, rain_ref, slope_ref, dir_ref)):
        ends = []
        for at in (slice(0, 2 * h), slice(rows - 2 * h, rows)):
            own = ref[at, :].astype(f32)
            if i == 2:
                own = runoff_coef * jnp.sqrt(own)
            ends.append(jnp.concatenate([own, side_ref[i, at, :]], 1))
        fields.append(jnp.concatenate([above[i * h : (i + 1) * h], *ends, below[i * h : (i + 1) * h]], 0))
    level_at = substeps(*fields, *scratch, 16)
    out_ref[h : rows - h, :] = inner_ref[h : rows - h, :]
    out_ref[0:h, :] = level_at(0, h, h)[:, 0:cols]
    out_ref[rows - h :, :] = level_at(0, 4 * h, h)[:, 0:cols]


def flow_scratch(rows, cols):
    return [
        pltpu.VMEM((rows, cols), f32),
        pltpu.VMEM((rows, cols), f32),
        pltpu.VMEM((8, rows, cols), f32),
        pltpu.VMEM((2, rows, cols), f32),
        pltpu.VMEM((2, rows + 2 * SUBSTEPS, cols), f32),
        pltpu.VMEM((2, rows + 2 * SUBSTEPS, cols), f32),
    ]


def hbm_specs(n):
    return [pl.BlockSpec(memory_space=pltpu.HBM)] * n


def vmem_specs(n):
    return [pl.BlockSpec(memory_space=pltpu.VMEM)] * n


def per_device(
    sar_image, kernel_first, kernel_second, kernel_third, kernel_last,
    geo_weight, cell_index, block_tile, block_row, depth, slope, flow_dir, rain,
):
    both = ("tx", "ty")
    devices = lax.axis_size(both)
    az_lines, range_px = geo_weight.shape
    tile_rows, tile_cols = depth.shape
    capacity = max(2, 2 * az_lines // devices)

    n_tx, n_ty = lax.axis_size("tx"), lax.axis_size("ty")

    def swaps(first, second, stride):
        size = devices // stride
        out = []
        for start, x in ((1, second), (0, first)):
            to = {}
            for place in range(start, size, 2):
                for k in range(stride):
                    i, j = place * stride + k, (place + 1) % size * stride + k
                    if place == size - 1 and stride > 1:
                        ends = (i, i ^ 1), (j, j ^ 1)
                    else:
                        ends = (i, j), (j, i)
                    to.update(ends)
            out.append(lax.ppermute(x, both, sorted(to.items())))
        return out[::-1]

    params = pltpu.CompilerParams(vmem_limit_bytes=VMEM_LIMIT)
    message = pltpu.VMEM((32, range_px), bf16)
    handed = (
        sar_image,
        jnp.transpose(kernel_first, (2, 3, 1, 0)),
        jnp.transpose(kernel_second, (2, 3, 0, 1)).reshape(9 * CH, CH),
        jnp.transpose(kernel_third, (2, 3, 0, 1)).reshape(9 * CH, CH),
        jnp.transpose(kernel_last[0], (1, 2, 0)),
        block_tile.reshape(1, az_lines),
        block_row.reshape(1, az_lines),
        geo_weight,
        cell_index,
    )
    first, second, sar_image, *handed = pl.pallas_call(
        edge_kernel,
        out_shape=(message, message, *[pltpu.VMEM(x.shape, x.dtype) for x in handed]),
        in_specs=hbm_specs(4 + len(handed)),
        out_specs=tuple(vmem_specs(2 + len(handed))),
        scratch_shapes=[
            *[pltpu.VMEM(x.shape, x.dtype) for x in (depth, slope, rain, flow_dir)],
            pltpu.SemaphoreType.DMA((4 + len(handed),)),
        ],
        compiler_params=pltpu.CompilerParams(vmem_limit_bytes=VMEM_MOST),
        name="edges",
    )(depth, slope, rain, flow_dir, *handed)
    geo_weight, cell_index = handed[-2:]
    halo = swaps(first, second, 1)

    rows, cols = OUT_LINES * CH, IN_LINES * CH
    slots = devices * capacity * 4
    send_rows = tile_cols // LANES * 4 * capacity + 8
    full = (az_lines + 4) // OUT_LINES + 1
    feats = (full * OUT_LINES + 3) * CH
    blocks_in = (az_lines + IN_LINES, range_px)

    def cost(flops):
        return pl.CostEstimate(flops=flops, bytes_accessed=4_000_000, transcendentals=0)

    prepared = pl.pallas_call(
        functools.partial(inner_kernel, devices, capacity),
        out_shape=(
            jax.ShapeDtypeStruct((rows, LANES), bf16),
            jax.ShapeDtypeStruct((MID_LINES * CH, cols), bf16),
            jax.ShapeDtypeStruct((MID_LINES * CH, cols), bf16),
            jax.ShapeDtypeStruct((3 * CH, cols), bf16),
            jax.ShapeDtypeStruct((slots, 2 * END_LINES * CH), bf16),
            jax.ShapeDtypeStruct((8 * devices, LANES), f32),
            jax.ShapeDtypeStruct((az_lines, range_px), bf16),
            jax.ShapeDtypeStruct((slots, tile_cols), f32),
            *[jax.ShapeDtypeStruct((4 * CH, range_px), bf16)] * 3,
        ),
        in_specs=vmem_specs(9),
        out_specs=tuple(vmem_specs(11)),
        scratch_shapes=[
            pltpu.VMEM((24, CH), f32),
            pltpu.VMEM((16, CH), f32),
            pltpu.VMEM((2, *blocks_in), f32),
            pltpu.VMEM((3, feats, range_px), bf16),
            pltpu.VMEM((3, feats, range_px), bf16),
            pltpu.VMEM((feats, range_px), bf16),
            pltpu.VMEM(blocks_in, f32),
            pltpu.VMEM(((az_lines - 2 * END_LINES) * CH, tile_cols // 4), f32),
        ],
        compiler_params=params,
        cost_estimate=cost(8_000_000_000),
        name="inner",
    )(
        *handed[:-2], sar_image, geo_weight, cell_index,
    )
    fraction, send = pl.pallas_call(
        functools.partial(ends_kernel, devices, capacity),
        out_shape=(
            jax.ShapeDtypeStruct((az_lines, range_px), bf16),
            jax.ShapeDtypeStruct((devices * send_rows, LANES), bf16),
        ),
        in_specs=vmem_specs(16),
        out_specs=tuple(vmem_specs(2)),
        scratch_shapes=[pltpu.VMEM((az_lines, range_px), f32)],
        compiler_params=params,
        name="ends",
    )(*halo, *prepared, sar_image, geo_weight, cell_index)

    got = lax.all_to_all(
        send.reshape(devices, send_rows, LANES), both, split_axis=0, concat_axis=0, tiled=True
    ).reshape(devices * send_rows, LANES)

    wide_cols = tile_cols + LANES
    edge = jax.ShapeDtypeStruct((4 * SUBSTEPS, wide_cols), bf16)
    level, side, first, second = pl.pallas_call(
        functools.partial(level_kernel, devices),
        out_shape=(
            jax.ShapeDtypeStruct((tile_rows, tile_cols), f32),
            jax.ShapeDtypeStruct((4, tile_rows, LANES), f32),
            edge,
            edge,
        ),
        in_specs=vmem_specs(7),
        out_specs=tuple(vmem_specs(4)),
        compiler_params=params,
        name="level",
    )(got, *halo, depth, slope, rain, flow_dir)

    row_halo = swaps(first, second, n_ty)

    inner = pl.pallas_call(
        flow_inner_kernel,
        out_shape=jax.ShapeDtypeStruct((tile_rows, tile_cols), f32),
        in_specs=vmem_specs(5),
        out_specs=vmem_specs(1)[0],
        scratch_shapes=flow_scratch(tile_rows, wide_cols),
        compiler_params=params,
        cost_estimate=cost(5_000_000_000),
        name="flow_inner",
    )(level, side, slope, flow_dir, rain)
    level = pl.pallas_call(
        flow_ends_kernel,
        out_shape=jax.ShapeDtypeStruct((tile_rows, tile_cols), f32),
        in_specs=vmem_specs(8),
        out_specs=vmem_specs(1)[0],
        scratch_shapes=flow_scratch(6 * SUBSTEPS, wide_cols),
        compiler_params=params,
        name="flow_ends",
    )(inner, level, side, slope, flow_dir, rain, *row_halo)
    return (fraction, level)


def solution(mesh):
    placed = (
        P(None, ("tx", "ty"), None),
        P(),
        P(),
        P(),
        P(),
        P(("tx", "ty"), None),
        P(("tx", "ty"), None),
        P(("tx", "ty"), None),
        P(("tx", "ty"), None),
        P("tx", "ty"),
        P("tx", "ty"),
        P("tx", "ty"),
        P("tx", "ty"),
    )
    return jax.shard_map(
        per_device,
        mesh=mesh,
        in_specs=placed,
        out_specs=(P(("tx", "ty"), None), P("tx", "ty")),
        check_vma=False,
    )
```

```python
import functools

import jax
import jax.numpy as jnp
from jax import lax
from jax.experimental import pallas as pl
from jax.experimental.pallas import tpu as pltpu
from jax.sharding import PartitionSpec as P

WIN_ROWS = 2
SUBSTEPS = 8
CH = 16
OUT_LINES = 14
IN_LINES = OUT_LINES + 2
MID_LINES = 3
MID_IN = MID_LINES + 2
HALO_LINES = 4
END_LINES = 8
LANES = 128
VMEM_LIMIT = 48 * 1024 * 1024
VMEM_MOST = 60160 * 1024

wet_depth = 0.5
runoff_coef = 0.25
bf16 = jnp.bfloat16
f32 = jnp.float32


def iota(shape, dim):
    return lax.broadcasted_iota(jnp.int32, shape, dim)


def quo(x, n):
    assert n & (n - 1) == 0
    return lax.shift_right_logical(x, jnp.int32(n.bit_length() - 1)) if n > 1 else x


def rem(x, n):
    assert n & (n - 1) == 0
    return x & (n - 1)


def dot(a, b):
    return lax.dot_general(a, b, (((1,), (0,)), ((), ())), preferred_element_type=f32)


def dot_0(a, b):
    return lax.dot_general(a, b, (((0,), (0,)), ((), ())), preferred_element_type=f32)


def dot_t(a, b):
    return lax.dot_general(a, b, (((1,), (1,)), ((), ())), preferred_element_type=f32)


def pixel_shifts(x):
    rows, width = x.shape
    lane = iota((rows, LANES), 1)
    zero = jnp.zeros((rows, LANES), x.dtype)
    first = lane.astype(f32).astype(x.dtype) == 0
    last = (LANES - 1 - lane).astype(f32).astype(x.dtype) == 0
    before = pltpu.roll(x, 1, 1)
    after = pltpu.roll(x, width - 1, 1)
    before = jnp.concatenate([jnp.where(first, zero, before[:, 0:LANES]), before[:, LANES:]], 1)
    after = jnp.concatenate([after[:, : width - LANES], jnp.where(last, zero, after[:, width - LANES :])], 1)
    return before, after


def merged(sums, n):
    before, _ = pixel_shifts(sums[0:n])
    _, after = pixel_shifts(sums[2 * n : 3 * n])
    return before + sums[n : 2 * n] + after


def image_columns(x):
    before, after = pixel_shifts(x)
    pad = jnp.zeros((LANES - 3 * x.shape[0], x.shape[1]), f32)
    return jnp.concatenate([before, x, after, pad], 0).astype(bf16)


def mid_columns(before, x, after):
    return jnp.concatenate([before, x, after, x[0:CH]], 0)


def sigmoid(x):
    return (1.0 / (1.0 + jnp.exp(-x))).astype(bf16)


def line_windows(cell, obs, cov, quarter):
    px = cell.shape[1]
    kind = iota((CH, px), 0)
    kind_part = rem(kind, CH // 2).astype(f32).astype(bf16)
    sub = kind.astype(f32).astype(bf16)
    one = jnp.ones((CH, px), bf16)
    nil = jnp.zeros((CH, px), bf16)
    part = quo(cell, quarter).astype(f32)
    col = rem(cell, quarter).astype(f32)

    def spread_row(x, i):
        return jnp.broadcast_to(x[i : i + 1], (CH, px)).astype(bf16)

    out = []
    for i in range(cell.shape[0]):
        pair = [jnp.broadcast_to(x[i : i + 1], (CH // 2, px)) for x in (obs, cov)]
        value = jnp.concatenate(pair, 0).astype(bf16)
        left = jnp.where(kind_part == spread_row(part, i), value, nil)
        where_col = spread_row(col, i)
        hot = jnp.concatenate([jnp.where(sub + g * CH == where_col, one, nil) for g in range(quarter // CH)], 0)
        out.append(dot_t(left, hot))
    return out


def window_goods(sums):
    rows, quarter = sums.shape
    cols = 4 * quarter
    repeat = (rem(iota((quarter, cols), 1), quarter) == iota((quarter, cols), 0)).astype(bf16)
    tiled = dot(sums.astype(bf16), repeat)
    mine = rem(iota((rows, cols), 0), 4) == quo(iota((rows, cols), 1), quarter)
    return jnp.where(mine, tiled, 0.0).astype(bf16)


def band_weights(tiled, rows, cols, per_row, line_of):
    out_line = quo(iota((rows, cols), 0), per_row)
    off = line_of(iota((rows, cols), 1)) - out_line
    out = jnp.zeros((rows, cols), f32)
    for ky in range(3):
        out = jnp.where(off == ky, tiled[ky], out)
    return out.astype(bf16)


def edge_kernel(
    depth_hbm, slope_hbm, rain_hbm, dir_hbm, sar_hbm, *refs
):
    n_on = (len(refs) - 8) // 2
    on_hbm = refs[:n_on]
    first_swap_ref, second_swap_ref, sar_ref, *on_refs = refs[n_on : 2 * n_on + 3]
    depth_ref, slope_ref, rain_ref, dir_ref, sems = refs[2 * n_on + 3 :]
    even = rem(lax.axis_index("tx") * lax.axis_size("ty") + lax.axis_index("ty"), 2) == 0
    lines, px = sar_hbm.shape[1:]
    cols = depth_hbm.shape[1]
    h = SUBSTEPS
    pairs = (
        (depth_hbm, depth_ref), (slope_hbm, slope_ref), (rain_hbm, rain_ref), (dir_hbm, dir_ref),
        (sar_hbm, sar_ref), *zip(on_hbm, on_refs),
    )
    copies = [pltpu.make_async_copy(src, dst, sems.at[i]) for i, (src, dst) in enumerate(pairs)]
    for copy in copies:
        copy.start()
    for copy in copies[0:5]:
        copy.wait()
    fields = (
        depth_ref[...],
        runoff_coef * jnp.sqrt(slope_ref[...]),
        rain_ref[...],
        dir_ref[...].astype(f32),
    )
    zeros = jnp.zeros((8, px), f32)
    messages = []
    for at, lo, strip in (
        (lines - 16, 16 - HALO_LINES, lambda x: jnp.transpose(x[:, cols - LANES :], (1, 0))[LANES - h :]),
        (0, 0, lambda x: jnp.transpose(x[:, 0:LANES], (1, 0))[0:h]),
    ):
        image = [sar_ref[ch, at : at + 16, :].astype(f32)[lo : lo + HALO_LINES] for ch in range(2)]
        strips = [strip(x) for x in fields]
        messages.append(
            jnp.concatenate([jnp.concatenate(strips[0:2], 1), jnp.concatenate(strips[2:4], 1), *image, zeros], 0)
        )
    first, second = in_turn(even, *messages)
    first_swap_ref[...] = first.astype(bf16)
    second_swap_ref[...] = second.astype(bf16)
    for copy in copies[5:]:
        copy.wait()


def in_turn(even, to_next, to_previous):
    return jnp.where(even, to_next, to_previous), jnp.where(even, to_previous, to_next)


def from_turns(place, size, first, second):
    even = rem(place, 2) == 0
    previous = jnp.where(even, second, first)
    following = jnp.where(even, first, second)
    return jnp.where(place > 0, previous, 0.0), jnp.where(place < size - 1, following, 0.0)


def strips_of(message, keep):
    both = jnp.where(keep, message, 0.0)
    cols = both.shape[1] // 2
    return [both[0:8, 0:cols], both[0:8, cols:], both[8:16, 0:cols], both[8:16, cols:]]


def inner_kernel(
    devices, capacity,
    k1_ref, k2_ref, k3_ref, k4_ref, tile_ref, row_ref, sar_ref, gw_ref, cell_ref,
    w1_ref, w2_ref, w3_ref, w4_ref, perm_ref, extra_ref, frac_ref, slots_ref, e1_ref, e2_ref, e3_ref,
    t1_ref, t4_ref, s_ref, xa_ref, xb_ref, x3_ref, logit_ref, wnd_ref,
):
    rows = OUT_LINES * CH
    cols = IN_LINES * CH

    n2 = MID_LINES * cols
    spot2 = rem(iota((CH, n2), 1), cols) - iota((CH, n2), 0)
    line2 = quo(iota((CH, n2), 1), cols)
    n1 = OUT_LINES * LANES
    group1 = quo(rem(iota((8, n1), 1), LANES), IN_LINES) == iota((8, n1), 0)
    line1 = rem(iota((8, n1), 1), IN_LINES) - quo(iota((8, n1), 1), LANES)
    spread1 = [(group1 & (line1 == ky)).astype(bf16) for ky in range(3)]
    tile4 = (rem(iota((CH, cols), 1), CH) == iota((CH, cols), 0)).astype(bf16)
    t1_ref[...] = jnp.zeros(t1_ref.shape, f32)
    t4_ref[...] = jnp.zeros(t4_ref.shape, f32)
    for ky in range(3):
        for kx in range(3):
            t1_ref[ky * 8 + 2 * kx : ky * 8 + 2 * kx + 2, :] = k1_ref[ky, kx].astype(f32)
        t4_ref[ky * 3 : ky * 3 + 3, :] = k4_ref[ky].astype(f32)
    wide1 = sum(dot_0(t1_ref[ky * 8 : ky * 8 + 8, :].astype(bf16), spread1[ky]) for ky in range(3))
    for i in range(OUT_LINES):
        w1_ref[i * CH : (i + 1) * CH, :] = wide1[:, i * LANES : (i + 1) * LANES].astype(bf16)
    spread2 = [
        (spot2 == (kx * MID_IN + ky + line2) * CH).astype(bf16) for ky in range(3) for kx in range(3)
    ]
    for k_ref, w_ref in ((k2_ref, w2_ref), (k3_ref, w3_ref)):
        wide = sum(dot(k_ref[n * CH : (n + 1) * CH, :], spread2[n]) for n in range(9))
        for i in range(MID_LINES):
            w_ref[i * CH : (i + 1) * CH, :] = wide[:, i * cols : (i + 1) * cols].astype(bf16)
    wide4 = dot(t4_ref[...].astype(bf16), tile4)
    w4_ref[...] = jnp.concatenate(
        [
            band_weights(
                [jnp.broadcast_to(wide4[ky * 3 + kx : ky * 3 + kx + 1], (CH, cols)) for ky in range(3)],
                CH, cols, 1, lambda k: quo(k, CH),
            )
            for kx in range(3)
        ],
        0,
    )

    lines = tile_ref.shape[1]
    tile = tile_ref[...].astype(f32)
    same = iota((lines, lines), 0) == iota((lines, lines), 1)
    tile_sub = jnp.sum(jnp.where(same, jnp.broadcast_to(tile, (lines, lines)), 0.0), 1, keepdims=True)
    rival = (tile_sub == tile) & (iota((lines, lines), 0) < iota((lines, lines), 1))
    slot = tile * capacity + jnp.sum(jnp.where(rival, 1.0, 0.0), 0, keepdims=True)
    slots = slots_ref.shape[0]
    wnd_rows = CH * lines
    per_line = CH
    widen = (quo(iota((lines, wnd_rows), 1), per_line) == iota((lines, wnd_rows), 0)).astype(bf16)
    slot_wide = dot(jnp.broadcast_to(slot, (8, lines)).astype(bf16), widen)[0:1]
    place = slot_wide.astype(jnp.int32) * 4 + rem(quo(iota((1, wnd_rows), 1), 4), 4)
    perm = jnp.where(iota((slots, wnd_rows), 0) == place, 1.0, 0.0).astype(bf16)
    end = END_LINES * CH
    perm_ref[...] = jnp.concatenate([perm[:, 0:end], perm[:, wnd_rows - end :]], 1)

    row_of = dot(
        jnp.where(same, jnp.broadcast_to(row_ref[...].astype(f32), (lines, lines)), 0.0).astype(bf16),
        jnp.ones((lines, LANES), bf16),
    )
    perm_line = jnp.where(quo(iota((slots, lines), 0), 4) == slot.astype(jnp.int32), 1.0, 0.0).astype(bf16)
    row_own = dot(perm_line, row_of.astype(bf16))
    per_tile = 4 * capacity
    lane = iota((slots, LANES), 1)
    entry = rem(iota((slots, LANES), 0), per_tile)
    info = jnp.zeros((slots, LANES), f32)
    for turn, value in enumerate((row_own, of_right(row_own, per_tile), of_left(row_own, per_tile))):
        info = jnp.where(lane == turn * per_tile + entry, value, info)
    info = jnp.sum(info.reshape(devices, per_tile, LANES), 1, keepdims=True)
    at = iota((devices, 8, LANES), 1)
    extra_ref[...] = jnp.where(at == 2, info, 0.0).reshape(8 * devices, LANES)


    px = sar_ref.shape[2]
    for ch in range(2):
        s_ref[ch, 0:lines, :] = sar_ref[ch].astype(f32)
        s_ref[ch, lines:, :] = jnp.zeros((s_ref.shape[1] - lines, px), f32)
    total = xa_ref.shape[1] // CH
    xa_ref[:, (total - 2) * CH :, :] = jnp.zeros((3, 2 * CH, px), bf16)

    def put(ref, line, acc):
        rows = acc.shape[0]
        feat = jnp.maximum(acc.astype(bf16), jnp.zeros(acc.shape, bf16))
        at = slice(line * CH, line * CH + rows)
        if len(ref.shape) == 2:
            ref[at, :] = feat
            return
        before, after = pixel_shifts(feat)
        ref[0, at, :] = before
        ref[1, at, :] = feat
        ref[2, at, :] = after

    full = (lines + 4) // OUT_LINES + 1
    for b in range(full):
        at = b * OUT_LINES
        x = jnp.concatenate([s_ref[0, at : at + IN_LINES, :], s_ref[1, at : at + IN_LINES, :]], 0)
        put(xa_ref, 1 + at, dot(w1_ref[...], image_columns(x)))
    stop = lines - 4
    for w_ref, src, dst, line, end_line in ((w2_ref, xa_ref, xb_ref, 2, stop), (w3_ref, xb_ref, x3_ref, 3, stop - 1)):
        for at in range(line, end_line, MID_LINES):
            x = src[:, (at - 1) * CH : (at - 1 + MID_IN) * CH, :]
            put(dst, at, dot(w_ref[...], mid_columns(*[x[i] for i in range(3)])))

    def ends_of(lo, center):
        hi = lines - lo - 2
        return jnp.concatenate([center[at * CH : (at + 2) * CH, :] for at in (lo, hi)], 0)

    e1_ref[...] = ends_of(3, xa_ref.at[1])
    e2_ref[...] = ends_of(4, xb_ref.at[1])
    e3_ref[...] = ends_of(5, x3_ref)
    logit_ref[0:END_LINES, :] = jnp.zeros((END_LINES, px), f32)
    starts = [3 + b * OUT_LINES for b in range(full - 2)] + [lines - 5 - IN_LINES]
    for at in starts:
        sums = dot(w4_ref[...], x3_ref[at * CH : at * CH + cols, :])
        logit_ref[at + 1 : at + 1 + CH, :] = merged(sums, CH)
    frac_ref[...] = sigmoid(logit_ref[0:lines, :])
    quarter = wnd_ref.shape[1]
    group = 16

    for g in range((lines - 2 * END_LINES) // group):
        at = slice(g * group + END_LINES, (g + 1) * group + END_LINES)
        cov = gw_ref[at, :]
        obs = sigmoid(logit_ref[at, :]).astype(f32) * cov
        for i, sums in enumerate(line_windows(cell_ref[at, :], obs, cov, quarter)):
            to = CH * (group * g + i)
            wnd_ref[to : to + CH, :] = sums
    slots_ref[...] = dot(perm[:, end : wnd_rows - end], window_goods(wnd_ref[...]))


def of_right(x, per_tile):
    return jnp.concatenate([x[per_tile:], jnp.zeros((per_tile, x.shape[1]), x.dtype)], 0)


def of_left(x, per_tile):
    return jnp.concatenate([jnp.zeros((per_tile, x.shape[1]), x.dtype), x[: x.shape[0] - per_tile]], 0)


def ends_kernel(
    devices, capacity,
    second_swap_ref, first_swap_ref, w1_ref, w2_ref, w3_ref, w4_ref, perm_ref, extra_ref, frac_in, slots_in, e1_ref, e2_ref, e3_ref,
    sar_ref, gw_ref, cell_ref,
    frac_ref, send_ref,
    f_ref,
):
    lines, px = gw_ref.shape
    n_ty = lax.axis_size("ty")
    me = lax.axis_index("tx") * n_ty + lax.axis_index("ty")
    rows = OUT_LINES * CH
    above, below = from_turns(
        me, devices, first_swap_ref[16:32, :].astype(f32), second_swap_ref[16:32, :].astype(f32)
    )
    n = HALO_LINES

    pieces = []
    for ch in range(2):
        own = sar_ref[ch].astype(f32)
        pieces += [above[ch * n : (ch + 1) * n], own[0:n], own[lines - n :], below[ch * n : (ch + 1) * n]]
    x = image_columns(jnp.concatenate(pieces, 0))
    half = 6 * CH
    out_line = quo(iota((half, px), 0), CH).astype(f32).astype(bf16)
    nil = jnp.zeros((half, px), bf16)
    low = jnp.where(me == 0, n, 0)
    high = jnp.where(me == devices - 1, OUT_LINES - 8 - n, OUT_LINES)
    for layer, (w_ref, e_ref) in enumerate(((w1_ref, e1_ref), (w2_ref, e2_ref), (w3_ref, e3_ref)), 1):
        if layer == 1:
            acc = dot(w_ref[...], x).astype(bf16)
            top, bottom = acc[0:half], acc[8 * CH :]
        else:
            before, after = pixel_shifts(block)
            top, bottom = [
                jnp.concatenate(
                    [
                        dot(w_ref[...], mid_columns(*[y[at * CH : (at + MID_IN) * CH] for y in (before, block, after)]))
                        for at in (first, first + MID_LINES)
                    ],
                    0,
                ).astype(bf16)
                for first in (0, 8)
            ]
        top = jnp.where(out_line >= (low - layer).astype(f32).astype(bf16), jnp.maximum(top, nil), nil)
        bottom = jnp.where(out_line < (high + layer).astype(f32).astype(bf16), jnp.maximum(bottom, nil), nil)
        block = jnp.concatenate([top, e_ref[...], bottom], 0)
    frac = sigmoid(merged(dot(w4_ref[...], block), CH)).astype(f32)
    f_ref[...] = frac_in[...].astype(f32)
    f_ref[0:6, :] = frac[0:6]
    f_ref[lines - 6 :, :] = frac[8:14]
    frac_ref[...] = f_ref[...].astype(bf16)
    quarter = slots_in.shape[1] // 4
    sums = []
    for at in (slice(0, END_LINES), slice(lines - END_LINES, lines)):
        cov = gw_ref[at, :]
        sums += line_windows(cell_ref[at, :], f_ref[at, :] * cov, cov, quarter)
    by_slot = slots_in[...] + dot(perm_ref[...], window_goods(jnp.concatenate(sums, 0)))

    per_tile = 4 * capacity
    slots, tile_cols = by_slot.shape
    h = SUBSTEPS
    entry = rem(iota((slots, LANES), 0), per_tile)
    here = quo(iota((slots, LANES), 1), h) == entry
    column = rem(quo(iota((slots, LANES), 0), per_tile), n_ty)
    source = iota((LANES, LANES), 0)
    spot = rem(iota((LANES, LANES), 1), h)

    def strip(x, first_lane, keep):
        take = ((spot + first_lane == source) & (source - first_lane < h)).astype(bf16)
        x = jnp.where(here & keep, dot(x.astype(bf16), take), 0.0)
        return jnp.sum(x.reshape(devices, per_tile, LANES), 1, keepdims=True)

    right_strip = strip(of_right(by_slot[:, 0:LANES], per_tile), 0, column < n_ty - 1)
    left_strip = strip(of_left(by_slot[:, tile_cols - LANES :], per_tile), LANES - h, column > 0)
    at = iota((devices, 8, LANES), 1)
    extra = extra_ref[...].reshape(devices, 8, LANES)
    extra = jnp.where(at == 0, right_strip, jnp.where(at == 1, left_strip, extra))
    halves = [by_slot[:, at : at + LANES].reshape(devices, per_tile, LANES) for at in range(0, tile_cols, LANES)]
    packed = jnp.concatenate([*halves, extra], 1)
    send_ref[...] = packed.reshape(send_ref.shape).astype(bf16)


def transposed(x):
    return jnp.transpose(x, (1, 0))


def level_kernel(
    devices,
    got_ref, second_swap_ref, first_swap_ref, depth_ref, slope_ref, rain_ref, dir_ref,
    level_ref, side_ref, first_ref, second_ref,
):
    tile_rows, tile_cols = depth_ref.shape
    h = SUBSTEPS
    halves = tile_cols // LANES
    n = (got_ref.shape[0] // devices - 8) // halves
    k = devices * n
    packed = got_ref[...].astype(f32).reshape(devices, halves * n + 8, LANES)
    main = jnp.concatenate([packed[:, i * n : (i + 1) * n].reshape(k, LANES) for i in range(halves)], 1)
    extra = packed[:, halves * n :]

    entry = rem(iota((k, LANES), 0), n)
    spread = quo(iota((k, LANES), 1), h) == entry

    def strip(r, first):
        rows = jnp.broadcast_to(extra[:, r : r + 1], (devices, n, LANES)).reshape(k, LANES)
        take = rem(iota((LANES, LANES), 0), h) + first == iota((LANES, LANES), 1)
        return dot(jnp.where(spread, rows, 0.0).astype(bf16), take.astype(bf16)).astype(bf16)

    lane = iota((1, k), 1)
    offset = rem(lane, 2) + tile_rows * rem(quo(lane, 2), 2)
    info = jnp.broadcast_to(extra[:, 2:3], (devices, n, LANES)).reshape(k, LANES)
    info = jnp.where(rem(iota((k, LANES), 1), n) == entry, info, 0.0).astype(bf16)
    turns = (quo(iota((LANES, LANES), 0), n) == iota((LANES, LANES), 1)).astype(bf16)
    lines = transposed(dot(info, turns))

    def placer(turn):
        target = lines[turn : turn + 1].astype(jnp.int32) + offset
        return jnp.where(iota((2 * tile_rows, k), 0) == target, 1.0, 0.0).astype(bf16)

    summed = dot(placer(0), main.astype(bf16))
    summed_side = dot(placer(1), strip(0, 0)) + dot(placer(2), strip(1, LANES - h))

    ty = lax.axis_index("ty")
    tx = lax.axis_index("tx")
    previous, following = from_turns(
        tx * lax.axis_size("ty") + ty, devices,
        first_swap_ref[0:16, :].astype(f32), second_swap_ref[0:16, :].astype(f32),
    )
    left = strips_of(previous, ty > 0)
    right = strips_of(following, ty < lax.axis_size("ty") - 1)
    gap = jnp.zeros((LANES - 2 * h, tile_rows), f32)
    depth_side, conv_side, rain_side, code_side = [
        transposed(jnp.concatenate([r, gap, l], 0)) for r, l in zip(right, left)
    ]

    def analysed(sums, depth):
        observed = sums[0:tile_rows]
        covered = sums[tile_rows:]
        wet = depth / (depth + wet_depth)
        innovation = (observed - covered * wet) / (covered + 1.0)
        return depth * jnp.exp(innovation)

    level = analysed(summed, depth_ref[...])
    level_ref[...] = level
    sides = (analysed(summed_side, depth_side), rain_side, conv_side, code_side)
    owns = (level, rain_ref, slope_ref, dir_ref)

    def end_rows(at):
        own = [x[at, :] for x in owns]
        own[2] = runoff_coef * jnp.sqrt(own[2])
        own[3] = own[3].astype(f32)
        return jnp.concatenate([jnp.concatenate([o, x[at]], 1) for o, x in zip(own, sides)], 0)

    for i, x in enumerate(sides):
        side_ref[i] = x
    first, second = in_turn(rem(tx, 2) == 0, end_rows(slice(tile_rows - h, tile_rows)), end_rows(slice(0, h)))
    first_ref[...] = first.astype(bf16)
    second_ref[...] = second.astype(bf16)


def substeps(level, rain, conv, code, rain_s, conv_s, m_ref, part_ref, up_ref, down_ref, chunk):
    rows, cols = level.shape
    h = SUBSTEPS
    for ref in (up_ref, down_ref):
        ref[0] = jnp.zeros(ref.shape[1:], f32)
        ref[1, 0:h, :] = jnp.zeros((h, cols), f32)
        ref[1, h + rows :, :] = jnp.zeros((h, cols), f32)
    part_ref[0] = level
    rain_s[...] = rain
    conv_s[...] = conv
    sides = (-1, 0, 1, -1, 1, -1, 0, 1)
    for direction, side in enumerate(sides):
        share = jnp.where(code == direction, conv, 0.0)
        m_ref[direction] = pltpu.roll(share, side % cols, 1) if side else share

    def level_at(buf, r, n):
        level = part_ref[buf, r : r + n, :]
        return level + up_ref[buf, h + r + 1 : h + r + 1 + n, :] + down_ref[buf, h + r - 1 : h + r - 1 + n, :]

    def substep(buf, new):
        for r in range(0, rows, chunk):
            level = level_at(buf, r, chunk)
            power = level * jnp.exp((2.0 / 3.0) * jnp.log(jnp.maximum(jnp.abs(level), 1e-30)))
            from_right = pltpu.roll(power, cols - 1, 1)
            from_left = pltpu.roll(power, 1, 1)
            m = [m_ref[d, r : r + chunk, :] for d in range(8)]
            up_ref[new, h + r : h + r + chunk, :] = m[0] * from_right + m[1] * power + m[2] * from_left
            down_ref[new, h + r : h + r + chunk, :] = m[5] * from_right + m[6] * power + m[7] * from_left
            part_ref[new, r : r + chunk, :] = (
                level + rain_s[r : r + chunk, :] - conv_s[r : r + chunk, :] * power
                + (m[3] * from_right + m[4] * from_left)
            )

    def substep_pair(i, carry):
        substep(0, 1)
        substep(1, 0)
        return carry

    if rows > LANES:
        lax.fori_loop(0, SUBSTEPS // 2, substep_pair, 0)
    else:
        for i in range(SUBSTEPS // 2):
            substep_pair(i, 0)
    return level_at


def flow_inner_kernel(level_ref, side_ref, slope_ref, dir_ref, rain_ref, out_ref, *scratch):
    rows, cols = level_ref.shape
    own = (level_ref[...], rain_ref[...], runoff_coef * jnp.sqrt(slope_ref[...]), dir_ref[...].astype(f32))
    level_at = substeps(*[jnp.concatenate([x, side_ref[i]], 1) for i, x in enumerate(own)], *scratch, 16)
    out_ref[...] = level_at(0, 0, rows)[:, 0:cols]


def flow_ends_kernel(inner_ref, level_ref, side_ref, slope_ref, dir_ref, rain_ref, first_swap_ref, second_swap_ref, out_ref, *scratch):
    rows, cols = level_ref.shape
    h = SUBSTEPS
    above, below = from_turns(
        lax.axis_index("tx"), lax.axis_size("tx"),
        first_swap_ref[...].astype(f32), second_swap_ref[...].astype(f32),
    )
    fields = []
    for i, ref in enumerate((level_ref, rain_ref, slope_ref, dir_ref)):
        ends = []
        for at in (slice(0, 2 * h), slice(rows - 2 * h, rows)):
            own = ref[at, :].astype(f32)
            if i == 2:
                own = runoff_coef * jnp.sqrt(own)
            ends.append(jnp.concatenate([own, side_ref[i, at, :]], 1))
        fields.append(jnp.concatenate([above[i * h : (i + 1) * h], *ends, below[i * h : (i + 1) * h]], 0))
    level_at = substeps(*fields, *scratch, 16)
    out_ref[h : rows - h, :] = inner_ref[h : rows - h, :]
    out_ref[0:h, :] = level_at(0, h, h)[:, 0:cols]
    out_ref[rows - h :, :] = level_at(0, 4 * h, h)[:, 0:cols]


def flow_scratch(rows, cols):
    return [
        pltpu.VMEM((rows, cols), f32),
        pltpu.VMEM((rows, cols), f32),
        pltpu.VMEM((8, rows, cols), f32),
        pltpu.VMEM((2, rows, cols), f32),
        pltpu.VMEM((2, rows + 2 * SUBSTEPS, cols), f32),
        pltpu.VMEM((2, rows + 2 * SUBSTEPS, cols), f32),
    ]


def hbm_specs(n):
    return [pl.BlockSpec(memory_space=pltpu.HBM)] * n


def vmem_specs(n):
    return [pl.BlockSpec(memory_space=pltpu.VMEM)] * n


def per_device(
    sar_image, kernel_first, kernel_second, kernel_third, kernel_last,
    geo_weight, cell_index, block_tile, block_row, depth, slope, flow_dir, rain,
):
    both = ("tx", "ty")
    devices = lax.axis_size(both)
    az_lines, range_px = geo_weight.shape
    tile_rows, tile_cols = depth.shape
    capacity = max(2, 2 * az_lines // devices)

    n_tx, n_ty = lax.axis_size("tx"), lax.axis_size("ty")

    def swaps(first, second, stride):
        size = devices // stride
        out = []
        for start, x in ((1, second), (0, first)):
            to = {}
            for place in range(start, size, 2):
                for k in range(stride):
                    i, j = place * stride + k, (place + 1) % size * stride + k
                    if place == size - 1 and stride > 1:
                        ends = (i, i ^ 1), (j, j ^ 1)
                    else:
                        ends = (i, j), (j, i)
                    to.update(ends)
            out.append(lax.ppermute(x, both, sorted(to.items())))
        return out[::-1]

    params = pltpu.CompilerParams(vmem_limit_bytes=VMEM_LIMIT)
    message = pltpu.VMEM((32, range_px), bf16)
    handed = (
        sar_image,
        jnp.transpose(kernel_first, (2, 3, 1, 0)),
        jnp.transpose(kernel_second, (2, 3, 0, 1)).reshape(9 * CH, CH),
        jnp.transpose(kernel_third, (2, 3, 0, 1)).reshape(9 * CH, CH),
        jnp.transpose(kernel_last[0], (1, 2, 0)),
        block_tile.reshape(1, az_lines),
        block_row.reshape(1, az_lines),
        geo_weight,
        cell_index,
    )
    first, second, sar_image, *handed = pl.pallas_call(
        edge_kernel,
        out_shape=(message, message, *[pltpu.VMEM(x.shape, x.dtype) for x in handed]),
        in_specs=hbm_specs(4 + len(handed)),
        out_specs=tuple(vmem_specs(2 + len(handed))),
        scratch_shapes=[
            *[pltpu.VMEM(x.shape, x.dtype) for x in (depth, slope, rain, flow_dir)],
            pltpu.SemaphoreType.DMA((4 + len(handed),)),
        ],
        compiler_params=pltpu.CompilerParams(vmem_limit_bytes=VMEM_MOST),
        name="edges",
    )(depth, slope, rain, flow_dir, *handed)
    geo_weight, cell_index = handed[-2:]
    halo = swaps(first, second, 1)

    rows, cols = OUT_LINES * CH, IN_LINES * CH
    slots = devices * capacity * 4
    send_rows = tile_cols // LANES * 4 * capacity + 8
    full = (az_lines + 4) // OUT_LINES + 1
    feats = (full * OUT_LINES + 3) * CH
    blocks_in = (az_lines + IN_LINES, range_px)

    def cost(flops):
        return pl.CostEstimate(flops=flops, bytes_accessed=4_000_000, transcendentals=0)

    prepared = pl.pallas_call(
        functools.partial(inner_kernel, devices, capacity),
        out_shape=(
            jax.ShapeDtypeStruct((rows, LANES), bf16),
            jax.ShapeDtypeStruct((MID_LINES * CH, cols), bf16),
            jax.ShapeDtypeStruct((MID_LINES * CH, cols), bf16),
            jax.ShapeDtypeStruct((3 * CH, cols), bf16),
            jax.ShapeDtypeStruct((slots, 2 * END_LINES * CH), bf16),
            jax.ShapeDtypeStruct((8 * devices, LANES), f32),
            jax.ShapeDtypeStruct((az_lines, range_px), bf16),
            jax.ShapeDtypeStruct((slots, tile_cols), f32),
            *[jax.ShapeDtypeStruct((4 * CH, range_px), bf16)] * 3,
        ),
        in_specs=vmem_specs(9),
        out_specs=tuple(vmem_specs(11)),
        scratch_shapes=[
            pltpu.VMEM((24, CH), f32),
            pltpu.VMEM((16, CH), f32),
            pltpu.VMEM((2, *blocks_in), f32),
            pltpu.VMEM((3, feats, range_px), bf16),
            pltpu.VMEM((3, feats, range_px), bf16),
            pltpu.VMEM((feats, range_px), bf16),
            pltpu.VMEM(blocks_in, f32),
            pltpu.VMEM(((az_lines - 2 * END_LINES) * CH, tile_cols // 4), f32),
        ],
        compiler_params=params,
        cost_estimate=cost(8_000_000_000),
        name="inner",
    )(
        *handed[:-2], sar_image, geo_weight, cell_index,
    )
    fraction, send = pl.pallas_call(
        functools.partial(ends_kernel, devices, capacity),
        out_shape=(
            jax.ShapeDtypeStruct((az_lines, range_px), bf16),
            jax.ShapeDtypeStruct((devices * send_rows, LANES), bf16),
        ),
        in_specs=vmem_specs(16),
        out_specs=tuple(vmem_specs(2)),
        scratch_shapes=[pltpu.VMEM((az_lines, range_px), f32)],
        compiler_params=params,
        name="ends",
    )(*halo[::-1], *prepared, sar_image, geo_weight, cell_index)

    got = lax.all_to_all(
        send.reshape(devices, send_rows, LANES), both, split_axis=0, concat_axis=0, tiled=True
    ).reshape(devices * send_rows, LANES)

    wide_cols = tile_cols + LANES
    edge = jax.ShapeDtypeStruct((4 * SUBSTEPS, wide_cols), bf16)
    level, side, first, second = pl.pallas_call(
        functools.partial(level_kernel, devices),
        out_shape=(
            jax.ShapeDtypeStruct((tile_rows, tile_cols), f32),
            jax.ShapeDtypeStruct((4, tile_rows, LANES), f32),
            edge,
            edge,
        ),
        in_specs=vmem_specs(7),
        out_specs=tuple(vmem_specs(4)),
        compiler_params=params,
        name="level",
    )(got, *halo[::-1], depth, slope, rain, flow_dir)

    row_halo = swaps(first, second, n_ty)

    inner = pl.pallas_call(
        flow_inner_kernel,
        out_shape=jax.ShapeDtypeStruct((tile_rows, tile_cols), f32),
        in_specs=vmem_specs(5),
        out_specs=vmem_specs(1)[0],
        scratch_shapes=flow_scratch(tile_rows, wide_cols),
        compiler_params=params,
        cost_estimate=cost(5_000_000_000),
        name="flow_inner",
    )(level, side, slope, flow_dir, rain)
    level = pl.pallas_call(
        flow_ends_kernel,
        out_shape=jax.ShapeDtypeStruct((tile_rows, tile_cols), f32),
        in_specs=vmem_specs(8),
        out_specs=vmem_specs(1)[0],
        scratch_shapes=flow_scratch(6 * SUBSTEPS, wide_cols),
        compiler_params=params,
        name="flow_ends",
    )(inner, level, side, slope, flow_dir, rain, *row_halo)
    return (fraction, level)


def solution(mesh):
    placed = (
        P(None, ("tx", "ty"), None),
        P(),
        P(),
        P(),
        P(),
        P(("tx", "ty"), None),
        P(("tx", "ty"), None),
        P(("tx", "ty"), None),
        P(("tx", "ty"), None),
        P("tx", "ty"),
        P("tx", "ty"),
        P("tx", "ty"),
        P("tx", "ty"),
    )
    return jax.shard_map(
        per_device,
        mesh=mesh,
        in_specs=placed,
        out_specs=(P(("tx", "ty"), None), P("tx", "ty")),
        check_vma=False,
    )
```

```python
import functools

import jax
import jax.numpy as jnp
from jax import lax
from jax.experimental import pallas as pl
from jax.experimental.pallas import tpu as pltpu
from jax.sharding import PartitionSpec as P

WIN_ROWS = 2
SUBSTEPS = 8
CH = 16
OUT_LINES = 14
IN_LINES = OUT_LINES + 2
MID_LINES = 3
MID_IN = MID_LINES + 2
HALO_LINES = 4
END_LINES = 8
LANES = 128
VMEM_LIMIT = 48 * 1024 * 1024
VMEM_MOST = 60160 * 1024

wet_depth = 0.5
runoff_coef = 0.25
bf16 = jnp.bfloat16
f32 = jnp.float32


def iota(shape, dim):
    return lax.broadcasted_iota(jnp.int32, shape, dim)


def quo(x, n):
    assert n & (n - 1) == 0
    return lax.shift_right_logical(x, jnp.int32(n.bit_length() - 1)) if n > 1 else x


def rem(x, n):
    assert n & (n - 1) == 0
    return x & (n - 1)


def dot(a, b):
    return lax.dot_general(a, b, (((1,), (0,)), ((), ())), preferred_element_type=f32)


def dot_0(a, b):
    return lax.dot_general(a, b, (((0,), (0,)), ((), ())), preferred_element_type=f32)


def dot_t(a, b):
    return lax.dot_general(a, b, (((1,), (1,)), ((), ())), preferred_element_type=f32)


def pixel_shifts(x):
    rows, width = x.shape
    lane = iota((rows, LANES), 1)
    zero = jnp.zeros((rows, LANES), x.dtype)
    first = lane.astype(f32).astype(x.dtype) == 0
    last = (LANES - 1 - lane).astype(f32).astype(x.dtype) == 0
    before = pltpu.roll(x, 1, 1)
    after = pltpu.roll(x, width - 1, 1)
    before = jnp.concatenate([jnp.where(first, zero, before[:, 0:LANES]), before[:, LANES:]], 1)
    after = jnp.concatenate([after[:, : width - LANES], jnp.where(last, zero, after[:, width - LANES :])], 1)
    return before, after


def merged(sums, n):
    before, _ = pixel_shifts(sums[0:n])
    _, after = pixel_shifts(sums[2 * n : 3 * n])
    return before + sums[n : 2 * n] + after


def image_columns(x):
    before, after = pixel_shifts(x)
    pad = jnp.zeros((LANES - 3 * x.shape[0], x.shape[1]), f32)
    return jnp.concatenate([before, x, after, pad], 0).astype(bf16)


def mid_columns(before, x, after):
    return jnp.concatenate([before, x, after, x[0:CH]], 0)


def sigmoid(x):
    return (1.0 / (1.0 + jnp.exp(-x))).astype(bf16)


def line_windows(cell, obs, cov, quarter):
    px = cell.shape[1]
    kind = iota((CH, px), 0)
    kind_part = rem(kind, CH // 2).astype(f32).astype(bf16)
    sub = kind.astype(f32).astype(bf16)
    one = jnp.ones((CH, px), bf16)
    nil = jnp.zeros((CH, px), bf16)
    part = quo(cell, quarter).astype(f32)
    col = rem(cell, quarter).astype(f32)

    def spread_row(x, i):
        return jnp.broadcast_to(x[i : i + 1], (CH, px)).astype(bf16)

    out = []
    for i in range(cell.shape[0]):
        pair = [jnp.broadcast_to(x[i : i + 1], (CH // 2, px)) for x in (obs, cov)]
        value = jnp.concatenate(pair, 0).astype(bf16)
        left = jnp.where(kind_part == spread_row(part, i), value, nil)
        where_col = spread_row(col, i)
        hot = jnp.concatenate([jnp.where(sub + g * CH == where_col, one, nil) for g in range(quarter // CH)], 0)
        out.append(dot_t(left, hot))
    return out


def window_goods(sums):
    rows, quarter = sums.shape
    cols = 4 * quarter
    repeat = (rem(iota((quarter, cols), 1), quarter) == iota((quarter, cols), 0)).astype(bf16)
    tiled = dot(sums.astype(bf16), repeat)
    mine = rem(iota((rows, cols), 0), 4) == quo(iota((rows, cols), 1), quarter)
    return jnp.where(mine, tiled, 0.0).astype(bf16)


def band_weights(tiled, rows, cols, per_row, line_of):
    out_line = quo(iota((rows, cols), 0), per_row)
    off = line_of(iota((rows, cols), 1)) - out_line
    out = jnp.zeros((rows, cols), f32)
    for ky in range(3):
        out = jnp.where(off == ky, tiled[ky], out)
    return out.astype(bf16)


def edge_kernel(
    depth_hbm, slope_hbm, rain_hbm, dir_hbm, sar_hbm, *refs
):
    n_on = (len(refs) - 8) // 2
    on_hbm = refs[:n_on]
    first_swap_ref, second_swap_ref, sar_ref, *on_refs = refs[n_on : 2 * n_on + 3]
    depth_ref, slope_ref, rain_ref, dir_ref, sems = refs[2 * n_on + 3 :]
    even = rem(lax.axis_index("tx") * lax.axis_size("ty") + lax.axis_index("ty"), 2) == 0
    lines, px = sar_hbm.shape[1:]
    cols = depth_hbm.shape[1]
    h = SUBSTEPS
    pairs = (
        (depth_hbm, depth_ref), (slope_hbm, slope_ref), (rain_hbm, rain_ref), (dir_hbm, dir_ref),
        (sar_hbm, sar_ref), *zip(on_hbm, on_refs),
    )
    copies = [pltpu.make_async_copy(src, dst, sems.at[i]) for i, (src, dst) in enumerate(pairs)]
    for copy in copies:
        copy.start()
    for copy in copies[0:5]:
        copy.wait()
    fields = (
        depth_ref[...],
        runoff_coef * jnp.sqrt(slope_ref[...]),
        rain_ref[...],
        dir_ref[...].astype(f32),
    )
    zeros = jnp.zeros((8, px), f32)
    messages = []
    for at, lo, strip in (
        (lines - 16, 16 - HALO_LINES, lambda x: jnp.transpose(x[:, cols - LANES :], (1, 0))[LANES - h :]),
        (0, 0, lambda x: jnp.transpose(x[:, 0:LANES], (1, 0))[0:h]),
    ):
        image = [sar_ref[ch, at : at + 16, :].astype(f32)[lo : lo + HALO_LINES] for ch in range(2)]
        strips = [strip(x) for x in fields]
        messages.append(
            jnp.concatenate([jnp.concatenate(strips[0:2], 1), jnp.concatenate(strips[2:4], 1), *image, zeros], 0)
        )
    first, second = in_turn(even, *messages)
    first_swap_ref[...] = first.astype(bf16)
    second_swap_ref[...] = second.astype(bf16)
    for copy in copies[5:]:
        copy.wait()


def in_turn(even, to_next, to_previous):
    return jnp.where(even, to_next, to_previous), jnp.where(even, to_previous, to_next)


def from_turns(place, size, first, second):
    even = rem(place, 2) == 0
    previous = jnp.where(even, second, first)
    following = jnp.where(even, first, second)
    return jnp.where(place > 0, previous, 0.0), jnp.where(place < size - 1, following, 0.0)


def strips_of(message, keep):
    both = jnp.where(keep, message, 0.0)
    cols = both.shape[1] // 2
    return [both[0:8, 0:cols], both[0:8, cols:], both[8:16, 0:cols], both[8:16, cols:]]


def inner_kernel(
    devices, capacity,
    k1_ref, k2_ref, k3_ref, k4_ref, tile_ref, row_ref, sar_ref, gw_ref, cell_ref,
    w1_ref, w2_ref, w3_ref, w4_ref, perm_ref, extra_ref, frac_ref, slots_ref, e1_ref, e2_ref, e3_ref,
    t1_ref, t4_ref, s_ref, xa_ref, xb_ref, x3_ref, logit_ref, wnd_ref,
):
    rows = OUT_LINES * CH
    cols = IN_LINES * CH

    n2 = MID_LINES * cols
    spot2 = rem(iota((CH, n2), 1), cols) - iota((CH, n2), 0)
    line2 = quo(iota((CH, n2), 1), cols)
    n1 = OUT_LINES * LANES
    group1 = quo(rem(iota((8, n1), 1), LANES), IN_LINES) == iota((8, n1), 0)
    line1 = rem(iota((8, n1), 1), IN_LINES) - quo(iota((8, n1), 1), LANES)
    spread1 = [(group1 & (line1 == ky)).astype(bf16) for ky in range(3)]
    tile4 = (rem(iota((CH, cols), 1), CH) == iota((CH, cols), 0)).astype(bf16)
    t1_ref[...] = jnp.zeros(t1_ref.shape, f32)
    t4_ref[...] = jnp.zeros(t4_ref.shape, f32)
    for ky in range(3):
        for kx in range(3):
            t1_ref[ky * 8 + 2 * kx : ky * 8 + 2 * kx + 2, :] = k1_ref[ky, kx].astype(f32)
        t4_ref[ky * 3 : ky * 3 + 3, :] = k4_ref[ky].astype(f32)
    wide1 = sum(dot_0(t1_ref[ky * 8 : ky * 8 + 8, :].astype(bf16), spread1[ky]) for ky in range(3))
    for i in range(OUT_LINES):
        w1_ref[i * CH : (i + 1) * CH, :] = wide1[:, i * LANES : (i + 1) * LANES].astype(bf16)
    spread2 = [
        (spot2 == (kx * MID_IN + ky + line2) * CH).astype(bf16) for ky in range(3) for kx in range(3)
    ]
    for k_ref, w_ref in ((k2_ref, w2_ref), (k3_ref, w3_ref)):
        wide = sum(dot(k_ref[n * CH : (n + 1) * CH, :], spread2[n]) for n in range(9))
        for i in range(MID_LINES):
            w_ref[i * CH : (i + 1) * CH, :] = wide[:, i * cols : (i + 1) * cols].astype(bf16)
    wide4 = dot(t4_ref[...].astype(bf16), tile4)
    w4_ref[...] = jnp.concatenate(
        [
            band_weights(
                [jnp.broadcast_to(wide4[ky * 3 + kx : ky * 3 + kx + 1], (CH, cols)) for ky in range(3)],
                CH, cols, 1, lambda k: quo(k, CH),
            )
            for kx in range(3)
        ],
        0,
    )

    lines = tile_ref.shape[1]
    tile = tile_ref[...].astype(f32)
    same = iota((lines, lines), 0) == iota((lines, lines), 1)
    tile_sub = jnp.sum(jnp.where(same, jnp.broadcast_to(tile, (lines, lines)), 0.0), 1, keepdims=True)
    rival = (tile_sub == tile) & (iota((lines, lines), 0) < iota((lines, lines), 1))
    slot = tile * capacity + jnp.sum(jnp.where(rival, 1.0, 0.0), 0, keepdims=True)
    slots = slots_ref.shape[0]
    wnd_rows = CH * lines
    per_line = CH
    widen = (quo(iota((lines, wnd_rows), 1), per_line) == iota((lines, wnd_rows), 0)).astype(bf16)
    slot_wide = dot(jnp.broadcast_to(slot, (8, lines)).astype(bf16), widen)[0:1]
    place = slot_wide.astype(jnp.int32) * 4 + rem(quo(iota((1, wnd_rows), 1), 4), 4)
    perm = jnp.where(iota((slots, wnd_rows), 0) == place, 1.0, 0.0).astype(bf16)
    end = END_LINES * CH
    perm_ref[...] = jnp.concatenate([perm[:, 0:end], perm[:, wnd_rows - end :]], 1)

    row_of = dot(
        jnp.where(same, jnp.broadcast_to(row_ref[...].astype(f32), (lines, lines)), 0.0).astype(bf16),
        jnp.ones((lines, LANES), bf16),
    )
    perm_line = jnp.where(quo(iota((slots, lines), 0), 4) == slot.astype(jnp.int32), 1.0, 0.0).astype(bf16)
    row_own = dot(perm_line, row_of.astype(bf16))
    per_tile = 4 * capacity
    lane = iota((slots, LANES), 1)
    entry = rem(iota((slots, LANES), 0), per_tile)
    info = jnp.zeros((slots, LANES), f32)
    for turn, value in enumerate((row_own, of_right(row_own, per_tile), of_left(row_own, per_tile))):
        info = jnp.where(lane == turn * per_tile + entry, value, info)
    info = jnp.sum(info.reshape(devices, per_tile, LANES), 1, keepdims=True)
    at = iota((devices, 8, LANES), 1)
    extra_ref[...] = jnp.where(at == 2, info, 0.0).reshape(8 * devices, LANES)


    px = sar_ref.shape[2]
    for ch in range(2):
        s_ref[ch, 0:lines, :] = sar_ref[ch].astype(f32)
        s_ref[ch, lines:, :] = jnp.zeros((s_ref.shape[1] - lines, px), f32)
    total = xa_ref.shape[1] // CH
    xa_ref[:, (total - 2) * CH :, :] = jnp.zeros((3, 2 * CH, px), bf16)

    def put(ref, line, acc):
        rows = acc.shape[0]
        feat = jnp.maximum(acc.astype(bf16), jnp.zeros(acc.shape, bf16))
        at = slice(line * CH, line * CH + rows)
        if len(ref.shape) == 2:
            ref[at, :] = feat
            return
        before, after = pixel_shifts(feat)
        ref[0, at, :] = before
        ref[1, at, :] = feat
        ref[2, at, :] = after

    full = (lines + 4) // OUT_LINES + 1
    for b in range(full):
        at = b * OUT_LINES
        x = jnp.concatenate([s_ref[0, at : at + IN_LINES, :], s_ref[1, at : at + IN_LINES, :]], 0)
        put(xa_ref, 1 + at, dot(w1_ref[...], image_columns(x)))
    stop = lines - 4
    for w_ref, src, dst, line, end_line in ((w2_ref, xa_ref, xb_ref, 2, stop), (w3_ref, xb_ref, x3_ref, 3, stop - 1)):
        for at in range(line, end_line, MID_LINES):
            x = src[:, (at - 1) * CH : (at - 1 + MID_IN) * CH, :]
            put(dst, at, dot(w_ref[...], mid_columns(*[x[i] for i in range(3)])))

    def ends_of(lo, center):
        hi = lines - lo - 2
        return jnp.concatenate([center[at * CH : (at + 2) * CH, :] for at in (lo, hi)], 0)

    e1_ref[...] = ends_of(3, xa_ref.at[1])
    e2_ref[...] = ends_of(4, xb_ref.at[1])
    e3_ref[...] = ends_of(5, x3_ref)
    logit_ref[0:END_LINES, :] = jnp.zeros((END_LINES, px), f32)
    starts = [3 + b * OUT_LINES for b in range(full - 2)] + [lines - 5 - IN_LINES]
    for at in starts:
        sums = dot(w4_ref[...], x3_ref[at * CH : at * CH + cols, :])
        logit_ref[at + 1 : at + 1 + CH, :] = merged(sums, CH)
    frac_ref[...] = sigmoid(logit_ref[0:lines, :])
    quarter = wnd_ref.shape[1]
    group = 16

    for g in range((lines - 2 * END_LINES) // group):
        at = slice(g * group + END_LINES, (g + 1) * group + END_LINES)
        cov = gw_ref[at, :]
        obs = sigmoid(logit_ref[at, :]).astype(f32) * cov
        for i, sums in enumerate(line_windows(cell_ref[at, :], obs, cov, quarter)):
            to = CH * (group * g + i)
            wnd_ref[to : to + CH, :] = sums
    slots_ref[...] = dot(perm[:, end : wnd_rows - end], window_goods(wnd_ref[...]))


def of_right(x, per_tile):
    return jnp.concatenate([x[per_tile:], jnp.zeros((per_tile, x.shape[1]), x.dtype)], 0)


def of_left(x, per_tile):
    return jnp.concatenate([jnp.zeros((per_tile, x.shape[1]), x.dtype), x[: x.shape[0] - per_tile]], 0)


def ends_kernel(
    devices, capacity,
    second_swap_ref, first_swap_ref, w1_ref, w2_ref, w3_ref, w4_ref, perm_ref, extra_ref, frac_in, slots_in, e1_ref, e2_ref, e3_ref,
    sar_ref, gw_ref, cell_ref,
    frac_ref, send_ref,
    f_ref,
):
    lines, px = gw_ref.shape
    n_ty = lax.axis_size("ty")
    me = lax.axis_index("tx") * n_ty + lax.axis_index("ty")
    rows = OUT_LINES * CH
    above, below = from_turns(
        me, devices, first_swap_ref[16:32, :].astype(f32), second_swap_ref[16:32, :].astype(f32)
    )
    n = HALO_LINES

    pieces = []
    for ch in range(2):
        own = sar_ref[ch].astype(f32)
        pieces += [above[ch * n : (ch + 1) * n], own[0:n], own[lines - n :], below[ch * n : (ch + 1) * n]]
    x = image_columns(jnp.concatenate(pieces, 0))
    half = 6 * CH
    out_line = quo(iota((half, px), 0), CH).astype(f32).astype(bf16)
    nil = jnp.zeros((half, px), bf16)
    low = jnp.where(me == 0, n, 0)
    high = jnp.where(me == devices - 1, OUT_LINES - 8 - n, OUT_LINES)
    for layer, (w_ref, e_ref) in enumerate(((w1_ref, e1_ref), (w2_ref, e2_ref), (w3_ref, e3_ref)), 1):
        if layer == 1:
            acc = dot(w_ref[...], x).astype(bf16)
            top, bottom = acc[0:half], acc[8 * CH :]
        else:
            before, after = pixel_shifts(block)
            top, bottom = [
                jnp.concatenate(
                    [
                        dot(w_ref[...], mid_columns(*[y[at * CH : (at + MID_IN) * CH] for y in (before, block, after)]))
                        for at in (first, first + MID_LINES)
                    ],
                    0,
                ).astype(bf16)
                for first in (0, 8)
            ]
        top = jnp.where(out_line >= (low - layer).astype(f32).astype(bf16), jnp.maximum(top, nil), nil)
        bottom = jnp.where(out_line < (high + layer).astype(f32).astype(bf16), jnp.maximum(bottom, nil), nil)
        block = jnp.concatenate([top, e_ref[...], bottom], 0)
    frac = sigmoid(merged(dot(w4_ref[...], block), CH)).astype(f32)
    f_ref[...] = frac_in[...].astype(f32)
    f_ref[0:6, :] = frac[0:6]
    f_ref[lines - 6 :, :] = frac[8:14]
    frac_ref[...] = f_ref[...].astype(bf16)
    quarter = slots_in.shape[1] // 4
    sums = []
    for at in (slice(0, END_LINES), slice(lines - END_LINES, lines)):
        cov = gw_ref[at, :]
        sums += line_windows(cell_ref[at, :], f_ref[at, :] * cov, cov, quarter)
    by_slot = slots_in[...] + dot(perm_ref[...], window_goods(jnp.concatenate(sums, 0)))

    per_tile = 4 * capacity
    slots, tile_cols = by_slot.shape
    h = SUBSTEPS
    entry = rem(iota((slots, LANES), 0), per_tile)
    here = quo(iota((slots, LANES), 1), h) == entry
    column = rem(quo(iota((slots, LANES), 0), per_tile), n_ty)
    source = iota((LANES, LANES), 0)
    spot = rem(iota((LANES, LANES), 1), h)

    def strip(x, first_lane, keep):
        take = ((spot + first_lane == source) & (source - first_lane < h)).astype(bf16)
        x = jnp.where(here & keep, dot(x.astype(bf16), take), 0.0)
        return jnp.sum(x.reshape(devices, per_tile, LANES), 1, keepdims=True)

    right_strip = strip(of_right(by_slot[:, 0:LANES], per_tile), 0, column < n_ty - 1)
    left_strip = strip(of_left(by_slot[:, tile_cols - LANES :], per_tile), LANES - h, column > 0)
    at = iota((devices, 8, LANES), 1)
    extra = extra_ref[...].reshape(devices, 8, LANES)
    extra = jnp.where(at == 0, right_strip, jnp.where(at == 1, left_strip, extra))
    halves = [by_slot[:, at : at + LANES].reshape(devices, per_tile, LANES) for at in range(0, tile_cols, LANES)]
    packed = jnp.concatenate([*halves, extra], 1)
    send_ref[...] = packed.reshape(send_ref.shape).astype(bf16)


def transposed(x):
    return jnp.transpose(x, (1, 0))


def level_kernel(
    devices,
    got_ref, second_swap_ref, first_swap_ref, depth_ref, slope_ref, rain_ref, dir_ref,
    level_ref, side_ref, first_ref, second_ref,
):
    tile_rows, tile_cols = depth_ref.shape
    h = SUBSTEPS
    halves = tile_cols // LANES
    n = (got_ref.shape[0] // devices - 8) // halves
    k = devices * n
    packed = got_ref[...].astype(f32).reshape(devices, halves * n + 8, LANES)
    main = jnp.concatenate([packed[:, i * n : (i + 1) * n].reshape(k, LANES) for i in range(halves)], 1)
    extra = packed[:, halves * n :]

    entry = rem(iota((k, LANES), 0), n)
    spread = quo(iota((k, LANES), 1), h) == entry

    def strip(r, first):
        rows = jnp.broadcast_to(extra[:, r : r + 1], (devices, n, LANES)).reshape(k, LANES)
        take = rem(iota((LANES, LANES), 0), h) + first == iota((LANES, LANES), 1)
        return dot(jnp.where(spread, rows, 0.0).astype(bf16), take.astype(bf16)).astype(bf16)

    lane = iota((1, k), 1)
    offset = rem(lane, 2) + tile_rows * rem(quo(lane, 2), 2)
    info = jnp.broadcast_to(extra[:, 2:3], (devices, n, LANES)).reshape(k, LANES)
    info = jnp.where(rem(iota((k, LANES), 1), n) == entry, info, 0.0).astype(bf16)
    turns = (quo(iota((LANES, LANES), 0), n) == iota((LANES, LANES), 1)).astype(bf16)
    lines = transposed(dot(info, turns))

    def placer(turn):
        target = lines[turn : turn + 1].astype(jnp.int32) + offset
        return jnp.where(iota((2 * tile_rows, k), 0) == target, 1.0, 0.0).astype(bf16)

    summed = dot(placer(0), main.astype(bf16))
    summed_side = dot(placer(1), strip(0, 0)) + dot(placer(2), strip(1, LANES - h))

    ty = lax.axis_index("ty")
    tx = lax.axis_index("tx")
    previous, following = from_turns(
        tx * lax.axis_size("ty") + ty, devices,
        first_swap_ref[0:16, :].astype(f32), second_swap_ref[0:16, :].astype(f32),
    )
    left = strips_of(previous, ty > 0)
    right = strips_of(following, ty < lax.axis_size("ty") - 1)
    gap = jnp.zeros((LANES - 2 * h, tile_rows), f32)
    depth_side, conv_side, rain_side, code_side = [
        transposed(jnp.concatenate([r, gap, l], 0)) for r, l in zip(right, left)
    ]

    def analysed(sums, depth):
        observed = sums[0:tile_rows]
        covered = sums[tile_rows:]
        wet = depth / (depth + wet_depth)
        innovation = (observed - covered * wet) / (covered + 1.0)
        return depth * jnp.exp(innovation)

    level = analysed(summed, depth_ref[...])
    level_ref[...] = level
    sides = (analysed(summed_side, depth_side), rain_side, conv_side, code_side)
    owns = (level, rain_ref, slope_ref, dir_ref)

    def end_rows(at):
        own = [x[at, :] for x in owns]
        own[2] = runoff_coef * jnp.sqrt(own[2])
        own[3] = own[3].astype(f32)
        return jnp.concatenate([jnp.concatenate([o, x[at]], 1) for o, x in zip(own, sides)], 0)

    for i, x in enumerate(sides):
        side_ref[i] = x
    first, second = in_turn(rem(tx, 2) == 0, end_rows(slice(tile_rows - h, tile_rows)), end_rows(slice(0, h)))
    first_ref[...] = first.astype(bf16)
    second_ref[...] = second.astype(bf16)


def substeps(level, rain, conv, code, rain_s, conv_s, m_ref, part_ref, up_ref, down_ref, chunk):
    rows, cols = level.shape
    h = SUBSTEPS
    for ref in (up_ref, down_ref):
        ref[0] = jnp.zeros(ref.shape[1:], f32)
        ref[1, 0:h, :] = jnp.zeros((h, cols), f32)
        ref[1, h + rows :, :] = jnp.zeros((h, cols), f32)
    part_ref[0] = level
    rain_s[...] = rain
    conv_s[...] = conv
    sides = (-1, 0, 1, -1, 1, -1, 0, 1)
    for direction, side in enumerate(sides):
        share = jnp.where(code == direction, conv, 0.0)
        m_ref[direction] = pltpu.roll(share, side % cols, 1) if side else share

    def level_at(buf, r, n):
        level = part_ref[buf, r : r + n, :]
        return level + up_ref[buf, h + r + 1 : h + r + 1 + n, :] + down_ref[buf, h + r - 1 : h + r - 1 + n, :]

    def substep(buf, new):
        for r in range(0, rows, chunk):
            level = level_at(buf, r, chunk)
            power = level * jnp.exp((2.0 / 3.0) * jnp.log(jnp.maximum(jnp.abs(level), 1e-30)))
            from_right = pltpu.roll(power, cols - 1, 1)
            from_left = pltpu.roll(power, 1, 1)
            m = [m_ref[d, r : r + chunk, :] for d in range(8)]
            up_ref[new, h + r : h + r + chunk, :] = m[0] * from_right + m[1] * power + m[2] * from_left
            down_ref[new, h + r : h + r + chunk, :] = m[5] * from_right + m[6] * power + m[7] * from_left
            part_ref[new, r : r + chunk, :] = (
                level + rain_s[r : r + chunk, :] - conv_s[r : r + chunk, :] * power
                + (m[3] * from_right + m[4] * from_left)
            )

    def substep_pair(i, carry):
        substep(0, 1)
        substep(1, 0)
        return carry

    if rows > LANES:
        lax.fori_loop(0, SUBSTEPS // 2, substep_pair, 0)
    else:
        for i in range(SUBSTEPS // 2):
            substep_pair(i, 0)
    return level_at


def flow_inner_kernel(level_ref, side_ref, slope_ref, dir_ref, rain_ref, out_ref, *scratch):
    rows, cols = level_ref.shape
    own = (level_ref[...], rain_ref[...], runoff_coef * jnp.sqrt(slope_ref[...]), dir_ref[...].astype(f32))
    level_at = substeps(*[jnp.concatenate([x, side_ref[i]], 1) for i, x in enumerate(own)], *scratch, 8)
    out_ref[...] = level_at(0, 0, rows)[:, 0:cols]


def flow_ends_kernel(inner_ref, level_ref, side_ref, slope_ref, dir_ref, rain_ref, second_swap_ref, first_swap_ref, out_ref, *scratch):
    rows, cols = level_ref.shape
    h = SUBSTEPS
    above, below = from_turns(
        lax.axis_index("tx"), lax.axis_size("tx"),
        first_swap_ref[...].astype(f32), second_swap_ref[...].astype(f32),
    )
    fields = []
    for i, ref in enumerate((level_ref, rain_ref, slope_ref, dir_ref)):
        ends = []
        for at in (slice(0, 2 * h), slice(rows - 2 * h, rows)):
            own = ref[at, :].astype(f32)
            if i == 2:
                own = runoff_coef * jnp.sqrt(own)
            ends.append(jnp.concatenate([own, side_ref[i, at, :]], 1))
        fields.append(jnp.concatenate([above[i * h : (i + 1) * h], *ends, below[i * h : (i + 1) * h]], 0))
    level_at = substeps(*fields, *scratch, 16)
    out_ref[h : rows - h, :] = inner_ref[h : rows - h, :]
    out_ref[0:h, :] = level_at(0, h, h)[:, 0:cols]
    out_ref[rows - h :, :] = level_at(0, 4 * h, h)[:, 0:cols]


def flow_scratch(rows, cols):
    return [
        pltpu.VMEM((rows, cols), f32),
        pltpu.VMEM((rows, cols), f32),
        pltpu.VMEM((8, rows, cols), f32),
        pltpu.VMEM((2, rows, cols), f32),
        pltpu.VMEM((2, rows + 2 * SUBSTEPS, cols), f32),
        pltpu.VMEM((2, rows + 2 * SUBSTEPS, cols), f32),
    ]


def hbm_specs(n):
    return [pl.BlockSpec(memory_space=pltpu.HBM)] * n


def vmem_specs(n):
    return [pl.BlockSpec(memory_space=pltpu.VMEM)] * n


def per_device(
    sar_image, kernel_first, kernel_second, kernel_third, kernel_last,
    geo_weight, cell_index, block_tile, block_row, depth, slope, flow_dir, rain,
):
    both = ("tx", "ty")
    devices = lax.axis_size(both)
    az_lines, range_px = geo_weight.shape
    tile_rows, tile_cols = depth.shape
    capacity = max(2, 2 * az_lines // devices)

    n_tx, n_ty = lax.axis_size("tx"), lax.axis_size("ty")

    def swaps(first, second, stride):
        size = devices // stride
        out = []
        for start, x in ((1, second), (0, first)):
            to = {}
            for place in range(start, size, 2):
                for k in range(stride):
                    i, j = place * stride + k, (place + 1) % size * stride + k
                    if place == size - 1 and stride > 1:
                        ends = (i, i ^ 1), (j, j ^ 1)
                    else:
                        ends = (i, j), (j, i)
                    to.update(ends)
            out.append(lax.ppermute(x, both, sorted(to.items())))
        return out[::-1]

    params = pltpu.CompilerParams(vmem_limit_bytes=VMEM_LIMIT)
    message = pltpu.VMEM((32, range_px), bf16)
    handed = (
        sar_image,
        jnp.transpose(kernel_first, (2, 3, 1, 0)),
        jnp.transpose(kernel_second, (2, 3, 0, 1)).reshape(9 * CH, CH),
        jnp.transpose(kernel_third, (2, 3, 0, 1)).reshape(9 * CH, CH),
        jnp.transpose(kernel_last[0], (1, 2, 0)),
        block_tile.reshape(1, az_lines),
        block_row.reshape(1, az_lines),
        geo_weight,
        cell_index,
    )
    first, second, sar_image, *handed = pl.pallas_call(
        edge_kernel,
        out_shape=(message, message, *[pltpu.VMEM(x.shape, x.dtype) for x in handed]),
        in_specs=hbm_specs(4 + len(handed)),
        out_specs=tuple(vmem_specs(2 + len(handed))),
        scratch_shapes=[
            *[pltpu.VMEM(x.shape, x.dtype) for x in (depth, slope, rain, flow_dir)],
            pltpu.SemaphoreType.DMA((4 + len(handed),)),
        ],
        compiler_params=pltpu.CompilerParams(vmem_limit_bytes=VMEM_MOST),
        name="edges",
    )(depth, slope, rain, flow_dir, *handed)
    geo_weight, cell_index = handed[-2:]
    halo = swaps(first, second, 1)

    rows, cols = OUT_LINES * CH, IN_LINES * CH
    slots = devices * capacity * 4
    send_rows = tile_cols // LANES * 4 * capacity + 8
    full = (az_lines + 4) // OUT_LINES + 1
    feats = (full * OUT_LINES + 3) * CH
    blocks_in = (az_lines + IN_LINES, range_px)

    def cost(flops):
        return pl.CostEstimate(flops=flops, bytes_accessed=4_000_000, transcendentals=0)

    prepared = pl.pallas_call(
        functools.partial(inner_kernel, devices, capacity),
        out_shape=(
            jax.ShapeDtypeStruct((rows, LANES), bf16),
            jax.ShapeDtypeStruct((MID_LINES * CH, cols), bf16),
            jax.ShapeDtypeStruct((MID_LINES * CH, cols), bf16),
            jax.ShapeDtypeStruct((3 * CH, cols), bf16),
            jax.ShapeDtypeStruct((slots, 2 * END_LINES * CH), bf16),
            jax.ShapeDtypeStruct((8 * devices, LANES), f32),
            jax.ShapeDtypeStruct((az_lines, range_px), bf16),
            jax.ShapeDtypeStruct((slots, tile_cols), f32),
            *[jax.ShapeDtypeStruct((4 * CH, range_px), bf16)] * 3,
        ),
        in_specs=vmem_specs(9),
        out_specs=tuple(vmem_specs(11)),
        scratch_shapes=[
            pltpu.VMEM((24, CH), f32),
            pltpu.VMEM((16, CH), f32),
            pltpu.VMEM((2, *blocks_in), f32),
            pltpu.VMEM((3, feats, range_px), bf16),
            pltpu.VMEM((3, feats, range_px), bf16),
            pltpu.VMEM((feats, range_px), bf16),
            pltpu.VMEM(blocks_in, f32),
            pltpu.VMEM(((az_lines - 2 * END_LINES) * CH, tile_cols // 4), f32),
        ],
        compiler_params=params,
        cost_estimate=cost(8_000_000_000),
        name="inner",
    )(
        *handed[:-2], sar_image, geo_weight, cell_index,
    )
    fraction, send = pl.pallas_call(
        functools.partial(ends_kernel, devices, capacity),
        out_shape=(
            jax.ShapeDtypeStruct((az_lines, range_px), bf16),
            jax.ShapeDtypeStruct((devices * send_rows, LANES), bf16),
        ),
        in_specs=vmem_specs(16),
        out_specs=tuple(vmem_specs(2)),
        scratch_shapes=[pltpu.VMEM((az_lines, range_px), f32)],
        compiler_params=params,
        name="ends",
    )(*halo[::-1], *prepared, sar_image, geo_weight, cell_index)

    got = lax.all_to_all(
        send.reshape(devices, send_rows, LANES), both, split_axis=0, concat_axis=0, tiled=True
    ).reshape(devices * send_rows, LANES)

    wide_cols = tile_cols + LANES
    edge = jax.ShapeDtypeStruct((4 * SUBSTEPS, wide_cols), bf16)
    level, side, first, second = pl.pallas_call(
        functools.partial(level_kernel, devices),
        out_shape=(
            jax.ShapeDtypeStruct((tile_rows, tile_cols), f32),
            jax.ShapeDtypeStruct((4, tile_rows, LANES), f32),
            edge,
            edge,
        ),
        in_specs=vmem_specs(7),
        out_specs=tuple(vmem_specs(4)),
        compiler_params=params,
        name="level",
    )(got, *halo[::-1], depth, slope, rain, flow_dir)

    row_halo = swaps(first, second, n_ty)

    inner = pl.pallas_call(
        flow_inner_kernel,
        out_shape=jax.ShapeDtypeStruct((tile_rows, tile_cols), f32),
        in_specs=vmem_specs(5),
        out_specs=vmem_specs(1)[0],
        scratch_shapes=flow_scratch(tile_rows, wide_cols),
        compiler_params=params,
        cost_estimate=cost(5_000_000_000),
        name="flow_inner",
    )(level, side, slope, flow_dir, rain)
    level = pl.pallas_call(
        flow_ends_kernel,
        out_shape=jax.ShapeDtypeStruct((tile_rows, tile_cols), f32),
        in_specs=vmem_specs(8),
        out_specs=vmem_specs(1)[0],
        scratch_shapes=flow_scratch(6 * SUBSTEPS, wide_cols),
        compiler_params=params,
        name="flow_ends",
    )(inner, level, side, slope, flow_dir, rain, *row_halo[::-1])
    return (fraction, level)


def solution(mesh):
    placed = (
        P(None, ("tx", "ty"), None),
        P(),
        P(),
        P(),
        P(),
        P(("tx", "ty"), None),
        P(("tx", "ty"), None),
        P(("tx", "ty"), None),
        P(("tx", "ty"), None),
        P("tx", "ty"),
        P("tx", "ty"),
        P("tx", "ty"),
        P("tx", "ty"),
    )
    return jax.shard_map(
        per_device,
        mesh=mesh,
        in_specs=placed,
        out_specs=(P(("tx", "ty"), None), P("tx", "ty")),
        check_vma=False,
    )
```

```python
import functools
import math

import jax
import jax.numpy as jnp
from jax import lax
from jax.experimental import pallas as pl
from jax.experimental.pallas import tpu as pltpu
from jax.sharding import PartitionSpec as P

WIN_ROWS = 2
SUBSTEPS = 8
CH = 16
OUT_LINES = 14
IN_LINES = OUT_LINES + 2
MID_LINES = 3
MID_IN = MID_LINES + 2
HALO_LINES = 4
END_LINES = 8
LANES = 128
VMEM_LIMIT = 48 * 1024 * 1024
VMEM_MOST = 60160 * 1024

wet_depth = 0.5
runoff_coef = 0.25
bf16 = jnp.bfloat16
f32 = jnp.float32


def iota(shape, dim):
    return lax.broadcasted_iota(jnp.int32, shape, dim)


def quo(x, n):
    assert n & (n - 1) == 0
    return lax.shift_right_logical(x, jnp.int32(n.bit_length() - 1)) if n > 1 else x


def rem(x, n):
    assert n & (n - 1) == 0
    return x & (n - 1)


def dot(a, b):
    return lax.dot_general(a, b, (((1,), (0,)), ((), ())), preferred_element_type=f32)


def dot_0(a, b):
    return lax.dot_general(a, b, (((0,), (0,)), ((), ())), preferred_element_type=f32)


def dot_t(a, b):
    return lax.dot_general(a, b, (((1,), (1,)), ((), ())), preferred_element_type=f32)


def pixel_shifts(x):
    rows, width = x.shape
    lane = iota((rows, LANES), 1)
    zero = jnp.zeros((rows, LANES), x.dtype)
    first = lane.astype(f32).astype(x.dtype) == 0
    last = (LANES - 1 - lane).astype(f32).astype(x.dtype) == 0
    before = pltpu.roll(x, 1, 1)
    after = pltpu.roll(x, width - 1, 1)
    before = jnp.concatenate([jnp.where(first, zero, before[:, 0:LANES]), before[:, LANES:]], 1)
    after = jnp.concatenate([after[:, : width - LANES], jnp.where(last, zero, after[:, width - LANES :])], 1)
    return before, after


def merged(sums, n):
    before, _ = pixel_shifts(sums[0:n])
    _, after = pixel_shifts(sums[2 * n : 3 * n])
    return before + sums[n : 2 * n] + after


def image_columns(x):
    before, after = pixel_shifts(x)
    pad = jnp.zeros((LANES - 3 * x.shape[0], x.shape[1]), f32)
    return jnp.concatenate([before, x, after, pad], 0).astype(bf16)


def mid_columns(before, x, after):
    return jnp.concatenate([before, x, after, x[0:CH]], 0)


def sigmoid(x):
    return (1.0 / (1.0 + jnp.exp(-x))).astype(bf16)


def line_windows(cell, obs, cov, quarter):
    px = cell.shape[1]
    kind = iota((CH, px), 0)
    kind_part = rem(kind, CH // 2).astype(f32).astype(bf16)
    sub = kind.astype(f32).astype(bf16)
    one = jnp.ones((CH, px), bf16)
    nil = jnp.zeros((CH, px), bf16)
    part = quo(cell, quarter).astype(f32)
    col = rem(cell, quarter).astype(f32)

    def spread_row(x, i):
        return jnp.broadcast_to(x[i : i + 1], (CH, px)).astype(bf16)

    out = []
    for i in range(cell.shape[0]):
        pair = [jnp.broadcast_to(x[i : i + 1], (CH // 2, px)) for x in (obs, cov)]
        value = jnp.concatenate(pair, 0).astype(bf16)
        left = jnp.where(kind_part == spread_row(part, i), value, nil)
        where_col = spread_row(col, i)
        hot = jnp.concatenate([jnp.where(sub + g * CH == where_col, one, nil) for g in range(quarter // CH)], 0)
        out.append(dot_t(left, hot))
    return out


def window_goods(sums):
    rows, quarter = sums.shape
    cols = 4 * quarter
    repeat = (rem(iota((quarter, cols), 1), quarter) == iota((quarter, cols), 0)).astype(bf16)
    tiled = dot(sums.astype(bf16), repeat)
    mine = rem(iota((rows, cols), 0), 4) == quo(iota((rows, cols), 1), quarter)
    return jnp.where(mine, tiled, 0.0).astype(bf16)


def band_weights(tiled, rows, cols, per_row, line_of):
    out_line = quo(iota((rows, cols), 0), per_row)
    off = line_of(iota((rows, cols), 1)) - out_line
    out = jnp.zeros((rows, cols), f32)
    for ky in range(3):
        out = jnp.where(off == ky, tiled[ky], out)
    return out.astype(bf16)


def edge_kernel(
    depth_hbm, slope_hbm, rain_hbm, dir_hbm, sar_hbm, *refs
):
    n_on = (len(refs) - 8) // 2
    on_hbm = refs[:n_on]
    first_swap_ref, second_swap_ref, sar_ref, *on_refs = refs[n_on : 2 * n_on + 3]
    depth_ref, slope_ref, rain_ref, dir_ref, sems = refs[2 * n_on + 3 :]
    even = rem(lax.axis_index("tx") * lax.axis_size("ty") + lax.axis_index("ty"), 2) == 0
    lines, px = sar_hbm.shape[1:]
    cols = depth_hbm.shape[1]
    h = SUBSTEPS
    pairs = (
        (depth_hbm, depth_ref), (slope_hbm, slope_ref), (rain_hbm, rain_ref), (dir_hbm, dir_ref),
        (sar_hbm, sar_ref), *zip(on_hbm, on_refs),
    )
    copies = [pltpu.make_async_copy(src, dst, sems.at[i]) for i, (src, dst) in enumerate(pairs)]
    for copy in copies:
        copy.start()
    for copy in copies[0:5]:
        copy.wait()
    fields = (
        depth_ref[...],
        runoff_coef * jnp.sqrt(slope_ref[...]),
        rain_ref[...],
        dir_ref[...].astype(f32),
    )
    zeros = jnp.zeros((8, px), f32)
    messages = []
    for at, lo, strip in (
        (lines - 16, 16 - HALO_LINES, lambda x: jnp.transpose(x[:, cols - LANES :], (1, 0))[LANES - h :]),
        (0, 0, lambda x: jnp.transpose(x[:, 0:LANES], (1, 0))[0:h]),
    ):
        image = [sar_ref[ch, at : at + 16, :].astype(f32)[lo : lo + HALO_LINES] for ch in range(2)]
        strips = [strip(x) for x in fields]
        messages.append(
            jnp.concatenate([jnp.concatenate(strips[0:2], 1), jnp.concatenate(strips[2:4], 1), *image, zeros], 0)
        )
    first, second = in_turn(even, *messages)
    first_swap_ref[...] = first.astype(bf16)
    second_swap_ref[...] = second.astype(bf16)
    for copy in copies[5:]:
        copy.wait()


def in_turn(even, to_next, to_previous):
    return jnp.where(even, to_next, to_previous), jnp.where(even, to_previous, to_next)


def from_turns(place, size, first, second):
    even = rem(place, 2) == 0
    previous = jnp.where(even, second, first)
    following = jnp.where(even, first, second)
    return jnp.where(place > 0, previous, 0.0), jnp.where(place < size - 1, following, 0.0)


def strips_of(message, keep):
    both = jnp.where(keep, message, 0.0)
    cols = both.shape[1] // 2
    return [both[0:8, 0:cols], both[0:8, cols:], both[8:16, 0:cols], both[8:16, cols:]]


def inner_kernel(
    devices, capacity,
    k1_ref, k2_ref, k3_ref, k4_ref, tile_ref, row_ref, sar_ref, gw_ref, cell_ref,
    w1_ref, w2_ref, w3_ref, w4_ref, perm_ref, extra_ref, frac_ref, slots_ref, e1_ref, e2_ref, e3_ref,
    t1_ref, t4_ref, s_ref, xa_ref, xb_ref, x3_ref, logit_ref, wnd_ref,
):
    rows = OUT_LINES * CH
    cols = IN_LINES * CH

    n2 = MID_LINES * cols
    spot2 = rem(iota((CH, n2), 1), cols) - iota((CH, n2), 0)
    line2 = quo(iota((CH, n2), 1), cols)
    n1 = OUT_LINES * LANES
    group1 = quo(rem(iota((8, n1), 1), LANES), IN_LINES) == iota((8, n1), 0)
    line1 = rem(iota((8, n1), 1), IN_LINES) - quo(iota((8, n1), 1), LANES)
    spread1 = [(group1 & (line1 == ky)).astype(bf16) for ky in range(3)]
    tile4 = (rem(iota((CH, cols), 1), CH) == iota((CH, cols), 0)).astype(bf16)
    t1_ref[...] = jnp.zeros(t1_ref.shape, f32)
    t4_ref[...] = jnp.zeros(t4_ref.shape, f32)
    for ky in range(3):
        for kx in range(3):
            t1_ref[ky * 8 + 2 * kx : ky * 8 + 2 * kx + 2, :] = k1_ref[ky, kx].astype(f32)
        t4_ref[ky * 3 : ky * 3 + 3, :] = k4_ref[ky].astype(f32)
    wide1 = sum(dot_0(t1_ref[ky * 8 : ky * 8 + 8, :].astype(bf16), spread1[ky]) for ky in range(3))
    for i in range(OUT_LINES):
        w1_ref[i * CH : (i + 1) * CH, :] = wide1[:, i * LANES : (i + 1) * LANES].astype(bf16)
    spread2 = [
        (spot2 == (kx * MID_IN + ky + line2) * CH).astype(bf16) for ky in range(3) for kx in range(3)
    ]
    for k_ref, w_ref in ((k2_ref, w2_ref), (k3_ref, w3_ref)):
        wide = sum(dot(k_ref[n * CH : (n + 1) * CH, :], spread2[n]) for n in range(9))
        for i in range(MID_LINES):
            w_ref[i * CH : (i + 1) * CH, :] = wide[:, i * cols : (i + 1) * cols].astype(bf16)
    wide4 = dot(t4_ref[...].astype(bf16), tile4)
    w4_ref[...] = jnp.concatenate(
        [
            band_weights(
                [jnp.broadcast_to(wide4[ky * 3 + kx : ky * 3 + kx + 1], (CH, cols)) for ky in range(3)],
                CH, cols, 1, lambda k: quo(k, CH),
            )
            for kx in range(3)
        ],
        0,
    )

    lines = tile_ref.shape[1]
    tile = tile_ref[...].astype(f32)
    same = iota((lines, lines), 0) == iota((lines, lines), 1)
    tile_sub = jnp.sum(jnp.where(same, jnp.broadcast_to(tile, (lines, lines)), 0.0), 1, keepdims=True)
    rival = (tile_sub == tile) & (iota((lines, lines), 0) < iota((lines, lines), 1))
    slot = tile * capacity + jnp.sum(jnp.where(rival, 1.0, 0.0), 0, keepdims=True)
    slots = slots_ref.shape[0]
    wnd_rows = CH * lines
    per_line = CH
    widen = (quo(iota((lines, wnd_rows), 1), per_line) == iota((lines, wnd_rows), 0)).astype(bf16)
    slot_wide = dot(jnp.broadcast_to(slot, (8, lines)).astype(bf16), widen)[0:1]
    place = slot_wide.astype(jnp.int32) * 4 + rem(quo(iota((1, wnd_rows), 1), 4), 4)
    perm = jnp.where(iota((slots, wnd_rows), 0) == place, 1.0, 0.0).astype(bf16)
    end = END_LINES * CH
    perm_ref[...] = jnp.concatenate([perm[:, 0:end], perm[:, wnd_rows - end :]], 1)

    row_of = dot(
        jnp.where(same, jnp.broadcast_to(row_ref[...].astype(f32), (lines, lines)), 0.0).astype(bf16),
        jnp.ones((lines, LANES), bf16),
    )
    perm_line = jnp.where(quo(iota((slots, lines), 0), 4) == slot.astype(jnp.int32), 1.0, 0.0).astype(bf16)
    row_own = dot(perm_line, row_of.astype(bf16))
    per_tile = 4 * capacity
    lane = iota((slots, LANES), 1)
    entry = rem(iota((slots, LANES), 0), per_tile)
    info = jnp.zeros((slots, LANES), f32)
    for turn, value in enumerate((row_own, of_right(row_own, per_tile), of_left(row_own, per_tile))):
        info = jnp.where(lane == turn * per_tile + entry, value, info)
    info = jnp.sum(info.reshape(devices, per_tile, LANES), 1, keepdims=True)
    at = iota((devices, 8, LANES), 1)
    extra_ref[...] = jnp.where(at == 2, info, 0.0).reshape(8 * devices, LANES)


    px = sar_ref.shape[2]
    for ch in range(2):
        s_ref[ch, 0:lines, :] = sar_ref[ch].astype(f32)
        s_ref[ch, lines:, :] = jnp.zeros((s_ref.shape[1] - lines, px), f32)
    total = xa_ref.shape[1] // CH
    xa_ref[:, (total - 2) * CH :, :] = jnp.zeros((3, 2 * CH, px), bf16)

    def put(ref, line, acc):
        rows = acc.shape[0]
        feat = jnp.maximum(acc.astype(bf16), jnp.zeros(acc.shape, bf16))
        at = slice(line * CH, line * CH + rows)
        if len(ref.shape) == 2:
            ref[at, :] = feat
            return
        before, after = pixel_shifts(feat)
        ref[0, at, :] = before
        ref[1, at, :] = feat
        ref[2, at, :] = after

    full = (lines + 4) // OUT_LINES + 1
    for b in range(full):
        at = b * OUT_LINES
        x = jnp.concatenate([s_ref[0, at : at + IN_LINES, :], s_ref[1, at : at + IN_LINES, :]], 0)
        put(xa_ref, 1 + at, dot(w1_ref[...], image_columns(x)))
    stop = lines - 4
    for w_ref, src, dst, line, end_line in ((w2_ref, xa_ref, xb_ref, 2, stop), (w3_ref, xb_ref, x3_ref, 3, stop - 1)):
        for at in range(line, end_line, MID_LINES):
            x = src[:, (at - 1) * CH : (at - 1 + MID_IN) * CH, :]
            put(dst, at, dot(w_ref[...], mid_columns(*[x[i] for i in range(3)])))

    def ends_of(lo, center):
        hi = lines - lo - 2
        return jnp.concatenate([center[at * CH : (at + 2) * CH, :] for at in (lo, hi)], 0)

    e1_ref[...] = ends_of(3, xa_ref.at[1])
    e2_ref[...] = ends_of(4, xb_ref.at[1])
    e3_ref[...] = ends_of(5, x3_ref)
    logit_ref[0:END_LINES, :] = jnp.zeros((END_LINES, px), f32)
    starts = [3 + b * OUT_LINES for b in range(full - 2)] + [lines - 5 - IN_LINES]
    for at in starts:
        sums = dot(w4_ref[...], x3_ref[at * CH : at * CH + cols, :])
        logit_ref[at + 1 : at + 1 + CH, :] = merged(sums, CH)
    frac_ref[...] = sigmoid(logit_ref[0:lines, :])
    quarter = wnd_ref.shape[1]
    group = 16

    for g in range((lines - 2 * END_LINES) // group):
        at = slice(g * group + END_LINES, (g + 1) * group + END_LINES)
        cov = gw_ref[at, :]
        obs = sigmoid(logit_ref[at, :]).astype(f32) * cov
        for i, sums in enumerate(line_windows(cell_ref[at, :], obs, cov, quarter)):
            to = CH * (group * g + i)
            wnd_ref[to : to + CH, :] = sums
    slots_ref[...] = dot(perm[:, end : wnd_rows - end], window_goods(wnd_ref[...]))


def of_right(x, per_tile):
    return jnp.concatenate([x[per_tile:], jnp.zeros((per_tile, x.shape[1]), x.dtype)], 0)


def of_left(x, per_tile):
    return jnp.concatenate([jnp.zeros((per_tile, x.shape[1]), x.dtype), x[: x.shape[0] - per_tile]], 0)


def ends_kernel(
    devices, capacity,
    second_swap_ref, first_swap_ref, w1_ref, w2_ref, w3_ref, w4_ref, perm_ref, extra_ref, frac_in, slots_in, e1_ref, e2_ref, e3_ref,
    sar_ref, gw_ref, cell_ref,
    frac_ref, send_ref,
    f_ref,
):
    lines, px = gw_ref.shape
    n_ty = lax.axis_size("ty")
    me = lax.axis_index("tx") * n_ty + lax.axis_index("ty")
    rows = OUT_LINES * CH
    above, below = from_turns(
        me, devices, first_swap_ref[16:32, :].astype(f32), second_swap_ref[16:32, :].astype(f32)
    )
    n = HALO_LINES

    pieces = []
    for ch in range(2):
        own = sar_ref[ch].astype(f32)
        pieces += [above[ch * n : (ch + 1) * n], own[0:n], own[lines - n :], below[ch * n : (ch + 1) * n]]
    x = image_columns(jnp.concatenate(pieces, 0))
    half = 6 * CH
    out_line = quo(iota((half, px), 0), CH).astype(f32).astype(bf16)
    nil = jnp.zeros((half, px), bf16)
    low = jnp.where(me == 0, n, 0)
    high = jnp.where(me == devices - 1, OUT_LINES - 8 - n, OUT_LINES)
    for layer, (w_ref, e_ref) in enumerate(((w1_ref, e1_ref), (w2_ref, e2_ref), (w3_ref, e3_ref)), 1):
        if layer == 1:
            acc = dot(w_ref[...], x).astype(bf16)
            top, bottom = acc[0:half], acc[8 * CH :]
        else:
            before, after = pixel_shifts(block)
            top, bottom = [
                jnp.concatenate(
                    [
                        dot(w_ref[...], mid_columns(*[y[at * CH : (at + MID_IN) * CH] for y in (before, block, after)]))
                        for at in (first, first + MID_LINES)
                    ],
                    0,
                ).astype(bf16)
                for first in (0, 8)
            ]
        top = jnp.where(out_line >= (low - layer).astype(f32).astype(bf16), jnp.maximum(top, nil), nil)
        bottom = jnp.where(out_line < (high + layer).astype(f32).astype(bf16), jnp.maximum(bottom, nil), nil)
        block = jnp.concatenate([top, e_ref[...], bottom], 0)
    frac = sigmoid(merged(dot(w4_ref[...], block), CH)).astype(f32)
    f_ref[...] = frac_in[...].astype(f32)
    f_ref[0:6, :] = frac[0:6]
    f_ref[lines - 6 :, :] = frac[8:14]
    frac_ref[...] = f_ref[...].astype(bf16)
    quarter = slots_in.shape[1] // 4
    sums = []
    for at in (slice(0, END_LINES), slice(lines - END_LINES, lines)):
        cov = gw_ref[at, :]
        sums += line_windows(cell_ref[at, :], f_ref[at, :] * cov, cov, quarter)
    by_slot = slots_in[...] + dot(perm_ref[...], window_goods(jnp.concatenate(sums, 0)))

    per_tile = 4 * capacity
    slots, tile_cols = by_slot.shape
    h = SUBSTEPS
    entry = rem(iota((slots, LANES), 0), per_tile)
    here = quo(iota((slots, LANES), 1), h) == entry
    column = rem(quo(iota((slots, LANES), 0), per_tile), n_ty)
    source = iota((LANES, LANES), 0)
    spot = rem(iota((LANES, LANES), 1), h)

    def strip(x, first_lane, keep):
        take = ((spot + first_lane == source) & (source - first_lane < h)).astype(bf16)
        x = jnp.where(here & keep, dot(x.astype(bf16), take), 0.0)
        return jnp.sum(x.reshape(devices, per_tile, LANES), 1, keepdims=True)

    right_strip = strip(of_right(by_slot[:, 0:LANES], per_tile), 0, column < n_ty - 1)
    left_strip = strip(of_left(by_slot[:, tile_cols - LANES :], per_tile), LANES - h, column > 0)
    at = iota((devices, 8, LANES), 1)
    extra = extra_ref[...].reshape(devices, 8, LANES)
    extra = jnp.where(at == 0, right_strip, jnp.where(at == 1, left_strip, extra))
    halves = [by_slot[:, at : at + LANES].reshape(devices, per_tile, LANES) for at in range(0, tile_cols, LANES)]
    packed = jnp.concatenate([*halves, extra], 1)
    send_ref[...] = packed.reshape(send_ref.shape).astype(bf16)


def transposed(x):
    return jnp.transpose(x, (1, 0))


def level_kernel(
    devices,
    got_ref, second_swap_ref, first_swap_ref, depth_ref, slope_ref, rain_ref, dir_ref,
    level_ref, side_ref, first_ref, second_ref,
):
    tile_rows, tile_cols = depth_ref.shape
    h = SUBSTEPS
    halves = tile_cols // LANES
    n = (got_ref.shape[0] // devices - 8) // halves
    k = devices * n
    packed = got_ref[...].astype(f32).reshape(devices, halves * n + 8, LANES)
    main = jnp.concatenate([packed[:, i * n : (i + 1) * n].reshape(k, LANES) for i in range(halves)], 1)
    extra = packed[:, halves * n :]

    entry = rem(iota((k, LANES), 0), n)
    spread = quo(iota((k, LANES), 1), h) == entry

    def strip(r, first):
        rows = jnp.broadcast_to(extra[:, r : r + 1], (devices, n, LANES)).reshape(k, LANES)
        take = rem(iota((LANES, LANES), 0), h) + first == iota((LANES, LANES), 1)
        return dot(jnp.where(spread, rows, 0.0).astype(bf16), take.astype(bf16)).astype(bf16)

    lane = iota((1, k), 1)
    offset = rem(lane, 2) + tile_rows * rem(quo(lane, 2), 2)
    info = jnp.broadcast_to(extra[:, 2:3], (devices, n, LANES)).reshape(k, LANES)
    info = jnp.where(rem(iota((k, LANES), 1), n) == entry, info, 0.0).astype(bf16)
    turns = (quo(iota((LANES, LANES), 0), n) == iota((LANES, LANES), 1)).astype(bf16)
    lines = transposed(dot(info, turns))

    def placer(turn):
        target = lines[turn : turn + 1].astype(jnp.int32) + offset
        return jnp.where(iota((2 * tile_rows, k), 0) == target, 1.0, 0.0).astype(bf16)

    summed = dot(placer(0), main.astype(bf16))
    summed_side = dot(placer(1), strip(0, 0)) + dot(placer(2), strip(1, LANES - h))

    ty = lax.axis_index("ty")
    tx = lax.axis_index("tx")
    previous, following = from_turns(
        tx * lax.axis_size("ty") + ty, devices,
        first_swap_ref[0:16, :].astype(f32), second_swap_ref[0:16, :].astype(f32),
    )
    left = strips_of(previous, ty > 0)
    right = strips_of(following, ty < lax.axis_size("ty") - 1)
    gap = jnp.zeros((LANES - 2 * h, tile_rows), f32)
    depth_side, conv_side, rain_side, code_side = [
        transposed(jnp.concatenate([r, gap, l], 0)) for r, l in zip(right, left)
    ]

    def analysed(sums, depth):
        observed = sums[0:tile_rows]
        covered = sums[tile_rows:]
        wet = depth / (depth + wet_depth)
        innovation = (observed - covered * wet) / (covered + 1.0)
        return depth * jnp.exp(innovation)

    level = analysed(summed, depth_ref[...])
    level_ref[...] = level
    sides = (analysed(summed_side, depth_side), rain_side, conv_side, code_side)
    owns = (level, rain_ref, slope_ref, dir_ref)

    def end_rows(at):
        own = [x[at, :] for x in owns]
        own[2] = runoff_coef * jnp.sqrt(own[2])
        own[3] = own[3].astype(f32)
        return jnp.concatenate([jnp.concatenate([o, x[at]], 1) for o, x in zip(own, sides)], 0)

    for i, x in enumerate(sides):
        side_ref[i] = x
    first, second = in_turn(rem(tx, 2) == 0, end_rows(slice(tile_rows - h, tile_rows)), end_rows(slice(0, h)))
    first_ref[...] = first.astype(bf16)
    second_ref[...] = second.astype(bf16)


def substeps(level, rain, conv, code, rain_s, conv_s, m_ref, part_ref, up_ref, down_ref, chunk):
    rows, cols = level.shape
    h = SUBSTEPS
    for ref in (up_ref, down_ref):
        ref[0] = jnp.zeros(ref.shape[1:], f32)
        ref[1, 0:h, :] = jnp.zeros((h, cols), f32)
        ref[1, h + rows :, :] = jnp.zeros((h, cols), f32)
    part_ref[0] = level
    rain_s[...] = rain
    conv_s[...] = conv
    sides = (-1, 0, 1, -1, 1, -1, 0, 1)
    for direction, side in enumerate(sides):
        share = jnp.where(code == direction, conv, 0.0)
        m_ref[direction] = pltpu.roll(share, side % cols, 1) if side else share

    def level_at(buf, r, n):
        level = part_ref[buf, r : r + n, :]
        return level + up_ref[buf, h + r + 1 : h + r + 1 + n, :] + down_ref[buf, h + r - 1 : h + r - 1 + n, :]

    def substep(buf, new):
        for r in range(0, rows, chunk):
            level = level_at(buf, r, chunk)
            power = level * jnp.exp2((2.0 / 3.0 / math.log(2.0)) * jnp.log(jnp.maximum(jnp.abs(level), 1e-30)))
            from_right = pltpu.roll(power, cols - 1, 1)
            from_left = pltpu.roll(power, 1, 1)
            m = [m_ref[d, r : r + chunk, :] for d in range(8)]
            up_ref[new, h + r : h + r + chunk, :] = m[0] * from_right + m[1] * power + m[2] * from_left
            down_ref[new, h + r : h + r + chunk, :] = m[5] * from_right + m[6] * power + m[7] * from_left
            part_ref[new, r : r + chunk, :] = (
                level + rain_s[r : r + chunk, :] - conv_s[r : r + chunk, :] * power
                + (m[3] * from_right + m[4] * from_left)
            )

    def substep_pair(i, carry):
        substep(0, 1)
        substep(1, 0)
        return carry

    if rows > LANES:
        lax.fori_loop(0, SUBSTEPS // 2, substep_pair, 0)
    else:
        for i in range(SUBSTEPS // 2):
            substep_pair(i, 0)
    return level_at


def flow_inner_kernel(level_ref, side_ref, slope_ref, dir_ref, rain_ref, out_ref, *scratch):
    rows, cols = level_ref.shape
    own = (level_ref[...], rain_ref[...], runoff_coef * jnp.sqrt(slope_ref[...]), dir_ref[...].astype(f32))
    level_at = substeps(*[jnp.concatenate([x, side_ref[i]], 1) for i, x in enumerate(own)], *scratch, 32)
    out_ref[...] = level_at(0, 0, rows)[:, 0:cols]


def flow_ends_kernel(inner_ref, level_ref, side_ref, slope_ref, dir_ref, rain_ref, first_swap_ref, second_swap_ref, out_ref, *scratch):
    rows, cols = level_ref.shape
    h = SUBSTEPS
    above, below = from_turns(
        lax.axis_index("tx"), lax.axis_size("tx"),
        first_swap_ref[...].astype(f32), second_swap_ref[...].astype(f32),
    )
    fields = []
    for i, ref in enumerate((level_ref, rain_ref, slope_ref, dir_ref)):
        ends = []
        for at in (slice(0, 2 * h), slice(rows - 2 * h, rows)):
            own = ref[at, :].astype(f32)
            if i == 2:
                own = runoff_coef * jnp.sqrt(own)
            ends.append(jnp.concatenate([own, side_ref[i, at, :]], 1))
        fields.append(jnp.concatenate([above[i * h : (i + 1) * h], *ends, below[i * h : (i + 1) * h]], 0))
    level_at = substeps(*fields, *scratch, 16)
    out_ref[h : rows - h, :] = inner_ref[h : rows - h, :]
    out_ref[0:h, :] = level_at(0, h, h)[:, 0:cols]
    out_ref[rows - h :, :] = level_at(0, 4 * h, h)[:, 0:cols]


def flow_scratch(rows, cols):
    return [
        pltpu.VMEM((rows, cols), f32),
        pltpu.VMEM((rows, cols), f32),
        pltpu.VMEM((8, rows, cols), f32),
        pltpu.VMEM((2, rows, cols), f32),
        pltpu.VMEM((2, rows + 2 * SUBSTEPS, cols), f32),
        pltpu.VMEM((2, rows + 2 * SUBSTEPS, cols), f32),
    ]


def hbm_specs(n):
    return [pl.BlockSpec(memory_space=pltpu.HBM)] * n


def vmem_specs(n):
    return [pl.BlockSpec(memory_space=pltpu.VMEM)] * n


def per_device(
    sar_image, kernel_first, kernel_second, kernel_third, kernel_last,
    geo_weight, cell_index, block_tile, block_row, depth, slope, flow_dir, rain,
):
    both = ("tx", "ty")
    devices = lax.axis_size(both)
    az_lines, range_px = geo_weight.shape
    tile_rows, tile_cols = depth.shape
    capacity = max(2, 2 * az_lines // devices)

    n_tx, n_ty = lax.axis_size("tx"), lax.axis_size("ty")

    def swaps(first, second, stride):
        size = devices // stride
        out = []
        for start, x in ((1, second), (0, first)):
            to = {}
            for place in range(start, size, 2):
                for k in range(stride):
                    i, j = place * stride + k, (place + 1) % size * stride + k
                    if place == size - 1 and stride > 1:
                        ends = (i, i ^ 1), (j, j ^ 1)
                    else:
                        ends = (i, j), (j, i)
                    to.update(ends)
            out.append(lax.ppermute(x, both, sorted(to.items())))
        return out[::-1]

    params = pltpu.CompilerParams(vmem_limit_bytes=VMEM_LIMIT)
    message = pltpu.VMEM((32, range_px), bf16)
    handed = (
        sar_image,
        jnp.transpose(kernel_first, (2, 3, 1, 0)),
        jnp.transpose(kernel_second, (2, 3, 0, 1)).reshape(9 * CH, CH),
        jnp.transpose(kernel_third, (2, 3, 0, 1)).reshape(9 * CH, CH),
        jnp.transpose(kernel_last[0], (1, 2, 0)),
        block_tile.reshape(1, az_lines),
        block_row.reshape(1, az_lines),
        geo_weight,
        cell_index,
    )
    first, second, sar_image, *handed = pl.pallas_call(
        edge_kernel,
        out_shape=(message, message, *[pltpu.VMEM(x.shape, x.dtype) for x in handed]),
        in_specs=hbm_specs(4 + len(handed)),
        out_specs=tuple(vmem_specs(2 + len(handed))),
        scratch_shapes=[
            *[pltpu.VMEM(x.shape, x.dtype) for x in (depth, slope, rain, flow_dir)],
            pltpu.SemaphoreType.DMA((4 + len(handed),)),
        ],
        compiler_params=pltpu.CompilerParams(vmem_limit_bytes=VMEM_MOST),
        name="edges",
    )(depth, slope, rain, flow_dir, *handed)
    geo_weight, cell_index = handed[-2:]
    halo = swaps(first, second, 1)

    rows, cols = OUT_LINES * CH, IN_LINES * CH
    slots = devices * capacity * 4
    send_rows = tile_cols // LANES * 4 * capacity + 8
    full = (az_lines + 4) // OUT_LINES + 1
    feats = (full * OUT_LINES + 3) * CH
    blocks_in = (az_lines + IN_LINES, range_px)

    def cost(flops):
        return pl.CostEstimate(flops=flops, bytes_accessed=4_000_000, transcendentals=0)

    prepared = pl.pallas_call(
        functools.partial(inner_kernel, devices, capacity),
        out_shape=(
            jax.ShapeDtypeStruct((rows, LANES), bf16),
            jax.ShapeDtypeStruct((MID_LINES * CH, cols), bf16),
            jax.ShapeDtypeStruct((MID_LINES * CH, cols), bf16),
            jax.ShapeDtypeStruct((3 * CH, cols), bf16),
            jax.ShapeDtypeStruct((slots, 2 * END_LINES * CH), bf16),
            jax.ShapeDtypeStruct((8 * devices, LANES), f32),
            jax.ShapeDtypeStruct((az_lines, range_px), bf16),
            jax.ShapeDtypeStruct((slots, tile_cols), f32),
            *[jax.ShapeDtypeStruct((4 * CH, range_px), bf16)] * 3,
        ),
        in_specs=vmem_specs(9),
        out_specs=tuple(vmem_specs(11)),
        scratch_shapes=[
            pltpu.VMEM((24, CH), f32),
            pltpu.VMEM((16, CH), f32),
            pltpu.VMEM((2, *blocks_in), f32),
            pltpu.VMEM((3, feats, range_px), bf16),
            pltpu.VMEM((3, feats, range_px), bf16),
            pltpu.VMEM((feats, range_px), bf16),
            pltpu.VMEM(blocks_in, f32),
            pltpu.VMEM(((az_lines - 2 * END_LINES) * CH, tile_cols // 4), f32),
        ],
        compiler_params=params,
        cost_estimate=cost(8_000_000_000),
        name="inner",
    )(
        *handed[:-2], sar_image, geo_weight, cell_index,
    )
    fraction, send = pl.pallas_call(
        functools.partial(ends_kernel, devices, capacity),
        out_shape=(
            jax.ShapeDtypeStruct((az_lines, range_px), bf16),
            jax.ShapeDtypeStruct((devices * send_rows, LANES), bf16),
        ),
        in_specs=vmem_specs(16),
        out_specs=tuple(vmem_specs(2)),
        scratch_shapes=[pltpu.VMEM((az_lines, range_px), f32)],
        compiler_params=params,
        name="ends",
    )(*halo[::-1], *prepared, sar_image, geo_weight, cell_index)

    got = lax.all_to_all(
        send.reshape(devices, send_rows, LANES), both, split_axis=0, concat_axis=0, tiled=True
    ).reshape(devices * send_rows, LANES)

    wide_cols = tile_cols + LANES
    edge = jax.ShapeDtypeStruct((4 * SUBSTEPS, wide_cols), bf16)
    level, side, first, second = pl.pallas_call(
        functools.partial(level_kernel, devices),
        out_shape=(
            jax.ShapeDtypeStruct((tile_rows, tile_cols), f32),
            jax.ShapeDtypeStruct((4, tile_rows, LANES), f32),
            edge,
            edge,
        ),
        in_specs=vmem_specs(7),
        out_specs=tuple(vmem_specs(4)),
        compiler_params=params,
        name="level",
    )(got, *halo[::-1], depth, slope, rain, flow_dir)

    row_halo = swaps(first, second, n_ty)

    inner = pl.pallas_call(
        flow_inner_kernel,
        out_shape=jax.ShapeDtypeStruct((tile_rows, tile_cols), f32),
        in_specs=vmem_specs(5),
        out_specs=vmem_specs(1)[0],
        scratch_shapes=flow_scratch(tile_rows, wide_cols),
        compiler_params=params,
        cost_estimate=cost(5_000_000_000),
        name="flow_inner",
    )(level, side, slope, flow_dir, rain)
    level = pl.pallas_call(
        flow_ends_kernel,
        out_shape=jax.ShapeDtypeStruct((tile_rows, tile_cols), f32),
        in_specs=vmem_specs(8),
        out_specs=vmem_specs(1)[0],
        scratch_shapes=flow_scratch(6 * SUBSTEPS, wide_cols),
        compiler_params=params,
        name="flow_ends",
    )(inner, level, side, slope, flow_dir, rain, *row_halo)
    return (fraction, level)


def solution(mesh):
    placed = (
        P(None, ("tx", "ty"), None),
        P(),
        P(),
        P(),
        P(),
        P(("tx", "ty"), None),
        P(("tx", "ty"), None),
        P(("tx", "ty"), None),
        P(("tx", "ty"), None),
        P("tx", "ty"),
        P("tx", "ty"),
        P("tx", "ty"),
        P("tx", "ty"),
    )
    return jax.shard_map(
        per_device,
        mesh=mesh,
        in_specs=placed,
        out_specs=(P(("tx", "ty"), None), P("tx", "ty")),
        check_vma=False,
    )
```

```python
import functools
import math

import jax
import jax.numpy as jnp
from jax import lax
from jax.experimental import pallas as pl
from jax.experimental.pallas import tpu as pltpu
from jax.sharding import PartitionSpec as P

WIN_ROWS = 2
SUBSTEPS = 8
CH = 16
OUT_LINES = 14
IN_LINES = OUT_LINES + 2
MID_LINES = 3
MID_IN = MID_LINES + 2
HALO_LINES = 4
END_LINES = 8
LANES = 128
VMEM_LIMIT = 48 * 1024 * 1024
VMEM_MOST = 60160 * 1024

wet_depth = 0.5
runoff_coef = 0.25
bf16 = jnp.bfloat16
f32 = jnp.float32


def iota(shape, dim):
    return lax.broadcasted_iota(jnp.int32, shape, dim)


def quo(x, n):
    assert n & (n - 1) == 0
    return lax.shift_right_logical(x, jnp.int32(n.bit_length() - 1)) if n > 1 else x


def rem(x, n):
    assert n & (n - 1) == 0
    return x & (n - 1)


def dot(a, b):
    return lax.dot_general(a, b, (((1,), (0,)), ((), ())), preferred_element_type=f32)


def dot_0(a, b):
    return lax.dot_general(a, b, (((0,), (0,)), ((), ())), preferred_element_type=f32)


def dot_t(a, b):
    return lax.dot_general(a, b, (((1,), (1,)), ((), ())), preferred_element_type=f32)


def pixel_shifts(x):
    rows, width = x.shape
    lane = iota((rows, LANES), 1)
    zero = jnp.zeros((rows, LANES), x.dtype)
    first = lane.astype(f32).astype(x.dtype) == 0
    last = (LANES - 1 - lane).astype(f32).astype(x.dtype) == 0
    before = pltpu.roll(x, 1, 1)
    after = pltpu.roll(x, width - 1, 1)
    before = jnp.concatenate([jnp.where(first, zero, before[:, 0:LANES]), before[:, LANES:]], 1)
    after = jnp.concatenate([after[:, : width - LANES], jnp.where(last, zero, after[:, width - LANES :])], 1)
    return before, after


def merged(sums, n):
    before, _ = pixel_shifts(sums[0:n])
    _, after = pixel_shifts(sums[2 * n : 3 * n])
    return before + sums[n : 2 * n] + after


def image_columns(x):
    before, after = pixel_shifts(x)
    pad = jnp.zeros((LANES - 3 * x.shape[0], x.shape[1]), f32)
    return jnp.concatenate([before, x, after, pad], 0).astype(bf16)


def mid_columns(before, x, after):
    return jnp.concatenate([before, x, after, x[0:CH]], 0)


def sigmoid(x):
    return (1.0 / (1.0 + jnp.exp(-x))).astype(bf16)


def line_windows(cell, obs, cov, quarter):
    px = cell.shape[1]
    kind = iota((CH, px), 0)
    kind_part = rem(kind, CH // 2).astype(f32).astype(bf16)
    sub = kind.astype(f32).astype(bf16)
    one = jnp.ones((CH, px), bf16)
    nil = jnp.zeros((CH, px), bf16)
    part = quo(cell, quarter).astype(f32)
    col = rem(cell, quarter).astype(f32)

    def spread_row(x, i):
        return jnp.broadcast_to(x[i : i + 1], (CH, px)).astype(bf16)

    out = []
    for i in range(cell.shape[0]):
        pair = [jnp.broadcast_to(x[i : i + 1], (CH // 2, px)) for x in (obs, cov)]
        value = jnp.concatenate(pair, 0).astype(bf16)
        left = jnp.where(kind_part == spread_row(part, i), value, nil)
        where_col = spread_row(col, i)
        hot = jnp.concatenate([jnp.where(sub + g * CH == where_col, one, nil) for g in range(quarter // CH)], 0)
        out.append(dot_t(left, hot))
    return out


def window_goods(sums):
    rows, quarter = sums.shape
    cols = 4 * quarter
    repeat = (rem(iota((quarter, cols), 1), quarter) == iota((quarter, cols), 0)).astype(bf16)
    tiled = dot(sums.astype(bf16), repeat)
    mine = rem(iota((rows, cols), 0), 4) == quo(iota((rows, cols), 1), quarter)
    return jnp.where(mine, tiled, 0.0).astype(bf16)


def band_weights(tiled, rows, cols, per_row, line_of):
    out_line = quo(iota((rows, cols), 0), per_row)
    off = line_of(iota((rows, cols), 1)) - out_line
    out = jnp.zeros((rows, cols), f32)
    for ky in range(3):
        out = jnp.where(off == ky, tiled[ky], out)
    return out.astype(bf16)


def edge_kernel(
    depth_hbm, slope_hbm, rain_hbm, dir_hbm, sar_hbm, *refs
):
    n_on = (len(refs) - 8) // 2
    on_hbm = refs[:n_on]
    first_swap_ref, second_swap_ref, sar_ref, *on_refs = refs[n_on : 2 * n_on + 3]
    depth_ref, slope_ref, rain_ref, dir_ref, sems = refs[2 * n_on + 3 :]
    even = rem(lax.axis_index("tx") * lax.axis_size("ty") + lax.axis_index("ty"), 2) == 0
    lines, px = sar_hbm.shape[1:]
    cols = depth_hbm.shape[1]
    h = SUBSTEPS
    pairs = (
        (depth_hbm, depth_ref), (slope_hbm, slope_ref), (rain_hbm, rain_ref), (dir_hbm, dir_ref),
        (sar_hbm, sar_ref), *zip(on_hbm, on_refs),
    )
    copies = [pltpu.make_async_copy(src, dst, sems.at[i]) for i, (src, dst) in enumerate(pairs)]
    for copy in copies:
        copy.start()
    zeros = jnp.zeros((8, px), f32)
    strips = ([], [])
    for i, ref in enumerate((depth_ref, slope_ref, rain_ref, dir_ref)):
        copies[i].wait()
        own = [ref[:, cols - LANES :].astype(f32), ref[:, 0:LANES].astype(f32)]
        if i == 1:
            own = [runoff_coef * jnp.sqrt(x) for x in own]
        strips[0].append(jnp.transpose(own[0], (1, 0))[LANES - h :])
        strips[1].append(jnp.transpose(own[1], (1, 0))[0:h])
    copies[4].wait()
    messages = []
    for strip, at, lo in ((strips[0], lines - 16, 16 - HALO_LINES), (strips[1], 0, 0)):
        image = [sar_ref[ch, at : at + 16, :].astype(f32)[lo : lo + HALO_LINES] for ch in range(2)]
        messages.append(
            jnp.concatenate([jnp.concatenate(strip[0:2], 1), jnp.concatenate(strip[2:4], 1), *image, zeros], 0)
        )
    first, second = in_turn(even, *messages)
    first_swap_ref[...] = first.astype(bf16)
    second_swap_ref[...] = second.astype(bf16)
    for copy in copies[5:]:
        copy.wait()


def in_turn(even, to_next, to_previous):
    return jnp.where(even, to_next, to_previous), jnp.where(even, to_previous, to_next)


def from_turns(place, size, first, second):
    even = rem(place, 2) == 0
    previous = jnp.where(even, second, first)
    following = jnp.where(even, first, second)
    return jnp.where(place > 0, previous, 0.0), jnp.where(place < size - 1, following, 0.0)


def strips_of(message, keep):
    both = jnp.where(keep, message, 0.0)
    cols = both.shape[1] // 2
    return [both[0:8, 0:cols], both[0:8, cols:], both[8:16, 0:cols], both[8:16, cols:]]


def inner_kernel(
    devices, capacity,
    k1_ref, k2_ref, k3_ref, k4_ref, tile_ref, row_ref, sar_ref, gw_ref, cell_ref,
    w1_ref, w2_ref, w3_ref, w4_ref, perm_ref, extra_ref, frac_ref, slots_ref, e1_ref, e2_ref, e3_ref,
    t1_ref, t4_ref, s_ref, xa_ref, xb_ref, x3_ref, logit_ref, wnd_ref,
):
    rows = OUT_LINES * CH
    cols = IN_LINES * CH

    n2 = MID_LINES * cols
    spot2 = rem(iota((CH, n2), 1), cols) - iota((CH, n2), 0)
    line2 = quo(iota((CH, n2), 1), cols)
    n1 = OUT_LINES * LANES
    group1 = quo(rem(iota((8, n1), 1), LANES), IN_LINES) == iota((8, n1), 0)
    line1 = rem(iota((8, n1), 1), IN_LINES) - quo(iota((8, n1), 1), LANES)
    spread1 = [(group1 & (line1 == ky)).astype(bf16) for ky in range(3)]
    tile4 = (rem(iota((CH, cols), 1), CH) == iota((CH, cols), 0)).astype(bf16)
    t1_ref[...] = jnp.zeros(t1_ref.shape, f32)
    t4_ref[...] = jnp.zeros(t4_ref.shape, f32)
    for ky in range(3):
        for kx in range(3):
            t1_ref[ky * 8 + 2 * kx : ky * 8 + 2 * kx + 2, :] = k1_ref[ky, kx].astype(f32)
        t4_ref[ky * 3 : ky * 3 + 3, :] = k4_ref[ky].astype(f32)
    wide1 = sum(dot_0(t1_ref[ky * 8 : ky * 8 + 8, :].astype(bf16), spread1[ky]) for ky in range(3))
    for i in range(OUT_LINES):
        w1_ref[i * CH : (i + 1) * CH, :] = wide1[:, i * LANES : (i + 1) * LANES].astype(bf16)
    spread2 = [
        (spot2 == (kx * MID_IN + ky + line2) * CH).astype(bf16) for ky in range(3) for kx in range(3)
    ]
    for k_ref, w_ref in ((k2_ref, w2_ref), (k3_ref, w3_ref)):
        wide = sum(dot(k_ref[n * CH : (n + 1) * CH, :], spread2[n]) for n in range(9))
        for i in range(MID_LINES):
            w_ref[i * CH : (i + 1) * CH, :] = wide[:, i * cols : (i + 1) * cols].astype(bf16)
    wide4 = dot(t4_ref[...].astype(bf16), tile4)
    w4_ref[...] = jnp.concatenate(
        [
            band_weights(
                [jnp.broadcast_to(wide4[ky * 3 + kx : ky * 3 + kx + 1], (CH, cols)) for ky in range(3)],
                CH, cols, 1, lambda k: quo(k, CH),
            )
            for kx in range(3)
        ],
        0,
    )

    lines = tile_ref.shape[1]
    tile = tile_ref[...].astype(f32)
    same = iota((lines, lines), 0) == iota((lines, lines), 1)
    tile_sub = jnp.sum(jnp.where(same, jnp.broadcast_to(tile, (lines, lines)), 0.0), 1, keepdims=True)
    rival = (tile_sub == tile) & (iota((lines, lines), 0) < iota((lines, lines), 1))
    slot = tile * capacity + jnp.sum(jnp.where(rival, 1.0, 0.0), 0, keepdims=True)
    slots = slots_ref.shape[0]
    wnd_rows = CH * lines
    per_line = CH
    widen = (quo(iota((lines, wnd_rows), 1), per_line) == iota((lines, wnd_rows), 0)).astype(bf16)
    slot_wide = dot(jnp.broadcast_to(slot, (8, lines)).astype(bf16), widen)[0:1]
    place = slot_wide.astype(jnp.int32) * 4 + rem(quo(iota((1, wnd_rows), 1), 4), 4)
    perm = jnp.where(iota((slots, wnd_rows), 0) == place, 1.0, 0.0).astype(bf16)
    end = END_LINES * CH
    perm_ref[...] = jnp.concatenate([perm[:, 0:end], perm[:, wnd_rows - end :]], 1)

    row_of = dot(
        jnp.where(same, jnp.broadcast_to(row_ref[...].astype(f32), (lines, lines)), 0.0).astype(bf16),
        jnp.ones((lines, LANES), bf16),
    )
    perm_line = jnp.where(quo(iota((slots, lines), 0), 4) == slot.astype(jnp.int32), 1.0, 0.0).astype(bf16)
    row_own = dot(perm_line, row_of.astype(bf16))
    per_tile = 4 * capacity
    lane = iota((slots, LANES), 1)
    entry = rem(iota((slots, LANES), 0), per_tile)
    info = jnp.zeros((slots, LANES), f32)
    for turn, value in enumerate((row_own, of_right(row_own, per_tile), of_left(row_own, per_tile))):
        info = jnp.where(lane == turn * per_tile + entry, value, info)
    info = jnp.sum(info.reshape(devices, per_tile, LANES), 1, keepdims=True)
    at = iota((devices, 8, LANES), 1)
    extra_ref[...] = jnp.where(at == 2, info, 0.0).reshape(8 * devices, LANES)


    px = sar_ref.shape[2]
    for ch in range(2):
        s_ref[ch, 0:lines, :] = sar_ref[ch].astype(f32)
        s_ref[ch, lines:, :] = jnp.zeros((s_ref.shape[1] - lines, px), f32)
    total = xa_ref.shape[1] // CH
    xa_ref[:, (total - 2) * CH :, :] = jnp.zeros((3, 2 * CH, px), bf16)

    def put(ref, line, acc):
        rows = acc.shape[0]
        feat = jnp.maximum(acc.astype(bf16), jnp.zeros(acc.shape, bf16))
        at = slice(line * CH, line * CH + rows)
        if len(ref.shape) == 2:
            ref[at, :] = feat
            return
        before, after = pixel_shifts(feat)
        ref[0, at, :] = before
        ref[1, at, :] = feat
        ref[2, at, :] = after

    full = (lines + 4) // OUT_LINES + 1
    for b in range(full):
        at = b * OUT_LINES
        x = jnp.concatenate([s_ref[0, at : at + IN_LINES, :], s_ref[1, at : at + IN_LINES, :]], 0)
        put(xa_ref, 1 + at, dot(w1_ref[...], image_columns(x)))
    stop = lines - 4
    for w_ref, src, dst, line, end_line in ((w2_ref, xa_ref, xb_ref, 2, stop), (w3_ref, xb_ref, x3_ref, 3, stop - 1)):
        for at in range(line, end_line, MID_LINES):
            x = src[:, (at - 1) * CH : (at - 1 + MID_IN) * CH, :]
            put(dst, at, dot(w_ref[...], mid_columns(*[x[i] for i in range(3)])))

    def ends_of(lo, center):
        hi = lines - lo - 2
        return jnp.concatenate([center[at * CH : (at + 2) * CH, :] for at in (lo, hi)], 0)

    e1_ref[...] = ends_of(3, xa_ref.at[1])
    e2_ref[...] = ends_of(4, xb_ref.at[1])
    e3_ref[...] = ends_of(5, x3_ref)
    logit_ref[0:END_LINES, :] = jnp.zeros((END_LINES, px), f32)
    starts = [3 + b * OUT_LINES for b in range(full - 2)] + [lines - 5 - IN_LINES]
    for at in starts:
        sums = dot(w4_ref[...], x3_ref[at * CH : at * CH + cols, :])
        logit_ref[at + 1 : at + 1 + CH, :] = merged(sums, CH)
    frac_ref[...] = sigmoid(logit_ref[0:lines, :])
    quarter = wnd_ref.shape[1]
    group = 16

    for g in range((lines - 2 * END_LINES) // group):
        at = slice(g * group + END_LINES, (g + 1) * group + END_LINES)
        cov = gw_ref[at, :]
        obs = sigmoid(logit_ref[at, :]).astype(f32) * cov
        for i, sums in enumerate(line_windows(cell_ref[at, :], obs, cov, quarter)):
            to = CH * (group * g + i)
            wnd_ref[to : to + CH, :] = sums
    slots_ref[...] = dot(perm[:, end : wnd_rows - end], window_goods(wnd_ref[...]))


def of_right(x, per_tile):
    return jnp.concatenate([x[per_tile:], jnp.zeros((per_tile, x.shape[1]), x.dtype)], 0)


def of_left(x, per_tile):
    return jnp.concatenate([jnp.zeros((per_tile, x.shape[1]), x.dtype), x[: x.shape[0] - per_tile]], 0)


def ends_kernel(
    devices, capacity,
    second_swap_ref, first_swap_ref, w1_ref, w2_ref, w3_ref, w4_ref, perm_ref, extra_ref, frac_in, slots_in, e1_ref, e2_ref, e3_ref,
    sar_ref, gw_ref, cell_ref,
    frac_ref, send_ref,
    f_ref,
):
    lines, px = gw_ref.shape
    n_ty = lax.axis_size("ty")
    me = lax.axis_index("tx") * n_ty + lax.axis_index("ty")
    rows = OUT_LINES * CH
    above, below = from_turns(
        me, devices, first_swap_ref[16:32, :].astype(f32), second_swap_ref[16:32, :].astype(f32)
    )
    n = HALO_LINES

    pieces = []
    for ch in range(2):
        own = sar_ref[ch].astype(f32)
        pieces += [above[ch * n : (ch + 1) * n], own[0:n], own[lines - n :], below[ch * n : (ch + 1) * n]]
    x = image_columns(jnp.concatenate(pieces, 0))
    half = 6 * CH
    out_line = quo(iota((half, px), 0), CH).astype(f32).astype(bf16)
    nil = jnp.zeros((half, px), bf16)
    low = jnp.where(me == 0, n, 0)
    high = jnp.where(me == devices - 1, OUT_LINES - 8 - n, OUT_LINES)
    for layer, (w_ref, e_ref) in enumerate(((w1_ref, e1_ref), (w2_ref, e2_ref), (w3_ref, e3_ref)), 1):
        if layer == 1:
            acc = dot(w_ref[...], x).astype(bf16)
            top, bottom = acc[0:half], acc[8 * CH :]
        else:
            before, after = pixel_shifts(block)
            top, bottom = [
                jnp.concatenate(
                    [
                        dot(w_ref[...], mid_columns(*[y[at * CH : (at + MID_IN) * CH] for y in (before, block, after)]))
                        for at in (first, first + MID_LINES)
                    ],
                    0,
                ).astype(bf16)
                for first in (0, 8)
            ]
        top = jnp.where(out_line >= (low - layer).astype(f32).astype(bf16), jnp.maximum(top, nil), nil)
        bottom = jnp.where(out_line < (high + layer).astype(f32).astype(bf16), jnp.maximum(bottom, nil), nil)
        block = jnp.concatenate([top, e_ref[...], bottom], 0)
    frac = sigmoid(merged(dot(w4_ref[...], block), CH)).astype(f32)
    f_ref[...] = frac_in[...].astype(f32)
    f_ref[0:6, :] = frac[0:6]
    f_ref[lines - 6 :, :] = frac[8:14]
    frac_ref[...] = f_ref[...].astype(bf16)
    quarter = slots_in.shape[1] // 4
    sums = []
    for at in (slice(0, END_LINES), slice(lines - END_LINES, lines)):
        cov = gw_ref[at, :]
        sums += line_windows(cell_ref[at, :], f_ref[at, :] * cov, cov, quarter)
    by_slot = slots_in[...] + dot(perm_ref[...], window_goods(jnp.concatenate(sums, 0)))

    per_tile = 4 * capacity
    slots, tile_cols = by_slot.shape
    h = SUBSTEPS
    entry = rem(iota((slots, LANES), 0), per_tile)
    here = quo(iota((slots, LANES), 1), h) == entry
    column = rem(quo(iota((slots, LANES), 0), per_tile), n_ty)
    source = iota((LANES, LANES), 0)
    spot = rem(iota((LANES, LANES), 1), h)

    def strip(x, first_lane, keep):
        take = ((spot + first_lane == source) & (source - first_lane < h)).astype(bf16)
        x = jnp.where(here & keep, dot(x.astype(bf16), take), 0.0)
        return jnp.sum(x.reshape(devices, per_tile, LANES), 1, keepdims=True)

    right_strip = strip(of_right(by_slot[:, 0:LANES], per_tile), 0, column < n_ty - 1)
    left_strip = strip(of_left(by_slot[:, tile_cols - LANES :], per_tile), LANES - h, column > 0)
    at = iota((devices, 8, LANES), 1)
    extra = extra_ref[...].reshape(devices, 8, LANES)
    extra = jnp.where(at == 0, right_strip, jnp.where(at == 1, left_strip, extra))
    halves = [by_slot[:, at : at + LANES].reshape(devices, per_tile, LANES) for at in range(0, tile_cols, LANES)]
    packed = jnp.concatenate([*halves, extra], 1)
    send_ref[...] = packed.reshape(send_ref.shape).astype(bf16)


def transposed(x):
    return jnp.transpose(x, (1, 0))


def level_kernel(
    devices,
    got_ref, second_swap_ref, first_swap_ref, depth_ref, slope_ref, rain_ref, dir_ref,
    level_ref, side_ref, first_ref, second_ref,
):
    tile_rows, tile_cols = depth_ref.shape
    h = SUBSTEPS
    halves = tile_cols // LANES
    n = (got_ref.shape[0] // devices - 8) // halves
    k = devices * n
    packed = got_ref[...].astype(f32).reshape(devices, halves * n + 8, LANES)
    main = jnp.concatenate([packed[:, i * n : (i + 1) * n].reshape(k, LANES) for i in range(halves)], 1)
    extra = packed[:, halves * n :]

    entry = rem(iota((k, LANES), 0), n)
    spread = quo(iota((k, LANES), 1), h) == entry

    def strip(r, first):
        rows = jnp.broadcast_to(extra[:, r : r + 1], (devices, n, LANES)).reshape(k, LANES)
        take = rem(iota((LANES, LANES), 0), h) + first == iota((LANES, LANES), 1)
        return dot(jnp.where(spread, rows, 0.0).astype(bf16), take.astype(bf16)).astype(bf16)

    lane = iota((1, k), 1)
    offset = rem(lane, 2) + tile_rows * rem(quo(lane, 2), 2)
    info = jnp.broadcast_to(extra[:, 2:3], (devices, n, LANES)).reshape(k, LANES)
    info = jnp.where(rem(iota((k, LANES), 1), n) == entry, info, 0.0).astype(bf16)
    turns = (quo(iota((LANES, LANES), 0), n) == iota((LANES, LANES), 1)).astype(bf16)
    lines = transposed(dot(info, turns))

    def placer(turn):
        target = lines[turn : turn + 1].astype(jnp.int32) + offset
        return jnp.where(iota((2 * tile_rows, k), 0) == target, 1.0, 0.0).astype(bf16)

    summed = dot(placer(0), main.astype(bf16))
    summed_side = dot(placer(1), strip(0, 0)) + dot(placer(2), strip(1, LANES - h))

    ty = lax.axis_index("ty")
    tx = lax.axis_index("tx")
    previous, following = from_turns(
        tx * lax.axis_size("ty") + ty, devices,
        first_swap_ref[0:16, :].astype(f32), second_swap_ref[0:16, :].astype(f32),
    )
    left = strips_of(previous, ty > 0)
    right = strips_of(following, ty < lax.axis_size("ty") - 1)
    gap = jnp.zeros((LANES - 2 * h, tile_rows), f32)
    depth_side, conv_side, rain_side, code_side = [
        transposed(jnp.concatenate([r, gap, l], 0)) for r, l in zip(right, left)
    ]

    def analysed(sums, depth):
        observed = sums[0:tile_rows]
        covered = sums[tile_rows:]
        wet = depth / (depth + wet_depth)
        innovation = (observed - covered * wet) / (covered + 1.0)
        return depth * jnp.exp(innovation)

    level = analysed(summed, depth_ref[...])
    level_ref[...] = level
    sides = (analysed(summed_side, depth_side), rain_side, conv_side, code_side)
    owns = (level, rain_ref, slope_ref, dir_ref)

    def end_rows(at):
        own = [x[at, :] for x in owns]
        own[2] = runoff_coef * jnp.sqrt(own[2])
        own[3] = own[3].astype(f32)
        return jnp.concatenate([jnp.concatenate([o, x[at]], 1) for o, x in zip(own, sides)], 0)

    for i, x in enumerate(sides):
        side_ref[i] = x
    first, second = in_turn(rem(tx, 2) == 0, end_rows(slice(tile_rows - h, tile_rows)), end_rows(slice(0, h)))
    first_ref[...] = first.astype(bf16)
    second_ref[...] = second.astype(bf16)


def substeps(level, rain, conv, code, rain_s, conv_s, m_ref, part_ref, up_ref, down_ref, chunk):
    rows, cols = level.shape
    h = SUBSTEPS
    for ref in (up_ref, down_ref):
        ref[0] = jnp.zeros(ref.shape[1:], f32)
        ref[1, 0:h, :] = jnp.zeros((h, cols), f32)
        ref[1, h + rows :, :] = jnp.zeros((h, cols), f32)
    part_ref[0] = level
    rain_s[...] = rain
    conv_s[...] = conv
    sides = (-1, 0, 1, -1, 1, -1, 0, 1)
    for direction, side in enumerate(sides):
        share = jnp.where(code == direction, conv, 0.0)
        m_ref[direction] = pltpu.roll(share, side % cols, 1) if side else share

    def level_at(buf, r, n):
        level = part_ref[buf, r : r + n, :]
        return level + up_ref[buf, h + r + 1 : h + r + 1 + n, :] + down_ref[buf, h + r - 1 : h + r - 1 + n, :]

    def substep(buf, new):
        for r in range(0, rows, chunk):
            level = level_at(buf, r, chunk)
            power = level * jnp.exp2((2.0 / 3.0 / math.log(2.0)) * jnp.log(jnp.maximum(jnp.abs(level), 1e-30)))
            from_right = pltpu.roll(power, cols - 1, 1)
            from_left = pltpu.roll(power, 1, 1)
            m = [m_ref[d, r : r + chunk, :] for d in range(8)]
            up_ref[new, h + r : h + r + chunk, :] = m[0] * from_right + m[1] * power + m[2] * from_left
            down_ref[new, h + r : h + r + chunk, :] = m[5] * from_right + m[6] * power + m[7] * from_left
            part_ref[new, r : r + chunk, :] = (
                level + rain_s[r : r + chunk, :] - conv_s[r : r + chunk, :] * power
                + (m[3] * from_right + m[4] * from_left)
            )

    def substep_pair(i, carry):
        substep(0, 1)
        substep(1, 0)
        return carry

    if rows > LANES:
        lax.fori_loop(0, SUBSTEPS // 2, substep_pair, 0)
    else:
        for i in range(SUBSTEPS // 2):
            substep_pair(i, 0)
    return level_at


def flow_inner_kernel(level_ref, side_ref, slope_ref, dir_ref, rain_ref, out_ref, *scratch):
    rows, cols = level_ref.shape
    own = (level_ref[...], rain_ref[...], runoff_coef * jnp.sqrt(slope_ref[...]), dir_ref[...].astype(f32))
    level_at = substeps(*[jnp.concatenate([x, side_ref[i]], 1) for i, x in enumerate(own)], *scratch, 64)
    out_ref[...] = level_at(0, 0, rows)[:, 0:cols]


def flow_ends_kernel(inner_ref, level_ref, side_ref, slope_ref, dir_ref, rain_ref, first_swap_ref, second_swap_ref, out_ref, *scratch):
    rows, cols = level_ref.shape
    h = SUBSTEPS
    above, below = from_turns(
        lax.axis_index("tx"), lax.axis_size("tx"),
        first_swap_ref[...].astype(f32), second_swap_ref[...].astype(f32),
    )
    fields = []
    for i, ref in enumerate((level_ref, rain_ref, slope_ref, dir_ref)):
        ends = []
        for at in (slice(0, 2 * h), slice(rows - 2 * h, rows)):
            own = ref[at, :].astype(f32)
            if i == 2:
                own = runoff_coef * jnp.sqrt(own)
            ends.append(jnp.concatenate([own, side_ref[i, at, :]], 1))
        fields.append(jnp.concatenate([above[i * h : (i + 1) * h], *ends, below[i * h : (i + 1) * h]], 0))
    level_at = substeps(*fields, *scratch, 6 * h)
    out_ref[h : rows - h, :] = inner_ref[h : rows - h, :]
    out_ref[0:h, :] = level_at(0, h, h)[:, 0:cols]
    out_ref[rows - h :, :] = level_at(0, 4 * h, h)[:, 0:cols]


def flow_scratch(rows, cols):
    return [
        pltpu.VMEM((rows, cols), f32),
        pltpu.VMEM((rows, cols), f32),
        pltpu.VMEM((8, rows, cols), f32),
        pltpu.VMEM((2, rows, cols), f32),
        pltpu.VMEM((2, rows + 2 * SUBSTEPS, cols), f32),
        pltpu.VMEM((2, rows + 2 * SUBSTEPS, cols), f32),
    ]


def hbm_specs(n):
    return [pl.BlockSpec(memory_space=pltpu.HBM)] * n


def vmem_specs(n):
    return [pl.BlockSpec(memory_space=pltpu.VMEM)] * n


def per_device(
    sar_image, kernel_first, kernel_second, kernel_third, kernel_last,
    geo_weight, cell_index, block_tile, block_row, depth, slope, flow_dir, rain,
):
    both = ("tx", "ty")
    devices = lax.axis_size(both)
    az_lines, range_px = geo_weight.shape
    tile_rows, tile_cols = depth.shape
    capacity = max(2, 2 * az_lines // devices)

    n_tx, n_ty = lax.axis_size("tx"), lax.axis_size("ty")

    def swaps(first, second, stride):
        size = devices // stride
        out = []
        for start, x in ((1, second), (0, first)):
            to = {}
            for place in range(start, size, 2):
                for k in range(stride):
                    i, j = place * stride + k, (place + 1) % size * stride + k
                    if place == size - 1 and stride > 1:
                        ends = (i, i ^ 1), (j, j ^ 1)
                    else:
                        ends = (i, j), (j, i)
                    to.update(ends)
            out.append(lax.ppermute(x, both, sorted(to.items())))
        return out[::-1]

    params = pltpu.CompilerParams(vmem_limit_bytes=VMEM_LIMIT)
    message = pltpu.VMEM((32, range_px), bf16)
    handed = (
        sar_image,
        jnp.transpose(kernel_first, (2, 3, 1, 0)),
        jnp.transpose(kernel_second, (2, 3, 0, 1)).reshape(9 * CH, CH),
        jnp.transpose(kernel_third, (2, 3, 0, 1)).reshape(9 * CH, CH),
        jnp.transpose(kernel_last[0], (1, 2, 0)),
        block_tile.reshape(1, az_lines),
        block_row.reshape(1, az_lines),
        geo_weight,
        cell_index,
    )
    first, second, sar_image, *handed = pl.pallas_call(
        edge_kernel,
        out_shape=(message, message, *[pltpu.VMEM(x.shape, x.dtype) for x in handed]),
        in_specs=hbm_specs(4 + len(handed)),
        out_specs=tuple(vmem_specs(2 + len(handed))),
        scratch_shapes=[
            *[pltpu.VMEM(x.shape, x.dtype) for x in (depth, slope, rain, flow_dir)],
            pltpu.SemaphoreType.DMA((4 + len(handed),)),
        ],
        compiler_params=pltpu.CompilerParams(vmem_limit_bytes=VMEM_MOST),
        name="edges",
    )(depth, slope, rain, flow_dir, *handed)
    geo_weight, cell_index = handed[-2:]
    halo = swaps(first, second, 1)

    rows, cols = OUT_LINES * CH, IN_LINES * CH
    slots = devices * capacity * 4
    send_rows = tile_cols // LANES * 4 * capacity + 8
    full = (az_lines + 4) // OUT_LINES + 1
    feats = (full * OUT_LINES + 3) * CH
    blocks_in = (az_lines + IN_LINES, range_px)

    def cost(flops):
        return pl.CostEstimate(flops=flops, bytes_accessed=4_000_000, transcendentals=0)

    prepared = pl.pallas_call(
        functools.partial(inner_kernel, devices, capacity),
        out_shape=(
            jax.ShapeDtypeStruct((rows, LANES), bf16),
            jax.ShapeDtypeStruct((MID_LINES * CH, cols), bf16),
            jax.ShapeDtypeStruct((MID_LINES * CH, cols), bf16),
            jax.ShapeDtypeStruct((3 * CH, cols), bf16),
            jax.ShapeDtypeStruct((slots, 2 * END_LINES * CH), bf16),
            jax.ShapeDtypeStruct((8 * devices, LANES), f32),
            jax.ShapeDtypeStruct((az_lines, range_px), bf16),
            jax.ShapeDtypeStruct((slots, tile_cols), f32),
            *[jax.ShapeDtypeStruct((4 * CH, range_px), bf16)] * 3,
        ),
        in_specs=vmem_specs(9),
        out_specs=tuple(vmem_specs(11)),
        scratch_shapes=[
            pltpu.VMEM((24, CH), f32),
            pltpu.VMEM((16, CH), f32),
            pltpu.VMEM((2, *blocks_in), f32),
            pltpu.VMEM((3, feats, range_px), bf16),
            pltpu.VMEM((3, feats, range_px), bf16),
            pltpu.VMEM((feats, range_px), bf16),
            pltpu.VMEM(blocks_in, f32),
            pltpu.VMEM(((az_lines - 2 * END_LINES) * CH, tile_cols // 4), f32),
        ],
        compiler_params=params,
        cost_estimate=cost(8_000_000_000),
        name="inner",
    )(
        *handed[:-2], sar_image, geo_weight, cell_index,
    )
    fraction, send = pl.pallas_call(
        functools.partial(ends_kernel, devices, capacity),
        out_shape=(
            jax.ShapeDtypeStruct((az_lines, range_px), bf16),
            jax.ShapeDtypeStruct((devices * send_rows, LANES), bf16),
        ),
        in_specs=vmem_specs(16),
        out_specs=tuple(vmem_specs(2)),
        scratch_shapes=[pltpu.VMEM((az_lines, range_px), f32)],
        compiler_params=params,
        name="ends",
    )(*halo[::-1], *prepared, sar_image, geo_weight, cell_index)

    got = lax.all_to_all(
        send.reshape(devices, send_rows, LANES), both, split_axis=0, concat_axis=0, tiled=True
    ).reshape(devices * send_rows, LANES)

    wide_cols = tile_cols + LANES
    edge = jax.ShapeDtypeStruct((4 * SUBSTEPS, wide_cols), bf16)
    level, side, first, second = pl.pallas_call(
        functools.partial(level_kernel, devices),
        out_shape=(
            jax.ShapeDtypeStruct((tile_rows, tile_cols), f32),
            jax.ShapeDtypeStruct((4, tile_rows, LANES), f32),
            edge,
            edge,
        ),
        in_specs=vmem_specs(7),
        out_specs=tuple(vmem_specs(4)),
        compiler_params=params,
        name="level",
    )(got, *halo[::-1], depth, slope, rain, flow_dir)

    row_halo = swaps(first, second, n_ty)

    inner = pl.pallas_call(
        flow_inner_kernel,
        out_shape=jax.ShapeDtypeStruct((tile_rows, tile_cols), f32),
        in_specs=vmem_specs(5),
        out_specs=vmem_specs(1)[0],
        scratch_shapes=flow_scratch(tile_rows, wide_cols),
        compiler_params=params,
        cost_estimate=cost(5_000_000_000),
        name="flow_inner",
    )(level, side, slope, flow_dir, rain)
    level = pl.pallas_call(
        flow_ends_kernel,
        out_shape=jax.ShapeDtypeStruct((tile_rows, tile_cols), f32),
        in_specs=vmem_specs(8),
        out_specs=vmem_specs(1)[0],
        scratch_shapes=flow_scratch(6 * SUBSTEPS, wide_cols),
        compiler_params=params,
        name="flow_ends",
    )(inner, level, side, slope, flow_dir, rain, *row_halo)
    return (fraction, level)


def solution(mesh):
    placed = (
        P(None, ("tx", "ty"), None),
        P(),
        P(),
        P(),
        P(),
        P(("tx", "ty"), None),
        P(("tx", "ty"), None),
        P(("tx", "ty"), None),
        P(("tx", "ty"), None),
        P("tx", "ty"),
        P("tx", "ty"),
        P("tx", "ty"),
        P("tx", "ty"),
    )
    return jax.shard_map(
        per_device,
        mesh=mesh,
        in_specs=placed,
        out_specs=(P(("tx", "ty"), None), P("tx", "ty")),
        check_vma=False,
    )
```

```python
import functools
import math

import jax
import jax.numpy as jnp
from jax import lax
from jax.experimental import pallas as pl
from jax.experimental.pallas import tpu as pltpu
from jax.sharding import PartitionSpec as P

WIN_ROWS = 2
SUBSTEPS = 8
CH = 16
OUT_LINES = 14
IN_LINES = OUT_LINES + 2
MID_LINES = 3
MID_IN = MID_LINES + 2
HALO_LINES = 4
END_LINES = 8
LANES = 128
VMEM_LIMIT = 48 * 1024 * 1024
VMEM_MOST = 60160 * 1024

wet_depth = 0.5
runoff_coef = 0.25
bf16 = jnp.bfloat16
f32 = jnp.float32


def iota(shape, dim):
    return lax.broadcasted_iota(jnp.int32, shape, dim)


def quo(x, n):
    assert n & (n - 1) == 0
    return lax.shift_right_logical(x, jnp.int32(n.bit_length() - 1)) if n > 1 else x


def rem(x, n):
    assert n & (n - 1) == 0
    return x & (n - 1)


def dot(a, b):
    return lax.dot_general(a, b, (((1,), (0,)), ((), ())), preferred_element_type=f32)


def dot_0(a, b):
    return lax.dot_general(a, b, (((0,), (0,)), ((), ())), preferred_element_type=f32)


def dot_t(a, b):
    return lax.dot_general(a, b, (((1,), (1,)), ((), ())), preferred_element_type=f32)


def pixel_shifts(x):
    rows, width = x.shape
    lane = iota((rows, LANES), 1)
    zero = jnp.zeros((rows, LANES), x.dtype)
    first = lane.astype(f32).astype(x.dtype) == 0
    last = (LANES - 1 - lane).astype(f32).astype(x.dtype) == 0
    before = pltpu.roll(x, 1, 1)
    after = pltpu.roll(x, width - 1, 1)
    before = jnp.concatenate([jnp.where(first, zero, before[:, 0:LANES]), before[:, LANES:]], 1)
    after = jnp.concatenate([after[:, : width - LANES], jnp.where(last, zero, after[:, width - LANES :])], 1)
    return before, after


def merged(sums, n):
    before, _ = pixel_shifts(sums[0:n])
    _, after = pixel_shifts(sums[2 * n : 3 * n])
    return before + sums[n : 2 * n] + after


def image_columns(x):
    before, after = pixel_shifts(x)
    pad = jnp.zeros((LANES - 3 * x.shape[0], x.shape[1]), f32)
    return jnp.concatenate([before, x, after, pad], 0).astype(bf16)


def mid_columns(before, x, after):
    return jnp.concatenate([before, x, after, x[0:CH]], 0)


def sigmoid(x):
    return (1.0 / (1.0 + jnp.exp(-x))).astype(bf16)


def line_windows(cell, obs, cov, quarter):
    px = cell.shape[1]
    kind = iota((CH, px), 0)
    kind_part = rem(kind, CH // 2).astype(f32).astype(bf16)
    sub = kind.astype(f32).astype(bf16)
    one = jnp.ones((CH, px), bf16)
    nil = jnp.zeros((CH, px), bf16)
    part = quo(cell, quarter).astype(f32)
    col = rem(cell, quarter).astype(f32)

    def spread_row(x, i):
        return jnp.broadcast_to(x[i : i + 1], (CH, px)).astype(bf16)

    out = []
    for i in range(cell.shape[0]):
        pair = [jnp.broadcast_to(x[i : i + 1], (CH // 2, px)) for x in (obs, cov)]
        value = jnp.concatenate(pair, 0).astype(bf16)
        left = jnp.where(kind_part == spread_row(part, i), value, nil)
        where_col = spread_row(col, i)
        hot = jnp.concatenate([jnp.where(sub + g * CH == where_col, one, nil) for g in range(quarter // CH)], 0)
        out.append(dot_t(left, hot))
    return out


def window_goods(sums):
    rows, quarter = sums.shape
    cols = 4 * quarter
    repeat = (rem(iota((quarter, cols), 1), quarter) == iota((quarter, cols), 0)).astype(bf16)
    tiled = dot(sums.astype(bf16), repeat)
    mine = rem(iota((rows, cols), 0), 4) == quo(iota((rows, cols), 1), quarter)
    return jnp.where(mine, tiled, 0.0).astype(bf16)


def band_weights(tiled, rows, cols, per_row, line_of):
    out_line = quo(iota((rows, cols), 0), per_row)
    off = line_of(iota((rows, cols), 1)) - out_line
    out = jnp.zeros((rows, cols), f32)
    for ky in range(3):
        out = jnp.where(off == ky, tiled[ky], out)
    return out.astype(bf16)


def edge_kernel(
    depth_hbm, slope_hbm, rain_hbm, dir_hbm, sar_hbm, *refs
):
    n_on = (len(refs) - 8) // 2
    on_hbm = refs[:n_on]
    first_swap_ref, second_swap_ref, sar_ref, *on_refs = refs[n_on : 2 * n_on + 3]
    depth_ref, slope_ref, rain_ref, dir_ref, sems = refs[2 * n_on + 3 :]
    even = rem(lax.axis_index("tx") * lax.axis_size("ty") + lax.axis_index("ty"), 2) == 0
    lines, px = sar_hbm.shape[1:]
    cols = depth_hbm.shape[1]
    h = SUBSTEPS
    pairs = (
        (depth_hbm, depth_ref), (slope_hbm, slope_ref), (rain_hbm, rain_ref), (dir_hbm, dir_ref),
        (sar_hbm, sar_ref), *zip(on_hbm, on_refs),
    )
    copies = [pltpu.make_async_copy(src, dst, sems.at[i]) for i, (src, dst) in enumerate(pairs)]
    for copy in copies:
        copy.start()
    zeros = jnp.zeros((8, px), f32)
    strips = ([], [])
    for i, ref in enumerate((depth_ref, slope_ref, rain_ref, dir_ref)):
        copies[i].wait()
        own = [ref[:, cols - LANES :].astype(f32), ref[:, 0:LANES].astype(f32)]
        if i == 1:
            own = [runoff_coef * jnp.sqrt(x) for x in own]
        strips[0].append(jnp.transpose(own[0], (1, 0))[LANES - h :])
        strips[1].append(jnp.transpose(own[1], (1, 0))[0:h])
    copies[4].wait()
    messages = []
    for strip, at, lo in ((strips[0], lines - 16, 16 - HALO_LINES), (strips[1], 0, 0)):
        image = [sar_ref[ch, at : at + 16, :].astype(f32)[lo : lo + HALO_LINES] for ch in range(2)]
        messages.append(
            jnp.concatenate([jnp.concatenate(strip[0:2], 1), jnp.concatenate(strip[2:4], 1), *image, zeros], 0)
        )
    first, second = in_turn(even, *messages)
    first_swap_ref[...] = first.astype(bf16)
    second_swap_ref[...] = second.astype(bf16)
    for copy in copies[5:]:
        copy.wait()


def in_turn(even, to_next, to_previous):
    return jnp.where(even, to_next, to_previous), jnp.where(even, to_previous, to_next)


def from_turns(place, size, first, second):
    even = rem(place, 2) == 0
    previous = jnp.where(even, second, first)
    following = jnp.where(even, first, second)
    return jnp.where(place > 0, previous, 0.0), jnp.where(place < size - 1, following, 0.0)


def strips_of(message, keep):
    both = jnp.where(keep, message, 0.0)
    cols = both.shape[1] // 2
    return [both[0:8, 0:cols], both[0:8, cols:], both[8:16, 0:cols], both[8:16, cols:]]


def inner_kernel(
    devices, capacity,
    k1_ref, k2_ref, k3_ref, k4_ref, tile_ref, row_ref, sar_ref, gw_ref, cell_ref,
    w1_ref, w2_ref, w3_ref, w4_ref, perm_ref, extra_ref, frac_ref, slots_ref, e1_ref, e2_ref, e3_ref,
    t1_ref, t4_ref, s_ref, xa_ref, xb_ref, x3_ref, logit_ref, wnd_ref,
):
    rows = OUT_LINES * CH
    cols = IN_LINES * CH

    n2 = MID_LINES * cols
    spot2 = rem(iota((CH, n2), 1), cols) - iota((CH, n2), 0)
    line2 = quo(iota((CH, n2), 1), cols)
    n1 = OUT_LINES * LANES
    group1 = quo(rem(iota((8, n1), 1), LANES), IN_LINES) == iota((8, n1), 0)
    line1 = rem(iota((8, n1), 1), IN_LINES) - quo(iota((8, n1), 1), LANES)
    spread1 = [(group1 & (line1 == ky)).astype(bf16) for ky in range(3)]
    tile4 = (rem(iota((CH, cols), 1), CH) == iota((CH, cols), 0)).astype(bf16)
    t1_ref[...] = jnp.zeros(t1_ref.shape, f32)
    t4_ref[...] = jnp.zeros(t4_ref.shape, f32)
    for ky in range(3):
        for kx in range(3):
            t1_ref[ky * 8 + 2 * kx : ky * 8 + 2 * kx + 2, :] = k1_ref[ky, kx].astype(f32)
        t4_ref[ky * 3 : ky * 3 + 3, :] = k4_ref[ky].astype(f32)
    wide1 = sum(dot_0(t1_ref[ky * 8 : ky * 8 + 8, :].astype(bf16), spread1[ky]) for ky in range(3))
    for i in range(OUT_LINES):
        w1_ref[i * CH : (i + 1) * CH, :] = wide1[:, i * LANES : (i + 1) * LANES].astype(bf16)
    spread2 = [
        (spot2 == (kx * MID_IN + ky + line2) * CH).astype(bf16) for ky in range(3) for kx in range(3)
    ]
    for k_ref, w_ref in ((k2_ref, w2_ref), (k3_ref, w3_ref)):
        wide = sum(dot(k_ref[n * CH : (n + 1) * CH, :], spread2[n]) for n in range(9))
        for i in range(MID_LINES):
            w_ref[i * CH : (i + 1) * CH, :] = wide[:, i * cols : (i + 1) * cols].astype(bf16)
    wide4 = dot(t4_ref[...].astype(bf16), tile4)
    w4_ref[...] = jnp.concatenate(
        [
            band_weights(
                [jnp.broadcast_to(wide4[ky * 3 + kx : ky * 3 + kx + 1], (CH, cols)) for ky in range(3)],
                CH, cols, 1, lambda k: quo(k, CH),
            )
            for kx in range(3)
        ],
        0,
    )

    lines = tile_ref.shape[1]
    tile = tile_ref[...].astype(f32)
    same = iota((lines, lines), 0) == iota((lines, lines), 1)
    tile_sub = jnp.sum(jnp.where(same, jnp.broadcast_to(tile, (lines, lines)), 0.0), 1, keepdims=True)
    rival = (tile_sub == tile) & (iota((lines, lines), 0) < iota((lines, lines), 1))
    slot = tile * capacity + jnp.sum(jnp.where(rival, 1.0, 0.0), 0, keepdims=True)
    slots = slots_ref.shape[0]
    wnd_rows = CH * lines
    per_line = CH
    widen = (quo(iota((lines, wnd_rows), 1), per_line) == iota((lines, wnd_rows), 0)).astype(bf16)
    slot_wide = dot(jnp.broadcast_to(slot, (8, lines)).astype(bf16), widen)[0:1]
    place = slot_wide.astype(jnp.int32) * 4 + rem(quo(iota((1, wnd_rows), 1), 4), 4)
    perm = jnp.where(iota((slots, wnd_rows), 0) == place, 1.0, 0.0).astype(bf16)
    end = END_LINES * CH
    perm_ref[...] = jnp.concatenate([perm[:, 0:end], perm[:, wnd_rows - end :]], 1)

    row_of = dot(
        jnp.where(same, jnp.broadcast_to(row_ref[...].astype(f32), (lines, lines)), 0.0).astype(bf16),
        jnp.ones((lines, LANES), bf16),
    )
    perm_line = jnp.where(quo(iota((slots, lines), 0), 4) == slot.astype(jnp.int32), 1.0, 0.0).astype(bf16)
    row_own = dot(perm_line, row_of.astype(bf16))
    per_tile = 4 * capacity
    lane = iota((slots, LANES), 1)
    entry = rem(iota((slots, LANES), 0), per_tile)
    info = jnp.zeros((slots, LANES), f32)
    for turn, value in enumerate((row_own, of_right(row_own, per_tile), of_left(row_own, per_tile))):
        info = jnp.where(lane == turn * per_tile + entry, value, info)
    info = jnp.sum(info.reshape(devices, per_tile, LANES), 1, keepdims=True)
    at = iota((devices, 8, LANES), 1)
    extra_ref[...] = jnp.where(at == 2, info, 0.0).reshape(8 * devices, LANES)


    px = sar_ref.shape[2]
    for ch in range(2):
        s_ref[ch, 0:lines, :] = sar_ref[ch].astype(f32)
        s_ref[ch, lines:, :] = jnp.zeros((s_ref.shape[1] - lines, px), f32)
    total = xa_ref.shape[1] // CH
    xa_ref[:, (total - 2) * CH :, :] = jnp.zeros((3, 2 * CH, px), bf16)

    def put(ref, line, acc):
        rows = acc.shape[0]
        feat = jnp.maximum(acc.astype(bf16), jnp.zeros(acc.shape, bf16))
        at = slice(line * CH, line * CH + rows)
        if len(ref.shape) == 2:
            ref[at, :] = feat
            return
        before, after = pixel_shifts(feat)
        ref[0, at, :] = before
        ref[1, at, :] = feat
        ref[2, at, :] = after

    full = (lines + 4) // OUT_LINES + 1
    for b in range(full):
        at = b * OUT_LINES
        x = jnp.concatenate([s_ref[0, at : at + IN_LINES, :], s_ref[1, at : at + IN_LINES, :]], 0)
        put(xa_ref, 1 + at, dot(w1_ref[...], image_columns(x)))
    stop = lines - 4
    for w_ref, src, dst, line, end_line in ((w2_ref, xa_ref, xb_ref, 2, stop), (w3_ref, xb_ref, x3_ref, 3, stop - 1)):
        for at in range(line, end_line, MID_LINES):
            x = src[:, (at - 1) * CH : (at - 1 + MID_IN) * CH, :]
            put(dst, at, dot(w_ref[...], mid_columns(*[x[i] for i in range(3)])))

    def ends_of(lo, center):
        hi = lines - lo - 2
        return jnp.concatenate([center[at * CH : (at + 2) * CH, :] for at in (lo, hi)], 0)

    e1_ref[...] = ends_of(3, xa_ref.at[1])
    e2_ref[...] = ends_of(4, xb_ref.at[1])
    e3_ref[...] = ends_of(5, x3_ref)
    logit_ref[0:END_LINES, :] = jnp.zeros((END_LINES, px), f32)
    starts = [3 + b * OUT_LINES for b in range(full - 2)] + [lines - 5 - IN_LINES]
    for at in starts:
        sums = dot(w4_ref[...], x3_ref[at * CH : at * CH + cols, :])
        logit_ref[at + 1 : at + 1 + CH, :] = merged(sums, CH)
    frac_ref[...] = sigmoid(logit_ref[0:lines, :])
    quarter = wnd_ref.shape[1]
    group = 16

    for g in range((lines - 2 * END_LINES) // group):
        at = slice(g * group + END_LINES, (g + 1) * group + END_LINES)
        cov = gw_ref[at, :]
        obs = sigmoid(logit_ref[at, :]).astype(f32) * cov
        for i, sums in enumerate(line_windows(cell_ref[at, :], obs, cov, quarter)):
            to = CH * (group * g + i)
            wnd_ref[to : to + CH, :] = sums
    slots_ref[...] = dot(perm[:, end : wnd_rows - end], window_goods(wnd_ref[...]))


def of_right(x, per_tile):
    return jnp.concatenate([x[per_tile:], jnp.zeros((per_tile, x.shape[1]), x.dtype)], 0)


def of_left(x, per_tile):
    return jnp.concatenate([jnp.zeros((per_tile, x.shape[1]), x.dtype), x[: x.shape[0] - per_tile]], 0)


def ends_kernel(
    devices, capacity,
    second_swap_ref, first_swap_ref, w1_ref, w2_ref, w3_ref, w4_ref, perm_ref, extra_ref, frac_in, slots_in, e1_ref, e2_ref, e3_ref,
    sar_ref, gw_ref, cell_ref,
    frac_ref, send_ref,
    f_ref,
):
    lines, px = gw_ref.shape
    n_ty = lax.axis_size("ty")
    me = lax.axis_index("tx") * n_ty + lax.axis_index("ty")
    rows = OUT_LINES * CH
    above, below = from_turns(
        me, devices, first_swap_ref[16:32, :].astype(f32), second_swap_ref[16:32, :].astype(f32)
    )
    n = HALO_LINES

    pieces = []
    for ch in range(2):
        own = sar_ref[ch].astype(f32)
        pieces += [above[ch * n : (ch + 1) * n], own[0:n], own[lines - n :], below[ch * n : (ch + 1) * n]]
    x = image_columns(jnp.concatenate(pieces, 0))
    half = 6 * CH
    out_line = quo(iota((half, px), 0), CH).astype(f32).astype(bf16)
    nil = jnp.zeros((half, px), bf16)
    low = jnp.where(me == 0, n, 0)
    high = jnp.where(me == devices - 1, OUT_LINES - 8 - n, OUT_LINES)
    for layer, (w_ref, e_ref) in enumerate(((w1_ref, e1_ref), (w2_ref, e2_ref), (w3_ref, e3_ref)), 1):
        if layer == 1:
            acc = dot(w_ref[...], x).astype(bf16)
            top, bottom = acc[0:half], acc[8 * CH :]
        else:
            before, after = pixel_shifts(block)
            top, bottom = [
                jnp.concatenate(
                    [
                        dot(w_ref[...], mid_columns(*[y[at * CH : (at + MID_IN) * CH] for y in (before, block, after)]))
                        for at in (first, first + MID_LINES)
                    ],
                    0,
                ).astype(bf16)
                for first in (0, 8)
            ]
        top = jnp.where(out_line >= (low - layer).astype(f32).astype(bf16), jnp.maximum(top, nil), nil)
        bottom = jnp.where(out_line < (high + layer).astype(f32).astype(bf16), jnp.maximum(bottom, nil), nil)
        block = jnp.concatenate([top, e_ref[...], bottom], 0)
    frac = sigmoid(merged(dot(w4_ref[...], block), CH)).astype(f32)
    f_ref[...] = frac_in[...].astype(f32)
    f_ref[0:6, :] = frac[0:6]
    f_ref[lines - 6 :, :] = frac[8:14]
    frac_ref[...] = f_ref[...].astype(bf16)
    quarter = slots_in.shape[1] // 4
    sums = []
    for at in (slice(0, END_LINES), slice(lines - END_LINES, lines)):
        cov = gw_ref[at, :]
        sums += line_windows(cell_ref[at, :], f_ref[at, :] * cov, cov, quarter)
    by_slot = slots_in[...] + dot(perm_ref[...], window_goods(jnp.concatenate(sums, 0)))

    per_tile = 4 * capacity
    slots, tile_cols = by_slot.shape
    h = SUBSTEPS
    entry = rem(iota((slots, LANES), 0), per_tile)
    here = quo(iota((slots, LANES), 1), h) == entry
    column = rem(quo(iota((slots, LANES), 0), per_tile), n_ty)
    source = iota((LANES, LANES), 0)
    spot = rem(iota((LANES, LANES), 1), h)

    def strip(x, first_lane, keep):
        take = ((spot + first_lane == source) & (source - first_lane < h)).astype(bf16)
        x = jnp.where(here & keep, dot(x.astype(bf16), take), 0.0)
        return jnp.sum(x.reshape(devices, per_tile, LANES), 1, keepdims=True)

    right_strip = strip(of_right(by_slot[:, 0:LANES], per_tile), 0, column < n_ty - 1)
    left_strip = strip(of_left(by_slot[:, tile_cols - LANES :], per_tile), LANES - h, column > 0)
    at = iota((devices, 8, LANES), 1)
    extra = extra_ref[...].reshape(devices, 8, LANES)
    extra = jnp.where(at == 0, right_strip, jnp.where(at == 1, left_strip, extra))
    halves = [by_slot[:, at : at + LANES].reshape(devices, per_tile, LANES) for at in range(0, tile_cols, LANES)]
    packed = jnp.concatenate([*halves, extra], 1)
    send_ref[...] = packed.reshape(send_ref.shape).astype(bf16)


def transposed(x):
    return jnp.transpose(x, (1, 0))


def level_kernel(
    devices,
    got_ref, second_swap_ref, first_swap_ref, depth_ref, slope_ref, rain_ref, dir_ref,
    level_ref, side_ref, first_ref, second_ref,
):
    tile_rows, tile_cols = depth_ref.shape
    h = SUBSTEPS
    halves = tile_cols // LANES
    n = (got_ref.shape[0] // devices - 8) // halves
    k = devices * n
    packed = got_ref[...].astype(f32).reshape(devices, halves * n + 8, LANES)
    main = jnp.concatenate([packed[:, i * n : (i + 1) * n].reshape(k, LANES) for i in range(halves)], 1)
    extra = packed[:, halves * n :]

    entry = rem(iota((k, LANES), 0), n)
    spread = quo(iota((k, LANES), 1), h) == entry

    def strip(r, first):
        rows = jnp.broadcast_to(extra[:, r : r + 1], (devices, n, LANES)).reshape(k, LANES)
        take = rem(iota((LANES, LANES), 0), h) + first == iota((LANES, LANES), 1)
        return dot(jnp.where(spread, rows, 0.0).astype(bf16), take.astype(bf16)).astype(bf16)

    lane = iota((1, k), 1)
    info = jnp.broadcast_to(extra[:, 2:3], (devices, n, LANES)).reshape(k, LANES)
    info = jnp.where(rem(iota((k, LANES), 1), n) == entry, info, 0.0).astype(bf16)
    turns = (quo(iota((LANES, LANES), 0), n) == iota((LANES, LANES), 1)).astype(bf16)
    lines = transposed(dot(info, turns))

    row = iota((tile_rows, LANES), 0).astype(f32).astype(bf16)
    one = jnp.ones((tile_rows, LANES), bf16)
    nil = jnp.zeros((tile_rows, LANES), bf16)

    def placer(turn):
        line = lines[turn : turn + 1] + rem(lane, 2).astype(f32)
        parts = []
        for quantity in range(2):
            target = jnp.where(rem(quo(lane, 2), 2) == quantity, line, -1.0)
            pieces = []
            for at in range(0, k, LANES):
                tile = jnp.broadcast_to(target[:, at : at + LANES], (CH, LANES)).astype(bf16)
                tile = jnp.broadcast_to(tile[None], (tile_rows // CH, CH, LANES)).reshape(tile_rows, LANES)
                pieces.append(jnp.where(row == tile, one, nil))
            parts.append(jnp.concatenate(pieces, 1))
        return jnp.concatenate(parts, 0)

    summed = dot(placer(0), main.astype(bf16))
    summed_side = dot(placer(1), strip(0, 0)) + dot(placer(2), strip(1, LANES - h))

    ty = lax.axis_index("ty")
    tx = lax.axis_index("tx")
    previous, following = from_turns(
        tx * lax.axis_size("ty") + ty, devices,
        first_swap_ref[0:16, :].astype(f32), second_swap_ref[0:16, :].astype(f32),
    )
    left = strips_of(previous, ty > 0)
    right = strips_of(following, ty < lax.axis_size("ty") - 1)
    gap = jnp.zeros((LANES - 2 * h, tile_rows), f32)
    depth_side, conv_side, rain_side, code_side = [
        transposed(jnp.concatenate([r, gap, l], 0)) for r, l in zip(right, left)
    ]

    def analysed(sums, depth):
        observed = sums[0:tile_rows]
        covered = sums[tile_rows:]
        wet = depth / (depth + wet_depth)
        innovation = (observed - covered * wet) / (covered + 1.0)
        return depth * jnp.exp(innovation)

    level = analysed(summed, depth_ref[...])
    level_ref[...] = level
    sides = (analysed(summed_side, depth_side), rain_side, conv_side, code_side)
    owns = (level, rain_ref, slope_ref, dir_ref)

    def end_rows(at):
        own = [x[at, :] for x in owns]
        own[2] = runoff_coef * jnp.sqrt(own[2])
        own[3] = own[3].astype(f32)
        return jnp.concatenate([jnp.concatenate([o, x[at]], 1) for o, x in zip(own, sides)], 0)

    for i, x in enumerate(sides):
        side_ref[i] = x
    first, second = in_turn(rem(tx, 2) == 0, end_rows(slice(tile_rows - h, tile_rows)), end_rows(slice(0, h)))
    first_ref[...] = first.astype(bf16)
    second_ref[...] = second.astype(bf16)


def substeps(level, rain, conv, code, rain_s, conv_s, m_ref, part_ref, up_ref, down_ref, chunk):
    rows, cols = level.shape
    h = SUBSTEPS
    for ref in (up_ref, down_ref):
        ref[0] = jnp.zeros(ref.shape[1:], f32)
        ref[1, 0:h, :] = jnp.zeros((h, cols), f32)
        ref[1, h + rows :, :] = jnp.zeros((h, cols), f32)
    part_ref[0] = level
    rain_s[...] = rain
    conv_s[...] = conv
    sides = (-1, 0, 1, -1, 1, -1, 0, 1)
    for direction, side in enumerate(sides):
        share = jnp.where(code == direction, conv, 0.0)
        m_ref[direction] = pltpu.roll(share, side % cols, 1) if side else share

    def level_at(buf, r, n):
        level = part_ref[buf, r : r + n, :]
        return level + up_ref[buf, h + r + 1 : h + r + 1 + n, :] + down_ref[buf, h + r - 1 : h + r - 1 + n, :]

    def substep(buf, new):
        for r in range(0, rows, chunk):
            level = level_at(buf, r, chunk)
            power = level * jnp.exp2((2.0 / 3.0 / math.log(2.0)) * jnp.log(jnp.maximum(jnp.abs(level), 1e-30)))
            from_right = pltpu.roll(power, cols - 1, 1)
            from_left = pltpu.roll(power, 1, 1)
            m = [m_ref[d, r : r + chunk, :] for d in range(8)]
            up_ref[new, h + r : h + r + chunk, :] = m[0] * from_right + m[1] * power + m[2] * from_left
            down_ref[new, h + r : h + r + chunk, :] = m[5] * from_right + m[6] * power + m[7] * from_left
            part_ref[new, r : r + chunk, :] = (
                level + rain_s[r : r + chunk, :] - conv_s[r : r + chunk, :] * power
                + (m[3] * from_right + m[4] * from_left)
            )

    def substep_pair(i, carry):
        substep(0, 1)
        substep(1, 0)
        return carry

    if rows > LANES:
        lax.fori_loop(0, SUBSTEPS // 2, substep_pair, 0)
    else:
        for i in range(SUBSTEPS // 2):
            substep_pair(i, 0)
    return level_at


def flow_inner_kernel(level_ref, side_ref, slope_ref, dir_ref, rain_ref, out_ref, *scratch):
    rows, cols = level_ref.shape
    own = (level_ref[...], rain_ref[...], runoff_coef * jnp.sqrt(slope_ref[...]), dir_ref[...].astype(f32))
    level_at = substeps(*[jnp.concatenate([x, side_ref[i]], 1) for i, x in enumerate(own)], *scratch, 32)
    out_ref[...] = level_at(0, 0, rows)[:, 0:cols]


def flow_ends_kernel(inner_ref, level_ref, side_ref, slope_ref, dir_ref, rain_ref, first_swap_ref, second_swap_ref, out_ref, *scratch):
    rows, cols = level_ref.shape
    h = SUBSTEPS
    above, below = from_turns(
        lax.axis_index("tx"), lax.axis_size("tx"),
        first_swap_ref[...].astype(f32), second_swap_ref[...].astype(f32),
    )
    fields = []
    for i, ref in enumerate((level_ref, rain_ref, slope_ref, dir_ref)):
        ends = []
        for at in (slice(0, 2 * h), slice(rows - 2 * h, rows)):
            own = ref[at, :].astype(f32)
            if i == 2:
                own = runoff_coef * jnp.sqrt(own)
            ends.append(jnp.concatenate([own, side_ref[i, at, :]], 1))
        fields.append(jnp.concatenate([above[i * h : (i + 1) * h], *ends, below[i * h : (i + 1) * h]], 0))
    level_at = substeps(*fields, *scratch, 6 * h)
    out_ref[h : rows - h, :] = inner_ref[h : rows - h, :]
    out_ref[0:h, :] = level_at(0, h, h)[:, 0:cols]
    out_ref[rows - h :, :] = level_at(0, 4 * h, h)[:, 0:cols]


def flow_scratch(rows, cols):
    return [
        pltpu.VMEM((rows, cols), f32),
        pltpu.VMEM((rows, cols), f32),
        pltpu.VMEM((8, rows, cols), f32),
        pltpu.VMEM((2, rows, cols), f32),
        pltpu.VMEM((2, rows + 2 * SUBSTEPS, cols), f32),
        pltpu.VMEM((2, rows + 2 * SUBSTEPS, cols), f32),
    ]


def hbm_specs(n):
    return [pl.BlockSpec(memory_space=pltpu.HBM)] * n


def vmem_specs(n):
    return [pl.BlockSpec(memory_space=pltpu.VMEM)] * n


def per_device(
    sar_image, kernel_first, kernel_second, kernel_third, kernel_last,
    geo_weight, cell_index, block_tile, block_row, depth, slope, flow_dir, rain,
):
    both = ("tx", "ty")
    devices = lax.axis_size(both)
    az_lines, range_px = geo_weight.shape
    tile_rows, tile_cols = depth.shape
    capacity = max(2, 2 * az_lines // devices)

    n_tx, n_ty = lax.axis_size("tx"), lax.axis_size("ty")

    def swaps(first, second, stride):
        size = devices // stride
        out = []
        for start, x in ((1, second), (0, first)):
            to = {}
            for place in range(start, size, 2):
                for k in range(stride):
                    i, j = place * stride + k, (place + 1) % size * stride + k
                    if place == size - 1 and stride > 1:
                        ends = (i, i ^ 1), (j, j ^ 1)
                    else:
                        ends = (i, j), (j, i)
                    to.update(ends)
            out.append(lax.ppermute(x, both, sorted(to.items())))
        return out[::-1]

    params = pltpu.CompilerParams(vmem_limit_bytes=VMEM_LIMIT)
    message = pltpu.VMEM((32, range_px), bf16)
    handed = (
        sar_image,
        jnp.transpose(kernel_first, (2, 3, 1, 0)),
        jnp.transpose(kernel_second, (2, 3, 0, 1)).reshape(9 * CH, CH),
        jnp.transpose(kernel_third, (2, 3, 0, 1)).reshape(9 * CH, CH),
        jnp.transpose(kernel_last[0], (1, 2, 0)),
        block_tile.reshape(1, az_lines),
        block_row.reshape(1, az_lines),
        geo_weight,
        cell_index,
    )
    first, second, sar_image, *handed = pl.pallas_call(
        edge_kernel,
        out_shape=(message, message, *[pltpu.VMEM(x.shape, x.dtype) for x in handed]),
        in_specs=hbm_specs(4 + len(handed)),
        out_specs=tuple(vmem_specs(2 + len(handed))),
        scratch_shapes=[
            *[pltpu.VMEM(x.shape, x.dtype) for x in (depth, slope, rain, flow_dir)],
            pltpu.SemaphoreType.DMA((4 + len(handed),)),
        ],
        compiler_params=pltpu.CompilerParams(vmem_limit_bytes=VMEM_MOST),
        name="edges",
    )(depth, slope, rain, flow_dir, *handed)
    geo_weight, cell_index = handed[-2:]
    halo = swaps(first, second, 1)

    rows, cols = OUT_LINES * CH, IN_LINES * CH
    slots = devices * capacity * 4
    send_rows = tile_cols // LANES * 4 * capacity + 8
    full = (az_lines + 4) // OUT_LINES + 1
    feats = (full * OUT_LINES + 3) * CH
    blocks_in = (az_lines + IN_LINES, range_px)

    def cost(flops):
        return pl.CostEstimate(flops=flops, bytes_accessed=4_000_000, transcendentals=0)

    prepared = pl.pallas_call(
        functools.partial(inner_kernel, devices, capacity),
        out_shape=(
            jax.ShapeDtypeStruct((rows, LANES), bf16),
            jax.ShapeDtypeStruct((MID_LINES * CH, cols), bf16),
            jax.ShapeDtypeStruct((MID_LINES * CH, cols), bf16),
            jax.ShapeDtypeStruct((3 * CH, cols), bf16),
            jax.ShapeDtypeStruct((slots, 2 * END_LINES * CH), bf16),
            jax.ShapeDtypeStruct((8 * devices, LANES), f32),
            jax.ShapeDtypeStruct((az_lines, range_px), bf16),
            jax.ShapeDtypeStruct((slots, tile_cols), f32),
            *[jax.ShapeDtypeStruct((4 * CH, range_px), bf16)] * 3,
        ),
        in_specs=vmem_specs(9),
        out_specs=tuple(vmem_specs(11)),
        scratch_shapes=[
            pltpu.VMEM((24, CH), f32),
            pltpu.VMEM((16, CH), f32),
            pltpu.VMEM((2, *blocks_in), f32),
            pltpu.VMEM((3, feats, range_px), bf16),
            pltpu.VMEM((3, feats, range_px), bf16),
            pltpu.VMEM((feats, range_px), bf16),
            pltpu.VMEM(blocks_in, f32),
            pltpu.VMEM(((az_lines - 2 * END_LINES) * CH, tile_cols // 4), f32),
        ],
        compiler_params=params,
        cost_estimate=cost(8_000_000_000),
        name="inner",
    )(
        *handed[:-2], sar_image, geo_weight, cell_index,
    )
    fraction, send = pl.pallas_call(
        functools.partial(ends_kernel, devices, capacity),
        out_shape=(
            jax.ShapeDtypeStruct((az_lines, range_px), bf16),
            jax.ShapeDtypeStruct((devices * send_rows, LANES), bf16),
        ),
        in_specs=vmem_specs(16),
        out_specs=tuple(vmem_specs(2)),
        scratch_shapes=[pltpu.VMEM((az_lines, range_px), f32)],
        compiler_params=params,
        name="ends",
    )(*halo[::-1], *prepared, sar_image, geo_weight, cell_index)

    got = lax.all_to_all(
        send.reshape(devices, send_rows, LANES), both, split_axis=0, concat_axis=0, tiled=True
    ).reshape(devices * send_rows, LANES)

    wide_cols = tile_cols + LANES
    edge = jax.ShapeDtypeStruct((4 * SUBSTEPS, wide_cols), bf16)
    level, side, first, second = pl.pallas_call(
        functools.partial(level_kernel, devices),
        out_shape=(
            jax.ShapeDtypeStruct((tile_rows, tile_cols), f32),
            jax.ShapeDtypeStruct((4, tile_rows, LANES), f32),
            edge,
            edge,
        ),
        in_specs=vmem_specs(7),
        out_specs=tuple(vmem_specs(4)),
        compiler_params=params,
        name="level",
    )(got, *halo[::-1], depth, slope, rain, flow_dir)

    row_halo = swaps(first, second, n_ty)

    inner = pl.pallas_call(
        flow_inner_kernel,
        out_shape=jax.ShapeDtypeStruct((tile_rows, tile_cols), f32),
        in_specs=vmem_specs(5),
        out_specs=vmem_specs(1)[0],
        scratch_shapes=flow_scratch(tile_rows, wide_cols),
        compiler_params=params,
        cost_estimate=cost(5_000_000_000),
        name="flow_inner",
    )(level, side, slope, flow_dir, rain)
    level = pl.pallas_call(
        flow_ends_kernel,
        out_shape=jax.ShapeDtypeStruct((tile_rows, tile_cols), f32),
        in_specs=vmem_specs(8),
        out_specs=vmem_specs(1)[0],
        scratch_shapes=flow_scratch(6 * SUBSTEPS, wide_cols),
        compiler_params=params,
        name="flow_ends",
    )(inner, level, side, slope, flow_dir, rain, *row_halo)
    return (fraction, level)


def solution(mesh):
    placed = (
        P(None, ("tx", "ty"), None),
        P(),
        P(),
        P(),
        P(),
        P(("tx", "ty"), None),
        P(("tx", "ty"), None),
        P(("tx", "ty"), None),
        P(("tx", "ty"), None),
        P("tx", "ty"),
        P("tx", "ty"),
        P("tx", "ty"),
        P("tx", "ty"),
    )
    return jax.shard_map(
        per_device,
        mesh=mesh,
        in_specs=placed,
        out_specs=(P(("tx", "ty"), None), P("tx", "ty")),
        check_vma=False,
    )
```

```python
import functools
import math

import jax
import jax.numpy as jnp
from jax import lax
from jax.experimental import pallas as pl
from jax.experimental.pallas import tpu as pltpu
from jax.sharding import PartitionSpec as P

WIN_ROWS = 2
SUBSTEPS = 8
CH = 16
OUT_LINES = 14
IN_LINES = OUT_LINES + 2
MID_LINES = 3
MID_IN = MID_LINES + 2
HALO_LINES = 4
END_LINES = 8
LANES = 128
VMEM_LIMIT = 48 * 1024 * 1024
VMEM_MOST = 60160 * 1024

wet_depth = 0.5
runoff_coef = 0.25
bf16 = jnp.bfloat16
f32 = jnp.float32


def iota(shape, dim):
    return lax.broadcasted_iota(jnp.int32, shape, dim)


def quo(x, n):
    assert n & (n - 1) == 0
    return lax.shift_right_logical(x, jnp.int32(n.bit_length() - 1)) if n > 1 else x


def rem(x, n):
    assert n & (n - 1) == 0
    return x & (n - 1)


def dot(a, b):
    return lax.dot_general(a, b, (((1,), (0,)), ((), ())), preferred_element_type=f32)


def dot_0(a, b):
    return lax.dot_general(a, b, (((0,), (0,)), ((), ())), preferred_element_type=f32)


def dot_t(a, b):
    return lax.dot_general(a, b, (((1,), (1,)), ((), ())), preferred_element_type=f32)


def pixel_shifts(x):
    rows, width = x.shape
    lane = iota((rows, LANES), 1)
    zero = jnp.zeros((rows, LANES), x.dtype)
    first = lane.astype(f32).astype(x.dtype) == 0
    last = (LANES - 1 - lane).astype(f32).astype(x.dtype) == 0
    before = pltpu.roll(x, 1, 1)
    after = pltpu.roll(x, width - 1, 1)
    before = jnp.concatenate([jnp.where(first, zero, before[:, 0:LANES]), before[:, LANES:]], 1)
    after = jnp.concatenate([after[:, : width - LANES], jnp.where(last, zero, after[:, width - LANES :])], 1)
    return before, after


def merged(sums, n):
    before, _ = pixel_shifts(sums[0:n])
    _, after = pixel_shifts(sums[2 * n : 3 * n])
    return before + sums[n : 2 * n] + after


def image_columns(x):
    before, after = pixel_shifts(x)
    pad = jnp.zeros((LANES - 3 * x.shape[0], x.shape[1]), f32)
    return jnp.concatenate([before, x, after, pad], 0).astype(bf16)


def mid_columns(before, x, after):
    return jnp.concatenate([before, x, after, x[0:CH]], 0)


def sigmoid(x):
    return (1.0 / (1.0 + jnp.exp(-x))).astype(bf16)


def line_windows(cell, obs, cov, quarter):
    px = cell.shape[1]
    kind = iota((CH, px), 0)
    kind_part = rem(kind, CH // 2).astype(f32).astype(bf16)
    sub = kind.astype(f32).astype(bf16)
    one = jnp.ones((CH, px), bf16)
    nil = jnp.zeros((CH, px), bf16)
    part = quo(cell, quarter).astype(f32)
    col = rem(cell, quarter).astype(f32)

    def spread_row(x, i):
        return jnp.broadcast_to(x[i : i + 1], (CH, px)).astype(bf16)

    out = []
    for i in range(cell.shape[0]):
        pair = [jnp.broadcast_to(x[i : i + 1], (CH // 2, px)) for x in (obs, cov)]
        value = jnp.concatenate(pair, 0).astype(bf16)
        left = jnp.where(kind_part == spread_row(part, i), value, nil)
        where_col = spread_row(col, i)
        hot = jnp.concatenate([jnp.where(sub + g * CH == where_col, one, nil) for g in range(quarter // CH)], 0)
        out.append(dot_t(left, hot))
    return out


def window_goods(sums):
    rows, quarter = sums.shape
    cols = 4 * quarter
    repeat = (rem(iota((quarter, cols), 1), quarter) == iota((quarter, cols), 0)).astype(bf16)
    tiled = dot(sums.astype(bf16), repeat)
    mine = rem(iota((rows, cols), 0), 4) == quo(iota((rows, cols), 1), quarter)
    return jnp.where(mine, tiled, 0.0).astype(bf16)


def band_weights(tiled, rows, cols, per_row, line_of):
    out_line = quo(iota((rows, cols), 0), per_row)
    off = line_of(iota((rows, cols), 1)) - out_line
    out = jnp.zeros((rows, cols), f32)
    for ky in range(3):
        out = jnp.where(off == ky, tiled[ky], out)
    return out.astype(bf16)


def edge_kernel(
    depth_hbm, slope_hbm, rain_hbm, dir_hbm, sar_hbm, *refs
):
    n_on = (len(refs) - 8) // 2
    on_hbm = refs[:n_on]
    first_swap_ref, second_swap_ref, sar_ref, *on_refs = refs[n_on : 2 * n_on + 3]
    depth_ref, slope_ref, rain_ref, dir_ref, sems = refs[2 * n_on + 3 :]
    even = rem(lax.axis_index("tx") * lax.axis_size("ty") + lax.axis_index("ty"), 2) == 0
    lines, px = sar_hbm.shape[1:]
    cols = depth_hbm.shape[1]
    h = SUBSTEPS
    pairs = (
        (depth_hbm, depth_ref), (slope_hbm, slope_ref), (rain_hbm, rain_ref), (dir_hbm, dir_ref),
        (sar_hbm, sar_ref), *zip(on_hbm, on_refs),
    )
    copies = [pltpu.make_async_copy(src, dst, sems.at[i]) for i, (src, dst) in enumerate(pairs)]
    for copy in copies:
        copy.start()
    zeros = jnp.zeros((8, px), f32)
    strips = ([], [])
    for i, ref in enumerate((depth_ref, slope_ref, rain_ref, dir_ref)):
        copies[i].wait()
        own = [ref[:, cols - LANES :].astype(f32), ref[:, 0:LANES].astype(f32)]
        if i == 1:
            own = [runoff_coef * jnp.sqrt(x) for x in own]
        strips[0].append(jnp.transpose(own[0], (1, 0))[LANES - h :])
        strips[1].append(jnp.transpose(own[1], (1, 0))[0:h])
    copies[4].wait()
    messages = []
    for strip, at, lo in ((strips[0], lines - 16, 16 - HALO_LINES), (strips[1], 0, 0)):
        image = [sar_ref[ch, at : at + 16, :].astype(f32)[lo : lo + HALO_LINES] for ch in range(2)]
        messages.append(
            jnp.concatenate([jnp.concatenate(strip[0:2], 1), jnp.concatenate(strip[2:4], 1), *image, zeros], 0)
        )
    first, second = in_turn(even, *messages)
    first_swap_ref[...] = first.astype(bf16)
    second_swap_ref[...] = second.astype(bf16)
    for copy in copies[5:]:
        copy.wait()


def in_turn(even, to_next, to_previous):
    return jnp.where(even, to_next, to_previous), jnp.where(even, to_previous, to_next)


def from_turns(place, size, first, second):
    even = rem(place, 2) == 0
    previous = jnp.where(even, second, first)
    following = jnp.where(even, first, second)
    return jnp.where(place > 0, previous, 0.0), jnp.where(place < size - 1, following, 0.0)


def strips_of(message, keep):
    both = jnp.where(keep, message, 0.0)
    cols = both.shape[1] // 2
    return [both[0:8, 0:cols], both[0:8, cols:], both[8:16, 0:cols], both[8:16, cols:]]


def inner_kernel(
    devices, capacity,
    k1_ref, k2_ref, k3_ref, k4_ref, tile_ref, row_ref, sar_ref, gw_ref, cell_ref,
    w1_ref, w2_ref, w3_ref, w4_ref, perm_ref, extra_ref, frac_ref, slots_ref, e1_ref, e2_ref, e3_ref,
    t1_ref, t4_ref, s_ref, xa_ref, xb_ref, x3_ref, logit_ref, wnd_ref,
):
    rows = OUT_LINES * CH
    cols = IN_LINES * CH

    n2 = MID_LINES * cols
    spot2 = rem(iota((CH, n2), 1), cols) - iota((CH, n2), 0)
    line2 = quo(iota((CH, n2), 1), cols)
    n1 = OUT_LINES * LANES
    group1 = quo(rem(iota((8, n1), 1), LANES), IN_LINES) == iota((8, n1), 0)
    line1 = rem(iota((8, n1), 1), IN_LINES) - quo(iota((8, n1), 1), LANES)
    spread1 = [(group1 & (line1 == ky)).astype(bf16) for ky in range(3)]
    tile4 = (rem(iota((CH, cols), 1), CH) == iota((CH, cols), 0)).astype(bf16)
    t1_ref[...] = jnp.zeros(t1_ref.shape, f32)
    t4_ref[...] = jnp.zeros(t4_ref.shape, f32)
    for ky in range(3):
        for kx in range(3):
            t1_ref[ky * 8 + 2 * kx : ky * 8 + 2 * kx + 2, :] = k1_ref[ky, kx].astype(f32)
        t4_ref[ky * 3 : ky * 3 + 3, :] = k4_ref[ky].astype(f32)
    wide1 = sum(dot_0(t1_ref[ky * 8 : ky * 8 + 8, :].astype(bf16), spread1[ky]) for ky in range(3))
    for i in range(OUT_LINES):
        w1_ref[i * CH : (i + 1) * CH, :] = wide1[:, i * LANES : (i + 1) * LANES].astype(bf16)
    spread2 = [
        (spot2 == (kx * MID_IN + ky + line2) * CH).astype(bf16) for ky in range(3) for kx in range(3)
    ]
    for k_ref, w_ref in ((k2_ref, w2_ref), (k3_ref, w3_ref)):
        wide = sum(dot(k_ref[n * CH : (n + 1) * CH, :], spread2[n]) for n in range(9))
        for i in range(MID_LINES):
            w_ref[i * CH : (i + 1) * CH, :] = wide[:, i * cols : (i + 1) * cols].astype(bf16)
    wide4 = dot(t4_ref[...].astype(bf16), tile4)
    w4_ref[...] = jnp.concatenate(
        [
            band_weights(
                [jnp.broadcast_to(wide4[ky * 3 + kx : ky * 3 + kx + 1], (CH, cols)) for ky in range(3)],
                CH, cols, 1, lambda k: quo(k, CH),
            )
            for kx in range(3)
        ],
        0,
    )

    lines = tile_ref.shape[1]
    tile = tile_ref[...].astype(f32)
    same = iota((lines, lines), 0) == iota((lines, lines), 1)
    tile_sub = jnp.sum(jnp.where(same, jnp.broadcast_to(tile, (lines, lines)), 0.0), 1, keepdims=True)
    rival = (tile_sub == tile) & (iota((lines, lines), 0) < iota((lines, lines), 1))
    slot = tile * capacity + jnp.sum(jnp.where(rival, 1.0, 0.0), 0, keepdims=True)
    slots = slots_ref.shape[0]
    wnd_rows = CH * lines
    per_line = CH
    widen = (quo(iota((lines, wnd_rows), 1), per_line) == iota((lines, wnd_rows), 0)).astype(bf16)
    slot_wide = dot(jnp.broadcast_to(slot, (8, lines)).astype(bf16), widen)[0:1]
    place = slot_wide.astype(jnp.int32) * 4 + rem(quo(iota((1, wnd_rows), 1), 4), 4)
    perm = jnp.where(iota((slots, wnd_rows), 0) == place, 1.0, 0.0).astype(bf16)
    end = END_LINES * CH
    perm_ref[...] = jnp.concatenate([perm[:, 0:end], perm[:, wnd_rows - end :]], 1)

    row_of = dot(
        jnp.where(same, jnp.broadcast_to(row_ref[...].astype(f32), (lines, lines)), 0.0).astype(bf16),
        jnp.ones((lines, LANES), bf16),
    )
    perm_line = jnp.where(quo(iota((slots, lines), 0), 4) == slot.astype(jnp.int32), 1.0, 0.0).astype(bf16)
    row_own = dot(perm_line, row_of.astype(bf16))
    per_tile = 4 * capacity
    lane = iota((slots, LANES), 1)
    entry = rem(iota((slots, LANES), 0), per_tile)
    info = jnp.zeros((slots, LANES), f32)
    for turn, value in enumerate((row_own, of_right(row_own, per_tile), of_left(row_own, per_tile))):
        info = jnp.where(lane == turn * per_tile + entry, value, info)
    info = jnp.sum(info.reshape(devices, per_tile, LANES), 1, keepdims=True)
    at = iota((devices, 8, LANES), 1)
    extra_ref[...] = jnp.where(at == 2, info, 0.0).reshape(8 * devices, LANES)


    px = sar_ref.shape[2]
    for ch in range(2):
        s_ref[ch, 0:lines, :] = sar_ref[ch].astype(f32)
        s_ref[ch, lines:, :] = jnp.zeros((s_ref.shape[1] - lines, px), f32)
    total = xa_ref.shape[1] // CH
    xa_ref[:, (total - 2) * CH :, :] = jnp.zeros((3, 2 * CH, px), bf16)

    def put(ref, line, acc):
        rows = acc.shape[0]
        feat = jnp.maximum(acc.astype(bf16), jnp.zeros(acc.shape, bf16))
        at = slice(line * CH, line * CH + rows)
        if len(ref.shape) == 2:
            ref[at, :] = feat
            return
        before, after = pixel_shifts(feat)
        ref[0, at, :] = before
        ref[1, at, :] = feat
        ref[2, at, :] = after

    full = (lines + 4) // OUT_LINES + 1
    for b in range(full):
        at = b * OUT_LINES
        x = jnp.concatenate([s_ref[0, at : at + IN_LINES, :], s_ref[1, at : at + IN_LINES, :]], 0)
        put(xa_ref, 1 + at, dot(w1_ref[...], image_columns(x)))
    stop = lines - 4
    for w_ref, src, dst, line, end_line in ((w2_ref, xa_ref, xb_ref, 2, stop), (w3_ref, xb_ref, x3_ref, 3, stop - 1)):
        for at in range(line, end_line, MID_LINES):
            x = src[:, (at - 1) * CH : (at - 1 + MID_IN) * CH, :]
            put(dst, at, dot(w_ref[...], mid_columns(*[x[i] for i in range(3)])))

    def ends_of(lo, center):
        hi = lines - lo - 2
        return jnp.concatenate([center[at * CH : (at + 2) * CH, :] for at in (lo, hi)], 0)

    e1_ref[...] = ends_of(3, xa_ref.at[1])
    e2_ref[...] = ends_of(4, xb_ref.at[1])
    e3_ref[...] = ends_of(5, x3_ref)
    logit_ref[0:END_LINES, :] = jnp.zeros((END_LINES, px), f32)
    starts = [3 + b * OUT_LINES for b in range(full - 2)] + [lines - 5 - IN_LINES]
    for at in starts:
        sums = dot(w4_ref[...], x3_ref[at * CH : at * CH + cols, :])
        logit_ref[at + 1 : at + 1 + CH, :] = merged(sums, CH)
    frac_ref[...] = sigmoid(logit_ref[0:lines, :])
    quarter = wnd_ref.shape[1]
    group = 16

    for g in range((lines - 2 * END_LINES) // group):
        at = slice(g * group + END_LINES, (g + 1) * group + END_LINES)
        cov = gw_ref[at, :]
        obs = sigmoid(logit_ref[at, :]).astype(f32) * cov
        for i, sums in enumerate(line_windows(cell_ref[at, :], obs, cov, quarter)):
            to = CH * (group * g + i)
            wnd_ref[to : to + CH, :] = sums
    slots_ref[...] = dot(perm[:, end : wnd_rows - end], window_goods(wnd_ref[...]))


def of_right(x, per_tile):
    return jnp.concatenate([x[per_tile:], jnp.zeros((per_tile, x.shape[1]), x.dtype)], 0)


def of_left(x, per_tile):
    return jnp.concatenate([jnp.zeros((per_tile, x.shape[1]), x.dtype), x[: x.shape[0] - per_tile]], 0)


def ends_kernel(
    devices, capacity,
    second_swap_ref, first_swap_ref, w1_ref, w2_ref, w3_ref, w4_ref, perm_ref, extra_ref, frac_in, slots_in, e1_ref, e2_ref, e3_ref,
    sar_ref, gw_ref, cell_ref,
    frac_ref, send_ref,
    f_ref,
):
    lines, px = gw_ref.shape
    n_ty = lax.axis_size("ty")
    me = lax.axis_index("tx") * n_ty + lax.axis_index("ty")
    rows = OUT_LINES * CH
    above, below = from_turns(
        me, devices, first_swap_ref[16:32, :].astype(f32), second_swap_ref[16:32, :].astype(f32)
    )
    n = HALO_LINES

    pieces = []
    for ch in range(2):
        own = sar_ref[ch].astype(f32)
        pieces += [above[ch * n : (ch + 1) * n], own[0:n], own[lines - n :], below[ch * n : (ch + 1) * n]]
    x = image_columns(jnp.concatenate(pieces, 0))
    half = 6 * CH
    out_line = quo(iota((half, px), 0), CH).astype(f32).astype(bf16)
    nil = jnp.zeros((half, px), bf16)
    low = jnp.where(me == 0, n, 0)
    high = jnp.where(me == devices - 1, OUT_LINES - 8 - n, OUT_LINES)
    for layer, (w_ref, e_ref) in enumerate(((w1_ref, e1_ref), (w2_ref, e2_ref), (w3_ref, e3_ref)), 1):
        if layer == 1:
            acc = dot(w_ref[...], x).astype(bf16)
            top, bottom = acc[0:half], acc[8 * CH :]
        else:
            before, after = pixel_shifts(block)
            top, bottom = [
                jnp.concatenate(
                    [
                        dot(w_ref[...], mid_columns(*[y[at * CH : (at + MID_IN) * CH] for y in (before, block, after)]))
                        for at in (first, first + MID_LINES)
                    ],
                    0,
                ).astype(bf16)
                for first in (0, 8)
            ]
        top = jnp.where(out_line >= (low - layer).astype(f32).astype(bf16), jnp.maximum(top, nil), nil)
        bottom = jnp.where(out_line < (high + layer).astype(f32).astype(bf16), jnp.maximum(bottom, nil), nil)
        block = jnp.concatenate([top, e_ref[...], bottom], 0)
    frac = sigmoid(merged(dot(w4_ref[...], block), CH)).astype(f32)
    f_ref[...] = frac_in[...].astype(f32)
    f_ref[0:6, :] = frac[0:6]
    f_ref[lines - 6 :, :] = frac[8:14]
    frac_ref[...] = f_ref[...].astype(bf16)
    quarter = slots_in.shape[1] // 4
    sums = []
    for at in (slice(0, END_LINES), slice(lines - END_LINES, lines)):
        cov = gw_ref[at, :]
        sums += line_windows(cell_ref[at, :], f_ref[at, :] * cov, cov, quarter)
    by_slot = slots_in[...] + dot(perm_ref[...], window_goods(jnp.concatenate(sums, 0)))

    per_tile = 4 * capacity
    slots, tile_cols = by_slot.shape
    h = SUBSTEPS
    entry = rem(iota((slots, LANES), 0), per_tile)
    here = quo(iota((slots, LANES), 1), h) == entry
    column = rem(quo(iota((slots, LANES), 0), per_tile), n_ty)
    source = iota((LANES, LANES), 0)
    spot = rem(iota((LANES, LANES), 1), h)

    def strip(x, first_lane, keep):
        take = ((spot + first_lane == source) & (source - first_lane < h)).astype(bf16)
        x = jnp.where(here & keep, dot(x.astype(bf16), take), 0.0)
        return jnp.sum(x.reshape(devices, per_tile, LANES), 1, keepdims=True)

    right_strip = strip(of_right(by_slot[:, 0:LANES], per_tile), 0, column < n_ty - 1)
    left_strip = strip(of_left(by_slot[:, tile_cols - LANES :], per_tile), LANES - h, column > 0)
    at = iota((devices, 8, LANES), 1)
    extra = extra_ref[...].reshape(devices, 8, LANES)
    extra = jnp.where(at == 0, right_strip, jnp.where(at == 1, left_strip, extra))
    halves = [by_slot[:, at : at + LANES].reshape(devices, per_tile, LANES) for at in range(0, tile_cols, LANES)]
    packed = jnp.concatenate([*halves, extra], 1)
    send_ref[...] = packed.reshape(send_ref.shape).astype(bf16)


def transposed(x):
    return jnp.transpose(x, (1, 0))


def level_kernel(
    devices,
    got_ref, second_swap_ref, first_swap_ref, depth_ref, slope_ref, rain_ref, dir_ref,
    level_ref, side_ref, first_ref, second_ref,
):
    tile_rows, tile_cols = depth_ref.shape
    h = SUBSTEPS
    halves = tile_cols // LANES
    n = (got_ref.shape[0] // devices - 8) // halves
    k = devices * n
    packed = got_ref[...].astype(f32).reshape(devices, halves * n + 8, LANES)
    main = jnp.concatenate([packed[:, i * n : (i + 1) * n].reshape(k, LANES) for i in range(halves)], 1)
    extra = packed[:, halves * n :]

    entry = rem(iota((k, LANES), 0), n)
    spread = quo(iota((k, LANES), 1), h) == entry

    def strip(r, first):
        rows = jnp.broadcast_to(extra[:, r : r + 1], (devices, n, LANES)).reshape(k, LANES)
        take = rem(iota((LANES, LANES), 0), h) + first == iota((LANES, LANES), 1)
        return dot(jnp.where(spread, rows, 0.0).astype(bf16), take.astype(bf16)).astype(bf16)

    lane = iota((1, k), 1)
    info = jnp.broadcast_to(extra[:, 2:3], (devices, n, LANES)).reshape(k, LANES)
    info = jnp.where(rem(iota((k, LANES), 1), n) == entry, info, 0.0).astype(bf16)
    turns = (quo(iota((LANES, LANES), 0), n) == iota((LANES, LANES), 1)).astype(bf16)
    lines = transposed(dot(info, turns))

    row = iota((tile_rows, LANES), 0).astype(f32).astype(bf16)
    one = jnp.ones((tile_rows, LANES), bf16)
    nil = jnp.zeros((tile_rows, LANES), bf16)

    def placer(turn):
        line = lines[turn : turn + 1] + rem(lane, 2).astype(f32)
        parts = []
        for quantity in range(2):
            target = jnp.where(rem(quo(lane, 2), 2) == quantity, line, -1.0)
            pieces = []
            for at in range(0, k, LANES):
                tile = jnp.broadcast_to(target[:, at : at + LANES], (CH, LANES)).astype(bf16)
                tile = jnp.broadcast_to(tile[None], (tile_rows // CH, CH, LANES)).reshape(tile_rows, LANES)
                pieces.append(jnp.where(row == tile, one, nil))
            parts.append(jnp.concatenate(pieces, 1))
        return jnp.concatenate(parts, 0)

    summed = dot(placer(0), main.astype(bf16))
    summed_side = dot(placer(1), strip(0, 0)) + dot(placer(2), strip(1, LANES - h))

    ty = lax.axis_index("ty")
    tx = lax.axis_index("tx")
    previous, following = from_turns(
        tx * lax.axis_size("ty") + ty, devices,
        first_swap_ref[0:16, :].astype(f32), second_swap_ref[0:16, :].astype(f32),
    )
    left = strips_of(previous, ty > 0)
    right = strips_of(following, ty < lax.axis_size("ty") - 1)
    gap = jnp.zeros((LANES - 2 * h, tile_rows), f32)
    depth_side, conv_side, rain_side, code_side = [
        transposed(jnp.concatenate([r, gap, l], 0)) for r, l in zip(right, left)
    ]

    def analysed(sums, depth):
        observed = sums[0:tile_rows]
        covered = sums[tile_rows:]
        wet = depth / (depth + wet_depth)
        innovation = (observed - covered * wet) / (covered + 1.0)
        return depth * jnp.exp(innovation)

    level = analysed(summed, depth_ref[...])
    level_ref[...] = level
    sides = (analysed(summed_side, depth_side), rain_side, conv_side, code_side)
    owns = (level, rain_ref, slope_ref, dir_ref)

    def end_rows(at):
        own = [x[at, :] for x in owns]
        own[2] = runoff_coef * jnp.sqrt(own[2])
        own[3] = own[3].astype(f32)
        return jnp.concatenate([jnp.concatenate([o, x[at]], 1) for o, x in zip(own, sides)], 0)

    for i, x in enumerate(sides):
        side_ref[i] = x
    first, second = in_turn(rem(tx, 2) == 0, end_rows(slice(tile_rows - h, tile_rows)), end_rows(slice(0, h)))
    first_ref[...] = first.astype(bf16)
    second_ref[...] = second.astype(bf16)


def substeps(level, rain, conv, code, rain_s, conv_s, m_ref, part_ref, up_ref, down_ref, chunk):
    rows, cols = level.shape
    h = SUBSTEPS
    for ref in (up_ref, down_ref):
        ref[0] = jnp.zeros(ref.shape[1:], f32)
        ref[1, 0:h, :] = jnp.zeros((h, cols), f32)
        ref[1, h + rows :, :] = jnp.zeros((h, cols), f32)
    part_ref[0] = level
    rain_s[...] = rain
    conv_s[...] = conv
    sides = (-1, 0, 1, -1, 1, -1, 0, 1)
    for direction, side in enumerate(sides):
        share = jnp.where(code == direction, conv, 0.0)
        m_ref[direction] = pltpu.roll(share, side % cols, 1) if side else share

    def level_at(buf, r, n):
        level = part_ref[buf, r : r + n, :]
        return level + up_ref[buf, h + r + 1 : h + r + 1 + n, :] + down_ref[buf, h + r - 1 : h + r - 1 + n, :]

    def substep(buf, new):
        for r in range(0, rows, chunk):
            level = level_at(buf, r, chunk)
            power = level * jnp.exp2((2.0 / 3.0 / math.log(2.0)) * jnp.log(jnp.maximum(jnp.abs(level), 1e-30)))
            from_right = pltpu.roll(power, cols - 1, 1)
            from_left = pltpu.roll(power, 1, 1)
            m = [m_ref[d, r : r + chunk, :] for d in range(8)]
            up_ref[new, h + r : h + r + chunk, :] = m[0] * from_right + m[1] * power + m[2] * from_left
            down_ref[new, h + r : h + r + chunk, :] = m[5] * from_right + m[6] * power + m[7] * from_left
            part_ref[new, r : r + chunk, :] = (
                level + rain_s[r : r + chunk, :] - conv_s[r : r + chunk, :] * power
                + (m[3] * from_right + m[4] * from_left)
            )

    def substep_pair(i, carry):
        substep(0, 1)
        substep(1, 0)
        return carry

    if rows > 8 * LANES:
        lax.fori_loop(0, SUBSTEPS // 2, substep_pair, 0)
    else:
        for i in range(SUBSTEPS // 2):
            substep_pair(i, 0)
    return level_at


def flow_inner_kernel(level_ref, side_ref, slope_ref, dir_ref, rain_ref, out_ref, *scratch):
    rows, cols = level_ref.shape
    own = (level_ref[...], rain_ref[...], runoff_coef * jnp.sqrt(slope_ref[...]), dir_ref[...].astype(f32))
    level_at = substeps(*[jnp.concatenate([x, side_ref[i]], 1) for i, x in enumerate(own)], *scratch, 32)
    out_ref[...] = level_at(0, 0, rows)[:, 0:cols]


def flow_ends_kernel(inner_ref, level_ref, side_ref, slope_ref, dir_ref, rain_ref, first_swap_ref, second_swap_ref, out_ref, *scratch):
    rows, cols = level_ref.shape
    h = SUBSTEPS
    above, below = from_turns(
        lax.axis_index("tx"), lax.axis_size("tx"),
        first_swap_ref[...].astype(f32), second_swap_ref[...].astype(f32),
    )
    fields = []
    for i, ref in enumerate((level_ref, rain_ref, slope_ref, dir_ref)):
        ends = []
        for at in (slice(0, 2 * h), slice(rows - 2 * h, rows)):
            own = ref[at, :].astype(f32)
            if i == 2:
                own = runoff_coef * jnp.sqrt(own)
            ends.append(jnp.concatenate([own, side_ref[i, at, :]], 1))
        fields.append(jnp.concatenate([above[i * h : (i + 1) * h], *ends, below[i * h : (i + 1) * h]], 0))
    level_at = substeps(*fields, *scratch, 6 * h)
    out_ref[h : rows - h, :] = inner_ref[h : rows - h, :]
    out_ref[0:h, :] = level_at(0, h, h)[:, 0:cols]
    out_ref[rows - h :, :] = level_at(0, 4 * h, h)[:, 0:cols]


def flow_scratch(rows, cols):
    return [
        pltpu.VMEM((rows, cols), f32),
        pltpu.VMEM((rows, cols), f32),
        pltpu.VMEM((8, rows, cols), f32),
        pltpu.VMEM((2, rows, cols), f32),
        pltpu.VMEM((2, rows + 2 * SUBSTEPS, cols), f32),
        pltpu.VMEM((2, rows + 2 * SUBSTEPS, cols), f32),
    ]


def hbm_specs(n):
    return [pl.BlockSpec(memory_space=pltpu.HBM)] * n


def vmem_specs(n):
    return [pl.BlockSpec(memory_space=pltpu.VMEM)] * n


def per_device(
    sar_image, kernel_first, kernel_second, kernel_third, kernel_last,
    geo_weight, cell_index, block_tile, block_row, depth, slope, flow_dir, rain,
):
    both = ("tx", "ty")
    devices = lax.axis_size(both)
    az_lines, range_px = geo_weight.shape
    tile_rows, tile_cols = depth.shape
    capacity = max(2, 2 * az_lines // devices)

    n_tx, n_ty = lax.axis_size("tx"), lax.axis_size("ty")

    def swaps(first, second, stride):
        size = devices // stride
        out = []
        for start, x in ((1, second), (0, first)):
            to = {}
            for place in range(start, size, 2):
                for k in range(stride):
                    i, j = place * stride + k, (place + 1) % size * stride + k
                    if place == size - 1 and stride > 1:
                        ends = (i, i ^ 1), (j, j ^ 1)
                    else:
                        ends = (i, j), (j, i)
                    to.update(ends)
            out.append(lax.ppermute(x, both, sorted(to.items())))
        return out[::-1]

    params = pltpu.CompilerParams(vmem_limit_bytes=VMEM_LIMIT)
    message = pltpu.VMEM((32, range_px), bf16)
    handed = (
        sar_image,
        jnp.transpose(kernel_first, (2, 3, 1, 0)),
        jnp.transpose(kernel_second, (2, 3, 0, 1)).reshape(9 * CH, CH),
        jnp.transpose(kernel_third, (2, 3, 0, 1)).reshape(9 * CH, CH),
        jnp.transpose(kernel_last[0], (1, 2, 0)),
        block_tile.reshape(1, az_lines),
        block_row.reshape(1, az_lines),
        geo_weight,
        cell_index,
    )
    first, second, sar_image, *handed = pl.pallas_call(
        edge_kernel,
        out_shape=(message, message, *[pltpu.VMEM(x.shape, x.dtype) for x in handed]),
        in_specs=hbm_specs(4 + len(handed)),
        out_specs=tuple(vmem_specs(2 + len(handed))),
        scratch_shapes=[
            *[pltpu.VMEM(x.shape, x.dtype) for x in (depth, slope, rain, flow_dir)],
            pltpu.SemaphoreType.DMA((4 + len(handed),)),
        ],
        compiler_params=pltpu.CompilerParams(vmem_limit_bytes=VMEM_MOST),
        name="edges",
    )(depth, slope, rain, flow_dir, *handed)
    geo_weight, cell_index = handed[-2:]
    halo = swaps(first, second, 1)

    rows, cols = OUT_LINES * CH, IN_LINES * CH
    slots = devices * capacity * 4
    send_rows = tile_cols // LANES * 4 * capacity + 8
    full = (az_lines + 4) // OUT_LINES + 1
    feats = (full * OUT_LINES + 3) * CH
    blocks_in = (az_lines + IN_LINES, range_px)

    def cost(flops):
        return pl.CostEstimate(flops=flops, bytes_accessed=4_000_000, transcendentals=0)

    prepared = pl.pallas_call(
        functools.partial(inner_kernel, devices, capacity),
        out_shape=(
            jax.ShapeDtypeStruct((rows, LANES), bf16),
            jax.ShapeDtypeStruct((MID_LINES * CH, cols), bf16),
            jax.ShapeDtypeStruct((MID_LINES * CH, cols), bf16),
            jax.ShapeDtypeStruct((3 * CH, cols), bf16),
            jax.ShapeDtypeStruct((slots, 2 * END_LINES * CH), bf16),
            jax.ShapeDtypeStruct((8 * devices, LANES), f32),
            jax.ShapeDtypeStruct((az_lines, range_px), bf16),
            jax.ShapeDtypeStruct((slots, tile_cols), f32),
            *[jax.ShapeDtypeStruct((4 * CH, range_px), bf16)] * 3,
        ),
        in_specs=vmem_specs(9),
        out_specs=tuple(vmem_specs(11)),
        scratch_shapes=[
            pltpu.VMEM((24, CH), f32),
            pltpu.VMEM((16, CH), f32),
            pltpu.VMEM((2, *blocks_in), f32),
            pltpu.VMEM((3, feats, range_px), bf16),
            pltpu.VMEM((3, feats, range_px), bf16),
            pltpu.VMEM((feats, range_px), bf16),
            pltpu.VMEM(blocks_in, f32),
            pltpu.VMEM(((az_lines - 2 * END_LINES) * CH, tile_cols // 4), f32),
        ],
        compiler_params=params,
        cost_estimate=cost(8_000_000_000),
        name="inner",
    )(
        *handed[:-2], sar_image, geo_weight, cell_index,
    )
    fraction, send = pl.pallas_call(
        functools.partial(ends_kernel, devices, capacity),
        out_shape=(
            jax.ShapeDtypeStruct((az_lines, range_px), bf16),
            jax.ShapeDtypeStruct((devices * send_rows, LANES), bf16),
        ),
        in_specs=vmem_specs(16),
        out_specs=tuple(vmem_specs(2)),
        scratch_shapes=[pltpu.VMEM((az_lines, range_px), f32)],
        compiler_params=params,
        name="ends",
    )(*halo[::-1], *prepared, sar_image, geo_weight, cell_index)

    got = lax.all_to_all(
        send.reshape(devices, send_rows, LANES), both, split_axis=0, concat_axis=0, tiled=True
    ).reshape(devices * send_rows, LANES)

    wide_cols = tile_cols + LANES
    edge = jax.ShapeDtypeStruct((4 * SUBSTEPS, wide_cols), bf16)
    level, side, first, second = pl.pallas_call(
        functools.partial(level_kernel, devices),
        out_shape=(
            jax.ShapeDtypeStruct((tile_rows, tile_cols), f32),
            jax.ShapeDtypeStruct((4, tile_rows, LANES), f32),
            edge,
            edge,
        ),
        in_specs=vmem_specs(7),
        out_specs=tuple(vmem_specs(4)),
        compiler_params=params,
        name="level",
    )(got, *halo[::-1], depth, slope, rain, flow_dir)

    row_halo = swaps(first, second, n_ty)

    inner = pl.pallas_call(
        flow_inner_kernel,
        out_shape=jax.ShapeDtypeStruct((tile_rows, tile_cols), f32),
        in_specs=vmem_specs(5),
        out_specs=vmem_specs(1)[0],
        scratch_shapes=flow_scratch(tile_rows, wide_cols),
        compiler_params=params,
        cost_estimate=cost(5_000_000_000),
        name="flow_inner",
    )(level, side, slope, flow_dir, rain)
    level = pl.pallas_call(
        flow_ends_kernel,
        out_shape=jax.ShapeDtypeStruct((tile_rows, tile_cols), f32),
        in_specs=vmem_specs(8),
        out_specs=vmem_specs(1)[0],
        scratch_shapes=flow_scratch(6 * SUBSTEPS, wide_cols),
        compiler_params=params,
        name="flow_ends",
    )(inner, level, side, slope, flow_dir, rain, *row_halo)
    return (fraction, level)


def solution(mesh):
    placed = (
        P(None, ("tx", "ty"), None),
        P(),
        P(),
        P(),
        P(),
        P(("tx", "ty"), None),
        P(("tx", "ty"), None),
        P(("tx", "ty"), None),
        P(("tx", "ty"), None),
        P("tx", "ty"),
        P("tx", "ty"),
        P("tx", "ty"),
        P("tx", "ty"),
    )
    return jax.shard_map(
        per_device,
        mesh=mesh,
        in_specs=placed,
        out_specs=(P(("tx", "ty"), None), P("tx", "ty")),
        check_vma=False,
    )
```
